32 devices in a mesh: dp: 8 (over z, y), seq: 4 (over x, core).
Axes of the slice: x: 2, y: 2, z: 4, core: 2. Of those that a mesh axis runs over, the one named last changes fastest.
Arguments:
- frames: bfloat16 [16384, 1024], P(('dp', 'seq')), may hold values from -6 to 6
- cotangent: bfloat16 [16384, 1024], P(('dp', 'seq')), may hold values from -6 to 6
- clip_len: int32 [8, 3], P('dp'), may hold values from 128 to 1792, as said below
- ln1_gain: float32 [1024], replicated, may hold values from 0.5 to 1.5
- ln1_bias: float32 [1024], replicated, may hold values from -1.75 to 1.75
- w_qkv: bfloat16 [1024, 3072], replicated, may hold values from -0.1875 to 0.1875
- w_out: bfloat16 [1024, 1024], replicated, may hold values from -0.75 to 0.75
- scale_attn: float32 [1024], replicated, may hold values from 0.5 to 1.5
- ln2_gain: float32 [1024], replicated, may hold values from 0.5 to 1.5
- ln2_bias: float32 [1024], replicated, may hold values from -1.75 to 1.75
- w_gate_up: bfloat16 [1024, 8192], replicated, may hold values from -0.1875 to 0.1875
- w_down: bfloat16 [4096, 1024], replicated, may hold values from -0.1875 to 0.1875
- scale_mlp: float32 [1024], replicated, may hold values from 0.5 to 1.5
Outputs:
- out_frames: bfloat16 [16384, 1024], P(('dp', 'seq'))
- input_grad: float32 [16384, 1024], P(('dp', 'seq'))
- grad_ln1_gain: float32 [1024], replicated
- grad_ln1_bias: float32 [1024], replicated
- grad_w_qkv: float32 [1024, 3072], P('dp', 'seq')
- grad_w_out: float32 [1024, 1024], P('dp', 'seq')
- grad_scale_attn: float32 [1024], replicated
- grad_ln2_gain: float32 [1024], replicated
- grad_ln2_bias: float32 [1024], replicated
- grad_w_gate_up: float32 [1024, 8192], P('dp', 'seq')
- grad_w_down: float32 [4096, 1024], P('dp', 'seq')
- grad_scale_mlp: float32 [1024], replicated
The draws below stay inside these ranges and needn't reach their ends.
Inputs may be any that keep to these rules, and one draw needn't show every extreme that they name: `clip_len`: each group's clips, followed by padding of at most 32 frames, fill its 2048 frames; one clip of each group begins within the group's first 512 frames and ends within its last 512 frames.
All inputs are finite; a program needn't handle non-finite values.
Results may differ from the reference program's by a relative error of at most 0.015.
Values may be sent and summed in bfloat16 or wider, within the bound.
A program may use at most 256 MiB of HBM per device.

```python
import math
import jax
import jax.numpy as jnp
from jax import lax

D = 1024
HEADS = 16
HEAD_DIM = 64
FF = 4096
HALF = 64
CLIPS = 3
TOK_DEV = 512
QBLK = 512
GROUP = 2048
FRAMES = 16384
N_DP = 8


def draw_clip_len(key, part):
    key = jax.random.fold_in(key, 11)
    subkeys = jax.random.split(key, 4)
    least_len = TOK_DEV // 4
    most_len = 7 * TOK_DEV // 16
    shorts = jax.random.randint(subkeys[0], (N_DP, CLIPS - 1), least_len, most_len)
    padding = jax.random.randint(subkeys[1], (N_DP, 1), 0, TOK_DEV // 16 + 1)
    chosen = jax.random.randint(subkeys[3], (), 0, N_DP)
    is_chosen = jnp.arange(N_DP)[:, None] == chosen
    shorts = jnp.where(is_chosen, least_len, shorts)
    padding = jnp.where(is_chosen, 0, padding)
    longest = GROUP - padding - jnp.sum(shorts, axis=1, keepdims=True)
    long_slot = jax.random.randint(subkeys[2], (N_DP, 1), 0, CLIPS)
    column = jnp.arange(CLIPS)[None, :]
    short_index = jnp.clip(column - (column > long_slot).astype(jnp.int32), 0, CLIPS - 2)
    picked = jnp.take_along_axis(shorts, jnp.broadcast_to(short_index, (N_DP, CLIPS)), axis=1)
    return jnp.where(column == long_slot, longest, picked).astype(jnp.int32)


def block_scale(own_key, dims, shards, least, top_value):
    loudness = 1.0
    for axis_at, shards_of in shards:
        draws = jax.random.uniform(jax.random.fold_in(jax.random.fold_in(own_key, 6), axis_at), (shards_of,), jnp.float32, least / len(shards), top_value / len(shards))
        loudness = loudness * jnp.repeat(jnp.exp(draws), dims[axis_at] // shards_of).reshape((-1,) + (1,) * (len(dims) - 1 - axis_at))
    return loudness


def scatter_about(stream_key, shape, spread, most, cuts=(), held_as=jnp.bfloat16):
    level = block_scale(stream_key, shape, cuts, -0.22, 0.18) if cuts else 1.0
    result = jax.random.normal(stream_key, shape, jnp.float32) * spread * level
    return jnp.minimum(jnp.maximum(result, -most), most).astype(held_as)


def setup_inputs(seed: int = 0) -> dict:
    key_list = jax.random.split(jax.random.key(seed), 14)
    return {
        "frames": scatter_about(key_list[0], (FRAMES, D), 1.0, 6.0, ((0, 32),)),
        "cotangent": scatter_about(key_list[1], (FRAMES, D), 1.0, 6.0, ((0, 32),)),
        "clip_len": draw_clip_len(jax.random.fold_in(key_list[13], 71), 0),
        "ln1_gain": jnp.clip(1.0 + 0.1 * jax.random.normal(key_list[3], (D,), jnp.float32), 0.5, 1.5),
        "ln1_bias": scatter_about(key_list[4], (D,), 0.3, 1.75, (), jnp.float32),
        "w_qkv": scatter_about(key_list[5], (D, 3 * D), D ** -0.5, 0.1875),
        "w_out": scatter_about(key_list[6], (D, D), (D // 16) ** -0.5, 0.75),
        "scale_attn": jnp.clip(jnp.exp(jax.random.uniform(key_list[7], (D,), jnp.float32, math.log(0.5), math.log(1.5))), 0.5, 1.5),
        "ln2_gain": jnp.clip(1.0 + 0.1 * jax.random.normal(key_list[8], (D,), jnp.float32), 0.5, 1.5),
        "ln2_bias": scatter_about(key_list[9], (D,), 0.3, 1.75, (), jnp.float32),
        "w_gate_up": scatter_about(key_list[10], (D, 2 * FF), D ** -0.5, 0.1875),
        "w_down": scatter_about(key_list[11], (FF, D), (FF // 4) ** -0.5, 0.1875),
        "scale_mlp": jnp.clip(jnp.exp(jax.random.uniform(key_list[12], (D,), jnp.float32, math.log(0.5), math.log(1.5))), 0.5, 1.5),
    }


EPS = 1e-05
NEG = -1e+30
HIGH = lax.Precision.HIGHEST

@jax.custom_vjp
def low(v):
    return lax.optimization_barrier(v.astype(jnp.bfloat16)).astype(jnp.float32)

@jax.custom_vjp
def low_back(v):
    return v

def low_keep(v):
    return (low(v), None)

def low_pass(kept, grad):
    return (grad,)

def back_keep(v):
    return (v, None)

def back_low(kept, grad):
    return (low(grad),)
low.defvjp(low_keep, low_pass)
low_back.defvjp(back_keep, back_low)

def layer_norm(values, ln_gain, ln_bias):
    average = lax.optimization_barrier(jnp.mean(values, -1, keepdims=True))
    centered = values - average
    variance = lax.optimization_barrier(jnp.mean(centered * centered, -1, keepdims=True))
    return centered * lax.rsqrt(variance + EPS) * ln_gain + ln_bias

def rotate(values, positions):
    half_dim = values.shape[-1] // 2
    inv_freq = 10000.0 ** (-jnp.arange(half_dim, dtype=jnp.float32) / half_dim)
    angles = positions.astype(jnp.float32)[:, None] * inv_freq[None, :]
    cosine = jnp.cos(angles)[:, None, :]
    sine = jnp.sin(angles)[:, None, :]
    first = values[..., :half_dim]
    second = values[..., half_dim:]
    return jnp.concatenate([first * cosine - second * sine, second * cosine + first * sine], -1)

def segment_ids(lengths, positions, group_len):
    clip_ends = jnp.cumsum(lengths)
    number_ids = lax.optimization_barrier(jnp.sum((positions[:, None] >= clip_ends[None, :]).astype(jnp.int32), axis=1))
    inside = (positions >= 0) & (positions < group_len)
    return jnp.where(inside, number_ids, -1)

def window_mask(query_ids, key_ids):
    offsets = jnp.arange(key_ids.shape[0])[None, :] - jnp.arange(query_ids.shape[0])[:, None]
    return (query_ids[:, None] == key_ids[None, :]) & (offsets >= 0) & (offsets < 2 * HALF)

def window_attention(queries, keys, values, query_ids, key_ids):
    extent = QBLK + 2 * HALF

    def one_block(index):
        start = (index * QBLK).astype(jnp.int32)
        q_block = lax.dynamic_slice_in_dim(queries, start, QBLK, 0)
        k_block = lax.dynamic_slice_in_dim(keys, start, extent, 0)
        v_block = lax.dynamic_slice_in_dim(values, start, extent, 0)
        allowed = window_mask(lax.dynamic_slice_in_dim(query_ids, start, QBLK, 0), lax.dynamic_slice_in_dim(key_ids, start, extent, 0))
        scores = low_back(HEAD_DIM ** (-0.5) * jnp.einsum('qhd,khd->hqk', q_block, k_block, precision=HIGH))
        scores = jnp.where(allowed[None], scores, NEG)
        peaks = lax.optimization_barrier(jnp.max(scores, -1, keepdims=True))
        exponent = jnp.exp(scores - peaks)
        probs = exponent / lax.optimization_barrier(jnp.sum(exponent, -1, keepdims=True))
        return jnp.einsum('hqk,khd->qhd', low(probs), v_block, precision=HIGH)
    blocks_out = lax.map(jax.checkpoint(one_block), jnp.arange(queries.shape[0] // QBLK, dtype=jnp.int32))
    return blocks_out.reshape(queries.shape)

def group_forward(inputs, lengths, params):
    ln1_gain, ln1_bias, w_qkv, w_out, scale_attn, ln2_gain, ln2_bias, w_gate_up, w_down, scale_mlp = params
    positions = jnp.arange(GROUP, dtype=jnp.int32)
    key_pos = jnp.arange(-HALF, GROUP + HALF, dtype=jnp.int32)
    query_ids = segment_ids(lengths, positions, GROUP)
    key_ids = segment_ids(lengths, key_pos, GROUP)
    normed = low(layer_norm(inputs, ln1_gain, ln1_bias))
    projected = low_back(jnp.dot(normed, w_qkv, precision=HIGH))
    turned = rotate(projected[:, :2 * D].reshape(GROUP, 2 * HEADS, HEAD_DIM), positions)
    queries = low(turned[:, :HEADS])
    keys = low(turned[:, HEADS:])
    values = low(projected[:, 2 * D:].reshape(GROUP, HEADS, HEAD_DIM))
    margin = ((HALF, HALF), (0, 0), (0, 0))
    attended = window_attention(queries, jnp.pad(keys, margin), jnp.pad(values, margin), query_ids, key_ids)
    attended = low(low_back(attended.reshape(GROUP, D)))
    branch = low_back(jnp.dot(attended, w_out, precision=HIGH))
    middle = inputs + scale_attn * branch
    normed_two = low(layer_norm(middle, ln2_gain, ln2_bias))
    gate_up = low_back(jnp.dot(normed_two, w_gate_up, precision=HIGH))
    hidden = low(jax.nn.silu(gate_up[:, :FF]) * gate_up[:, FF:])
    mlp_out = low_back(jnp.dot(hidden, w_down, precision=HIGH))
    return middle + scale_mlp * mlp_out

def reference(frames, cotangent, clip_len, ln1_gain, ln1_bias, w_qkv, w_out, scale_attn, ln2_gain, ln2_bias, w_gate_up, w_down, scale_mlp):
    params = (ln1_gain.astype(jnp.float32), ln1_bias.astype(jnp.float32), w_qkv.astype(jnp.float32), w_out.astype(jnp.float32), scale_attn.astype(jnp.float32), ln2_gain.astype(jnp.float32), ln2_bias.astype(jnp.float32), w_gate_up.astype(jnp.float32), w_down.astype(jnp.float32), scale_mlp.astype(jnp.float32))
    grouped = frames.astype(jnp.float32).reshape(N_DP, GROUP, D)

    def forward(inputs, weights):

        def per_group(group_item):
            return jax.checkpoint(group_forward)(group_item[0], group_item[1], weights)
        return lax.map(per_group, (inputs, clip_len))
    outputs, pullback = jax.vjp(forward, grouped, params)
    input_grad, grads = pullback(cotangent.astype(jnp.float32).reshape(N_DP, GROUP, D))
    return (outputs.reshape(FRAMES, D).astype(jnp.bfloat16), input_grad.reshape(FRAMES, D), grads[0], grads[1], grads[2], grads[3], grads[4], grads[5], grads[6], grads[7], grads[8], grads[9])
```

```python
import functools

import jax
import jax.numpy as jnp
from jax import lax
from jax.experimental import pallas as pl
from jax.experimental.pallas import tpu as pltpu
from jax.sharding import PartitionSpec as P

D = 1024
HEADS = 16
HEAD_DIM = 64
FF = 4096
HALF = 64
QBLK = 512


EPS = 1e-05
NEG = -1e30


def layer_norm(values, ln_gain, ln_bias):
    average = jnp.mean(values, -1, keepdims=True)
    centered = values - average
    variance = jnp.mean(centered * centered, -1, keepdims=True)
    return centered * lax.rsqrt(variance + EPS) * ln_gain + ln_bias


def rotate(values, positions):
    half_dim = values.shape[-1] // 2
    inv_freq = 10000.0 ** (-jnp.arange(half_dim, dtype=jnp.float32) / half_dim)
    angles = positions.astype(jnp.float32)[:, None] * inv_freq[None, :]
    cosine = jnp.cos(angles)[:, None, :]
    sine = jnp.sin(angles)[:, None, :]
    first = values[..., :half_dim]
    second = values[..., half_dim:]
    return jnp.concatenate([first * cosine - second * sine, second * cosine + first * sine], -1)


def segment_ids(lengths, positions, group_len):
    clip_ends = jnp.cumsum(lengths)
    number_ids = jnp.sum((positions[:, None] >= clip_ends[None, :]).astype(jnp.int32), axis=1)
    inside = (positions >= 0) & (positions < group_len)
    return jnp.where(inside, number_ids, -1)


def window_mask(query_ids, key_ids):
    offsets = jnp.arange(key_ids.shape[0])[None, :] - jnp.arange(query_ids.shape[0])[:, None]
    return (query_ids[:, None] == key_ids[None, :]) & (offsets >= 0) & (offsets < 2 * HALF)


def gating(gate_up):
    return jax.nn.silu(gate_up[:, :FF]) * gate_up[:, FF:]


def contract_rows(left, right):
    return lax.dot_general(
        left, right, (((0,), (0,)), ((), ())), preferred_element_type=jnp.float32
    )


def contract_back(grads, weight):
    return lax.dot_general(
        grads, weight, (((1,), (1,)), ((), ())), preferred_element_type=jnp.float32
    )


def block_scores(queries, keys, query_ids, key_ids, start):
    extent = QBLK + 2 * HALF
    q_block = lax.dynamic_slice_in_dim(queries, start, QBLK, 0)
    k_block = lax.dynamic_slice_in_dim(keys, start, extent, 0)
    allowed = window_mask(
        lax.dynamic_slice_in_dim(query_ids, start, QBLK, 0),
        lax.dynamic_slice_in_dim(key_ids, start, extent, 0),
    )
    scores = jnp.einsum(
        "qhd,khd->hqk", q_block, k_block, preferred_element_type=jnp.float32
    ) * HEAD_DIM ** (-0.5)
    return (jnp.where(allowed[None], scores, NEG), q_block, k_block)


def attention_forward(queries, keys, values, query_ids, key_ids):

    def one_block(index):
        start = index * QBLK
        scores, q_block, k_block = block_scores(queries, keys, query_ids, key_ids, start)
        v_block = lax.dynamic_slice_in_dim(values, start, QBLK + 2 * HALF, 0)
        peaks = jnp.max(scores, -1, keepdims=True)
        exponent = jnp.exp(scores - peaks)
        totals = jnp.sum(exponent, -1, keepdims=True)
        probs = (exponent / totals).astype(jnp.bfloat16)
        attended = jnp.einsum("hqk,khd->qhd", probs, v_block, preferred_element_type=jnp.float32)
        return (attended, peaks, totals)

    attended, peaks, totals = lax.map(
        one_block, jnp.arange(queries.shape[0] // QBLK, dtype=jnp.int32)
    )
    return (attended.reshape(queries.shape[0], queries.shape[1], queries.shape[2]), peaks, totals)


def attention_backward(queries, keys, values, out_grads, query_ids, key_ids, peaks, totals):
    extent = QBLK + 2 * HALF
    score_scale = HEAD_DIM ** (-0.5)

    def one_block(carry, inputs):
        key_grads, value_grads = carry
        index, peak_block, total_block = inputs
        start = index * QBLK
        scores, q_block, k_block = block_scores(queries, keys, query_ids, key_ids, start)
        v_block = lax.dynamic_slice_in_dim(values, start, extent, 0)
        g_block = lax.dynamic_slice_in_dim(out_grads, start, QBLK, 0)
        probs = jnp.exp(scores - peak_block) / total_block
        value_part = jnp.einsum(
            "hqk,qhd->khd", probs.astype(jnp.bfloat16), g_block, preferred_element_type=jnp.float32
        )
        prob_grads = jnp.einsum(
            "qhd,khd->hqk", g_block, v_block, preferred_element_type=jnp.float32
        )
        inner = jnp.sum(probs * prob_grads, -1, keepdims=True)
        score_grads = (probs * (prob_grads - inner)).astype(jnp.bfloat16)
        query_part = (
            jnp.einsum("hqk,khd->qhd", score_grads, k_block, preferred_element_type=jnp.float32)
            * score_scale
        )
        key_part = (
            jnp.einsum("hqk,qhd->khd", score_grads, q_block, preferred_element_type=jnp.float32)
            * score_scale
        )
        key_grads = lax.dynamic_update_slice_in_dim(
            key_grads, lax.dynamic_slice_in_dim(key_grads, start, extent, 0) + key_part, start, 0
        )
        value_grads = lax.dynamic_update_slice_in_dim(
            value_grads,
            lax.dynamic_slice_in_dim(value_grads, start, extent, 0) + value_part,
            start,
            0,
        )
        return ((key_grads, value_grads), query_part)

    zeros_kv = jnp.zeros(keys.shape, jnp.float32)
    block_count = queries.shape[0] // QBLK
    (key_grads, value_grads), query_grads = lax.scan(
        one_block, (zeros_kv, zeros_kv), (jnp.arange(block_count, dtype=jnp.int32), peaks, totals)
    )
    return (
        query_grads.reshape(queries.shape[0], queries.shape[1], queries.shape[2]),
        key_grads,
        value_grads,
    )


def to_blocks(matrix, data_count, seq_count):
    row_total, col_total = matrix.shape
    shaped = matrix.reshape(data_count, row_total // data_count, seq_count, col_total // seq_count)
    return shaped.transpose(0, 2, 1, 3).reshape(
        data_count * seq_count, row_total // data_count, col_total // seq_count
    )


MESH = pl.DeviceIdType.MESH
TOK = 512
PARTS = (0, 48, 96, 128)

UNITS = (
    [(2, 0, 128, 2, 2048, 256 * v, 2, 0) for v in range(8)]
    + [(3, 128 * v, 512, 3, 256, 0, 3, 128 * v) for v in range(4)]
    + [(1, 0, 128, 1, 256, 0, 1, 0)]
    + [(0, 0, 128, 0, 768, 256 * v, 0, 0) for v in range(3)]
)
LAG = 1


def tn_dot(left, right):
    return lax.dot_general(
        left, right, (((0,), (0,)), ((), ())), preferred_element_type=jnp.float32
    )


def scatter_kernel(
    left0, left1, left2, left3, right0, right1, right2, right3, vec_ref,
    out0, out1, out2, out3, vec_out,
    far_left0, far_left1, far_left2, far_left3, far_right,
    xbuf, ybuf, part_a, part_b, part_c,
    recv_a1, recv_a2, recv_az, recv_b1, recv_b2, recv_bz, recv_cz, recv_c1, recv_c2,
    vec_sum, vec_recv, vec_z,
    far_send, far_recv, load_sem, send_sem, recv_sem, vec_send, vec_rsem,
):
    lefts = (left0, left1, left2, left3)
    rights = (right0, right1, right2, right3)
    outs = (out0, out1, out2, out3)
    far_lefts = (far_left0, far_left1, far_left2, far_left3)
    dp = lax.axis_index("dp")
    seq = lax.axis_index("seq")
    z, y = dp // 2, dp % 2
    x, c = seq // 2, seq % 2
    dev_c = (dp, x * 2 + 1 - c)
    dev_x = (dp, (1 - x) * 2 + c)
    dev_y = (z * 2 + 1 - y, seq)
    dev_z = [(lax.rem(z + k, 4) * 2 + y, seq) for k in (1, 2, 3)]
    count = len(UNITS)

    barrier = pltpu.get_barrier_semaphore()
    for device in [dev_c, dev_x, dev_y] + dev_z:
        pl.semaphore_signal(barrier, inc=1, device_id=device, device_id_type=MESH)
    pl.semaphore_wait(barrier, 6)

    def remote(src, dst, ssem, rsem, device):
        return pltpu.make_async_remote_copy(
            src_ref=src, dst_ref=dst, send_sem=ssem, recv_sem=rsem,
            device_id=device, device_id_type=MESH,
        )

    sends = []

    def block_columns(unit, block):
        _, _, _, right, width, offset, _, _ = UNITS[unit]
        start = pl.multiple_of(block * width + offset, 128)
        return rights[right].at[:, pl.ds(start, 256)]

    left_copy = {}
    right_copies = []
    for unit in range(count):
        left = UNITS[unit][0]
        if left not in left_copy:
            copy = remote(
                lefts[left], far_lefts[left], far_send.at[left], far_recv.at[left], dev_c
            )
            copy.start()
            left_copy[left] = copy
            sends.append(copy)
        pair = []
        for other_x in range(2):
            slot = 4 + 2 * unit + other_x
            copy = remote(
                block_columns(unit, 2 * other_x + 1 - c), far_right.at[unit, other_x],
                far_send.at[slot], far_recv.at[slot], dev_c,
            )
            copy.start()
            pair.append(copy)
            sends.append(copy)
        right_copies.append(pair)

    left_key = [(u[0], u[1]) for u in UNITS]
    left_slot = []
    for unit in range(count):
        if unit and left_key[unit] == left_key[unit - 1]:
            left_slot.append(left_slot[-1])
        else:
            left_slot.append(1 - left_slot[-1] if unit else 0)

    waited_left = set()

    def load(unit):
        left, offset, width, _, _, _, _, _ = UNITS[unit]
        started = []
        if unit == 0 or left_key[unit] != left_key[unit - 1]:
            if left not in waited_left:
                left_copy[left].wait_recv()
                waited_left.add(left)
            slot = left_slot[unit]
            for side, array in enumerate((lefts[left], far_lefts[left])):
                sem = load_sem.at[slot, side]
                if width == 128:
                    copy = pltpu.make_async_copy(array, xbuf.at[slot, side], sem)
                    copy.start()
                    started.append(copy)
                else:
                    for block in range(8):
                        pltpu.make_async_copy(
                            array.at[:, pl.ds(block * width + offset, 128)],
                            xbuf.at[slot, side, :, pl.ds(block * 128, 128)],
                            sem,
                        ).start()
                    started.append(
                        pltpu.make_async_copy(
                            array.at[:, pl.ds(0, 1024)], xbuf.at[slot, side], sem
                        )
                    )
        slot = unit % 2
        for other_x in range(2):
            right_copies[unit][other_x].wait_recv()
            for side in range(2):
                source = (
                    block_columns(unit, 2 * other_x + c) if side == 0 else far_right.at[unit, other_x]
                )
                copy = pltpu.make_async_copy(
                    source,
                    ybuf.at[slot, side, :, pl.ds(other_x * 256, 256)],
                    load_sem.at[2 + slot, 2 * other_x + side],
                )
                copy.start()
                started.append(copy)
        return started

    def multiply(unit):
        xs, ys = left_slot[unit], unit % 2

        def step(zi, carry):
            columns = pl.ds(pl.multiple_of(zi * 256, 256), 256)
            total = tn_dot(xbuf[xs, 0, :, columns], ybuf[ys, 0]) + tn_dot(
                xbuf[xs, 1, :, columns], ybuf[ys, 1]
            )
            total = total.astype(jnp.bfloat16)
            for yi in range(2):
                for xi in range(2):
                    block = total[yi * 128 : yi * 128 + 128, xi * 256 : xi * 256 + 256]
                    part_a[unit, xi, yi, zi] = block[PARTS[0] : PARTS[1]]
                    part_b[unit, yi, xi, zi] = block[PARTS[1] : PARTS[2]]
                    part_c[unit, zi, xi, yi] = block[PARTS[2] : PARTS[3]]
            return carry

        lax.fori_loop(0, 4, step, 0)

    is_end = (z == 0) | (z == 3)
    is_mid = (z == 1) | (z == 2)

    end_low = jnp.where(z == 0, 1, 0)
    end_dir = jnp.where(z == 0, 0, 1)
    end_next = (jnp.where(z == 0, 1, 2) * 2 + y, seq)
    mid_dir = jnp.where(z == 1, 0, 1)
    mid_low = jnp.where(z == 1, 1, 0)
    mid_keep = jnp.where(z == 1, 2, 0)
    mid_next = ((3 - z) * 2 + y, seq)
    back_dir = 1 - mid_dir
    back_low = jnp.where(z == 2, 2, 0)
    back_keep = jnp.where(z == 2, 3, 0)
    back_next = (jnp.where(z == 2, 3, 0) * 2 + y, seq)

    def z_send(unit, which, pieces, recv, number):
        ssem, rsem = send_sem.at[unit, which], recv_sem.at[unit, which]
        if number == 0:
            low, size, way, device = end_low, 3, end_dir, end_next
        elif number == 1:
            low, size, way, device = mid_keep, 2, mid_dir, mid_next
        else:
            low, size, way, device = back_keep, 1, back_dir, back_next
        return remote(
            pieces.at[pl.ds(low, size)], recv.at[way, pl.ds(low, size)],
            ssem.at[2 + number // 2], rsem.at[2 + way], device,
        )

    def z_wait(unit, which, recv, direction, low, size):
        view = recv.at[direction, pl.ds(low, size)]
        pltpu.make_async_copy(view, view, recv_sem.at[unit, which, 2 + direction]).wait()

    def z_round0(unit, which, pieces, recv):
        @pl.when(is_end)
        def _():
            z_send(unit, which, pieces, recv, 0).start()

    def z_round1(unit, which, pieces, recv):
        @pl.when(is_mid)
        def _():
            z_wait(unit, which, recv, mid_dir, mid_low, 3)
            keep = pl.ds(mid_keep, 2)
            pieces[keep] = pieces[keep] + recv[mid_dir, keep]
            z_send(unit, which, pieces, recv, 1).start()

    def z_round2(unit, which, pieces, recv):
        @pl.when(is_mid)
        def _():
            z_wait(unit, which, recv, back_dir, back_low, 2)
            keep = pl.ds(back_keep, 1)
            pieces[keep] = pieces[keep] + recv[back_dir, keep]
            z_send(unit, which, pieces, recv, 2).start()

    def z_final(unit, which, pieces, recv, finish):
        @pl.when(is_end)
        def _():
            z_wait(unit, which, recv, 1 - end_dir, z, 1)
            finish(
                pieces[z].astype(jnp.float32) + recv[1 - end_dir, z].astype(jnp.float32)
            )

        @pl.when(is_mid)
        def _():
            finish(
                pieces[z].astype(jnp.float32)
                + recv[0, z].astype(jnp.float32)
                + recv[1, z].astype(jnp.float32)
            )

    def send(unit, which, index, source, target, device):
        copy = remote(
            source, target, send_sem.at[unit, which, index], recv_sem.at[unit, which, index], device
        )
        copy.start()
        sends.append(copy)
        return copy

    hops = {}

    def put(unit, which, block):
        _, _, _, _, _, offset, out, row = UNITS[unit]
        outs[out][
            row + PARTS[which] : row + PARTS[which + 1], offset : offset + 256
        ] = block

    def stage(unit, number):
        a, b, cc = part_a.at[unit], part_b.at[unit], part_c.at[unit]
        a_z, b_z = a.at[x, y], b.at[y, x]
        rz_a, rz_b, rz_c = recv_az.at[unit], recv_bz.at[unit], recv_cz.at[unit]
        if number == 0:
            hops[unit, 0, 0] = send(unit, 0, 0, a.at[1 - x], recv_a1.at[unit], dev_x)
            hops[unit, 1, 0] = send(unit, 1, 0, b.at[1 - y], recv_b1.at[unit], dev_y)
            z_round0(unit, 2, cc, rz_c)
        if number == 1:
            hops[unit, 0, 0].wait_recv()
            a[x] = a[x] + recv_a1[unit]
            hops[unit, 0, 1] = send(unit, 0, 1, a.at[x, 1 - y], recv_a2.at[unit], dev_y)
            hops[unit, 1, 0].wait_recv()
            b[y] = b[y] + recv_b1[unit]
            hops[unit, 1, 1] = send(unit, 1, 1, b.at[y, 1 - x], recv_b2.at[unit], dev_x)
            z_round1(unit, 2, cc, rz_c)
        if number == 2:
            hops[unit, 0, 1].wait_recv()
            a[x, y] = a[x, y] + recv_a2[unit]
            z_round0(unit, 0, a_z, rz_a)
            hops[unit, 1, 1].wait_recv()
            b[y, x] = b[y, x] + recv_b2[unit]
            z_round0(unit, 1, b_z, rz_b)
            z_round2(unit, 2, cc, rz_c)
        if number == 3:
            z_round1(unit, 0, a_z, rz_a)
            z_round1(unit, 1, b_z, rz_b)

            def keep(value):
                cc[z] = value.astype(jnp.bfloat16)

            z_final(unit, 2, cc, rz_c, keep)
            hops[unit, 2, 0] = send(unit, 2, 0, cc.at[z, 1 - x], recv_c1.at[unit], dev_x)
        if number == 4:
            z_round2(unit, 0, a_z, rz_a)
            z_round2(unit, 1, b_z, rz_b)
            hops[unit, 2, 0].wait_recv()
            cc[z, x] = cc[z, x] + recv_c1[unit]
            hops[unit, 2, 1] = send(unit, 2, 1, cc.at[z, x, 1 - y], recv_c2.at[unit], dev_y)
        if number == 5:
            z_final(unit, 0, a_z, rz_a, functools.partial(put, unit, 0))
            z_final(unit, 1, b_z, rz_b, functools.partial(put, unit, 1))
            hops[unit, 2, 1].wait_recv()
            put(unit, 2, cc[z, x, y].astype(jnp.float32) + recv_c2[unit].astype(jnp.float32))

    vec_hops = {}

    def vec_stage(number):
        if number == 0:
            vec_sum[0] = vec_ref[...]
        elif number <= 3:
            vec_hops[number - 1].wait_recv()
            vec_sum[number] = vec_sum[number - 1] + vec_recv[number - 1]
        if number < 3:
            copy = remote(
                vec_sum.at[number], vec_recv.at[number], vec_send.at[number],
                vec_rsem.at[number], (dev_c, dev_x, dev_y)[number],
            )
            copy.start()
            sends.append(copy)
            vec_hops[number] = copy
        elif number == 3:
            vec_z[z] = vec_sum[3]
            for k in range(3):
                copy = remote(
                    vec_sum.at[3], vec_z.at[z], vec_send.at[3 + k], vec_rsem.at[3 + k], dev_z[k]
                )
                copy.start()
                sends.append(copy)
                vec_hops[3 + k] = copy
        elif number == 4:
            for k in range(3):
                source = lax.rem(z + 3 - k, 4)
                view = vec_z.at[source]
                pltpu.make_async_copy(view, view, vec_rsem.at[3 + k]).wait()
            vec_out[...] = vec_z[0] + vec_z[1] + vec_z[2] + vec_z[3]

    loads = {0: load(0)}
    for slot in range(count + 5 + LAG):
        if slot + 1 < count:
            loads[slot + 1] = load(slot + 1)
        if slot < count:
            for copy in loads[slot]:
                copy.wait()
            multiply(slot)
            stage(slot, 0)
        for number in range(1, 6):
            unit = slot - number - LAG
            if 0 <= unit < count:
                stage(unit, number)
        if slot < 5:
            vec_stage(slot)

    for copy in sends:
        copy.wait_send()
    for unit in range(count):
        for which, (pieces, recv) in enumerate(
            (
                (part_a.at[unit, x, y], recv_az.at[unit]),
                (part_b.at[unit, y, x], recv_bz.at[unit]),
                (part_c.at[unit], recv_cz.at[unit]),
            )
        ):

            @pl.when(is_end)
            def _():
                z_send(unit, which, pieces, recv, 0).wait_send()

            @pl.when(is_mid)
            def _():
                z_send(unit, which, pieces, recv, 1).wait_send()
                z_send(unit, which, pieces, recv, 2).wait_send()


def reduce_weights(lefts, rights, vectors):
    count = len(UNITS)
    bf = jnp.bfloat16
    hbm = pl.BlockSpec(memory_space=pl.ANY)
    vmem = pl.BlockSpec(memory_space=pltpu.VMEM)
    size = (PARTS[1], PARTS[2] - PARTS[1], PARTS[3] - PARTS[2])
    f32 = jnp.float32
    scratch = [
        pltpu.VMEM((2, 2, TOK, 1024), bf),
        pltpu.VMEM((2, 2, TOK, 512), bf),
        pltpu.VMEM((count, 2, 2, 4, size[0], 256), bf),
        pltpu.VMEM((count, 2, 2, 4, size[1], 256), bf),
        pltpu.VMEM((count, 4, 2, 2, size[2], 256), bf),
        pltpu.VMEM((count, 2, 4, size[0], 256), bf),
        pltpu.VMEM((count, 4, size[0], 256), bf),
        pltpu.VMEM((count, 2, 4, size[0], 256), bf),
        pltpu.VMEM((count, 2, 4, size[1], 256), bf),
        pltpu.VMEM((count, 4, size[1], 256), bf),
        pltpu.VMEM((count, 2, 4, size[1], 256), bf),
        pltpu.VMEM((count, 2, 4, 2, 2, size[2], 256), bf),
        pltpu.VMEM((count, 2, size[2], 256), bf),
        pltpu.VMEM((count, size[2], 256), bf),
        pltpu.VMEM((4, 8, 1024), f32),
        pltpu.VMEM((3, 8, 1024), f32),
        pltpu.VMEM((4, 8, 1024), f32),
        pltpu.SemaphoreType.DMA((4 + 2 * count,)),
        pltpu.SemaphoreType.DMA((4 + 2 * count,)),
        pltpu.SemaphoreType.DMA((4, 4)),
        pltpu.SemaphoreType.DMA((count, 3, 4)),
        pltpu.SemaphoreType.DMA((count, 3, 4)),
        pltpu.SemaphoreType.DMA((6,)),
        pltpu.SemaphoreType.DMA((6,)),
    ]
    shape = jax.ShapeDtypeStruct
    return pl.pallas_call(
        scatter_kernel,
        out_shape=[
            shape((128, 768), f32),
            shape((128, 256), f32),
            shape((128, 2048), f32),
            shape((512, 256), f32),
            shape((8, 1024), f32),
        ]
        + [shape(v.shape, bf) for v in lefts]
        + [shape((count, 2, TOK, 256), bf)],
        in_specs=[hbm] * 8 + [vmem],
        out_specs=[vmem] * 5 + [hbm] * 5,
        scratch_shapes=scratch,
        compiler_params=pltpu.CompilerParams(
            collective_id=1, has_side_effects=True, vmem_limit_bytes=62 * 2**20
        ),
        name="scatter_sums",
    )(*lefts, *rights, vectors)[:5]


def local(
    frames,
    cotangent,
    clip_len,
    ln1_gain,
    ln1_bias,
    w_qkv,
    w_out,
    scale_attn,
    ln2_gain,
    ln2_bias,
    w_gate_up,
    w_down,
    scale_mlp,
):
    row_count = frames.shape[0]
    seq_count = lax.axis_size("seq")
    group_len = row_count * seq_count
    lengths = clip_len[0]
    own_pos = lax.axis_index("seq") * row_count + jnp.arange(row_count, dtype=jnp.int32)
    inputs32 = frames.astype(jnp.float32)
    normed, norm_back = jax.vjp(layer_norm, inputs32, ln1_gain, ln1_bias)
    normed_b = normed.astype(jnp.bfloat16)
    projected = jnp.dot(normed_b, w_qkv, preferred_element_type=jnp.float32)
    turned = rotate(projected[:, : 2 * D].reshape(row_count, 2 * HEADS, HEAD_DIM), own_pos)
    rotated = jnp.concatenate([turned.reshape(row_count, 2 * D), projected[:, 2 * D :]], 1).astype(
        jnp.bfloat16
    )
    margin = ((HALF, HALF), (0, 0), (0, 0))
    q_heads, k_heads, v_heads = (
        lax.all_to_all(rotated[:, :D], "seq", split_axis=1, concat_axis=0, tiled=True),
        lax.all_to_all(rotated[:, D : 2 * D], "seq", split_axis=1, concat_axis=0, tiled=True),
        lax.all_to_all(rotated[:, 2 * D :], "seq", split_axis=1, concat_axis=0, tiled=True),
    )
    local_heads = HEADS // seq_count
    all_pos = jnp.arange(group_len, dtype=jnp.int32)
    query_ids = segment_ids(lengths, all_pos, group_len)
    key_ids = segment_ids(lengths, jnp.arange(-HALF, group_len + HALF, dtype=jnp.int32), group_len)
    queries = q_heads.reshape(group_len, local_heads, HEAD_DIM)
    keys = jnp.pad(k_heads.reshape(group_len, local_heads, HEAD_DIM), margin)
    values = jnp.pad(v_heads.reshape(group_len, local_heads, HEAD_DIM), margin)
    attended, peaks, totals = attention_forward(queries, keys, values, query_ids, key_ids)
    attended_t = lax.all_to_all(
        attended.reshape(group_len, local_heads * HEAD_DIM).astype(jnp.bfloat16),
        "seq",
        split_axis=0,
        concat_axis=1,
        tiled=True,
    )
    branch = jnp.dot(attended_t, w_out, preferred_element_type=jnp.float32)
    middle = inputs32 + scale_attn * branch
    normed_two, norm_two_back = jax.vjp(layer_norm, middle, ln2_gain, ln2_bias)
    normed_two_b = normed_two.astype(jnp.bfloat16)
    gate_up = jnp.dot(normed_two_b, w_gate_up, preferred_element_type=jnp.float32)
    hidden, gate_back = jax.vjp(gating, gate_up)
    hidden_b = hidden.astype(jnp.bfloat16)
    mlp_out = jnp.dot(hidden_b, w_down, preferred_element_type=jnp.float32)
    out_frames = (middle + scale_mlp * mlp_out).astype(jnp.bfloat16)
    out_grad = cotangent.astype(jnp.float32)
    grad_scale_mlp = jnp.sum(out_grad * mlp_out, 0)
    mlp_grad = (out_grad * scale_mlp).astype(jnp.bfloat16)
    hidden_grad = contract_back(mlp_grad, w_down)
    (gate_up_grad,) = gate_back(hidden_grad)
    gate_up_b = gate_up_grad.astype(jnp.bfloat16)
    middle_part, grad_ln2_gain, grad_ln2_bias = norm_two_back(contract_back(gate_up_b, w_gate_up))
    middle_grad = out_grad + middle_part
    grad_scale_attn = jnp.sum(middle_grad * branch, 0)
    branch_grad = (middle_grad * scale_attn).astype(jnp.bfloat16)
    attended_grad = contract_back(branch_grad, w_out).astype(jnp.bfloat16)
    grad_heads = lax.all_to_all(attended_grad, "seq", split_axis=1, concat_axis=0, tiled=True)
    query_grads, key_grads, value_grads = attention_backward(
        queries,
        keys,
        values,
        grad_heads.reshape(group_len, local_heads, HEAD_DIM),
        query_ids,
        key_ids,
        peaks,
        totals,
    )
    query_back = (
        rotate(query_grads, -all_pos)
        .reshape(group_len, local_heads * HEAD_DIM)
        .astype(jnp.bfloat16)
    )
    key_back = (
        rotate(key_grads[HALF : HALF + group_len], -all_pos)
        .reshape(group_len, local_heads * HEAD_DIM)
        .astype(jnp.bfloat16)
    )
    value_back = (
        value_grads[HALF : HALF + group_len]
        .reshape(group_len, local_heads * HEAD_DIM)
        .astype(jnp.bfloat16)
    )
    query_own, key_own, value_own = (
        lax.all_to_all(query_back, "seq", split_axis=0, concat_axis=1, tiled=True),
        lax.all_to_all(key_back, "seq", split_axis=0, concat_axis=1, tiled=True),
        lax.all_to_all(value_back, "seq", split_axis=0, concat_axis=1, tiled=True),
    )
    projected_grad = jnp.concatenate([query_own, key_own, value_own], 1)
    input_part, grad_ln1_gain, grad_ln1_bias = norm_back(contract_back(projected_grad, w_qkv))
    input_grad = middle_grad + input_part
    vector_grads = jnp.stack(
        [
            grad_ln1_gain,
            grad_ln1_bias,
            grad_scale_attn,
            grad_ln2_gain,
            grad_ln2_bias,
            grad_scale_mlp,
        ],
        0,
    )
    data_count = lax.axis_size("dp")
    lefts = (normed_b, attended_t, normed_two_b, hidden_b)
    rights = (projected_grad, branch_grad, gate_up_b, mlp_grad)
    if (data_count, seq_count, row_count) == (8, 4, TOK):
        padded = jnp.concatenate([vector_grads, jnp.zeros((2, D), jnp.float32)], 0)
        sum_qkv, sum_out, sum_gate_up, sum_down, vector_total = reduce_weights(
            lefts, rights, padded
        )
    else:
        vector_total = lax.psum(vector_grads, ("dp", "seq"))
        sum_qkv, sum_out, sum_gate_up, sum_down = [
            lax.psum_scatter(
                to_blocks(contract_rows(left, right), data_count, seq_count),
                ("dp", "seq"),
                scatter_dimension=0,
                tiled=True,
            )[0]
            for left, right in zip(lefts, rights)
        ]
    return (
        out_frames,
        input_grad,
        vector_total[0],
        vector_total[1],
        sum_qkv,
        sum_out,
        vector_total[2],
        vector_total[3],
        vector_total[4],
        sum_gate_up,
        sum_down,
        vector_total[5],
    )


def solution(mesh):
    return jax.shard_map(
        local,
        mesh=mesh,
        in_specs=(
            P(("dp", "seq"), None),
            P(("dp", "seq"), None),
            P("dp", None),
            P(),
            P(),
            P(),
            P(),
            P(),
            P(),
            P(),
            P(),
            P(),
            P(),
        ),
        out_specs=(
            P(("dp", "seq"), None),
            P(("dp", "seq"), None),
            P(),
            P(),
            P("dp", "seq"),
            P("dp", "seq"),
            P(),
            P(),
            P(),
            P("dp", "seq"),
            P("dp", "seq"),
            P(),
        ),
        check_vma=False,
    )
```

```python
import functools

import jax
import jax.numpy as jnp
from jax import lax
from jax.experimental import pallas as pl
from jax.experimental.pallas import tpu as pltpu
from jax.sharding import PartitionSpec as P

D = 1024
HEADS = 16
HEAD_DIM = 64
FF = 4096
HALF = 64
QBLK = 512


EPS = 1e-05
NEG = -1e30


def contract_rows(left, right):
    return lax.dot_general(
        left, right, (((0,), (0,)), ((), ())), preferred_element_type=jnp.float32
    )


def contract_back(grads, weight):
    return lax.dot_general(
        grads, weight, (((1,), (1,)), ((), ())), preferred_element_type=jnp.float32
    )


def to_blocks(matrix, data_count, seq_count):
    row_total, col_total = matrix.shape
    shaped = matrix.reshape(data_count, row_total // data_count, seq_count, col_total // seq_count)
    return shaped.transpose(0, 2, 1, 3).reshape(
        data_count * seq_count, row_total // data_count, col_total // seq_count
    )


MESH = pl.DeviceIdType.MESH
TOK = 512
PARTS = (0, 48, 96, 128)

UNITS = (
    [(2, 0, 128, 2, 2048, 256 * v, 2, 0) for v in range(8)]
    + [(3, 128 * v, 512, 3, 256, 0, 3, 128 * v) for v in range(4)]
    + [(1, 0, 128, 1, 256, 0, 1, 0)]
    + [(0, 0, 128, 0, 768, 256 * v, 0, 0) for v in range(3)]
)
LAG = 1


def tn_dot(left, right):
    return lax.dot_general(
        left, right, (((0,), (0,)), ((), ())), preferred_element_type=jnp.float32
    )


def scatter_kernel(
    left0, left1, left2, left3, right0, right1, right2, right3, vec_ref,
    out0, out1, out2, out3, vec_out,
    far_left0, far_left1, far_left2, far_left3, far_right,
    xbuf, ybuf, part_a, part_b, part_c,
    recv_a1, recv_a2, recv_az, recv_b1, recv_b2, recv_bz, recv_cz, recv_c1, recv_c2,
    vec_sum, vec_recv, vec_z,
    far_send, far_recv, load_sem, send_sem, recv_sem, vec_send, vec_rsem,
):
    lefts = (left0, left1, left2, left3)
    rights = (right0, right1, right2, right3)
    outs = (out0, out1, out2, out3)
    far_lefts = (far_left0, far_left1, far_left2, far_left3)
    dp = lax.axis_index("dp")
    seq = lax.axis_index("seq")
    z, y = dp // 2, dp % 2
    x, c = seq // 2, seq % 2
    dev_c = (dp, x * 2 + 1 - c)
    dev_x = (dp, (1 - x) * 2 + c)
    dev_y = (z * 2 + 1 - y, seq)
    dev_z = [(lax.rem(z + k, 4) * 2 + y, seq) for k in (1, 2, 3)]
    count = len(UNITS)

    barrier = pltpu.get_barrier_semaphore()
    for device in [dev_c, dev_x, dev_y] + dev_z:
        pl.semaphore_signal(barrier, inc=1, device_id=device, device_id_type=MESH)
    pl.semaphore_wait(barrier, 6)

    def remote(src, dst, ssem, rsem, device):
        return pltpu.make_async_remote_copy(
            src_ref=src, dst_ref=dst, send_sem=ssem, recv_sem=rsem,
            device_id=device, device_id_type=MESH,
        )

    sends = []

    def block_columns(unit, block):
        _, _, _, right, width, offset, _, _ = UNITS[unit]
        start = pl.multiple_of(block * width + offset, 128)
        return rights[right].at[:, pl.ds(start, 256)]

    left_copy = {}
    right_copies = []
    for unit in range(count):
        left = UNITS[unit][0]
        if left not in left_copy:
            copy = remote(
                lefts[left], far_lefts[left], far_send.at[left], far_recv.at[left], dev_c
            )
            copy.start()
            left_copy[left] = copy
            sends.append(copy)
        pair = []
        for other_x in range(2):
            slot = 4 + 2 * unit + other_x
            copy = remote(
                block_columns(unit, 2 * other_x + 1 - c), far_right.at[unit, other_x],
                far_send.at[slot], far_recv.at[slot], dev_c,
            )
            copy.start()
            pair.append(copy)
            sends.append(copy)
        right_copies.append(pair)

    left_key = [(u[0], u[1]) for u in UNITS]
    left_slot = []
    for unit in range(count):
        if unit and left_key[unit] == left_key[unit - 1]:
            left_slot.append(left_slot[-1])
        else:
            left_slot.append(1 - left_slot[-1] if unit else 0)

    waited_left = set()

    def load(unit):
        left, offset, width, _, _, _, _, _ = UNITS[unit]
        started = []
        if unit == 0 or left_key[unit] != left_key[unit - 1]:
            if left not in waited_left:
                left_copy[left].wait_recv()
                waited_left.add(left)
            slot = left_slot[unit]
            for side, array in enumerate((lefts[left], far_lefts[left])):
                sem = load_sem.at[slot, side]
                if width == 128:
                    copy = pltpu.make_async_copy(array, xbuf.at[slot, side], sem)
                    copy.start()
                    started.append(copy)
                else:
                    for block in range(8):
                        pltpu.make_async_copy(
                            array.at[:, pl.ds(block * width + offset, 128)],
                            xbuf.at[slot, side, :, pl.ds(block * 128, 128)],
                            sem,
                        ).start()
                    started.append(
                        pltpu.make_async_copy(
                            array.at[:, pl.ds(0, 1024)], xbuf.at[slot, side], sem
                        )
                    )
        slot = unit % 2
        for other_x in range(2):
            right_copies[unit][other_x].wait_recv()
            for side in range(2):
                source = (
                    block_columns(unit, 2 * other_x + c) if side == 0 else far_right.at[unit, other_x]
                )
                copy = pltpu.make_async_copy(
                    source,
                    ybuf.at[slot, side, :, pl.ds(other_x * 256, 256)],
                    load_sem.at[2 + slot, 2 * other_x + side],
                )
                copy.start()
                started.append(copy)
        return started

    def multiply(unit):
        xs, ys = left_slot[unit], unit % 2

        def step(zi, carry):
            columns = pl.ds(pl.multiple_of(zi * 256, 256), 256)
            total = tn_dot(xbuf[xs, 0, :, columns], ybuf[ys, 0]) + tn_dot(
                xbuf[xs, 1, :, columns], ybuf[ys, 1]
            )
            total = total.astype(jnp.bfloat16)
            for yi in range(2):
                for xi in range(2):
                    block = total[yi * 128 : yi * 128 + 128, xi * 256 : xi * 256 + 256]
                    part_a[unit, xi, yi, zi] = block[PARTS[0] : PARTS[1]]
                    part_b[unit, yi, xi, zi] = block[PARTS[1] : PARTS[2]]
                    part_c[unit, zi, xi, yi] = block[PARTS[2] : PARTS[3]]
            return carry

        lax.fori_loop(0, 4, step, 0)

    is_end = (z == 0) | (z == 3)
    is_mid = (z == 1) | (z == 2)

    end_low = jnp.where(z == 0, 1, 0)
    end_dir = jnp.where(z == 0, 0, 1)
    end_next = (jnp.where(z == 0, 1, 2) * 2 + y, seq)
    mid_dir = jnp.where(z == 1, 0, 1)
    mid_low = jnp.where(z == 1, 1, 0)
    mid_keep = jnp.where(z == 1, 2, 0)
    mid_next = ((3 - z) * 2 + y, seq)
    back_dir = 1 - mid_dir
    back_low = jnp.where(z == 2, 2, 0)
    back_keep = jnp.where(z == 2, 3, 0)
    back_next = (jnp.where(z == 2, 3, 0) * 2 + y, seq)

    def z_send(unit, which, pieces, recv, number):
        ssem, rsem = send_sem.at[unit, which], recv_sem.at[unit, which]
        if number == 0:
            low, size, way, device = end_low, 3, end_dir, end_next
        elif number == 1:
            low, size, way, device = mid_keep, 2, mid_dir, mid_next
        else:
            low, size, way, device = back_keep, 1, back_dir, back_next
        return remote(
            pieces.at[pl.ds(low, size)], recv.at[way, pl.ds(low, size)],
            ssem.at[2 + number // 2], rsem.at[2 + way], device,
        )

    def z_wait(unit, which, recv, direction, low, size):
        view = recv.at[direction, pl.ds(low, size)]
        pltpu.make_async_copy(view, view, recv_sem.at[unit, which, 2 + direction]).wait()

    def z_round0(unit, which, pieces, recv):
        @pl.when(is_end)
        def _():
            z_send(unit, which, pieces, recv, 0).start()

    def z_round1(unit, which, pieces, recv):
        @pl.when(is_mid)
        def _():
            z_wait(unit, which, recv, mid_dir, mid_low, 3)
            keep = pl.ds(mid_keep, 2)
            pieces[keep] = pieces[keep] + recv[mid_dir, keep]
            z_send(unit, which, pieces, recv, 1).start()

    def z_round2(unit, which, pieces, recv):
        @pl.when(is_mid)
        def _():
            z_wait(unit, which, recv, back_dir, back_low, 2)
            keep = pl.ds(back_keep, 1)
            pieces[keep] = pieces[keep] + recv[back_dir, keep]
            z_send(unit, which, pieces, recv, 2).start()

    def z_final(unit, which, pieces, recv, finish):
        @pl.when(is_end)
        def _():
            z_wait(unit, which, recv, 1 - end_dir, z, 1)
            finish(
                pieces[z].astype(jnp.float32) + recv[1 - end_dir, z].astype(jnp.float32)
            )

        @pl.when(is_mid)
        def _():
            finish(
                pieces[z].astype(jnp.float32)
                + recv[0, z].astype(jnp.float32)
                + recv[1, z].astype(jnp.float32)
            )

    def send(unit, which, index, source, target, device):
        copy = remote(
            source, target, send_sem.at[unit, which, index], recv_sem.at[unit, which, index], device
        )
        copy.start()
        sends.append(copy)
        return copy

    hops = {}

    def put(unit, which, block):
        _, _, _, _, _, offset, out, row = UNITS[unit]
        outs[out][
            row + PARTS[which] : row + PARTS[which + 1], offset : offset + 256
        ] = block

    def stage(unit, number):
        a, b, cc = part_a.at[unit], part_b.at[unit], part_c.at[unit]
        a_z, b_z = a.at[x, y], b.at[y, x]
        rz_a, rz_b, rz_c = recv_az.at[unit], recv_bz.at[unit], recv_cz.at[unit]
        if number == 0:
            hops[unit, 0, 0] = send(unit, 0, 0, a.at[1 - x], recv_a1.at[unit], dev_x)
            hops[unit, 1, 0] = send(unit, 1, 0, b.at[1 - y], recv_b1.at[unit], dev_y)
            z_round0(unit, 2, cc, rz_c)
        if number == 1:
            hops[unit, 0, 0].wait_recv()
            a[x] = a[x] + recv_a1[unit]
            hops[unit, 0, 1] = send(unit, 0, 1, a.at[x, 1 - y], recv_a2.at[unit], dev_y)
            hops[unit, 1, 0].wait_recv()
            b[y] = b[y] + recv_b1[unit]
            hops[unit, 1, 1] = send(unit, 1, 1, b.at[y, 1 - x], recv_b2.at[unit], dev_x)
            z_round1(unit, 2, cc, rz_c)
        if number == 2:
            hops[unit, 0, 1].wait_recv()
            a[x, y] = a[x, y] + recv_a2[unit]
            z_round0(unit, 0, a_z, rz_a)
            hops[unit, 1, 1].wait_recv()
            b[y, x] = b[y, x] + recv_b2[unit]
            z_round0(unit, 1, b_z, rz_b)
            z_round2(unit, 2, cc, rz_c)
        if number == 3:
            z_round1(unit, 0, a_z, rz_a)
            z_round1(unit, 1, b_z, rz_b)

            def keep(value):
                cc[z] = value.astype(jnp.bfloat16)

            z_final(unit, 2, cc, rz_c, keep)
            hops[unit, 2, 0] = send(unit, 2, 0, cc.at[z, 1 - x], recv_c1.at[unit], dev_x)
        if number == 4:
            z_round2(unit, 0, a_z, rz_a)
            z_round2(unit, 1, b_z, rz_b)
            hops[unit, 2, 0].wait_recv()
            cc[z, x] = cc[z, x] + recv_c1[unit]
            hops[unit, 2, 1] = send(unit, 2, 1, cc.at[z, x, 1 - y], recv_c2.at[unit], dev_y)
        if number == 5:
            z_final(unit, 0, a_z, rz_a, functools.partial(put, unit, 0))
            z_final(unit, 1, b_z, rz_b, functools.partial(put, unit, 1))
            hops[unit, 2, 1].wait_recv()
            put(unit, 2, cc[z, x, y].astype(jnp.float32) + recv_c2[unit].astype(jnp.float32))

    vec_hops = {}

    def vec_stage(number):
        if number == 0:
            vec_sum[0] = vec_ref[...]
        elif number <= 3:
            vec_hops[number - 1].wait_recv()
            vec_sum[number] = vec_sum[number - 1] + vec_recv[number - 1]
        if number < 3:
            copy = remote(
                vec_sum.at[number], vec_recv.at[number], vec_send.at[number],
                vec_rsem.at[number], (dev_c, dev_x, dev_y)[number],
            )
            copy.start()
            sends.append(copy)
            vec_hops[number] = copy
        elif number == 3:
            vec_z[z] = vec_sum[3]
            for k in range(3):
                copy = remote(
                    vec_sum.at[3], vec_z.at[z], vec_send.at[3 + k], vec_rsem.at[3 + k], dev_z[k]
                )
                copy.start()
                sends.append(copy)
                vec_hops[3 + k] = copy
        elif number == 4:
            for k in range(3):
                source = lax.rem(z + 3 - k, 4)
                view = vec_z.at[source]
                pltpu.make_async_copy(view, view, vec_rsem.at[3 + k]).wait()
            vec_out[...] = vec_z[0] + vec_z[1] + vec_z[2] + vec_z[3]

    loads = {0: load(0)}
    for slot in range(count + 5 + LAG):
        if slot + 1 < count:
            loads[slot + 1] = load(slot + 1)
        if slot < count:
            for copy in loads[slot]:
                copy.wait()
            multiply(slot)
            stage(slot, 0)
        for number in range(1, 6):
            unit = slot - number - LAG
            if 0 <= unit < count:
                stage(unit, number)
        if slot < 5:
            vec_stage(slot)

    for copy in sends:
        copy.wait_send()
    for unit in range(count):
        for which, (pieces, recv) in enumerate(
            (
                (part_a.at[unit, x, y], recv_az.at[unit]),
                (part_b.at[unit, y, x], recv_bz.at[unit]),
                (part_c.at[unit], recv_cz.at[unit]),
            )
        ):

            @pl.when(is_end)
            def _():
                z_send(unit, which, pieces, recv, 0).wait_send()

            @pl.when(is_mid)
            def _():
                z_send(unit, which, pieces, recv, 1).wait_send()
                z_send(unit, which, pieces, recv, 2).wait_send()


def rotated(values, cosines, sines):
    lane = lax.broadcasted_iota(jnp.int32, values.shape, 1)
    partner = jnp.where(
        lane % HEAD_DIM < HEAD_DIM // 2,
        pltpu.roll(values, 128 - HEAD_DIM // 2, 1),
        pltpu.roll(values, HEAD_DIM // 2, 1),
    )
    return values * cosines + partner * sines


def head_masks():
    lane = lax.broadcasted_iota(jnp.int32, (128, 128), 1)
    return lane < HEAD_DIM


def stacked(pair):
    first = head_masks()
    zero = jnp.zeros_like(pair)
    return jnp.concatenate([jnp.where(first, pair, zero), jnp.where(first, zero, pair)], 0)


def merged(rows):
    return jnp.where(head_masks(), rows[:128], rows[128:])


def clip_number(positions, ends, group_len):
    total = jnp.zeros_like(positions)
    for end in ends:
        total = total + (positions >= end).astype(jnp.int32)
    return jnp.where((positions >= 0) & (positions < group_len), total, -1)


def normalize(values):
    average = jnp.mean(values, -1, keepdims=True)
    centered = values - average
    inverse = lax.rsqrt(jnp.mean(centered * centered, -1, keepdims=True) + EPS)
    return centered * inverse, inverse


def dot(left, right):
    return jnp.dot(left, right, preferred_element_type=jnp.float32)


def norm_backward(grads, hat, inverse, gain):
    scaled = grads * gain
    return inverse * (
        scaled
        - jnp.mean(scaled, -1, keepdims=True)
        - hat * jnp.mean(scaled * hat, -1, keepdims=True)
    )


def window_bias(bias_ref, clip_ref, group_len, keys_first):
    seq = lax.axis_index("seq")
    first_end = clip_ref[0, 0]
    second_end = first_end + clip_ref[0, 1]
    ends = (first_end, second_end, second_end + clip_ref[0, 2])
    for block in range(TOK // 128):
        start = seq * TOK + block * 128
        shape = (2 * 128, 2 * 128)
        k_axis = 0 if keys_first else 1
        k_at = lax.broadcasted_iota(jnp.int32, shape, k_axis)
        q_at = lax.rem(lax.broadcasted_iota(jnp.int32, shape, 1 - k_axis), 128)
        q_shape = (1, 256) if keys_first else (256, 1)
        k_shape = (256, 1) if keys_first else (1, 256)
        q_ids = clip_number(
            start + lax.rem(lax.broadcasted_iota(jnp.int32, q_shape, 1 - k_axis), 128),
            ends, group_len,
        )
        k_ids = clip_number(
            start - HALF + lax.broadcasted_iota(jnp.int32, k_shape, k_axis), ends, group_len
        )
        seen = (q_ids == k_ids) & (k_at >= q_at) & (k_at < q_at + 2 * HALF)
        bias_ref[block] = jnp.where(seen, 0.0, NEG)


def greet_sides(seq_count):
    dp, seq = lax.axis_index("dp"), lax.axis_index("seq")
    barrier = pltpu.get_barrier_semaphore()
    has_left, has_right = seq > 0, seq < seq_count - 1

    @pl.when(has_left)
    def _():
        pl.semaphore_signal(barrier, inc=1, device_id=(dp, seq - 1), device_id_type=MESH)

    @pl.when(has_right)
    def _():
        pl.semaphore_signal(barrier, inc=1, device_id=(dp, seq + 1), device_id_type=MESH)

    pl.semaphore_wait(barrier, has_left.astype(jnp.int32) + has_right.astype(jnp.int32))

    return (dp, seq - 1), (dp, seq + 1), has_left, has_right


def forward_kernel(
    seq_count, clip_ref, x_ref, gain_ref, gain_bias_ref, scale_ref, w_qkv, w_out, cos_all, sin_all,
    normed_ref, q_ref, kv_ref, att_ref, branch_ref,
    wq_v, wo_v, cos_v, sin_v, bias_v, load_sem, send_sem, recv_sem,
):
    dp, seq = lax.axis_index("dp"), lax.axis_index("seq")
    rows = pl.ds(pl.multiple_of(seq * TOK, TOK), TOK)
    copies = []
    order = [2, 3, 4, 5, 0, 1]
    tables = [
        pltpu.make_async_copy(cos_all.at[rows], cos_v, load_sem.at[0]),
        pltpu.make_async_copy(sin_all.at[rows], sin_v, load_sem.at[1]),
    ]
    chunks = {
        k: pltpu.make_async_copy(
            w_qkv.at[:, pl.ds(k * 512, 512)], wq_v.at[k], load_sem.at[2 + k]
        )
        for k in order
    }
    out_copy = pltpu.make_async_copy(w_out, wo_v, load_sem.at[8])
    for copy in tables + [chunks[k] for k in order] + [out_copy]:
        copy.start()
    left, right, has_left, has_right = greet_sides(seq_count)

    hat, _ = normalize(x_ref[...].astype(jnp.float32))
    normed_ref[...] = (hat * gain_ref[...] + gain_bias_ref[...]).astype(jnp.bfloat16)
    for copy in tables:
        copy.wait()

    def project(k):
        chunks[k].wait()
        for part in range(2):
            cols = slice(part * 256, part * 256 + 256)
            full = dot(normed_ref[...], wq_v[k, :, cols])
            for half in range(2):
                block = full[:, half * 128 : half * 128 + 128]
                at = (k % 2) * 512 + part * 256 + half * 128
                if k < 4:
                    block = rotated(block, cos_v[...], sin_v[...])
                block = block.astype(jnp.bfloat16)
                if k < 2:
                    q_ref[:, at : at + 128] = block
                else:
                    kv_ref[k // 2 - 1, HALF : HALF + TOK, at : at + 128] = block

    for k in order[:4]:
        project(k)

    to_left = pltpu.make_async_remote_copy(
        src_ref=kv_ref.at[:, pl.ds(HALF, HALF)], dst_ref=kv_ref.at[:, pl.ds(HALF + TOK, HALF)],
        send_sem=send_sem.at[0], recv_sem=recv_sem.at[0], device_id=left, device_id_type=MESH,
    )
    to_right = pltpu.make_async_remote_copy(
        src_ref=kv_ref.at[:, pl.ds(TOK, HALF)], dst_ref=kv_ref.at[:, pl.ds(0, HALF)],
        send_sem=send_sem.at[1], recv_sem=recv_sem.at[1], device_id=right, device_id_type=MESH,
    )

    @pl.when(has_left)
    def _():
        to_left.start()

    @pl.when(has_right)
    def _():
        to_right.start()

    @pl.when(jnp.logical_not(has_left))
    def _():
        kv_ref[:, 0:HALF] = jnp.zeros((2, HALF, D), jnp.bfloat16)

    @pl.when(jnp.logical_not(has_right))
    def _():
        kv_ref[:, HALF + TOK :] = jnp.zeros((2, HALF, D), jnp.bfloat16)

    for k in order[4:]:
        project(k)
    window_bias(bias_v, clip_ref, seq_count * TOK, False)

    def attend(blocks):
        def step(pair, carry):
            lanes = pl.ds(pl.multiple_of(pair * 128, 128), 128)
            for block in blocks:
                queries = q_ref[block * 128 : block * 128 + 128, lanes] * 0.125
                keys = kv_ref[0, block * 128 : block * 128 + 256, lanes]
                values = kv_ref[1, block * 128 : block * 128 + 256, lanes]
                scores = contract_back(stacked(queries), keys) + bias_v[block]
                exponent = jnp.exp(scores - jnp.max(scores, -1, keepdims=True))
                total = jnp.sum(exponent, -1, keepdims=True)
                probs = (exponent * (1.0 / total)).astype(jnp.bfloat16)
                att_ref[block * 128 : block * 128 + 128, lanes] = merged(
                    dot(probs, values)
                ).astype(jnp.bfloat16)
            return carry

        lax.fori_loop(0, D // 128, step, 0)

    last = TOK // 128 - 1
    attend(list(range(1, last)))

    @pl.when(has_left)
    def _():
        to_right.wait_recv()

    @pl.when(has_right)
    def _():
        to_left.wait_recv()

    attend([0, last])
    out_copy.wait()
    for part in range(4):
        cols = slice(part * 256, part * 256 + 256)
        branch_ref[:, cols] = dot(att_ref[...], wo_v[:, cols])

    @pl.when(has_left)
    def _():
        to_left.wait_send()

    @pl.when(has_right)
    def _():
        to_right.wait_send()


def rotary_tables(group_len):
    half = HEAD_DIM // 2
    inv_freq = (10000.0 ** (-jnp.arange(half, dtype=jnp.float32) / half))[None, :]
    angles = jnp.arange(group_len, dtype=jnp.float32)[:, None] * inv_freq
    cosine, sine = jnp.cos(angles), jnp.sin(angles)
    return jnp.concatenate([cosine] * 4, 1), jnp.concatenate([-sine, sine] * 2, 1)


def forward_attention(frames, lengths, gain, bias, scale, w_qkv, w_out, tables, seq_count):
    bf, f32 = jnp.bfloat16, jnp.float32
    hbm = pl.BlockSpec(memory_space=pl.ANY)
    vmem = pl.BlockSpec(memory_space=pltpu.VMEM)
    smem = pl.BlockSpec(memory_space=pltpu.SMEM)
    shape = jax.ShapeDtypeStruct
    return pl.pallas_call(
        functools.partial(forward_kernel, seq_count),
        out_shape=[
            shape((TOK, D), bf),
            shape((TOK, D), bf),
            shape((2, TOK + 2 * HALF, D), bf),
            shape((TOK, D), bf),
            shape((TOK, D), f32),
        ],
        in_specs=[smem] + [vmem] * 4 + [hbm] * 4,
        out_specs=[vmem] * 5,
        scratch_shapes=[
            pltpu.VMEM((6, D, 512), bf),
            pltpu.VMEM((D, D), bf),
            pltpu.VMEM((TOK, 128), f32),
            pltpu.VMEM((TOK, 128), f32),
            pltpu.VMEM((TOK // 128, 256, 256), f32),
            pltpu.SemaphoreType.DMA((9,)),
            pltpu.SemaphoreType.DMA((2,)),
            pltpu.SemaphoreType.DMA((2,)),
        ],
        compiler_params=pltpu.CompilerParams(
            collective_id=2, has_side_effects=True, vmem_limit_bytes=48 * 2**20
        ),
        name="attention_forward",
    )(lengths, frames, gain[None], bias[None], scale[None], w_qkv, w_out, *tables)


FBLK = 512


def mlp_kernel(
    x_ref, c_ref, branch_ref, gain_ref, bias_ref, scale_attn_ref, scale_mlp_ref, w_gate_up, w_down,
    out_ref, n2_ref, hidden_ref, dgu_ref, dm_ref, db_ref, dmid_ref, vec_ref,
    wg_v, wu_v, wd_v, mlp_v, dn_v, load_sem,
):
    count = FF // FBLK

    def copies(step, slot):
        at = pl.multiple_of(step * FBLK, FBLK)
        return [
            pltpu.make_async_copy(
                w_gate_up.at[:, pl.ds(at, FBLK)], wg_v.at[slot], load_sem.at[slot, 0]
            ),
            pltpu.make_async_copy(
                w_gate_up.at[:, pl.ds(FF + at, FBLK)], wu_v.at[slot], load_sem.at[slot, 1]
            ),
            pltpu.make_async_copy(
                w_down.at[pl.ds(at, FBLK)], wd_v.at[slot], load_sem.at[slot, 2]
            ),
        ]

    for copy in copies(0, 0):
        copy.start()
    middle = x_ref[...].astype(jnp.float32) + scale_attn_ref[...] * branch_ref[...]
    hat, inverse = normalize(middle)
    n2_ref[...] = (hat * gain_ref[...] + bias_ref[...]).astype(jnp.bfloat16)
    dm_ref[...] = (c_ref[...].astype(jnp.float32) * scale_mlp_ref[...]).astype(jnp.bfloat16)
    mlp_v[...] = jnp.zeros_like(mlp_v)
    dn_v[...] = jnp.zeros_like(dn_v)

    def step(number, carry):
        slot = lax.rem(number, 2)

        @pl.when(number + 1 < count)
        def _():
            for copy in copies(number + 1, 1 - slot):
                copy.start()

        for copy in copies(number, slot):
            copy.wait()
        for part in range(FBLK // 256):
            cols = slice(part * 256, part * 256 + 256)
            at = pl.multiple_of(number * FBLK + part * 256, 256)
            gate = dot(n2_ref[...], wg_v[slot, :, cols])
            up = dot(n2_ref[...], wu_v[slot, :, cols])
            dh = contract_back(dm_ref[...], wd_v[slot, cols, :])
            sigmoid = 1.0 / (1.0 + jnp.exp(-gate))
            silu = gate * sigmoid
            hidden_ref[:, pl.ds(at, 256)] = (silu * up).astype(jnp.bfloat16)
            dgate = dh * up * (sigmoid * (1.0 + gate * (1.0 - sigmoid)))
            dgu_ref[:, pl.ds(at, 256)] = dgate.astype(jnp.bfloat16)
            dgu_ref[:, pl.ds(FF + at, 256)] = (dh * silu).astype(jnp.bfloat16)
        at = pl.multiple_of(number * FBLK, FBLK)
        mlp_v[...] += dot(hidden_ref[:, pl.ds(at, FBLK)], wd_v[slot])
        dn_v[...] += contract_back(dgu_ref[:, pl.ds(at, FBLK)], wg_v[slot]) + contract_back(
            dgu_ref[:, pl.ds(FF + at, FBLK)], wu_v[slot]
        )
        return carry

    lax.fori_loop(0, count, step, 0)
    cot = c_ref[...].astype(jnp.float32)
    branch = branch_ref[...]
    middle = x_ref[...].astype(jnp.float32) + scale_attn_ref[...] * branch
    mlp_out = mlp_v[...]
    out_ref[...] = (middle + scale_mlp_ref[...] * mlp_out).astype(jnp.bfloat16)
    vec_ref[0:1] = jnp.sum(cot * mlp_out, 0, keepdims=True)
    hat, inverse = normalize(middle)
    dn = dn_v[...]
    vec_ref[1:2] = jnp.sum(dn * hat, 0, keepdims=True)
    vec_ref[2:3] = jnp.sum(dn, 0, keepdims=True)
    dmid = cot + norm_backward(dn, hat, inverse, gain_ref[...])
    dmid_ref[...] = dmid
    vec_ref[3:4] = jnp.sum(dmid * branch, 0, keepdims=True)
    vec_ref[4:8] = jnp.zeros((4, D), jnp.float32)
    db_ref[...] = (dmid * scale_attn_ref[...]).astype(jnp.bfloat16)


def feed_forward(frames, cotangent, branch, gain, bias, scale_attn, scale_mlp, w_gate_up, w_down):
    bf, f32 = jnp.bfloat16, jnp.float32
    hbm = pl.BlockSpec(memory_space=pl.ANY)
    vmem = pl.BlockSpec(memory_space=pltpu.VMEM)
    shape = jax.ShapeDtypeStruct
    return pl.pallas_call(
        mlp_kernel,
        out_shape=[
            shape((TOK, D), bf),
            shape((TOK, D), bf),
            shape((TOK, FF), bf),
            shape((TOK, 2 * FF), bf),
            shape((TOK, D), bf),
            shape((TOK, D), bf),
            shape((TOK, D), f32),
            shape((8, D), f32),
        ],
        in_specs=[vmem] * 7 + [hbm] * 2,
        out_specs=[vmem] * 8,
        scratch_shapes=[
            pltpu.VMEM((2, D, FBLK), bf),
            pltpu.VMEM((2, D, FBLK), bf),
            pltpu.VMEM((2, FBLK, D), bf),
            pltpu.VMEM((TOK, D), f32),
            pltpu.VMEM((TOK, D), f32),
            pltpu.SemaphoreType.DMA((2, 3)),
        ],
        compiler_params=pltpu.CompilerParams(vmem_limit_bytes=56 * 2**20),
        name="feed_forward",
    )(
        frames, cotangent, branch, gain[None], bias[None], scale_attn[None], scale_mlp[None],
        w_gate_up, w_down,
    )


def backward_kernel(
    seq_count, clip_ref, x_ref, gain_ref, q_ref, kv_ref, db_ref, dmid_ref, w_qkv, w_out,
    cos_all, sin_all,
    dproj_ref, grad_ref, vec_ref,
    wq_v, wo_v, cos_v, sin_v, bias_v, datt_v, dkv_v, edge_v, far_v, load_sem, send_sem, recv_sem,
):
    seq = lax.axis_index("seq")
    rows = pl.ds(pl.multiple_of(seq * TOK, TOK), TOK)
    out_copy = pltpu.make_async_copy(w_out, wo_v, load_sem.at[8])
    tables = [
        pltpu.make_async_copy(cos_all.at[rows], cos_v, load_sem.at[0]),
        pltpu.make_async_copy(sin_all.at[rows], sin_v, load_sem.at[1]),
    ]
    chunks = [
        pltpu.make_async_copy(
            w_qkv.at[:, pl.ds(k * 512, 512)], wq_v.at[k], load_sem.at[2 + k]
        )
        for k in range(6)
    ]
    for copy in [out_copy] + tables + chunks:
        copy.start()
    left, right, has_left, has_right = greet_sides(seq_count)
    window_bias(bias_v, clip_ref, seq_count * TOK, True)
    out_copy.wait()
    for part in range(4):
        cols = slice(part * 256, part * 256 + 256)
        datt_v[:, cols] = contract_back(db_ref[...], wo_v[cols, :]).astype(jnp.bfloat16)
    for copy in tables:
        copy.wait()
    last = TOK // 128 - 1

    def attend(blocks):
        def step(pair, carry):
            lanes = pl.ds(pl.multiple_of(pair * 128, 128), 128)
            for block in blocks:
                own = slice(block * 128, block * 128 + 128)
                window = slice(block * 128, block * 128 + 256)
                queries = stacked(q_ref[own, lanes] * 0.125)
                grads = stacked(datt_v[own, lanes])
                keys = kv_ref[0, window, lanes]
                scores = contract_back(keys, queries) + bias_v[block]
                exponent = jnp.exp(scores - jnp.max(scores, 0, keepdims=True))
                total = jnp.sum(exponent, 0, keepdims=True)
                probs = exponent * (1.0 / total)
                d_probs = contract_back(kv_ref[1, window, lanes], grads)
                inner = jnp.sum(probs * d_probs, 0, keepdims=True)
                d_scores = (probs * (d_probs - inner)).astype(jnp.bfloat16)
                d_keys = dot(d_scores, queries)
                d_values = dot(probs.astype(jnp.bfloat16), grads)
                for which, update in ((0, d_keys), (1, d_values)):
                    if block in (0, last):
                        dkv_v[which, window, lanes] = update
                    elif block == 1:
                        dkv_v[which, 128:256, lanes] += update[:128]
                        dkv_v[which, 256:384, lanes] = update[128:]
                    else:
                        dkv_v[which, window, lanes] += update
                d_queries = merged(tn_dot(d_scores, keys)) * 0.125
                dproj_ref[own, lanes] = rotated(
                    d_queries, cos_v[own, :], -sin_v[own, :]
                ).astype(jnp.bfloat16)
            return carry

        lax.fori_loop(0, D // 128, step, 0)

    attend([0, last])
    edge_v[0] = dkv_v[:, 0:HALF].astype(jnp.bfloat16)
    edge_v[1] = dkv_v[:, HALF + TOK :].astype(jnp.bfloat16)
    to_left = pltpu.make_async_remote_copy(
        src_ref=edge_v.at[0], dst_ref=far_v.at[1],
        send_sem=send_sem.at[0], recv_sem=recv_sem.at[0], device_id=left, device_id_type=MESH,
    )
    to_right = pltpu.make_async_remote_copy(
        src_ref=edge_v.at[1], dst_ref=far_v.at[0],
        send_sem=send_sem.at[1], recv_sem=recv_sem.at[1], device_id=right, device_id_type=MESH,
    )

    @pl.when(has_left)
    def _():
        to_left.start()

    @pl.when(has_right)
    def _():
        to_right.start()

    attend(list(range(1, last)))

    @pl.when(has_left)
    def _():
        to_right.wait_recv()
        dkv_v[:, HALF : 2 * HALF] += far_v[0].astype(jnp.float32)

    @pl.when(has_right)
    def _():
        to_left.wait_recv()
        dkv_v[:, TOK : TOK + HALF] += far_v[1].astype(jnp.float32)

    for k in range(D // 128):
        lanes = slice(k * 128, k * 128 + 128)
        dproj_ref[:, D + k * 128 : D + k * 128 + 128] = rotated(
            dkv_v[0, HALF : HALF + TOK, lanes], cos_v[...], -sin_v[...]
        ).astype(jnp.bfloat16)
        dproj_ref[:, 2 * D + k * 128 : 2 * D + k * 128 + 128] = dkv_v[
            1, HALF : HALF + TOK, lanes
        ].astype(jnp.bfloat16)
    for copy in chunks:
        copy.wait()
    dn = contract_back(dproj_ref[:, 0:512], wq_v[0])
    for k in range(1, 6):
        dn += contract_back(dproj_ref[:, k * 512 : k * 512 + 512], wq_v[k])
    hat, inverse = normalize(x_ref[...].astype(jnp.float32))
    vec_ref[0:1] = jnp.sum(dn * hat, 0, keepdims=True)
    vec_ref[1:2] = jnp.sum(dn, 0, keepdims=True)
    vec_ref[2:8] = jnp.zeros((6, D), jnp.float32)
    grad_ref[...] = dmid_ref[...] + norm_backward(dn, hat, inverse, gain_ref[...])

    @pl.when(has_left)
    def _():
        to_left.wait_send()

    @pl.when(has_right)
    def _():
        to_right.wait_send()


def backward_attention(
    frames, lengths, gain, queries, kv, db, dmid, w_qkv, w_out, tables, seq_count
):
    bf, f32 = jnp.bfloat16, jnp.float32
    hbm = pl.BlockSpec(memory_space=pl.ANY)
    vmem = pl.BlockSpec(memory_space=pltpu.VMEM)
    smem = pl.BlockSpec(memory_space=pltpu.SMEM)
    shape = jax.ShapeDtypeStruct
    ext = TOK + 2 * HALF
    return pl.pallas_call(
        functools.partial(backward_kernel, seq_count),
        out_shape=[shape((TOK, 3 * D), bf), shape((TOK, D), f32), shape((8, D), f32)],
        in_specs=[smem] + [vmem] * 6 + [hbm] * 4,
        out_specs=[vmem] * 3,
        scratch_shapes=[
            pltpu.VMEM((6, D, 512), bf),
            pltpu.VMEM((D, D), bf),
            pltpu.VMEM((TOK, 128), f32),
            pltpu.VMEM((TOK, 128), f32),
            pltpu.VMEM((TOK // 128, 256, 256), f32),
            pltpu.VMEM((TOK, D), bf),
            pltpu.VMEM((2, ext, D), f32),
            pltpu.VMEM((2, 2, HALF, D), bf),
            pltpu.VMEM((2, 2, HALF, D), bf),
            pltpu.SemaphoreType.DMA((9,)),
            pltpu.SemaphoreType.DMA((2,)),
            pltpu.SemaphoreType.DMA((2,)),
        ],
        compiler_params=pltpu.CompilerParams(
            collective_id=3, has_side_effects=True, vmem_limit_bytes=56 * 2**20
        ),
        name="attention_backward",
    )(lengths, frames, gain[None], queries, kv, db, dmid, w_qkv, w_out, *tables)


def reduce_weights(lefts, rights, vectors):
    count = len(UNITS)
    bf = jnp.bfloat16
    hbm = pl.BlockSpec(memory_space=pl.ANY)
    vmem = pl.BlockSpec(memory_space=pltpu.VMEM)
    size = (PARTS[1], PARTS[2] - PARTS[1], PARTS[3] - PARTS[2])
    f32 = jnp.float32
    scratch = [
        pltpu.VMEM((2, 2, TOK, 1024), bf),
        pltpu.VMEM((2, 2, TOK, 512), bf),
        pltpu.VMEM((count, 2, 2, 4, size[0], 256), bf),
        pltpu.VMEM((count, 2, 2, 4, size[1], 256), bf),
        pltpu.VMEM((count, 4, 2, 2, size[2], 256), bf),
        pltpu.VMEM((count, 2, 4, size[0], 256), bf),
        pltpu.VMEM((count, 4, size[0], 256), bf),
        pltpu.VMEM((count, 2, 4, size[0], 256), bf),
        pltpu.VMEM((count, 2, 4, size[1], 256), bf),
        pltpu.VMEM((count, 4, size[1], 256), bf),
        pltpu.VMEM((count, 2, 4, size[1], 256), bf),
        pltpu.VMEM((count, 2, 4, 2, 2, size[2], 256), bf),
        pltpu.VMEM((count, 2, size[2], 256), bf),
        pltpu.VMEM((count, size[2], 256), bf),
        pltpu.VMEM((4, 8, 1024), f32),
        pltpu.VMEM((3, 8, 1024), f32),
        pltpu.VMEM((4, 8, 1024), f32),
        pltpu.SemaphoreType.DMA((4 + 2 * count,)),
        pltpu.SemaphoreType.DMA((4 + 2 * count,)),
        pltpu.SemaphoreType.DMA((4, 4)),
        pltpu.SemaphoreType.DMA((count, 3, 4)),
        pltpu.SemaphoreType.DMA((count, 3, 4)),
        pltpu.SemaphoreType.DMA((6,)),
        pltpu.SemaphoreType.DMA((6,)),
    ]
    shape = jax.ShapeDtypeStruct
    return pl.pallas_call(
        scatter_kernel,
        out_shape=[
            shape((128, 768), f32),
            shape((128, 256), f32),
            shape((128, 2048), f32),
            shape((512, 256), f32),
            shape((8, 1024), f32),
        ]
        + [shape(v.shape, bf) for v in lefts]
        + [shape((count, 2, TOK, 256), bf)],
        in_specs=[hbm] * 8 + [vmem],
        out_specs=[vmem] * 5 + [hbm] * 5,
        scratch_shapes=scratch,
        compiler_params=pltpu.CompilerParams(
            collective_id=1, has_side_effects=True, vmem_limit_bytes=62 * 2**20
        ),
        name="scatter_sums",
    )(*lefts, *rights, vectors)[:5]


def local(
    frames,
    cotangent,
    clip_len,
    ln1_gain,
    ln1_bias,
    w_qkv,
    w_out,
    scale_attn,
    ln2_gain,
    ln2_bias,
    w_gate_up,
    w_down,
    scale_mlp,
):
    row_count = frames.shape[0]
    seq_count = lax.axis_size("seq")
    tables = rotary_tables(row_count * seq_count)
    normed_b, queries, kv, attended_t, branch = forward_attention(
        frames, clip_len, ln1_gain, ln1_bias, scale_attn, w_qkv, w_out, tables, seq_count
    )
    out_frames, normed_two_b, hidden_b, gate_up_b, mlp_grad, branch_grad, middle_grad, vec_two = (
        feed_forward(
            frames, cotangent, branch, ln2_gain, ln2_bias, scale_attn, scale_mlp, w_gate_up, w_down
        )
    )
    projected_grad, input_grad, vec_one = backward_attention(
        frames, clip_len, ln1_gain, queries, kv, branch_grad, middle_grad, w_qkv, w_out, tables,
        seq_count,
    )
    vector_grads = jnp.stack(
        [vec_one[0], vec_one[1], vec_two[3], vec_two[1], vec_two[2], vec_two[0]], 0
    )
    data_count = lax.axis_size("dp")
    lefts = (normed_b, attended_t, normed_two_b, hidden_b)
    rights = (projected_grad, branch_grad, gate_up_b, mlp_grad)
    if (data_count, seq_count, row_count) == (8, 4, TOK):
        padded = jnp.concatenate([vector_grads, jnp.zeros((2, D), jnp.float32)], 0)
        sum_qkv, sum_out, sum_gate_up, sum_down, vector_total = reduce_weights(
            lefts, rights, padded
        )
    else:
        vector_total = lax.psum(vector_grads, ("dp", "seq"))
        sum_qkv, sum_out, sum_gate_up, sum_down = [
            lax.psum_scatter(
                to_blocks(contract_rows(left, right), data_count, seq_count),
                ("dp", "seq"),
                scatter_dimension=0,
                tiled=True,
            )[0]
            for left, right in zip(lefts, rights)
        ]
    return (
        out_frames,
        input_grad,
        vector_total[0],
        vector_total[1],
        sum_qkv,
        sum_out,
        vector_total[2],
        vector_total[3],
        vector_total[4],
        sum_gate_up,
        sum_down,
        vector_total[5],
    )


def solution(mesh):
    return jax.shard_map(
        local,
        mesh=mesh,
        in_specs=(
            P(("dp", "seq"), None),
            P(("dp", "seq"), None),
            P("dp", None),
            P(),
            P(),
            P(),
            P(),
            P(),
            P(),
            P(),
            P(),
            P(),
            P(),
        ),
        out_specs=(
            P(("dp", "seq"), None),
            P(("dp", "seq"), None),
            P(),
            P(),
            P("dp", "seq"),
            P("dp", "seq"),
            P(),
            P(),
            P(),
            P("dp", "seq"),
            P("dp", "seq"),
            P(),
        ),
        check_vma=False,
    )
```

```python
import functools

import jax
import jax.numpy as jnp
import numpy as np
from jax import lax
from jax.experimental import pallas as pl
from jax.experimental.pallas import tpu as pltpu
from jax.sharding import PartitionSpec as P

D = 1024
HEADS = 16
HEAD_DIM = 64
FF = 4096
HALF = 64
QBLK = 512


EPS = 1e-05
NEG = -1e30


def contract_rows(left, right):
    return lax.dot_general(
        left, right, (((0,), (0,)), ((), ())), preferred_element_type=jnp.float32
    )


def contract_back(grads, weight):
    return lax.dot_general(
        grads, weight, (((1,), (1,)), ((), ())), preferred_element_type=jnp.float32
    )


def to_blocks(matrix, data_count, seq_count):
    row_total, col_total = matrix.shape
    shaped = matrix.reshape(data_count, row_total // data_count, seq_count, col_total // seq_count)
    return shaped.transpose(0, 2, 1, 3).reshape(
        data_count * seq_count, row_total // data_count, col_total // seq_count
    )


MESH = pl.DeviceIdType.MESH
TOK = 512
PARTS = (0, 48, 96, 128)

UNITS = (
    [(2, 0, 128, 2, 2048, 256 * v, 2, 0) for v in range(8)]
    + [(3, 128 * v, 512, 3, 256, 0, 3, 128 * v) for v in range(4)]
    + [(1, 0, 128, 1, 256, 0, 1, 0)]
    + [(0, 0, 128, 0, 768, 256 * v, 0, 0) for v in range(3)]
)


def tn_dot(left, right):
    return lax.dot_general(
        left, right, (((0,), (0,)), ((), ())), preferred_element_type=jnp.float32
    )


def rotated(values, cosines, sines):
    lane = lax.broadcasted_iota(jnp.int32, values.shape, 1)
    partner = jnp.where(
        lane % HEAD_DIM < HEAD_DIM // 2,
        pltpu.roll(values, 128 - HEAD_DIM // 2, 1),
        pltpu.roll(values, HEAD_DIM // 2, 1),
    )
    return values * cosines + partner * sines


def head_masks():
    lane = lax.broadcasted_iota(jnp.int32, (128, 128), 1)
    return lane < HEAD_DIM


def stacked(pair):
    first = head_masks()
    zero = jnp.zeros_like(pair)
    return jnp.concatenate([jnp.where(first, pair, zero), jnp.where(first, zero, pair)], 0)


def merged(rows):
    return jnp.where(head_masks(), rows[:128], rows[128:])


def clip_number(positions, ends, group_len):
    total = jnp.zeros_like(positions)
    for end in ends:
        total = total + (positions >= end).astype(jnp.int32)
    return jnp.where((positions >= 0) & (positions < group_len), total, -1)


def normalize(values):
    average = jnp.mean(values, -1, keepdims=True)
    centered = values - average
    inverse = lax.rsqrt(jnp.mean(centered * centered, -1, keepdims=True) + EPS)
    return centered * inverse, inverse


def dot(left, right):
    return jnp.dot(left, right, preferred_element_type=jnp.float32)


def norm_backward(grads, hat, inverse, gain):
    scaled = grads * gain
    return inverse * (
        scaled
        - jnp.mean(scaled, -1, keepdims=True)
        - hat * jnp.mean(scaled * hat, -1, keepdims=True)
    )


def window_bias(bias_ref, clip_ref, group_len, keys_first):
    seq = lax.axis_index("seq")
    first_end = clip_ref[0, 0]
    second_end = first_end + clip_ref[0, 1]
    ends = (first_end, second_end, second_end + clip_ref[0, 2])
    for block in range(TOK // 128):
        start = seq * TOK + block * 128
        shape = (2 * 128, 2 * 128)
        k_axis = 0 if keys_first else 1
        k_at = lax.broadcasted_iota(jnp.int32, shape, k_axis)
        q_at = lax.rem(lax.broadcasted_iota(jnp.int32, shape, 1 - k_axis), 128)
        q_shape = (1, 256) if keys_first else (256, 1)
        k_shape = (256, 1) if keys_first else (1, 256)
        q_ids = clip_number(
            start + lax.rem(lax.broadcasted_iota(jnp.int32, q_shape, 1 - k_axis), 128),
            ends, group_len,
        )
        k_ids = clip_number(
            start - HALF + lax.broadcasted_iota(jnp.int32, k_shape, k_axis), ends, group_len
        )
        seen = (q_ids == k_ids) & (k_at >= q_at) & (k_at < q_at + 2 * HALF)
        bias_ref[block] = jnp.where(seen, 0.0, NEG)


def greet_sides(seq_count):
    dp, seq = lax.axis_index("dp"), lax.axis_index("seq")
    barrier = pltpu.get_barrier_semaphore()
    has_left, has_right = seq > 0, seq < seq_count - 1

    @pl.when(has_left)
    def _():
        pl.semaphore_signal(barrier, inc=1, device_id=(dp, seq - 1), device_id_type=MESH)

    @pl.when(has_right)
    def _():
        pl.semaphore_signal(barrier, inc=1, device_id=(dp, seq + 1), device_id_type=MESH)

    pl.semaphore_wait(barrier, has_left.astype(jnp.int32) + has_right.astype(jnp.int32))

    return (dp, seq - 1), (dp, seq + 1), has_left, has_right


def forward_kernel(
    seq_count, clip_ref, x_ref, gain_ref, gain_bias_ref, scale_ref, w_qkv, w_out, cos_all, sin_all,
    normed_ref, q_ref, kv_ref, att_ref, branch_ref,
    wq_v, wo_v, cos_v, sin_v, bias_v, load_sem, send_sem, recv_sem,
):
    dp, seq = lax.axis_index("dp"), lax.axis_index("seq")
    rows = pl.ds(pl.multiple_of(seq * TOK, TOK), TOK)
    copies = []
    order = [2, 3, 4, 5, 0, 1]
    tables = [
        pltpu.make_async_copy(cos_all.at[rows], cos_v, load_sem.at[0]),
        pltpu.make_async_copy(sin_all.at[rows], sin_v, load_sem.at[1]),
    ]
    chunks = {
        k: pltpu.make_async_copy(
            w_qkv.at[:, pl.ds(k * 512, 512)], wq_v.at[k], load_sem.at[2 + k]
        )
        for k in order
    }
    out_copy = pltpu.make_async_copy(w_out, wo_v, load_sem.at[8])
    for copy in tables + [chunks[k] for k in order] + [out_copy]:
        copy.start()
    left, right, has_left, has_right = greet_sides(seq_count)

    hat, _ = normalize(x_ref[...].astype(jnp.float32))
    normed_ref[...] = (hat * gain_ref[...] + gain_bias_ref[...]).astype(jnp.bfloat16)
    for copy in tables:
        copy.wait()

    def project(k):
        chunks[k].wait()
        for part in range(2):
            cols = slice(part * 256, part * 256 + 256)
            full = dot(normed_ref[...], wq_v[k, :, cols])
            for half in range(2):
                block = full[:, half * 128 : half * 128 + 128]
                at = (k % 2) * 512 + part * 256 + half * 128
                if k < 4:
                    block = rotated(block, cos_v[...], sin_v[...])
                block = block.astype(jnp.bfloat16)
                if k < 2:
                    q_ref[:, at : at + 128] = block
                else:
                    kv_ref[k // 2 - 1, HALF : HALF + TOK, at : at + 128] = block

    for k in order[:4]:
        project(k)

    to_left = pltpu.make_async_remote_copy(
        src_ref=kv_ref.at[:, pl.ds(HALF, HALF)], dst_ref=kv_ref.at[:, pl.ds(HALF + TOK, HALF)],
        send_sem=send_sem.at[0], recv_sem=recv_sem.at[0], device_id=left, device_id_type=MESH,
    )
    to_right = pltpu.make_async_remote_copy(
        src_ref=kv_ref.at[:, pl.ds(TOK, HALF)], dst_ref=kv_ref.at[:, pl.ds(0, HALF)],
        send_sem=send_sem.at[1], recv_sem=recv_sem.at[1], device_id=right, device_id_type=MESH,
    )

    @pl.when(has_left)
    def _():
        to_left.start()

    @pl.when(has_right)
    def _():
        to_right.start()

    @pl.when(jnp.logical_not(has_left))
    def _():
        kv_ref[:, 0:HALF] = jnp.zeros((2, HALF, D), jnp.bfloat16)

    @pl.when(jnp.logical_not(has_right))
    def _():
        kv_ref[:, HALF + TOK :] = jnp.zeros((2, HALF, D), jnp.bfloat16)

    for k in order[4:]:
        project(k)
    window_bias(bias_v, clip_ref, seq_count * TOK, False)

    heads = 4
    lanes_of = heads * HEAD_DIM

    def attend(blocks):
        def step(group, carry):
            lanes = pl.ds(pl.multiple_of(group * lanes_of, lanes_of), lanes_of)
            scores = []
            for block in blocks:
                queries = q_ref[block * 128 : block * 128 + 128, lanes] * 0.125
                keys = kv_ref[0, block * 128 : block * 128 + 256, lanes]
                bias = jnp.concatenate([bias_v[block]] * (heads // 2), 0)
                scores.append(contract_back(stacked_heads(queries, heads), keys) + bias)
            probs = []
            for score in scores:
                exponent = jnp.exp(score - jnp.max(score, -1, keepdims=True))
                total = jnp.sum(exponent, -1, keepdims=True)
                probs.append((exponent * (1.0 / total)).astype(jnp.bfloat16))
            for block, prob in zip(blocks, probs):
                values = kv_ref[1, block * 128 : block * 128 + 256, lanes]
                att_ref[block * 128 : block * 128 + 128, lanes] = merged_heads(
                    dot(prob, values), heads
                ).astype(jnp.bfloat16)
            return carry

        lax.fori_loop(0, D // lanes_of, step, 0)

    last = TOK // 128 - 1
    attend(list(range(1, last)))

    @pl.when(has_left)
    def _():
        to_right.wait_recv()

    @pl.when(has_right)
    def _():
        to_left.wait_recv()

    attend([0, last])
    out_copy.wait()
    for part in range(4):
        cols = slice(part * 256, part * 256 + 256)
        branch_ref[:, cols] = dot(att_ref[...], wo_v[:, cols])

    @pl.when(has_left)
    def _():
        to_left.wait_send()

    @pl.when(has_right)
    def _():
        to_right.wait_send()


def rotary_tables(group_len):
    half = HEAD_DIM // 2
    inv_freq = (10000.0 ** (-np.arange(half) / half)).astype(np.float32)[None, :]
    angles = np.arange(group_len, dtype=np.float32)[:, None] * inv_freq
    cosine, sine = np.cos(angles), np.sin(angles)
    return (
        np.concatenate([cosine] * 4, 1).astype(np.float32),
        np.concatenate([-sine, sine] * 2, 1).astype(np.float32),
    )


def forward_attention(frames, lengths, gain, bias, scale, w_qkv, w_out, tables, seq_count):
    bf, f32 = jnp.bfloat16, jnp.float32
    hbm = pl.BlockSpec(memory_space=pl.ANY)
    vmem = pl.BlockSpec(memory_space=pltpu.VMEM)
    smem = pl.BlockSpec(memory_space=pltpu.SMEM)
    shape = jax.ShapeDtypeStruct
    return pl.pallas_call(
        functools.partial(forward_kernel, seq_count),
        out_shape=[
            shape((TOK, D), bf),
            shape((TOK, D), bf),
            shape((2, TOK + 2 * HALF, D), bf),
            shape((TOK, D), bf),
            shape((TOK, D), f32),
        ],
        in_specs=[smem] + [vmem] * 4 + [hbm] * 4,
        out_specs=[vmem] * 5,
        scratch_shapes=[
            pltpu.VMEM((6, D, 512), bf),
            pltpu.VMEM((D, D), bf),
            pltpu.VMEM((TOK, 128), f32),
            pltpu.VMEM((TOK, 128), f32),
            pltpu.VMEM((TOK // 128, 256, 256), f32),
            pltpu.SemaphoreType.DMA((9,)),
            pltpu.SemaphoreType.DMA((2,)),
            pltpu.SemaphoreType.DMA((2,)),
        ],
        compiler_params=pltpu.CompilerParams(
            collective_id=2, has_side_effects=True, vmem_limit_bytes=48 * 2**20
        ),
        name="attention_forward",
    )(lengths, frames, gain[None], bias[None], scale[None], w_qkv, w_out, *tables)


FBLK = 512


def mlp_kernel(
    x_ref, c_ref, branch_ref, gain_ref, bias_ref, scale_attn_ref, scale_mlp_ref, w_gate_up, w_down,
    out_ref, n2_ref, hidden_ref, dgu_ref, dm_ref, db_ref, dmid_ref, vec_ref,
    wg_v, wu_v, wd_v, mlp_v, dn_v, load_sem,
):
    count = FF // FBLK

    def copies(step, slot):
        at = pl.multiple_of(step * FBLK, FBLK)
        return [
            pltpu.make_async_copy(
                w_gate_up.at[:, pl.ds(at, FBLK)], wg_v.at[slot], load_sem.at[slot, 0]
            ),
            pltpu.make_async_copy(
                w_gate_up.at[:, pl.ds(FF + at, FBLK)], wu_v.at[slot], load_sem.at[slot, 1]
            ),
            pltpu.make_async_copy(
                w_down.at[pl.ds(at, FBLK)], wd_v.at[slot], load_sem.at[slot, 2]
            ),
        ]

    for copy in copies(0, 0):
        copy.start()
    middle = x_ref[...].astype(jnp.float32) + scale_attn_ref[...] * branch_ref[...]
    hat, inverse = normalize(middle)
    n2_ref[...] = (hat * gain_ref[...] + bias_ref[...]).astype(jnp.bfloat16)
    dm_ref[...] = (c_ref[...].astype(jnp.float32) * scale_mlp_ref[...]).astype(jnp.bfloat16)
    mlp_v[...] = jnp.zeros_like(mlp_v)
    dn_v[...] = jnp.zeros_like(dn_v)

    def step(number, carry):
        slot = lax.rem(number, 2)

        @pl.when(number + 1 < count)
        def _():
            for copy in copies(number + 1, 1 - slot):
                copy.start()

        for copy in copies(number, slot):
            copy.wait()
        for part in range(FBLK // 256):
            cols = slice(part * 256, part * 256 + 256)
            at = pl.multiple_of(number * FBLK + part * 256, 256)
            gate = dot(n2_ref[...], wg_v[slot, :, cols])
            up = dot(n2_ref[...], wu_v[slot, :, cols])
            dh = contract_back(dm_ref[...], wd_v[slot, cols, :])
            sigmoid = 1.0 / (1.0 + jnp.exp(-gate))
            silu = gate * sigmoid
            hidden_ref[:, pl.ds(at, 256)] = (silu * up).astype(jnp.bfloat16)
            dgate = dh * up * (sigmoid * (1.0 + gate * (1.0 - sigmoid)))
            dgu_ref[:, pl.ds(at, 256)] = dgate.astype(jnp.bfloat16)
            dgu_ref[:, pl.ds(FF + at, 256)] = (dh * silu).astype(jnp.bfloat16)
        at = pl.multiple_of(number * FBLK, FBLK)
        mlp_v[...] += dot(hidden_ref[:, pl.ds(at, FBLK)], wd_v[slot])
        dn_v[...] += contract_back(dgu_ref[:, pl.ds(at, FBLK)], wg_v[slot]) + contract_back(
            dgu_ref[:, pl.ds(FF + at, FBLK)], wu_v[slot]
        )
        return carry

    lax.fori_loop(0, count, step, 0)
    cot = c_ref[...].astype(jnp.float32)
    branch = branch_ref[...]
    middle = x_ref[...].astype(jnp.float32) + scale_attn_ref[...] * branch
    mlp_out = mlp_v[...]
    out_ref[...] = (middle + scale_mlp_ref[...] * mlp_out).astype(jnp.bfloat16)
    vec_ref[0:1] = jnp.sum(cot * mlp_out, 0, keepdims=True)
    hat, inverse = normalize(middle)
    dn = dn_v[...]
    vec_ref[1:2] = jnp.sum(dn * hat, 0, keepdims=True)
    vec_ref[2:3] = jnp.sum(dn, 0, keepdims=True)
    dmid = cot + norm_backward(dn, hat, inverse, gain_ref[...])
    dmid_ref[...] = dmid
    vec_ref[3:4] = jnp.sum(dmid * branch, 0, keepdims=True)
    vec_ref[4:8] = jnp.zeros((4, D), jnp.float32)
    db_ref[...] = (dmid * scale_attn_ref[...]).astype(jnp.bfloat16)


def feed_forward(frames, cotangent, branch, gain, bias, scale_attn, scale_mlp, w_gate_up, w_down):
    bf, f32 = jnp.bfloat16, jnp.float32
    hbm = pl.BlockSpec(memory_space=pl.ANY)
    vmem = pl.BlockSpec(memory_space=pltpu.VMEM)
    shape = jax.ShapeDtypeStruct
    return pl.pallas_call(
        mlp_kernel,
        out_shape=[
            shape((TOK, D), bf),
            shape((TOK, D), bf),
            shape((TOK, FF), bf),
            shape((TOK, 2 * FF), bf),
            shape((TOK, D), bf),
            shape((TOK, D), bf),
            shape((TOK, D), f32),
            shape((8, D), f32),
        ],
        in_specs=[vmem] * 7 + [hbm] * 2,
        out_specs=[vmem] * 8,
        scratch_shapes=[
            pltpu.VMEM((2, D, FBLK), bf),
            pltpu.VMEM((2, D, FBLK), bf),
            pltpu.VMEM((2, FBLK, D), bf),
            pltpu.VMEM((TOK, D), f32),
            pltpu.VMEM((TOK, D), f32),
            pltpu.SemaphoreType.DMA((2, 3)),
        ],
        compiler_params=pltpu.CompilerParams(vmem_limit_bytes=56 * 2**20),
        name="feed_forward",
    )(
        frames, cotangent, branch, gain[None], bias[None], scale_attn[None], scale_mlp[None],
        w_gate_up, w_down,
    )


def backward_kernel(
    seq_count, clip_ref, x_ref, gain_ref, q_ref, kv_ref, db_ref, dmid_ref, w_qkv, w_out,
    cos_all, sin_all,
    dproj_ref, grad_ref, vec_ref,
    wq_v, wo_v, cos_v, sin_v, bias_v, datt_v, dkv_v, edge_v, far_v, load_sem, send_sem, recv_sem,
):
    seq = lax.axis_index("seq")
    rows = pl.ds(pl.multiple_of(seq * TOK, TOK), TOK)
    out_copy = pltpu.make_async_copy(w_out, wo_v, load_sem.at[8])
    tables = [
        pltpu.make_async_copy(cos_all.at[rows], cos_v, load_sem.at[0]),
        pltpu.make_async_copy(sin_all.at[rows], sin_v, load_sem.at[1]),
    ]
    chunks = [
        pltpu.make_async_copy(
            w_qkv.at[:, pl.ds(k * 512, 512)], wq_v.at[k], load_sem.at[2 + k]
        )
        for k in range(6)
    ]
    for copy in [out_copy] + tables + chunks:
        copy.start()
    left, right, has_left, has_right = greet_sides(seq_count)
    window_bias(bias_v, clip_ref, seq_count * TOK, True)
    out_copy.wait()
    for part in range(4):
        cols = slice(part * 256, part * 256 + 256)
        datt_v[:, cols] = contract_back(db_ref[...], wo_v[cols, :]).astype(jnp.bfloat16)
    for copy in tables:
        copy.wait()
    last = TOK // 128 - 1

    def attend(blocks):
        def step(pair, carry):
            lanes = pl.ds(pl.multiple_of(pair * 128, 128), 128)
            for block in blocks:
                own = slice(block * 128, block * 128 + 128)
                window = slice(block * 128, block * 128 + 256)
                queries = stacked(q_ref[own, lanes] * 0.125)
                grads = stacked(datt_v[own, lanes])
                keys = kv_ref[0, window, lanes]
                scores = contract_back(keys, queries) + bias_v[block]
                exponent = jnp.exp(scores - jnp.max(scores, 0, keepdims=True))
                total = jnp.sum(exponent, 0, keepdims=True)
                probs = exponent * (1.0 / total)
                d_probs = contract_back(kv_ref[1, window, lanes], grads)
                inner = jnp.sum(probs * d_probs, 0, keepdims=True)
                d_scores = (probs * (d_probs - inner)).astype(jnp.bfloat16)
                d_keys = dot(d_scores, queries)
                d_values = dot(probs.astype(jnp.bfloat16), grads)
                for which, update in ((0, d_keys), (1, d_values)):
                    if block in (0, last):
                        dkv_v[which, window, lanes] = update
                    elif block == 1:
                        dkv_v[which, 128:256, lanes] += update[:128]
                        dkv_v[which, 256:384, lanes] = update[128:]
                    else:
                        dkv_v[which, window, lanes] += update
                d_queries = merged(tn_dot(d_scores, keys)) * 0.125
                dproj_ref[own, lanes] = rotated(
                    d_queries, cos_v[own, :], -sin_v[own, :]
                ).astype(jnp.bfloat16)
            return carry

        lax.fori_loop(0, D // 128, step, 0)

    attend([0, last])
    edge_v[0] = dkv_v[:, 0:HALF].astype(jnp.bfloat16)
    edge_v[1] = dkv_v[:, HALF + TOK :].astype(jnp.bfloat16)
    to_left = pltpu.make_async_remote_copy(
        src_ref=edge_v.at[0], dst_ref=far_v.at[1],
        send_sem=send_sem.at[0], recv_sem=recv_sem.at[0], device_id=left, device_id_type=MESH,
    )
    to_right = pltpu.make_async_remote_copy(
        src_ref=edge_v.at[1], dst_ref=far_v.at[0],
        send_sem=send_sem.at[1], recv_sem=recv_sem.at[1], device_id=right, device_id_type=MESH,
    )

    @pl.when(has_left)
    def _():
        to_left.start()

    @pl.when(has_right)
    def _():
        to_right.start()

    attend(list(range(1, last)))

    @pl.when(has_left)
    def _():
        to_right.wait_recv()
        dkv_v[:, HALF : 2 * HALF] += far_v[0].astype(jnp.float32)

    @pl.when(has_right)
    def _():
        to_left.wait_recv()
        dkv_v[:, TOK : TOK + HALF] += far_v[1].astype(jnp.float32)

    for k in range(D // 128):
        lanes = slice(k * 128, k * 128 + 128)
        dproj_ref[:, D + k * 128 : D + k * 128 + 128] = rotated(
            dkv_v[0, HALF : HALF + TOK, lanes], cos_v[...], -sin_v[...]
        ).astype(jnp.bfloat16)
        dproj_ref[:, 2 * D + k * 128 : 2 * D + k * 128 + 128] = dkv_v[
            1, HALF : HALF + TOK, lanes
        ].astype(jnp.bfloat16)
    for copy in chunks:
        copy.wait()
    dn = contract_back(dproj_ref[:, 0:512], wq_v[0])
    for k in range(1, 6):
        dn += contract_back(dproj_ref[:, k * 512 : k * 512 + 512], wq_v[k])
    hat, inverse = normalize(x_ref[...].astype(jnp.float32))
    vec_ref[0:1] = jnp.sum(dn * hat, 0, keepdims=True)
    vec_ref[1:2] = jnp.sum(dn, 0, keepdims=True)
    vec_ref[2:8] = jnp.zeros((6, D), jnp.float32)
    grad_ref[...] = dmid_ref[...] + norm_backward(dn, hat, inverse, gain_ref[...])

    @pl.when(has_left)
    def _():
        to_left.wait_send()

    @pl.when(has_right)
    def _():
        to_right.wait_send()


def backward_attention(
    frames, lengths, gain, queries, kv, db, dmid, w_qkv, w_out, tables, seq_count
):
    bf, f32 = jnp.bfloat16, jnp.float32
    hbm = pl.BlockSpec(memory_space=pl.ANY)
    vmem = pl.BlockSpec(memory_space=pltpu.VMEM)
    smem = pl.BlockSpec(memory_space=pltpu.SMEM)
    shape = jax.ShapeDtypeStruct
    ext = TOK + 2 * HALF
    return pl.pallas_call(
        functools.partial(backward_kernel, seq_count),
        out_shape=[shape((TOK, 3 * D), bf), shape((TOK, D), f32), shape((8, D), f32)],
        in_specs=[smem] + [vmem] * 6 + [hbm] * 4,
        out_specs=[vmem] * 3,
        scratch_shapes=[
            pltpu.VMEM((6, D, 512), bf),
            pltpu.VMEM((D, D), bf),
            pltpu.VMEM((TOK, 128), f32),
            pltpu.VMEM((TOK, 128), f32),
            pltpu.VMEM((TOK // 128, 256, 256), f32),
            pltpu.VMEM((TOK, D), bf),
            pltpu.VMEM((2, ext, D), f32),
            pltpu.VMEM((2, 2, HALF, D), bf),
            pltpu.VMEM((2, 2, HALF, D), bf),
            pltpu.SemaphoreType.DMA((9,)),
            pltpu.SemaphoreType.DMA((2,)),
            pltpu.SemaphoreType.DMA((2,)),
        ],
        compiler_params=pltpu.CompilerParams(
            collective_id=3, has_side_effects=True, vmem_limit_bytes=56 * 2**20
        ),
        name="attention_backward",
    )(lengths, frames, gain[None], queries, kv, db, dmid, w_qkv, w_out, *tables)


RING = 8
COUNT = len(UNITS)


def stacked_heads(block, heads):
    lane = lax.broadcasted_iota(jnp.int32, block.shape, 1) // HEAD_DIM
    zero = jnp.zeros_like(block)
    return jnp.concatenate([jnp.where(lane == h, block, zero) for h in range(heads)], 0)


def merged_heads(rows, heads):
    lane = lax.broadcasted_iota(jnp.int32, (128, rows.shape[1]), 1) // HEAD_DIM
    total = rows[:128]
    for h in range(1, heads):
        total = jnp.where(lane == h, rows[128 * h : 128 * h + 128], total)
    return total


def layer_kernel(
    clip_ref, x_hbm, c_hbm, branch_hbm, q_hbm, kv_hbm, att_hbm, normed_hbm,
    gain1_ref, gain2_ref, bias2_ref, scale_attn_ref, scale_mlp_ref,
    w_qkv, w_out, w_gate_up, w_down, cos_all, sin_all,
    out_hbm, grad_hbm, out0, out1, out2, out3, vec_out, far_att, far_normed, hid_hbm, far_hid,
    part_a, part_b, part_c,
    recv_a1, recv_a2, recv_az, recv_b1, recv_b2, recv_bz, recv_cz, recv_c1, recv_c2,
    wide_v, deep_v, dkv_v, xbuf, ybuf, yfar, ydown, yout, other_v, hid_v,
    dm_v, db_v, datt_v, x_v, c_v, grad_v, q_v, kv_v, dproj_v, bias_v, cos_v, sin_v, edge_v, far_v,
    vec_sum, vec_recv, vec_z,
    send_sem, recv_sem, load_sem, far_send, far_recv, w_sem, hid_sem, hid_send, hid_recv,
    oth_send, oth_recv, q_send, q_recv, x_sem, edge_send, edge_recv, vec_send, vec_rsem, out_sem,
):
    outs = (out0, out1, out2, out3)
    dp = lax.axis_index("dp")
    seq = lax.axis_index("seq")
    z, y = dp // 2, dp % 2
    x, c = seq // 2, seq % 2
    dev_c = (dp, x * 2 + 1 - c)
    dev_x = (dp, (1 - x) * 2 + c)
    dev_y = (z * 2 + 1 - y, seq)
    dev_d = (dp, (1 - x) * 2 + 1 - c)
    dev_z = [(lax.rem(z + k, 4) * 2 + y, seq) for k in (1, 2, 3)]
    bf, f32 = jnp.bfloat16, jnp.float32

    def local_copy(src, dst, sem):
        return pltpu.make_async_copy(src, dst, sem)

    def remote(src, dst, ssem, rsem, device):
        return pltpu.make_async_remote_copy(
            src_ref=src, dst_ref=dst, send_sem=ssem, recv_sem=rsem,
            device_id=device, device_id_type=MESH,
        )

    def weights(step, slot):
        result = []
        for i in range(2):
            at = pl.multiple_of((c if i == 0 else 1 - c) * (FF // 2) + step * 256, 256)
            result += [
                local_copy(
                    w_gate_up.at[:, pl.ds(at, 256)], wide_v.at[4 * slot + i], w_sem.at[slot, i]
                ),
                local_copy(
                    w_gate_up.at[:, pl.ds(FF + at, 256)], wide_v.at[4 * slot + 2 + i],
                    w_sem.at[slot, 2 + i],
                ),
                local_copy(
                    w_down.at[pl.ds(at, 256)], deep_v.at[slot, pl.ds(256 * i, 256)],
                    w_sem.at[slot, 4 + i],
                ),
            ]
        return result

    rows = pl.ds(pl.multiple_of(seq * TOK, TOK), TOK)
    first = [
        local_copy(x_hbm, x_v, load_sem.at[0]),
        local_copy(branch_hbm, grad_v, load_sem.at[1]),
        local_copy(c_hbm, c_v, load_sem.at[2]),
    ]
    later = [
        local_copy(q_hbm, q_v, load_sem.at[3]),
        local_copy(kv_hbm, kv_v, load_sem.at[4]),
        local_copy(cos_all.at[rows], cos_v, load_sem.at[5]),
        local_copy(sin_all.at[rows], sin_v, load_sem.at[6]),
    ]
    for copy in first + weights(0, 0) + weights(1, 1):
        copy.start()

    barrier = pltpu.get_barrier_semaphore()
    for device in [dev_c, dev_x, dev_y, dev_d] + dev_z:
        pl.semaphore_signal(barrier, inc=1, device_id=device, device_id_type=MESH)
    pl.semaphore_wait(barrier, 7)

    is_end = (z == 0) | (z == 3)
    is_mid = (z == 1) | (z == 2)
    end_low = jnp.where(z == 0, 1, 0)
    end_dir = jnp.where(z == 0, 0, 1)
    end_next = (jnp.where(z == 0, 1, 2) * 2 + y, seq)
    mid_dir = jnp.where(z == 1, 0, 1)
    mid_low = jnp.where(z == 1, 1, 0)
    mid_keep = jnp.where(z == 1, 2, 0)
    mid_next = ((3 - z) * 2 + y, seq)
    back_dir = 1 - mid_dir
    back_low = jnp.where(z == 2, 2, 0)
    back_keep = jnp.where(z == 2, 3, 0)
    back_next = (jnp.where(z == 2, 3, 0) * 2 + y, seq)

    def z_send(slot, which, pieces, recv, number):
        ssem, rsem = send_sem.at[slot, which], recv_sem.at[slot, which]
        if number == 0:
            low, size, way, device = end_low, 3, end_dir, end_next
        elif number == 1:
            low, size, way, device = mid_keep, 2, mid_dir, mid_next
        else:
            low, size, way, device = back_keep, 1, back_dir, back_next
        return remote(
            pieces.at[pl.ds(low, size)], recv.at[way, pl.ds(low - 1 + way, size)],
            ssem.at[2 + number // 2], rsem.at[2 + way], device,
        )

    def z_wait(slot, which, recv, way, low, size):
        view = recv.at[way, pl.ds(low - 1 + way, size)]
        local_copy(view, view, recv_sem.at[slot, which, 2 + way]).wait()

    def z_round0(slot, which, pieces, recv):
        @pl.when(is_end)
        def _():
            z_send(slot, which, pieces, recv, 0).start()

    def z_round1(slot, which, pieces, recv):
        @pl.when(is_mid)
        def _():
            z_wait(slot, which, recv, mid_dir, mid_low, 3)
            keep = pl.ds(mid_keep, 2)
            pieces[keep] = pieces[keep] + recv[mid_dir, pl.ds(mid_keep - 1 + mid_dir, 2)]
            z_send(slot, which, pieces, recv, 1).start()

    def z_round2(slot, which, pieces, recv):
        @pl.when(is_mid)
        def _():
            z_wait(slot, which, recv, back_dir, back_low, 2)
            keep = pl.ds(back_keep, 1)
            pieces[keep] = pieces[keep] + recv[back_dir, pl.ds(back_keep - 1 + back_dir, 1)]
            z_send(slot, which, pieces, recv, 2).start()

    def z_final(slot, which, pieces, recv, finish):
        @pl.when(is_end)
        def _():
            way = 1 - end_dir
            z_wait(slot, which, recv, way, z, 1)
            finish(pieces[z].astype(f32) + recv[way, z - 1 + way].astype(f32))

        @pl.when(is_mid)
        def _():
            finish(
                pieces[z].astype(f32) + recv[0, z - 1].astype(f32) + recv[1, z].astype(f32)
            )

    def hop(slot, which, index):
        a, b, cc = part_a.at[slot], part_b.at[slot], part_c.at[slot]
        source, target, device = {
            (0, 0): lambda: (a.at[1 - x], recv_a1.at[slot], dev_x),
            (0, 1): lambda: (a.at[x, 1 - y], recv_a2.at[slot], dev_y),
            (1, 0): lambda: (b.at[1 - y], recv_b1.at[slot], dev_y),
            (1, 1): lambda: (b.at[y, 1 - x], recv_b2.at[slot], dev_x),
            (2, 0): lambda: (cc.at[z, 1 - x], recv_c1.at[slot], dev_x),
            (2, 1): lambda: (cc.at[z, x, 1 - y], recv_c2.at[slot], dev_y),
        }[which, index]()
        return remote(
            source, target, send_sem.at[slot, which, index], recv_sem.at[slot, which, index], device
        )

    def put(unit, which, block):
        _, _, _, _, _, offset, out, row = UNITS[unit]
        outs[out][row + PARTS[which] : row + PARTS[which + 1], offset : offset + 256] = block

    def stage(unit, number):
        slot = unit % RING if isinstance(unit, int) else lax.rem(unit, RING)
        a, b, cc = part_a.at[slot], part_b.at[slot], part_c.at[slot]
        a_z, b_z = a.at[x, y], b.at[y, x]
        rz_a, rz_b, rz_c = recv_az.at[slot], recv_bz.at[slot], recv_cz.at[slot]
        if number == 0:
            hop(slot, 0, 0).start()
            hop(slot, 1, 0).start()
            z_round0(slot, 2, cc, rz_c)
        if number == 1:
            hop(slot, 0, 0).wait_recv()
            a[x] = a[x] + recv_a1[slot]
            hop(slot, 0, 1).start()
            hop(slot, 1, 0).wait_recv()
            b[y] = b[y] + recv_b1[slot]
            hop(slot, 1, 1).start()
            z_round1(slot, 2, cc, rz_c)
        if number == 2:
            hop(slot, 0, 1).wait_recv()
            a[x, y] = a[x, y] + recv_a2[slot]
            z_round0(slot, 0, a_z, rz_a)
            hop(slot, 1, 1).wait_recv()
            b[y, x] = b[y, x] + recv_b2[slot]
            z_round0(slot, 1, b_z, rz_b)
            z_round2(slot, 2, cc, rz_c)
        if number == 3:
            z_round1(slot, 0, a_z, rz_a)
            z_round1(slot, 1, b_z, rz_b)

            def keep(value):
                cc[z] = value.astype(bf)

            z_final(slot, 2, cc, rz_c, keep)
            hop(slot, 2, 0).start()
        if number == 4:
            z_round2(slot, 0, a_z, rz_a)
            z_round2(slot, 1, b_z, rz_b)
            hop(slot, 2, 0).wait_recv()
            cc[z, x] = cc[z, x] + recv_c1[slot]
            hop(slot, 2, 1).start()
        if number == 5:
            z_final(slot, 0, a_z, rz_a, functools.partial(put, unit, 0))
            z_final(slot, 1, b_z, rz_b, functools.partial(put, unit, 1))
            hop(slot, 2, 1).wait_recv()
            put(unit, 2, cc[z, x, y].astype(f32) + recv_c2[slot].astype(f32))

    def sums(step):
        for number in range(1, 6):
            unit = step - number + 1
            if isinstance(step, int):
                if 0 <= unit < COUNT:
                    stage(unit, number)
            elif number < 5:

                @pl.when(unit >= 0)
                def _():
                    stage(unit, number)

    def sent(unit):
        slot = unit % RING
        for which in range(3):
            for index in range(2):
                hop(slot, which, index).wait_send()
        for which, (pieces, recv) in enumerate(
            (
                (part_a.at[slot, x, y], recv_az.at[slot]),
                (part_b.at[slot, y, x], recv_bz.at[slot]),
                (part_c.at[slot], recv_cz.at[slot]),
            )
        ):

            @pl.when(is_end)
            def _():
                z_send(slot, which, pieces, recv, 0).wait_send()

            @pl.when(is_mid)
            def _():
                z_send(slot, which, pieces, recv, 1).wait_send()
                z_send(slot, which, pieces, recv, 2).wait_send()

    def multiply(slot, xslot, own, far):
        def step(i, carry):
            columns = pl.ds(pl.multiple_of(i * 512, 512), 512)
            for xi in range(2):
                total = (
                    tn_dot(xbuf[xslot, 0, :, columns], own(xi))
                    + tn_dot(xbuf[xslot, 1, :, columns], far(xi))
                ).astype(bf)
                for k in range(4):
                    zi, yi = 2 * i + k // 2, k % 2
                    block = total[k * 128 : k * 128 + 128]
                    part_a[slot, xi, yi, zi] = block[PARTS[0] : PARTS[1]]
                    part_b[slot, yi, xi, zi] = block[PARTS[1] : PARTS[2]]
                    part_c[slot, zi, xi, yi] = block[PARTS[2] : PARTS[3]]
            return carry

        lax.fori_loop(0, 2, step, 0)

    def far_copy(src, dst, index):
        return remote(src, dst, far_send.at[index], far_recv.at[index], dev_c)

    def pair_columns(array, width, offset, core, xi):
        return array.at[:, pl.ds(pl.multiple_of((2 * xi + core) * width + offset, 256), 256)]

    far_n2 = far_copy(xbuf.at[0, 0], xbuf.at[0, 1], 0)
    far_a = far_copy(att_hbm, far_att, 1)
    far_n = far_copy(normed_hbm, far_normed, 2)
    far_dm = [
        far_copy(pair_columns(dm_v, 256, 0, 1 - c, xi), ydown.at[xi], 3 + xi) for xi in range(2)
    ]
    far_db = [
        far_copy(pair_columns(db_v, 256, 0, 1 - c, xi), yout.at[xi], 5 + xi) for xi in range(2)
    ]
    far_dq = [
        remote(
            pair_columns(dproj_v, 768, 256 * v, 1 - c, xi), yfar.at[v, xi],
            q_send.at[v, xi], q_recv.at[v, xi], dev_c,
        )
        for v in range(3)
        for xi in range(2)
    ]

    def far_other(step):
        return remote(
            other_v.at[lax.rem(step, 2)], yfar.at[lax.rem(step, 4)],
            oth_send.at[lax.rem(step, 2)], oth_recv.at[lax.rem(step, 4)], dev_c,
        )

    def hidden_copies(step):
        slot = lax.rem(step, 2)
        result = []
        for i in range(2):
            at = pl.multiple_of((c if i == 0 else 1 - c) * (FF // 2) + step * 256, 256)
            block = hid_v.at[slot, :, pl.ds(256 * i, 256)]
            result.append(local_copy(block, hid_hbm.at[:, pl.ds(at, 256)], hid_sem.at[slot, i]))
            result.append(
                remote(
                    block, far_hid.at[:, pl.ds(at, 256)],
                    hid_send.at[slot, i], hid_recv.at[step, i], dev_c,
                )
            )
        return result

    for copy in first:
        copy.wait()
    dkv_v[...] = jnp.zeros_like(dkv_v)
    vec_sum[0] = jnp.zeros((8, D), f32)

    def before(i, carry):
        at = pl.ds(pl.multiple_of(i * 128, 128), 128)
        middle = x_v[at, :].astype(f32) + scale_attn_ref[...] * grad_v[at, :]
        hat, _ = normalize(middle)
        xbuf[0, 0, at, :] = (hat * gain2_ref[...] + bias2_ref[...]).astype(bf)
        dm_v[at, :] = (c_v[at, :].astype(f32) * scale_mlp_ref[...]).astype(bf)
        return carry

    lax.fori_loop(0, TOK // 128, before, 0)
    for copy in [far_n2] + far_dm:
        copy.start()
    for copy in later:
        copy.start()

    def mlp(step):
        slot = lax.rem(step, 2)

        @pl.when(step >= 2)
        def _():
            far_other(step - 2).wait_send()
            for copy in hidden_copies(step - 2)[0::2]:
                copy.wait()
            for copy in hidden_copies(step - 2)[1::2]:
                copy.wait_send()

        for copy in weights(step, slot):
            copy.wait()
        normed = xbuf.at[0, 0]
        for i in range(2):
            gate = dot(normed[...], wide_v[4 * slot + i])
            up = dot(normed[...], wide_v[4 * slot + 2 + i])
            dh = contract_back(dm_v[...], deep_v[slot, 256 * i : 256 * i + 256])
            sigmoid = 1.0 / (1.0 + jnp.exp(-gate))
            silu = gate * sigmoid
            hid_v[slot, :, 256 * i : 256 * i + 256] = (silu * up).astype(bf)
            target = ybuf if i == 0 else other_v
            dgate = dh * up * (sigmoid * (1.0 + gate * (1.0 - sigmoid)))
            target[slot, 0] = dgate.astype(bf)
            target[slot, 1] = (dh * silu).astype(bf)
        far_other(step).start()
        for copy in hidden_copies(step):
            copy.start()
        dkv_v[0, 0:TOK] += dot(hid_v[slot], deep_v[slot])
        dkv_v[1, 0:TOK] += (
            contract_back(ybuf[slot, 0], wide_v[4 * slot])
            + contract_back(other_v[slot, 0], wide_v[4 * slot + 1])
            + contract_back(ybuf[slot, 1], wide_v[4 * slot + 2])
            + contract_back(other_v[slot, 1], wide_v[4 * slot + 3])
        )

        @pl.when(step + 2 < 8)
        def _():
            for copy in weights(step + 2, slot):
                copy.start()

    def gate_unit(step):
        far_other(step).wait_recv()
        multiply(
            step, 0, lambda xi: ybuf[lax.rem(step, 2), xi], lambda xi: yfar[lax.rem(step, 4), xi]
        )
        stage(step, 0)

    def mlp_step(step, carry):
        mlp(step)

        @pl.when(step == 0)
        def _():
            far_a.start()
            far_n.start()

        @pl.when(step == 1)
        def _():
            far_n2.wait_recv()

        @pl.when(step >= 1)
        def _():
            gate_unit(step - 1)

        @pl.when(step >= BEHIND)
        def _():
            sums(step - BEHIND)

        return carry

    lax.fori_loop(0, 8, mlp_step, 0)

    wo_copies = [
        local_copy(w_out.at[pl.ds(512 * k, 512)], deep_v.at[k], w_sem.at[k, 4]) for k in range(2)
    ]
    wq_copies = [
        local_copy(w_qkv.at[:, pl.ds(256 * k, 256)], wide_v.at[k % 8], w_sem.at[k % 8 // 4, k % 4])
        for k in range(12)
    ]
    for copy in wo_copies + wq_copies[:8]:
        copy.start()
    for step in (6, 7):
        far_other(step).wait_send()
        for copy in hidden_copies(step)[0::2]:
            copy.wait()
        for copy in hidden_copies(step)[1::2]:
            copy.wait_send()
    for step in range(8):
        for copy in hidden_copies(step)[1::2]:
            copy.wait_recv()

    def load_left(unit):
        left, offset, width, _, _, _, _, _ = UNITS[unit]
        slot = {8: 1, 9: 0, 10: 1, 11: 0, 12: 1, 13: 0}[unit]
        arrays = {3: (hid_hbm, far_hid), 1: (att_hbm, far_att), 0: (normed_hbm, far_normed)}[left]
        result = []
        for side in range(2):
            if width == 128:
                result.append(
                    local_copy(arrays[side], xbuf.at[slot, side], x_sem.at[slot, side, 0])
                )
                continue
            for block in range(8):
                result.append(
                    local_copy(
                        arrays[side].at[:, pl.ds(block * width + offset, 128)],
                        xbuf.at[slot, side, :, pl.ds(block * 128, 128)],
                        x_sem.at[slot, side, block],
                    )
                )
        return result

    def unit_sum(unit):
        if unit <= 13:
            for copy in load_left(unit):
                copy.wait()
        _, _, _, right, width, offset, _, _ = UNITS[unit]
        sent(unit - RING)
        slot, xslot = unit % RING, {8: 1, 9: 0, 10: 1, 11: 0, 12: 1}.get(unit, 0)
        own = {3: dm_v, 1: db_v, 0: dproj_v}[right]
        far = {3: ydown, 1: yout}.get(right, yfar.at[max(unit - 13, 0)])
        multiply(
            slot, xslot,
            lambda xi: pair_columns(own, width, offset, c, xi)[...],
            lambda xi: far[xi],
        )
        stage(unit, 0)
        if unit + 2 <= 13:
            if unit + 2 == 12:
                far_a.wait_recv()
            if unit + 2 == 13:
                far_n.wait_recv()
            for copy in load_left(unit + 2):
                copy.start()

    for copy in load_left(8):
        copy.start()
    gate_unit(7)
    for copy in [far_n2] + far_dm:
        copy.wait_send()
    for copy in load_left(9):
        copy.start()
    for copy in far_dm:
        copy.wait_recv()

    def after(i, carry):
        at = pl.ds(pl.multiple_of(i * 128, 128), 128)
        cot = c_v[at, :].astype(f32)
        branch = grad_v[at, :]
        middle = x_v[at, :].astype(f32) + scale_attn_ref[...] * branch
        mlp_out = dkv_v[0, at, :]
        dn = dkv_v[1, at, :]
        vec_sum[0, 5:6] += jnp.sum(cot * mlp_out, 0, keepdims=True)
        c_v[at, :] = (middle + scale_mlp_ref[...] * mlp_out).astype(bf)
        hat, inverse = normalize(middle)
        vec_sum[0, 3:4] += jnp.sum(dn * hat, 0, keepdims=True)
        vec_sum[0, 4:5] += jnp.sum(dn, 0, keepdims=True)
        dmid = cot + norm_backward(dn, hat, inverse, gain2_ref[...])
        vec_sum[0, 2:3] += jnp.sum(dmid * branch, 0, keepdims=True)
        grad_v[at, :] = dmid
        db_v[at, :] = (dmid * scale_attn_ref[...]).astype(bf)
        return carry

    out_copy = local_copy(c_v, out_hbm, out_sem.at[0])
    grad_copy = local_copy(grad_v, grad_hbm, out_sem.at[1])

    def norm_two_back():
        lax.fori_loop(0, TOK // 128, after, 0)
        out_copy.start()
        for copy in far_db:
            copy.start()

    def attended_grads():
        window_bias(bias_v, clip_ref, 4 * TOK, True)
        for k in range(2):
            wo_copies[k].wait()
        for k in range(2):
            datt_v[:, 512 * k : 512 * k + 512] = contract_back(db_v[...], deep_v[k]).astype(bf)
        for copy in far_db:
            copy.wait_recv()

    last = TOK // 128 - 1
    heads = 4
    lanes_of = heads * HEAD_DIM

    def attend(blocks):
        def step(group, carry):
            lanes = pl.ds(pl.multiple_of(group * lanes_of, lanes_of), lanes_of)
            held = []
            for block in blocks:
                own = slice(block * 128, block * 128 + 128)
                window = slice(block * 128, block * 128 + 256)
                queries = stacked_heads(q_v[own, lanes] * 0.125, heads)
                grads = stacked_heads(datt_v[own, lanes], heads)
                keys = kv_v[0, window, lanes]
                bias = jnp.concatenate([bias_v[block]] * (heads // 2), 1)
                scores = contract_back(keys, queries) + bias
                d_probs = contract_back(kv_v[1, window, lanes], grads)
                held.append((queries, grads, keys, scores, d_probs))
            ready = []
            for queries, grads, keys, scores, d_probs in held:
                exponent = jnp.exp(scores - jnp.max(scores, 0, keepdims=True))
                probs = exponent * (1.0 / jnp.sum(exponent, 0, keepdims=True))
                inner = jnp.sum(probs * d_probs, 0, keepdims=True)
                d_scores = (probs * (d_probs - inner)).astype(bf)
                ready.append((queries, grads, keys, d_scores, probs.astype(bf)))
            for block, (queries, grads, keys, d_scores, probs) in zip(blocks, ready):
                own = slice(block * 128, block * 128 + 128)
                window = slice(block * 128, block * 128 + 256)
                for which, update in ((0, dot(d_scores, queries)), (1, dot(probs, grads))):
                    if block in (0, last):
                        dkv_v[which, window, lanes] = update
                    elif block == 1:
                        dkv_v[which, 128:256, lanes] += update[:128]
                        dkv_v[which, 256:384, lanes] = update[128:]
                    else:
                        dkv_v[which, window, lanes] += update
                d_queries = merged_heads(tn_dot(d_scores, keys), heads) * 0.125
                for k in range(lanes_of // 128):
                    at = pl.ds(pl.multiple_of(group * lanes_of + 128 * k, 128), 128)
                    dproj_v[own, at] = rotated(
                        d_queries[:, 128 * k : 128 * k + 128], cos_v[own, :], -sin_v[own, :]
                    ).astype(bf)
            return carry

        lax.fori_loop(0, D // lanes_of, step, 0)

    has_left, has_right = seq > 0, seq < 3
    to_left = remote(
        edge_v.at[0], far_v.at[1], edge_send.at[0], edge_recv.at[0], (dp, seq - 1)
    )
    to_right = remote(
        edge_v.at[1], far_v.at[0], edge_send.at[1], edge_recv.at[1], (dp, seq + 1)
    )

    def edges_out():
        edge_v[0] = dkv_v[:, 0:HALF].astype(bf)
        edge_v[1] = dkv_v[:, HALF + TOK :].astype(bf)

        @pl.when(has_left)
        def _():
            to_left.start()

        @pl.when(has_right)
        def _():
            to_right.start()

    def edges_in():
        @pl.when(has_left)
        def _():
            to_right.wait_recv()
            dkv_v[:, HALF : 2 * HALF] += far_v[0].astype(f32)

        @pl.when(has_right)
        def _():
            to_left.wait_recv()
            dkv_v[:, TOK : TOK + HALF] += far_v[1].astype(f32)

        for k in range(D // 128):
            lanes = slice(k * 128, k * 128 + 128)
            dproj_v[:, D + k * 128 : D + k * 128 + 128] = rotated(
                dkv_v[0, HALF : HALF + TOK, lanes], cos_v[...], -sin_v[...]
            ).astype(bf)
            dproj_v[:, 2 * D + k * 128 : 2 * D + k * 128 + 128] = dkv_v[
                1, HALF : HALF + TOK, lanes
            ].astype(bf)
        for copy in far_dq:
            copy.start()

    def project_back(chunks, fresh):
        for k in chunks:
            wq_copies[k].wait()
        total = None
        for k in chunks:
            term = contract_back(dproj_v[:, 256 * k : 256 * k + 256], wide_v[k % 8])
            total = term if total is None else total + term
        if fresh:
            dkv_v[0, 0:TOK] = total
        else:
            dkv_v[0, 0:TOK] += total

    def last_norm(i, carry):
        at = pl.ds(pl.multiple_of(i * 128, 128), 128)
        hat, inverse = normalize(x_v[at, :].astype(f32))
        dn = dkv_v[0, at, :]
        vec_sum[0, 0:1] += jnp.sum(dn * hat, 0, keepdims=True)
        vec_sum[0, 1:2] += jnp.sum(dn, 0, keepdims=True)
        grad_v[at, :] += norm_backward(dn, hat, inverse, gain1_ref[...])
        return carry

    def norm_one_back():
        lax.fori_loop(0, TOK // 128, last_norm, 0)
        grad_copy.start()

    def vec_copy(number):
        return remote(
            vec_sum.at[number], vec_recv.at[number], vec_send.at[number], vec_rsem.at[number],
            (dev_c, dev_x, dev_y)[number],
        )

    vec_planes = [
        remote(vec_sum.at[3], vec_z.at[z], vec_send.at[3 + k], vec_rsem.at[3 + k], dev_z[k])
        for k in range(3)
    ]

    def vectors(number):
        if 0 < number <= 3:
            vec_copy(number - 1).wait_recv()
            vec_sum[number] = vec_sum[number - 1] + vec_recv[number - 1]
        if number < 3:
            vec_copy(number).start()
        elif number == 3:
            vec_z[z] = vec_sum[3]
            for copy in vec_planes:
                copy.start()
        else:
            for k in range(3):
                view = vec_z.at[lax.rem(z + 3 - k, 4)]
                local_copy(view, view, vec_rsem.at[3 + k]).wait()
            vec_out[...] = vec_z[0] + vec_z[1] + vec_z[2] + vec_z[3]

    def start_wq():
        for copy in wq_copies[8:]:
            copy.start()

    def far_dq_wait():
        for copy in far_dq:
            copy.wait_recv()

    actions = {
        "E": norm_two_back,
        "D": attended_grads,
        "A0": lambda: attend([0, last]),
        "O": edges_out,
        "A1": lambda: attend(list(range(1, last))),
        "I": edges_in,
        "W0": lambda: (project_back(range(8), True), start_wq()),
        "W1": lambda: project_back(range(8, 12), False),
        "N": norm_one_back,
        "Q": far_dq_wait,
    }
    for copy in later:
        copy.wait()
    for word in ORDER.split():
        if word in actions:
            actions[word]()
        elif word[0] == "P":
            unit_sum(int(word[1:]))
        elif word[0] == "S":
            sums(int(word[1:]))
        elif word[0] == "V":
            vectors(int(word[1:]))

    for unit in range(COUNT - RING, COUNT):
        sent(unit)
    for copy in [far_a, far_n] + far_db + far_dq + [vec_copy(k) for k in range(3)] + vec_planes:
        copy.wait_send()

    @pl.when(has_left)
    def _():
        to_left.wait_send()

    @pl.when(has_right)
    def _():
        to_right.wait_send()

    out_copy.wait()
    grad_copy.wait()


BEHIND = 4
ORDER = (
    "S4 P8 E S5 P9 D S6 P10 A0 O S7 P11 A1 I S8 P12 W0 S9 W1 Q P13 N S10 V0 P14 S11 V1 P15 S12 V2"
    " S13 V3 S14 V4 S15 S16 S17 S18 S19"
)


def layer(
    lengths, frames, cotangent, branch, queries, kv, attended, normed, vectors, w_qkv, w_out,
    w_gate_up, w_down, tables,
):
    bf, f32 = jnp.bfloat16, jnp.float32
    hbm = pl.BlockSpec(memory_space=pl.ANY)
    vmem = pl.BlockSpec(memory_space=pltpu.VMEM)
    smem = pl.BlockSpec(memory_space=pltpu.SMEM)
    shape = jax.ShapeDtypeStruct
    size = (PARTS[1], PARTS[2] - PARTS[1], PARTS[3] - PARTS[2])
    dma = pltpu.SemaphoreType.DMA
    ext = TOK + 2 * HALF
    scratch = [
        pltpu.VMEM((RING, 2, 2, 4, size[0], 256), bf),
        pltpu.VMEM((RING, 2, 2, 4, size[1], 256), bf),
        pltpu.VMEM((RING, 4, 2, 2, size[2], 256), bf),
        pltpu.VMEM((RING, 2, 4, size[0], 256), bf),
        pltpu.VMEM((RING, 4, size[0], 256), bf),
        pltpu.VMEM((RING, 2, 3, size[0], 256), bf),
        pltpu.VMEM((RING, 2, 4, size[1], 256), bf),
        pltpu.VMEM((RING, 4, size[1], 256), bf),
        pltpu.VMEM((RING, 2, 3, size[1], 256), bf),
        pltpu.VMEM((RING, 2, 3, 2, 2, size[2], 256), bf),
        pltpu.VMEM((RING, 2, size[2], 256), bf),
        pltpu.VMEM((RING, size[2], 256), bf),
        pltpu.VMEM((8, D, 256), bf),
        pltpu.VMEM((2, 512, D), bf),
        pltpu.VMEM((2, ext, D), f32),
        pltpu.VMEM((2, 2, TOK, D), bf),
        pltpu.VMEM((2, 2, TOK, 256), bf),
        pltpu.VMEM((4, 2, TOK, 256), bf),
        pltpu.VMEM((2, TOK, 256), bf),
        pltpu.VMEM((2, TOK, 256), bf),
        pltpu.VMEM((2, 2, TOK, 256), bf),
        pltpu.VMEM((2, TOK, 512), bf),
        pltpu.VMEM((TOK, D), bf),
        pltpu.VMEM((TOK, D), bf),
        pltpu.VMEM((TOK, D), bf),
        pltpu.VMEM((TOK, D), bf),
        pltpu.VMEM((TOK, D), bf),
        pltpu.VMEM((TOK, D), f32),
        pltpu.VMEM((TOK, D), bf),
        pltpu.VMEM((2, ext, D), bf),
        pltpu.VMEM((TOK, 3 * D), bf),
        pltpu.VMEM((TOK // 128, 256, 256), f32),
        pltpu.VMEM((TOK, 128), f32),
        pltpu.VMEM((TOK, 128), f32),
        pltpu.VMEM((2, 2, HALF, D), bf),
        pltpu.VMEM((2, 2, HALF, D), bf),
        pltpu.VMEM((4, 8, D), f32),
        pltpu.VMEM((3, 8, D), f32),
        pltpu.VMEM((4, 8, D), f32),
        dma((RING, 3, 4)),
        dma((RING, 3, 4)),
        dma((7,)),
        dma((7,)),
        dma((7,)),
        dma((2, 6)),
        dma((2, 2)),
        dma((2, 2)),
        dma((8, 2)),
        dma((2,)),
        dma((4,)),
        dma((3, 2)),
        dma((3, 2)),
        dma((2, 2, 8)),
        dma((2,)),
        dma((2,)),
        dma((6,)),
        dma((6,)),
        dma((2,)),
    ]
    return pl.pallas_call(
        layer_kernel,
        out_shape=[
            shape((TOK, D), bf),
            shape((TOK, D), f32),
            shape((128, 768), f32),
            shape((128, 256), f32),
            shape((128, 2048), f32),
            shape((512, 256), f32),
            shape((8, D), f32),
            shape((TOK, D), bf),
            shape((TOK, D), bf),
            shape((TOK, FF), bf),
            shape((TOK, FF), bf),
        ],
        in_specs=[smem] + [hbm] * 7 + [vmem] * 5 + [hbm] * 6,
        out_specs=[hbm] * 2 + [vmem] * 5 + [hbm] * 4,
        scratch_shapes=scratch,
        compiler_params=pltpu.CompilerParams(
            collective_id=4, has_side_effects=True, vmem_limit_bytes=64 * 2**20 - 2**16
        ),
        name="layer",
    )(
        lengths, frames, cotangent, branch, queries, kv, attended, normed,
        *[v[None] for v in vectors], w_qkv, w_out, w_gate_up, w_down, *tables,
    )[:7]


def local(
    frames,
    cotangent,
    clip_len,
    ln1_gain,
    ln1_bias,
    w_qkv,
    w_out,
    scale_attn,
    ln2_gain,
    ln2_bias,
    w_gate_up,
    w_down,
    scale_mlp,
):
    row_count = frames.shape[0]
    seq_count = lax.axis_size("seq")
    tables = rotary_tables(row_count * seq_count)
    normed_b, queries, kv, attended_t, branch = forward_attention(
        frames, clip_len, ln1_gain, ln1_bias, scale_attn, w_qkv, w_out, tables, seq_count
    )
    data_count = lax.axis_size("dp")
    if (data_count, seq_count, row_count) == (8, 4, TOK):
        out_frames, input_grad, sum_qkv, sum_out, sum_gate_up, sum_down, vector_total = layer(
            clip_len, frames, cotangent, branch, queries, kv, attended_t, normed_b,
            (ln1_gain, ln2_gain, ln2_bias, scale_attn, scale_mlp),
            w_qkv, w_out, w_gate_up, w_down, tables,
        )
    else:
        out_frames, normed_two_b, hidden_b, gate_up_b, mlp_grad, branch_grad, middle_grad, vec_two = (
            feed_forward(
                frames, cotangent, branch, ln2_gain, ln2_bias, scale_attn, scale_mlp, w_gate_up, w_down
            )
        )
        projected_grad, input_grad, vec_one = backward_attention(
            frames, clip_len, ln1_gain, queries, kv, branch_grad, middle_grad, w_qkv, w_out, tables,
            seq_count,
        )
        vector_grads = jnp.stack(
            [vec_one[0], vec_one[1], vec_two[3], vec_two[1], vec_two[2], vec_two[0]], 0
        )
        lefts = (normed_b, attended_t, normed_two_b, hidden_b)
        rights = (projected_grad, branch_grad, gate_up_b, mlp_grad)
        vector_total = lax.psum(vector_grads, ("dp", "seq"))
        sum_qkv, sum_out, sum_gate_up, sum_down = [
            lax.psum_scatter(
                to_blocks(contract_rows(left, right), data_count, seq_count),
                ("dp", "seq"),
                scatter_dimension=0,
                tiled=True,
            )[0]
            for left, right in zip(lefts, rights)
        ]
    return (
        out_frames,
        input_grad,
        vector_total[0],
        vector_total[1],
        sum_qkv,
        sum_out,
        vector_total[2],
        vector_total[3],
        vector_total[4],
        sum_gate_up,
        sum_down,
        vector_total[5],
    )


def solution(mesh):
    return jax.shard_map(
        local,
        mesh=mesh,
        in_specs=(
            P(("dp", "seq"), None),
            P(("dp", "seq"), None),
            P("dp", None),
            P(),
            P(),
            P(),
            P(),
            P(),
            P(),
            P(),
            P(),
            P(),
            P(),
        ),
        out_specs=(
            P(("dp", "seq"), None),
            P(("dp", "seq"), None),
            P(),
            P(),
            P("dp", "seq"),
            P("dp", "seq"),
            P(),
            P(),
            P(),
            P("dp", "seq"),
            P("dp", "seq"),
            P(),
        ),
        check_vma=False,
    )
```

```python
import functools

import jax
import jax.numpy as jnp
import numpy as np
from jax import lax
from jax.experimental import pallas as pl
from jax.experimental.pallas import tpu as pltpu
from jax.sharding import PartitionSpec as P

D = 1024
HEADS = 16
HEAD_DIM = 64
FF = 4096
HALF = 64
QBLK = 512


EPS = 1e-05
NEG = -1e30


def contract_rows(left, right):
    return lax.dot_general(
        left, right, (((0,), (0,)), ((), ())), preferred_element_type=jnp.float32
    )


def contract_back(grads, weight):
    return lax.dot_general(
        grads, weight, (((1,), (1,)), ((), ())), preferred_element_type=jnp.float32
    )


def to_blocks(matrix, data_count, seq_count):
    row_total, col_total = matrix.shape
    shaped = matrix.reshape(data_count, row_total // data_count, seq_count, col_total // seq_count)
    return shaped.transpose(0, 2, 1, 3).reshape(
        data_count * seq_count, row_total // data_count, col_total // seq_count
    )


MESH = pl.DeviceIdType.MESH
TOK = 512
PARTS = (0, 48, 96, 128)

UNITS = (
    [(2, 0, 128, 2, 2048, 256 * v, 2, 0) for v in range(8)]
    + [(3, 128 * v, 512, 3, 256, 0, 3, 128 * v) for v in range(4)]
    + [(1, 0, 128, 1, 256, 0, 1, 0)]
    + [(0, 0, 128, 0, 768, 256 * v, 0, 0) for v in range(3)]
)


def tn_dot(left, right):
    return lax.dot_general(
        left, right, (((0,), (0,)), ((), ())), preferred_element_type=jnp.float32
    )


def rotated(values, cosines, sines):
    lane = lax.broadcasted_iota(jnp.int32, values.shape, 1)
    partner = jnp.where(
        lane % HEAD_DIM < HEAD_DIM // 2,
        pltpu.roll(values, 128 - HEAD_DIM // 2, 1),
        pltpu.roll(values, HEAD_DIM // 2, 1),
    )
    return values * cosines + partner * sines


def head_masks():
    lane = lax.broadcasted_iota(jnp.int32, (128, 128), 1)
    return lane < HEAD_DIM


def stacked(pair):
    first = head_masks()
    zero = jnp.zeros_like(pair)
    return jnp.concatenate([jnp.where(first, pair, zero), jnp.where(first, zero, pair)], 0)


def merged(rows):
    return jnp.where(head_masks(), rows[:128], rows[128:])


def clip_number(positions, ends, group_len):
    total = jnp.zeros_like(positions)
    for end in ends:
        total = total + (positions >= end).astype(jnp.int32)
    return jnp.where((positions >= 0) & (positions < group_len), total, -1)


def normalize(values):
    average = jnp.mean(values, -1, keepdims=True)
    centered = values - average
    inverse = lax.rsqrt(jnp.mean(centered * centered, -1, keepdims=True) + EPS)
    return centered * inverse, inverse


def dot(left, right):
    return jnp.dot(left, right, preferred_element_type=jnp.float32)


def norm_backward(grads, hat, inverse, gain):
    scaled = grads * gain
    return inverse * (
        scaled
        - jnp.mean(scaled, -1, keepdims=True)
        - hat * jnp.mean(scaled * hat, -1, keepdims=True)
    )


def window_bias(bias_ref, clip_ref, group_len, keys_first):
    seq = lax.axis_index("seq")
    first_end = clip_ref[0, 0]
    second_end = first_end + clip_ref[0, 1]
    ends = (first_end, second_end, second_end + clip_ref[0, 2])
    for block in range(TOK // 128):
        start = seq * TOK + block * 128
        shape = (2 * 128, 2 * 128)
        k_axis = 0 if keys_first else 1
        k_at = lax.broadcasted_iota(jnp.int32, shape, k_axis)
        q_at = lax.rem(lax.broadcasted_iota(jnp.int32, shape, 1 - k_axis), 128)
        q_shape = (1, 256) if keys_first else (256, 1)
        k_shape = (256, 1) if keys_first else (1, 256)
        q_ids = clip_number(
            start + lax.rem(lax.broadcasted_iota(jnp.int32, q_shape, 1 - k_axis), 128),
            ends, group_len,
        )
        k_ids = clip_number(
            start - HALF + lax.broadcasted_iota(jnp.int32, k_shape, k_axis), ends, group_len
        )
        seen = (q_ids == k_ids) & (k_at >= q_at) & (k_at < q_at + 2 * HALF)
        bias_ref[block] = jnp.where(seen, 0.0, NEG)


def greet_sides(seq_count):
    dp, seq = lax.axis_index("dp"), lax.axis_index("seq")
    barrier = pltpu.get_barrier_semaphore()
    has_left, has_right = seq > 0, seq < seq_count - 1

    @pl.when(has_left)
    def _():
        pl.semaphore_signal(barrier, inc=1, device_id=(dp, seq - 1), device_id_type=MESH)

    @pl.when(has_right)
    def _():
        pl.semaphore_signal(barrier, inc=1, device_id=(dp, seq + 1), device_id_type=MESH)

    pl.semaphore_wait(barrier, has_left.astype(jnp.int32) + has_right.astype(jnp.int32))

    return (dp, seq - 1), (dp, seq + 1), has_left, has_right


def forward_kernel(
    seq_count, clip_ref, x_ref, gain_ref, gain_bias_ref, scale_ref, w_qkv, w_out, cos_all, sin_all,
    normed_ref, q_ref, kv_ref, att_ref, branch_ref,
    wq_v, wo_v, cos_v, sin_v, bias_v, load_sem, send_sem, recv_sem,
):
    dp, seq = lax.axis_index("dp"), lax.axis_index("seq")
    rows = pl.ds(pl.multiple_of(seq * TOK, TOK), TOK)
    copies = []
    order = [2, 3, 4, 5, 0, 1]
    tables = [
        pltpu.make_async_copy(cos_all.at[rows], cos_v, load_sem.at[0]),
        pltpu.make_async_copy(sin_all.at[rows], sin_v, load_sem.at[1]),
    ]
    chunks = {
        k: pltpu.make_async_copy(
            w_qkv.at[:, pl.ds(k * 512, 512)], wq_v.at[k], load_sem.at[2 + k]
        )
        for k in order
    }
    out_copy = pltpu.make_async_copy(w_out, wo_v, load_sem.at[8])
    for copy in tables + [chunks[k] for k in order] + [out_copy]:
        copy.start()
    left, right, has_left, has_right = greet_sides(seq_count)

    hat, _ = normalize(x_ref[...].astype(jnp.float32))
    normed_ref[...] = (hat * gain_ref[...] + gain_bias_ref[...]).astype(jnp.bfloat16)
    for copy in tables:
        copy.wait()

    def project(k):
        chunks[k].wait()
        for part in range(2):
            cols = slice(part * 256, part * 256 + 256)
            full = dot(normed_ref[...], wq_v[k, :, cols])
            for half in range(2):
                block = full[:, half * 128 : half * 128 + 128]
                at = (k % 2) * 512 + part * 256 + half * 128
                if k < 4:
                    block = rotated(block, cos_v[...], sin_v[...])
                block = block.astype(jnp.bfloat16)
                if k < 2:
                    q_ref[:, at : at + 128] = block
                else:
                    kv_ref[k // 2 - 1, HALF : HALF + TOK, at : at + 128] = block

    for k in order[:4]:
        project(k)

    to_left = pltpu.make_async_remote_copy(
        src_ref=kv_ref.at[:, pl.ds(HALF, HALF)], dst_ref=kv_ref.at[:, pl.ds(HALF + TOK, HALF)],
        send_sem=send_sem.at[0], recv_sem=recv_sem.at[0], device_id=left, device_id_type=MESH,
    )
    to_right = pltpu.make_async_remote_copy(
        src_ref=kv_ref.at[:, pl.ds(TOK, HALF)], dst_ref=kv_ref.at[:, pl.ds(0, HALF)],
        send_sem=send_sem.at[1], recv_sem=recv_sem.at[1], device_id=right, device_id_type=MESH,
    )

    @pl.when(has_left)
    def _():
        to_left.start()

    @pl.when(has_right)
    def _():
        to_right.start()

    @pl.when(jnp.logical_not(has_left))
    def _():
        kv_ref[:, 0:HALF] = jnp.zeros((2, HALF, D), jnp.bfloat16)

    @pl.when(jnp.logical_not(has_right))
    def _():
        kv_ref[:, HALF + TOK :] = jnp.zeros((2, HALF, D), jnp.bfloat16)

    for k in order[4:]:
        project(k)
    window_bias(bias_v, clip_ref, seq_count * TOK, False)

    heads = 4
    lanes_of = heads * HEAD_DIM

    def attend(blocks):
        def step(group, carry):
            lanes = pl.ds(pl.multiple_of(group * lanes_of, lanes_of), lanes_of)
            scores = []
            for block in blocks:
                queries = q_ref[block * 128 : block * 128 + 128, lanes] * 0.125
                keys = kv_ref[0, block * 128 : block * 128 + 256, lanes]
                bias = jnp.concatenate([bias_v[block]] * (heads // 2), 0)
                scores.append(contract_back(stacked_heads(queries, heads), keys) + bias)
            probs = []
            for score in scores:
                exponent = jnp.exp(score - jnp.max(score, -1, keepdims=True))
                total = jnp.sum(exponent, -1, keepdims=True)
                probs.append((exponent * (1.0 / total)).astype(jnp.bfloat16))
            for block, prob in zip(blocks, probs):
                values = kv_ref[1, block * 128 : block * 128 + 256, lanes]
                att_ref[block * 128 : block * 128 + 128, lanes] = merged_heads(
                    dot(prob, values), heads
                ).astype(jnp.bfloat16)
            return carry

        lax.fori_loop(0, D // lanes_of, step, 0)

    last = TOK // 128 - 1
    attend(list(range(1, last)))

    @pl.when(has_left)
    def _():
        to_right.wait_recv()

    @pl.when(has_right)
    def _():
        to_left.wait_recv()

    attend([0, last])
    out_copy.wait()
    for part in range(4):
        cols = slice(part * 256, part * 256 + 256)
        branch_ref[:, cols] = dot(att_ref[...], wo_v[:, cols])

    @pl.when(has_left)
    def _():
        to_left.wait_send()

    @pl.when(has_right)
    def _():
        to_right.wait_send()


def rotary_tables(group_len):
    half = HEAD_DIM // 2
    inv_freq = (10000.0 ** (-np.arange(half) / half)).astype(np.float32)[None, :]
    angles = np.arange(group_len, dtype=np.float32)[:, None] * inv_freq
    cosine, sine = np.cos(angles), np.sin(angles)
    return (
        np.concatenate([cosine] * 4, 1).astype(np.float32),
        np.concatenate([-sine, sine] * 2, 1).astype(np.float32),
    )


def forward_attention(frames, lengths, gain, bias, scale, w_qkv, w_out, tables, seq_count):
    bf, f32 = jnp.bfloat16, jnp.float32
    hbm = pl.BlockSpec(memory_space=pl.ANY)
    vmem = pl.BlockSpec(memory_space=pltpu.VMEM)
    smem = pl.BlockSpec(memory_space=pltpu.SMEM)
    shape = jax.ShapeDtypeStruct
    return pl.pallas_call(
        functools.partial(forward_kernel, seq_count),
        out_shape=[
            shape((TOK, D), bf),
            shape((TOK, D), bf),
            shape((2, TOK + 2 * HALF, D), bf),
            shape((TOK, D), bf),
            shape((TOK, D), f32),
        ],
        in_specs=[smem] + [vmem] * 4 + [hbm] * 4,
        out_specs=[vmem] * 5,
        scratch_shapes=[
            pltpu.VMEM((6, D, 512), bf),
            pltpu.VMEM((D, D), bf),
            pltpu.VMEM((TOK, 128), f32),
            pltpu.VMEM((TOK, 128), f32),
            pltpu.VMEM((TOK // 128, 256, 256), f32),
            pltpu.SemaphoreType.DMA((9,)),
            pltpu.SemaphoreType.DMA((2,)),
            pltpu.SemaphoreType.DMA((2,)),
        ],
        compiler_params=pltpu.CompilerParams(
            collective_id=2, has_side_effects=True, vmem_limit_bytes=56 * 2**20
        ),
        name="attention_forward",
    )(lengths, frames, gain[None], bias[None], scale[None], w_qkv, w_out, *tables)


FBLK = 512


def mlp_kernel(
    x_ref, c_ref, branch_ref, gain_ref, bias_ref, scale_attn_ref, scale_mlp_ref, w_gate_up, w_down,
    out_ref, n2_ref, hidden_ref, dgu_ref, dm_ref, db_ref, dmid_ref, vec_ref,
    wg_v, wu_v, wd_v, mlp_v, dn_v, load_sem,
):
    count = FF // FBLK

    def copies(step, slot):
        at = pl.multiple_of(step * FBLK, FBLK)
        return [
            pltpu.make_async_copy(
                w_gate_up.at[:, pl.ds(at, FBLK)], wg_v.at[slot], load_sem.at[slot, 0]
            ),
            pltpu.make_async_copy(
                w_gate_up.at[:, pl.ds(FF + at, FBLK)], wu_v.at[slot], load_sem.at[slot, 1]
            ),
            pltpu.make_async_copy(
                w_down.at[pl.ds(at, FBLK)], wd_v.at[slot], load_sem.at[slot, 2]
            ),
        ]

    for copy in copies(0, 0):
        copy.start()
    middle = x_ref[...].astype(jnp.float32) + scale_attn_ref[...] * branch_ref[...]
    hat, inverse = normalize(middle)
    n2_ref[...] = (hat * gain_ref[...] + bias_ref[...]).astype(jnp.bfloat16)
    dm_ref[...] = (c_ref[...].astype(jnp.float32) * scale_mlp_ref[...]).astype(jnp.bfloat16)
    mlp_v[...] = jnp.zeros_like(mlp_v)
    dn_v[...] = jnp.zeros_like(dn_v)

    def step(number, carry):
        slot = lax.rem(number, 2)

        @pl.when(number + 1 < count)
        def _():
            for copy in copies(number + 1, 1 - slot):
                copy.start()

        for copy in copies(number, slot):
            copy.wait()
        for part in range(FBLK // 256):
            cols = slice(part * 256, part * 256 + 256)
            at = pl.multiple_of(number * FBLK + part * 256, 256)
            gate = dot(n2_ref[...], wg_v[slot, :, cols])
            up = dot(n2_ref[...], wu_v[slot, :, cols])
            dh = contract_back(dm_ref[...], wd_v[slot, cols, :])
            sigmoid = 1.0 / (1.0 + jnp.exp(-gate))
            silu = gate * sigmoid
            hidden_ref[:, pl.ds(at, 256)] = (silu * up).astype(jnp.bfloat16)
            dgate = dh * up * (sigmoid * (1.0 + gate * (1.0 - sigmoid)))
            dgu_ref[:, pl.ds(at, 256)] = dgate.astype(jnp.bfloat16)
            dgu_ref[:, pl.ds(FF + at, 256)] = (dh * silu).astype(jnp.bfloat16)
        at = pl.multiple_of(number * FBLK, FBLK)
        mlp_v[...] += dot(hidden_ref[:, pl.ds(at, FBLK)], wd_v[slot])
        dn_v[...] += contract_back(dgu_ref[:, pl.ds(at, FBLK)], wg_v[slot]) + contract_back(
            dgu_ref[:, pl.ds(FF + at, FBLK)], wu_v[slot]
        )
        return carry

    lax.fori_loop(0, count, step, 0)
    cot = c_ref[...].astype(jnp.float32)
    branch = branch_ref[...]
    middle = x_ref[...].astype(jnp.float32) + scale_attn_ref[...] * branch
    mlp_out = mlp_v[...]
    out_ref[...] = (middle + scale_mlp_ref[...] * mlp_out).astype(jnp.bfloat16)
    vec_ref[0:1] = jnp.sum(cot * mlp_out, 0, keepdims=True)
    hat, inverse = normalize(middle)
    dn = dn_v[...]
    vec_ref[1:2] = jnp.sum(dn * hat, 0, keepdims=True)
    vec_ref[2:3] = jnp.sum(dn, 0, keepdims=True)
    dmid = cot + norm_backward(dn, hat, inverse, gain_ref[...])
    dmid_ref[...] = dmid
    vec_ref[3:4] = jnp.sum(dmid * branch, 0, keepdims=True)
    vec_ref[4:8] = jnp.zeros((4, D), jnp.float32)
    db_ref[...] = (dmid * scale_attn_ref[...]).astype(jnp.bfloat16)


def feed_forward(frames, cotangent, branch, gain, bias, scale_attn, scale_mlp, w_gate_up, w_down):
    bf, f32 = jnp.bfloat16, jnp.float32
    hbm = pl.BlockSpec(memory_space=pl.ANY)
    vmem = pl.BlockSpec(memory_space=pltpu.VMEM)
    shape = jax.ShapeDtypeStruct
    return pl.pallas_call(
        mlp_kernel,
        out_shape=[
            shape((TOK, D), bf),
            shape((TOK, D), bf),
            shape((TOK, FF), bf),
            shape((TOK, 2 * FF), bf),
            shape((TOK, D), bf),
            shape((TOK, D), bf),
            shape((TOK, D), f32),
            shape((8, D), f32),
        ],
        in_specs=[vmem] * 7 + [hbm] * 2,
        out_specs=[vmem] * 8,
        scratch_shapes=[
            pltpu.VMEM((2, D, FBLK), bf),
            pltpu.VMEM((2, D, FBLK), bf),
            pltpu.VMEM((2, FBLK, D), bf),
            pltpu.VMEM((TOK, D), f32),
            pltpu.VMEM((TOK, D), f32),
            pltpu.SemaphoreType.DMA((2, 3)),
        ],
        compiler_params=pltpu.CompilerParams(vmem_limit_bytes=56 * 2**20),
        name="feed_forward",
    )(
        frames, cotangent, branch, gain[None], bias[None], scale_attn[None], scale_mlp[None],
        w_gate_up, w_down,
    )


def backward_kernel(
    seq_count, clip_ref, x_ref, gain_ref, q_ref, kv_ref, db_ref, dmid_ref, w_qkv, w_out,
    cos_all, sin_all,
    dproj_ref, grad_ref, vec_ref,
    wq_v, wo_v, cos_v, sin_v, bias_v, datt_v, dkv_v, edge_v, far_v, load_sem, send_sem, recv_sem,
):
    seq = lax.axis_index("seq")
    rows = pl.ds(pl.multiple_of(seq * TOK, TOK), TOK)
    out_copy = pltpu.make_async_copy(w_out, wo_v, load_sem.at[8])
    tables = [
        pltpu.make_async_copy(cos_all.at[rows], cos_v, load_sem.at[0]),
        pltpu.make_async_copy(sin_all.at[rows], sin_v, load_sem.at[1]),
    ]
    chunks = [
        pltpu.make_async_copy(
            w_qkv.at[:, pl.ds(k * 512, 512)], wq_v.at[k], load_sem.at[2 + k]
        )
        for k in range(6)
    ]
    for copy in [out_copy] + tables + chunks:
        copy.start()
    left, right, has_left, has_right = greet_sides(seq_count)
    window_bias(bias_v, clip_ref, seq_count * TOK, True)
    out_copy.wait()
    for part in range(4):
        cols = slice(part * 256, part * 256 + 256)
        datt_v[:, cols] = contract_back(db_ref[...], wo_v[cols, :]).astype(jnp.bfloat16)
    for copy in tables:
        copy.wait()
    last = TOK // 128 - 1

    def attend(blocks):
        def step(pair, carry):
            lanes = pl.ds(pl.multiple_of(pair * 128, 128), 128)
            for block in blocks:
                own = slice(block * 128, block * 128 + 128)
                window = slice(block * 128, block * 128 + 256)
                queries = stacked(q_ref[own, lanes] * 0.125)
                grads = stacked(datt_v[own, lanes])
                keys = kv_ref[0, window, lanes]
                scores = contract_back(keys, queries) + bias_v[block]
                exponent = jnp.exp(scores - jnp.max(scores, 0, keepdims=True))
                total = jnp.sum(exponent, 0, keepdims=True)
                probs = exponent * (1.0 / total)
                d_probs = contract_back(kv_ref[1, window, lanes], grads)
                inner = jnp.sum(probs * d_probs, 0, keepdims=True)
                d_scores = (probs * (d_probs - inner)).astype(jnp.bfloat16)
                d_keys = dot(d_scores, queries)
                d_values = dot(probs.astype(jnp.bfloat16), grads)
                for which, update in ((0, d_keys), (1, d_values)):
                    if block in (0, last):
                        dkv_v[which, window, lanes] = update
                    elif block == 1:
                        dkv_v[which, 128:256, lanes] += update[:128]
                        dkv_v[which, 256:384, lanes] = update[128:]
                    else:
                        dkv_v[which, window, lanes] += update
                d_queries = merged(tn_dot(d_scores, keys)) * 0.125
                dproj_ref[own, lanes] = rotated(
                    d_queries, cos_v[own, :], -sin_v[own, :]
                ).astype(jnp.bfloat16)
            return carry

        lax.fori_loop(0, D // 128, step, 0)

    attend([0, last])
    edge_v[0] = dkv_v[:, 0:HALF].astype(jnp.bfloat16)
    edge_v[1] = dkv_v[:, HALF + TOK :].astype(jnp.bfloat16)
    to_left = pltpu.make_async_remote_copy(
        src_ref=edge_v.at[0], dst_ref=far_v.at[1],
        send_sem=send_sem.at[0], recv_sem=recv_sem.at[0], device_id=left, device_id_type=MESH,
    )
    to_right = pltpu.make_async_remote_copy(
        src_ref=edge_v.at[1], dst_ref=far_v.at[0],
        send_sem=send_sem.at[1], recv_sem=recv_sem.at[1], device_id=right, device_id_type=MESH,
    )

    @pl.when(has_left)
    def _():
        to_left.start()

    @pl.when(has_right)
    def _():
        to_right.start()

    attend(list(range(1, last)))

    @pl.when(has_left)
    def _():
        to_right.wait_recv()
        dkv_v[:, HALF : 2 * HALF] += far_v[0].astype(jnp.float32)

    @pl.when(has_right)
    def _():
        to_left.wait_recv()
        dkv_v[:, TOK : TOK + HALF] += far_v[1].astype(jnp.float32)

    for k in range(D // 128):
        lanes = slice(k * 128, k * 128 + 128)
        dproj_ref[:, D + k * 128 : D + k * 128 + 128] = rotated(
            dkv_v[0, HALF : HALF + TOK, lanes], cos_v[...], -sin_v[...]
        ).astype(jnp.bfloat16)
        dproj_ref[:, 2 * D + k * 128 : 2 * D + k * 128 + 128] = dkv_v[
            1, HALF : HALF + TOK, lanes
        ].astype(jnp.bfloat16)
    for copy in chunks:
        copy.wait()
    dn = contract_back(dproj_ref[:, 0:512], wq_v[0])
    for k in range(1, 6):
        dn += contract_back(dproj_ref[:, k * 512 : k * 512 + 512], wq_v[k])
    hat, inverse = normalize(x_ref[...].astype(jnp.float32))
    vec_ref[0:1] = jnp.sum(dn * hat, 0, keepdims=True)
    vec_ref[1:2] = jnp.sum(dn, 0, keepdims=True)
    vec_ref[2:8] = jnp.zeros((6, D), jnp.float32)
    grad_ref[...] = dmid_ref[...] + norm_backward(dn, hat, inverse, gain_ref[...])

    @pl.when(has_left)
    def _():
        to_left.wait_send()

    @pl.when(has_right)
    def _():
        to_right.wait_send()


def backward_attention(
    frames, lengths, gain, queries, kv, db, dmid, w_qkv, w_out, tables, seq_count
):
    bf, f32 = jnp.bfloat16, jnp.float32
    hbm = pl.BlockSpec(memory_space=pl.ANY)
    vmem = pl.BlockSpec(memory_space=pltpu.VMEM)
    smem = pl.BlockSpec(memory_space=pltpu.SMEM)
    shape = jax.ShapeDtypeStruct
    ext = TOK + 2 * HALF
    return pl.pallas_call(
        functools.partial(backward_kernel, seq_count),
        out_shape=[shape((TOK, 3 * D), bf), shape((TOK, D), f32), shape((8, D), f32)],
        in_specs=[smem] + [vmem] * 6 + [hbm] * 4,
        out_specs=[vmem] * 3,
        scratch_shapes=[
            pltpu.VMEM((6, D, 512), bf),
            pltpu.VMEM((D, D), bf),
            pltpu.VMEM((TOK, 128), f32),
            pltpu.VMEM((TOK, 128), f32),
            pltpu.VMEM((TOK // 128, 256, 256), f32),
            pltpu.VMEM((TOK, D), bf),
            pltpu.VMEM((2, ext, D), f32),
            pltpu.VMEM((2, 2, HALF, D), bf),
            pltpu.VMEM((2, 2, HALF, D), bf),
            pltpu.SemaphoreType.DMA((9,)),
            pltpu.SemaphoreType.DMA((2,)),
            pltpu.SemaphoreType.DMA((2,)),
        ],
        compiler_params=pltpu.CompilerParams(
            collective_id=3, has_side_effects=True, vmem_limit_bytes=56 * 2**20
        ),
        name="attention_backward",
    )(lengths, frames, gain[None], queries, kv, db, dmid, w_qkv, w_out, *tables)


RING = 8
COUNT = len(UNITS)


def stacked_heads(block, heads):
    lane = lax.broadcasted_iota(jnp.int32, block.shape, 1) // HEAD_DIM
    zero = jnp.zeros_like(block)
    return jnp.concatenate([jnp.where(lane == h, block, zero) for h in range(heads)], 0)


def merged_heads(rows, heads):
    lane = lax.broadcasted_iota(jnp.int32, (128, rows.shape[1]), 1) // HEAD_DIM
    total = rows[:128]
    for h in range(1, heads):
        total = jnp.where(lane == h, rows[128 * h : 128 * h + 128], total)
    return total


def layer_kernel(
    clip_ref, x_hbm, c_hbm, gain1_ref, bias1_ref, gain2_ref, bias2_ref, scale_attn_ref, scale_mlp_ref,
    w_qkv, w_out, w_gate_up, w_down, cos_all, sin_all,
    out_hbm, grad_hbm, out0, out1, out2, out3, vec_out, att_hbm, normed_hbm, far_att, far_normed, hid_hbm, far_hid,
    part_a, part_b, part_c,
    recv_a1, recv_a2, recv_az, recv_b1, recv_b2, recv_bz, recv_cz, recv_c1, recv_c2,
    wide_v, deep_v, dkv_v, xbuf, ybuf, yfar, ydown, yout, other_v, hid_v,
    dm_v, db_v, datt_v, x_v, c_v, grad_v, q_v, kv_v, dproj_v, bias_v, cos_v, sin_v, edge_v, far_v,
    vec_sum, vec_recv, vec_z,
    send_sem, recv_sem, load_sem, far_send, far_recv, w_sem, hid_sem, hid_send, hid_recv,
    oth_send, oth_recv, q_send, q_recv, x_sem, edge_send, edge_recv, vec_send, vec_rsem, out_sem, halo_send, halo_recv,
):
    outs = (out0, out1, out2, out3)
    dp = lax.axis_index("dp")
    seq = lax.axis_index("seq")
    z, y = dp // 2, dp % 2
    x, c = seq // 2, seq % 2
    dev_c = (dp, x * 2 + 1 - c)
    dev_x = (dp, (1 - x) * 2 + c)
    dev_y = (z * 2 + 1 - y, seq)
    dev_d = (dp, (1 - x) * 2 + 1 - c)
    dev_z = [(lax.rem(z + k, 4) * 2 + y, seq) for k in (1, 2, 3)]
    bf, f32 = jnp.bfloat16, jnp.float32

    def local_copy(src, dst, sem):
        return pltpu.make_async_copy(src, dst, sem)

    def remote(src, dst, ssem, rsem, device):
        return pltpu.make_async_remote_copy(
            src_ref=src, dst_ref=dst, send_sem=ssem, recv_sem=rsem,
            device_id=device, device_id_type=MESH,
        )

    def weights(step, slot):
        result = []
        for i in range(2):
            at = pl.multiple_of((c if i == 0 else 1 - c) * (FF // 2) + step * 256, 256)
            result += [
                local_copy(
                    w_gate_up.at[:, pl.ds(at, 256)], wide_v.at[4 * slot + i], w_sem.at[slot, i]
                ),
                local_copy(
                    w_gate_up.at[:, pl.ds(FF + at, 256)], wide_v.at[4 * slot + 2 + i],
                    w_sem.at[slot, 2 + i],
                ),
                local_copy(
                    w_down.at[pl.ds(at, 256)], deep_v.at[slot, pl.ds(256 * i, 256)],
                    w_sem.at[slot, 4 + i],
                ),
            ]
        return result

    rows = pl.ds(pl.multiple_of(seq * TOK, TOK), TOK)
    x_copy = local_copy(x_hbm, x_v, load_sem.at[0])
    c_copy = local_copy(c_hbm, c_v, load_sem.at[1])
    tables = [
        local_copy(cos_all.at[rows], cos_v, load_sem.at[2]),
        local_copy(sin_all.at[rows], sin_v, load_sem.at[3]),
    ]
    wo_first = [
        local_copy(
            w_out.at[pl.ds(512 * k, 512)], dproj_v.at[:, pl.ds(D * k, D)], load_sem.at[4 + k]
        )
        for k in range(2)
    ]
    wq_copies = [
        local_copy(w_qkv.at[:, pl.ds(256 * k, 256)], wide_v.at[k % 8], w_sem.at[k % 8 // 4, k % 4])
        for k in range(12)
    ]
    wq_first = {
        k: local_copy(
            w_qkv.at[:, pl.ds(256 * k, 256)], wide_v.at[k - 4 if k >= 4 else k],
            w_sem.at[k // 8, k % 4],
        )
        for k in [4, 5, 6, 7, 8, 9, 10, 11, 0, 1, 2, 3]
    }
    x_copy.start()
    for k in range(4, 8):
        wq_first[k].start()
    for copy in tables:
        copy.start()
    for k in range(8, 12):
        wq_first[k].start()
    for copy in wo_first + [c_copy]:
        copy.start()

    barrier = pltpu.get_barrier_semaphore()
    for device in [dev_c, dev_x, dev_y, dev_d] + dev_z:
        pl.semaphore_signal(barrier, inc=1, device_id=device, device_id_type=MESH)

    is_end = (z == 0) | (z == 3)
    is_mid = (z == 1) | (z == 2)
    end_low = jnp.where(z == 0, 1, 0)
    end_dir = jnp.where(z == 0, 0, 1)
    end_next = (jnp.where(z == 0, 1, 2) * 2 + y, seq)
    mid_dir = jnp.where(z == 1, 0, 1)
    mid_low = jnp.where(z == 1, 1, 0)
    mid_keep = jnp.where(z == 1, 2, 0)
    mid_next = ((3 - z) * 2 + y, seq)
    back_dir = 1 - mid_dir
    back_low = jnp.where(z == 2, 2, 0)
    back_keep = jnp.where(z == 2, 3, 0)
    back_next = (jnp.where(z == 2, 3, 0) * 2 + y, seq)

    def z_send(slot, which, pieces, recv, number):
        ssem, rsem = send_sem.at[slot, which], recv_sem.at[slot, which]
        if number == 0:
            low, size, way, device = end_low, 3, end_dir, end_next
        elif number == 1:
            low, size, way, device = mid_keep, 2, mid_dir, mid_next
        else:
            low, size, way, device = back_keep, 1, back_dir, back_next
        return remote(
            pieces.at[pl.ds(low, size)], recv.at[way, pl.ds(low - 1 + way, size)],
            ssem.at[2 + number // 2], rsem.at[2 + way], device,
        )

    def z_wait(slot, which, recv, way, low, size):
        view = recv.at[way, pl.ds(low - 1 + way, size)]
        local_copy(view, view, recv_sem.at[slot, which, 2 + way]).wait()

    def z_round0(slot, which, pieces, recv):
        @pl.when(is_end)
        def _():
            z_send(slot, which, pieces, recv, 0).start()

    def z_round1(slot, which, pieces, recv):
        @pl.when(is_mid)
        def _():
            z_wait(slot, which, recv, mid_dir, mid_low, 3)
            keep = pl.ds(mid_keep, 2)
            pieces[keep] = pieces[keep] + recv[mid_dir, pl.ds(mid_keep - 1 + mid_dir, 2)]
            z_send(slot, which, pieces, recv, 1).start()

    def z_round2(slot, which, pieces, recv):
        @pl.when(is_mid)
        def _():
            z_wait(slot, which, recv, back_dir, back_low, 2)
            keep = pl.ds(back_keep, 1)
            pieces[keep] = pieces[keep] + recv[back_dir, pl.ds(back_keep - 1 + back_dir, 1)]
            z_send(slot, which, pieces, recv, 2).start()

    def z_final(slot, which, pieces, recv, finish):
        @pl.when(is_end)
        def _():
            way = 1 - end_dir
            z_wait(slot, which, recv, way, z, 1)
            finish(pieces[z].astype(f32) + recv[way, z - 1 + way].astype(f32))

        @pl.when(is_mid)
        def _():
            finish(
                pieces[z].astype(f32) + recv[0, z - 1].astype(f32) + recv[1, z].astype(f32)
            )

    def hop(slot, which, index):
        a, b, cc = part_a.at[slot], part_b.at[slot], part_c.at[slot]
        source, target, device = {
            (0, 0): lambda: (a.at[1 - x], recv_a1.at[slot], dev_x),
            (0, 1): lambda: (a.at[x, 1 - y], recv_a2.at[slot], dev_y),
            (1, 0): lambda: (b.at[1 - y], recv_b1.at[slot], dev_y),
            (1, 1): lambda: (b.at[y, 1 - x], recv_b2.at[slot], dev_x),
            (2, 0): lambda: (cc.at[z, 1 - x], recv_c1.at[slot], dev_x),
            (2, 1): lambda: (cc.at[z, x, 1 - y], recv_c2.at[slot], dev_y),
        }[which, index]()
        return remote(
            source, target, send_sem.at[slot, which, index], recv_sem.at[slot, which, index], device
        )

    def put(unit, which, block):
        if not isinstance(unit, int):
            columns = pl.ds(pl.multiple_of(unit * 256, 256), 256)
            out2[PARTS[which] : PARTS[which + 1], columns] = block
            return
        _, _, _, _, _, offset, out, row = UNITS[unit]
        outs[out][row + PARTS[which] : row + PARTS[which + 1], offset : offset + 256] = block

    def stage(unit, number):
        slot = unit % RING if isinstance(unit, int) else lax.rem(unit, RING)
        a, b, cc = part_a.at[slot], part_b.at[slot], part_c.at[slot]
        a_z, b_z = a.at[x, y], b.at[y, x]
        rz_a, rz_b, rz_c = recv_az.at[slot], recv_bz.at[slot], recv_cz.at[slot]
        if number == 0:
            hop(slot, 0, 0).start()
            hop(slot, 1, 0).start()
            z_round0(slot, 2, cc, rz_c)
        if number == 1:
            hop(slot, 0, 0).wait_recv()
            a[x] = a[x] + recv_a1[slot]
            hop(slot, 0, 1).start()
            hop(slot, 1, 0).wait_recv()
            b[y] = b[y] + recv_b1[slot]
            hop(slot, 1, 1).start()
            z_round1(slot, 2, cc, rz_c)
        if number == 2:
            hop(slot, 0, 1).wait_recv()
            a[x, y] = a[x, y] + recv_a2[slot]
            z_round0(slot, 0, a_z, rz_a)
            hop(slot, 1, 1).wait_recv()
            b[y, x] = b[y, x] + recv_b2[slot]
            z_round0(slot, 1, b_z, rz_b)
            z_round2(slot, 2, cc, rz_c)
        if number == 3:
            z_round1(slot, 0, a_z, rz_a)
            z_round1(slot, 1, b_z, rz_b)

            def keep(value):
                cc[z] = value.astype(bf)

            z_final(slot, 2, cc, rz_c, keep)
            hop(slot, 2, 0).start()
        if number == 4:
            z_round2(slot, 0, a_z, rz_a)
            z_round2(slot, 1, b_z, rz_b)
            hop(slot, 2, 0).wait_recv()
            cc[z, x] = cc[z, x] + recv_c1[slot]
            hop(slot, 2, 1).start()
        if number == 5:
            z_final(slot, 0, a_z, rz_a, functools.partial(put, unit, 0))
            z_final(slot, 1, b_z, rz_b, functools.partial(put, unit, 1))
            hop(slot, 2, 1).wait_recv()
            put(unit, 2, cc[z, x, y].astype(f32) + recv_c2[slot].astype(f32))

    def sums(step):
        for number in range(1, 6):
            unit = step - number + 1
            if isinstance(step, int):
                if 0 <= unit < COUNT:
                    stage(unit, number)
            else:

                @pl.when(unit >= 0)
                def _():
                    stage(unit, number)

    def sent(unit):
        slot = unit % RING
        for which in range(3):
            for index in range(2):
                hop(slot, which, index).wait_send()
        for which, (pieces, recv) in enumerate(
            (
                (part_a.at[slot, x, y], recv_az.at[slot]),
                (part_b.at[slot, y, x], recv_bz.at[slot]),
                (part_c.at[slot], recv_cz.at[slot]),
            )
        ):

            @pl.when(is_end)
            def _():
                z_send(slot, which, pieces, recv, 0).wait_send()

            @pl.when(is_mid)
            def _():
                z_send(slot, which, pieces, recv, 1).wait_send()
                z_send(slot, which, pieces, recv, 2).wait_send()

    def multiply(slot, xslot, own, far):
        def step(i, carry):
            columns = pl.ds(pl.multiple_of(i * 512, 512), 512)
            for xi in range(2):
                total = (
                    tn_dot(xbuf[xslot, 0, :, columns], own(xi))
                    + tn_dot(xbuf[xslot, 1, :, columns], far(xi))
                ).astype(bf)
                for k in range(4):
                    zi, yi = 2 * i + k // 2, k % 2
                    block = total[k * 128 : k * 128 + 128]
                    part_a[slot, xi, yi, zi] = block[PARTS[0] : PARTS[1]]
                    part_b[slot, yi, xi, zi] = block[PARTS[1] : PARTS[2]]
                    part_c[slot, zi, xi, yi] = block[PARTS[2] : PARTS[3]]
            return carry

        lax.fori_loop(0, 2, step, 0)

    def far_copy(src, dst, index):
        return remote(src, dst, far_send.at[index], far_recv.at[index], dev_c)

    def pair_columns(array, width, offset, core, xi):
        return array.at[:, pl.ds(pl.multiple_of((2 * xi + core) * width + offset, 256), 256)]

    far_n2 = far_copy(xbuf.at[0, 0], xbuf.at[0, 1], 0)
    far_a = far_copy(xbuf.at[1, 1], far_att, 1)
    far_n = far_copy(xbuf.at[1, 0], far_normed, 2)
    far_dm = [
        far_copy(pair_columns(dm_v, 256, 0, 1 - c, xi), ydown.at[xi], 3 + xi) for xi in range(2)
    ]
    far_db = [
        far_copy(pair_columns(db_v, 256, 0, 1 - c, xi), yout.at[xi], 5 + xi) for xi in range(2)
    ]
    far_dq = [
        remote(
            pair_columns(dproj_v, 768, 256 * v, 1 - c, xi), yfar.at[v, xi],
            q_send.at[v, xi], q_recv.at[v, xi], dev_c,
        )
        for v in range(3)
        for xi in range(2)
    ]

    def far_other(step):
        return remote(
            other_v.at[lax.rem(step, 2)], yfar.at[lax.rem(step, 4)],
            oth_send.at[lax.rem(step, 2)], oth_recv.at[lax.rem(step, 4)], dev_c,
        )

    def hidden_copies(step):
        slot = lax.rem(step, 2)
        result = []
        for i in range(2):
            at = pl.multiple_of((c if i == 0 else 1 - c) * (FF // 2) + step * 256, 256)
            block = hid_v.at[slot, :, pl.ds(256 * i, 256)]
            result.append(local_copy(block, hid_hbm.at[:, pl.ds(at, 256)], hid_sem.at[slot, i]))
            result.append(
                remote(
                    block, far_hid.at[:, pl.ds(at, 256)],
                    hid_send.at[slot, i], hid_recv.at[step, i], dev_c,
                )
            )
        return result

    window_bias(bias_v, clip_ref, 4 * TOK, True)
    vec_sum[0] = jnp.zeros((8, D), f32)
    x_copy.wait()

    def first_norm(i, carry):
        at = pl.ds(pl.multiple_of(i * 128, 128), 128)
        hat, _ = normalize(x_v[at, :].astype(f32))
        xbuf[1, 0, at, :] = (hat * gain1_ref[...] + bias1_ref[...]).astype(bf)
        return carry

    lax.fori_loop(0, TOK // 128, first_norm, 0)
    normed_copy = local_copy(xbuf.at[1, 0], normed_hbm, out_sem.at[2])
    att_copy = local_copy(xbuf.at[1, 1], att_hbm, out_sem.at[3])
    normed_copy.start()
    for copy in tables:
        copy.wait()

    def project(k):
        full = dot(xbuf[1, 0], wide_v[k - 4 if k >= 4 else k])
        for half in range(2):
            block = full[:, half * 128 : half * 128 + 128]
            at = (k % 4) * 256 + half * 128
            if k < 8:
                block = rotated(block, cos_v[...], sin_v[...])
            block = block.astype(bf)
            if k < 4:
                q_v[:, at : at + 128] = block
            else:
                kv_v[k // 4 - 1, HALF : HALF + TOK, at : at + 128] = block

    def project_all(chunks):
        for k in chunks:
            wq_first[k].wait()
        for k in chunks:
            project(k)

    project_all(range(4, 8))
    for k in range(4):
        wq_first[k].start()
    project_all(range(8, 12))
    pl.semaphore_wait(barrier, 7)
    has_left, has_right = seq > 0, seq < 3
    halo_left = remote(
        kv_v.at[:, pl.ds(HALF, HALF)], kv_v.at[:, pl.ds(HALF + TOK, HALF)],
        halo_send.at[0], halo_recv.at[0], (dp, seq - 1),
    )
    halo_right = remote(
        kv_v.at[:, pl.ds(TOK, HALF)], kv_v.at[:, pl.ds(0, HALF)],
        halo_send.at[1], halo_recv.at[1], (dp, seq + 1),
    )

    @pl.when(has_left)
    def _():
        halo_left.start()

    @pl.when(has_right)
    def _():
        halo_right.start()

    @pl.when(jnp.logical_not(has_left))
    def _():
        kv_v[:, 0:HALF] = jnp.zeros((2, HALF, D), bf)

    @pl.when(jnp.logical_not(has_right))
    def _():
        kv_v[:, HALF + TOK :] = jnp.zeros((2, HALF, D), bf)

    far_n.start()
    project_all(range(4))
    for copy in weights(0, 0) + weights(1, 1):
        copy.start()
    last = TOK // 128 - 1
    heads = 4
    lanes_of = heads * HEAD_DIM

    def attend_forward(blocks):
        def step(group, carry):
            lanes = pl.ds(pl.multiple_of(group * lanes_of, lanes_of), lanes_of)
            scores = []
            for block in blocks:
                queries = q_v[block * 128 : block * 128 + 128, lanes] * 0.125
                keys = kv_v[0, block * 128 : block * 128 + 256, lanes]
                bias = jnp.concatenate([bias_v[block]] * (heads // 2), 1)
                scores.append(contract_back(keys, stacked_heads(queries, heads)) + bias)
            probs = []
            for score in scores:
                exponent = jnp.exp(score - jnp.max(score, 0, keepdims=True))
                total = jnp.sum(exponent, 0, keepdims=True)
                probs.append((exponent * (1.0 / total)).astype(bf))
            for block, prob in zip(blocks, probs):
                values = kv_v[1, block * 128 : block * 128 + 256, lanes]
                xbuf[1, 1, block * 128 : block * 128 + 128, lanes] = merged_heads(
                    tn_dot(prob, values), heads
                ).astype(bf)
            return carry

        lax.fori_loop(0, D // lanes_of, step, 0)

    attend_forward(list(range(1, last)))
    c_copy.wait()

    def scaled(i, carry):
        at = pl.ds(pl.multiple_of(i * 128, 128), 128)
        dm_v[at, :] = (c_v[at, :].astype(f32) * scale_mlp_ref[...]).astype(bf)
        return carry

    lax.fori_loop(0, TOK // 128, scaled, 0)
    for copy in far_dm:
        copy.start()
    dkv_v[...] = jnp.zeros_like(dkv_v)

    @pl.when(has_left)
    def _():
        halo_right.wait_recv()

    @pl.when(has_right)
    def _():
        halo_left.wait_recv()

    attend_forward([0, last])
    att_copy.start()
    far_a.start()
    for copy in wo_first:
        copy.wait()
    for part in range(4):
        cols = slice(part * 256, part * 256 + 256)
        grad_v[:, cols] = dot(xbuf[1, 1, :, 0:512], dproj_v[:, cols]) + dot(
            xbuf[1, 1, :, 512:1024], dproj_v[:, D + part * 256 : D + part * 256 + 256]
        )


    def before(i, carry):
        at = pl.ds(pl.multiple_of(i * 128, 128), 128)
        middle = x_v[at, :].astype(f32) + scale_attn_ref[...] * grad_v[at, :]
        hat, _ = normalize(middle)
        xbuf[0, 0, at, :] = (hat * gain2_ref[...] + bias2_ref[...]).astype(bf)
        return carry

    lax.fori_loop(0, TOK // 128, before, 0)
    far_n2.start()

    def mlp(step):
        slot = lax.rem(step, 2)

        @pl.when(step >= 2)
        def _():
            far_other(step - 2).wait_send()
            for copy in hidden_copies(step - 2)[0::2]:
                copy.wait()
            for copy in hidden_copies(step - 2)[1::2]:
                copy.wait_send()

        for copy in weights(step, slot):
            copy.wait()
        normed = xbuf.at[0, 0]
        for i in range(2):
            gate = dot(normed[...], wide_v[4 * slot + i])
            up = dot(normed[...], wide_v[4 * slot + 2 + i])
            dh = contract_back(dm_v[...], deep_v[slot, 256 * i : 256 * i + 256])
            sigmoid = 1.0 / (1.0 + jnp.exp(-gate))
            silu = gate * sigmoid
            hid_v[slot, :, 256 * i : 256 * i + 256] = (silu * up).astype(bf)
            target = ybuf if i == 0 else other_v
            dgate = dh * up * (sigmoid * (1.0 + gate * (1.0 - sigmoid)))
            target[slot, 0] = dgate.astype(bf)
            target[slot, 1] = (dh * silu).astype(bf)
        far_other(step).start()
        for copy in hidden_copies(step):
            copy.start()
        dkv_v[0, 0:TOK] += dot(hid_v[slot], deep_v[slot])
        dkv_v[1, 0:TOK] += (
            contract_back(ybuf[slot, 0], wide_v[4 * slot])
            + contract_back(other_v[slot, 0], wide_v[4 * slot + 1])
            + contract_back(ybuf[slot, 1], wide_v[4 * slot + 2])
            + contract_back(other_v[slot, 1], wide_v[4 * slot + 3])
        )

        @pl.when(step + 2 < 8)
        def _():
            for copy in weights(step + 2, slot):
                copy.start()

    def gate_unit(step):
        far_other(step).wait_recv()
        multiply(
            step, 0, lambda xi: ybuf[lax.rem(step, 2), xi], lambda xi: yfar[lax.rem(step, 4), xi]
        )
        stage(step, 0)

    def mlp_step(step, carry):
        mlp(step)

        @pl.when(step == 0)
        def _():
            far_n2.wait_recv()

        gate_unit(step)

        @pl.when(step >= BEHIND)
        def _():
            sums(step - BEHIND)

        return carry

    lax.fori_loop(0, 8, mlp_step, 0)

    wo_copies = [
        local_copy(w_out.at[pl.ds(512 * k, 512)], deep_v.at[k], w_sem.at[k, 4]) for k in range(2)
    ]
    for copy in wo_copies + wq_copies[:8]:
        copy.start()
    for step in (6, 7):
        far_other(step).wait_send()
        for copy in hidden_copies(step)[0::2]:
            copy.wait()
        for copy in hidden_copies(step)[1::2]:
            copy.wait_send()
    for step in range(8):
        for copy in hidden_copies(step)[1::2]:
            copy.wait_recv()

    def load_left(unit):
        left, offset, width, _, _, _, _, _ = UNITS[unit]
        slot = {8: 1, 9: 0, 10: 1, 11: 0, 12: 1, 13: 0}[unit]
        arrays = {3: (hid_hbm, far_hid), 1: (att_hbm, far_att), 0: (normed_hbm, far_normed)}[left]
        result = []
        for side in range(2):
            if width == 128:
                result.append(
                    local_copy(arrays[side], xbuf.at[slot, side], x_sem.at[slot, side, 0])
                )
                continue
            for block in range(8):
                result.append(
                    local_copy(
                        arrays[side].at[:, pl.ds(block * width + offset, 128)],
                        xbuf.at[slot, side, :, pl.ds(block * 128, 128)],
                        x_sem.at[slot, side, block],
                    )
                )
        return result

    def unit_sum(unit):
        if unit <= 13:
            for copy in load_left(unit):
                copy.wait()
        _, _, _, right, width, offset, _, _ = UNITS[unit]
        if unit >= RING:
            sent(unit - RING)
        slot, xslot = unit % RING, {8: 1, 9: 0, 10: 1, 11: 0, 12: 1}.get(unit, 0)
        own = {3: dm_v, 1: db_v, 0: dproj_v}[right]
        far = {3: ydown, 1: yout}.get(right, yfar.at[max(unit - 13, 0)])
        multiply(
            slot, xslot,
            lambda xi: pair_columns(own, width, offset, c, xi)[...],
            lambda xi: far[xi],
        )
        stage(unit, 0)
        if unit + 2 <= 13:
            if unit + 2 == 12:
                far_a.wait_recv()
            if unit + 2 == 13:
                far_n.wait_recv()
            for copy in load_left(unit + 2):
                copy.start()

    for copy in [far_n2, far_a, far_n] + far_dm:
        copy.wait_send()
    normed_copy.wait()
    att_copy.wait()
    for copy in load_left(8):
        copy.start()
    for copy in load_left(9):
        copy.start()
    for copy in far_dm:
        copy.wait_recv()

    def after(i, carry):
        at = pl.ds(pl.multiple_of(i * 128, 128), 128)
        cot = c_v[at, :].astype(f32)
        branch = grad_v[at, :]
        middle = x_v[at, :].astype(f32) + scale_attn_ref[...] * branch
        mlp_out = dkv_v[0, at, :]
        dn = dkv_v[1, at, :]
        vec_sum[0, 5:6] += jnp.sum(cot * mlp_out, 0, keepdims=True)
        c_v[at, :] = (middle + scale_mlp_ref[...] * mlp_out).astype(bf)
        hat, inverse = normalize(middle)
        vec_sum[0, 3:4] += jnp.sum(dn * hat, 0, keepdims=True)
        vec_sum[0, 4:5] += jnp.sum(dn, 0, keepdims=True)
        dmid = cot + norm_backward(dn, hat, inverse, gain2_ref[...])
        vec_sum[0, 2:3] += jnp.sum(dmid * branch, 0, keepdims=True)
        grad_v[at, :] = dmid
        db_v[at, :] = (dmid * scale_attn_ref[...]).astype(bf)
        return carry

    out_copy = local_copy(c_v, out_hbm, out_sem.at[0])
    grad_copy = local_copy(grad_v, grad_hbm, out_sem.at[1])

    def norm_two_back():
        lax.fori_loop(0, TOK // 128, after, 0)
        out_copy.start()
        for copy in far_db:
            copy.start()

    def attended_grads():
        for k in range(2):
            wo_copies[k].wait()
        for k in range(2):
            datt_v[:, 512 * k : 512 * k + 512] = contract_back(db_v[...], deep_v[k]).astype(bf)
        for copy in far_db:
            copy.wait_recv()

    def attend(blocks):
        def step(group, carry):
            lanes = pl.ds(pl.multiple_of(group * lanes_of, lanes_of), lanes_of)
            held = []
            for block in blocks:
                own = slice(block * 128, block * 128 + 128)
                window = slice(block * 128, block * 128 + 256)
                queries = stacked_heads(q_v[own, lanes] * 0.125, heads)
                grads = stacked_heads(datt_v[own, lanes], heads)
                keys = kv_v[0, window, lanes]
                bias = jnp.concatenate([bias_v[block]] * (heads // 2), 1)
                scores = contract_back(keys, queries) + bias
                d_probs = contract_back(kv_v[1, window, lanes], grads)
                held.append((queries, grads, keys, scores, d_probs))
            ready = []
            for queries, grads, keys, scores, d_probs in held:
                exponent = jnp.exp(scores - jnp.max(scores, 0, keepdims=True))
                probs = exponent * (1.0 / jnp.sum(exponent, 0, keepdims=True))
                inner = jnp.sum(probs * d_probs, 0, keepdims=True)
                d_scores = (probs * (d_probs - inner)).astype(bf)
                ready.append((queries, grads, keys, d_scores, probs.astype(bf)))
            for block, (queries, grads, keys, d_scores, probs) in zip(blocks, ready):
                own = slice(block * 128, block * 128 + 128)
                window = slice(block * 128, block * 128 + 256)
                for which, update in ((0, dot(d_scores, queries)), (1, dot(probs, grads))):
                    if block in (0, last):
                        dkv_v[which, window, lanes] = update
                    elif block == 1:
                        dkv_v[which, 128:256, lanes] += update[:128]
                        dkv_v[which, 256:384, lanes] = update[128:]
                    else:
                        dkv_v[which, window, lanes] += update
                d_queries = merged_heads(tn_dot(d_scores, keys), heads) * 0.125
                for k in range(lanes_of // 128):
                    at = pl.ds(pl.multiple_of(group * lanes_of + 128 * k, 128), 128)
                    dproj_v[own, at] = rotated(
                        d_queries[:, 128 * k : 128 * k + 128], cos_v[own, :], -sin_v[own, :]
                    ).astype(bf)
            return carry

        lax.fori_loop(0, D // lanes_of, step, 0)

    to_left = remote(
        edge_v.at[0], far_v.at[1], edge_send.at[0], edge_recv.at[0], (dp, seq - 1)
    )
    to_right = remote(
        edge_v.at[1], far_v.at[0], edge_send.at[1], edge_recv.at[1], (dp, seq + 1)
    )

    def edges_out():
        edge_v[0] = dkv_v[:, 0:HALF].astype(bf)
        edge_v[1] = dkv_v[:, HALF + TOK :].astype(bf)

        @pl.when(has_left)
        def _():
            to_left.start()

        @pl.when(has_right)
        def _():
            to_right.start()

    def edges_in():
        @pl.when(has_left)
        def _():
            to_right.wait_recv()
            dkv_v[:, HALF : 2 * HALF] += far_v[0].astype(f32)

        @pl.when(has_right)
        def _():
            to_left.wait_recv()
            dkv_v[:, TOK : TOK + HALF] += far_v[1].astype(f32)

        for k in range(D // 128):
            lanes = slice(k * 128, k * 128 + 128)
            dproj_v[:, D + k * 128 : D + k * 128 + 128] = rotated(
                dkv_v[0, HALF : HALF + TOK, lanes], cos_v[...], -sin_v[...]
            ).astype(bf)
            dproj_v[:, 2 * D + k * 128 : 2 * D + k * 128 + 128] = dkv_v[
                1, HALF : HALF + TOK, lanes
            ].astype(bf)
        for copy in far_dq:
            copy.start()

    def project_back(chunks, fresh):
        for k in chunks:
            wq_copies[k].wait()
        total = None
        for k in chunks:
            term = contract_back(dproj_v[:, 256 * k : 256 * k + 256], wide_v[k % 8])
            total = term if total is None else total + term
        if fresh:
            dkv_v[0, 0:TOK] = total
        else:
            dkv_v[0, 0:TOK] += total

    def last_norm(i, carry):
        at = pl.ds(pl.multiple_of(i * 128, 128), 128)
        hat, inverse = normalize(x_v[at, :].astype(f32))
        dn = dkv_v[0, at, :]
        vec_sum[0, 0:1] += jnp.sum(dn * hat, 0, keepdims=True)
        vec_sum[0, 1:2] += jnp.sum(dn, 0, keepdims=True)
        grad_v[at, :] += norm_backward(dn, hat, inverse, gain1_ref[...])
        return carry

    def norm_one_back():
        lax.fori_loop(0, TOK // 128, last_norm, 0)
        grad_copy.start()

    def vec_copy(number):
        return remote(
            vec_sum.at[number], vec_recv.at[number], vec_send.at[number], vec_rsem.at[number],
            (dev_c, dev_x, dev_y)[number],
        )

    vec_planes = [
        remote(vec_sum.at[3], vec_z.at[z], vec_send.at[3 + k], vec_rsem.at[3 + k], dev_z[k])
        for k in range(3)
    ]

    def vectors(number):
        if 0 < number <= 3:
            vec_copy(number - 1).wait_recv()
            vec_sum[number] = vec_sum[number - 1] + vec_recv[number - 1]
        if number < 3:
            vec_copy(number).start()
        elif number == 3:
            vec_z[z] = vec_sum[3]
            for copy in vec_planes:
                copy.start()
        else:
            for k in range(3):
                view = vec_z.at[lax.rem(z + 3 - k, 4)]
                local_copy(view, view, vec_rsem.at[3 + k]).wait()
            vec_out[...] = vec_z[0] + vec_z[1] + vec_z[2] + vec_z[3]

    def start_wq():
        for copy in wq_copies[8:]:
            copy.start()

    def far_dq_wait():
        for copy in far_dq:
            copy.wait_recv()

    actions = {
        "E": norm_two_back,
        "D": attended_grads,
        "A0": lambda: attend([0, last]),
        "O": edges_out,
        "A1": lambda: attend(list(range(1, last))),
        "I": edges_in,
        "W0": lambda: (project_back(range(8), True), start_wq()),
        "W1": lambda: project_back(range(8, 12), False),
        "N": norm_one_back,
        "Q": far_dq_wait,
    }
    for word in ORDER.split():
        if word in actions:
            actions[word]()
        elif word[0] == "P":
            unit_sum(int(word[1:]))
        elif word[0] == "S":
            sums(int(word[1:]))
        elif word[0] == "V":
            vectors(int(word[1:]))

    for unit in range(COUNT - RING, COUNT):
        sent(unit)
    for copy in far_db + far_dq + [vec_copy(k) for k in range(3)] + vec_planes:
        copy.wait_send()

    @pl.when(has_left)
    def _():
        halo_left.wait_send()
        to_left.wait_send()

    @pl.when(has_right)
    def _():
        halo_right.wait_send()
        to_right.wait_send()

    out_copy.wait()
    grad_copy.wait()


BEHIND = 4
ORDER = (
    "S4 P8 E S5 P9 D S6 P10 A0 O S7 P11 A1 I S8 P12 W0 S9 W1 Q P13 N S10 V0 P14 S11 V1 P15 S12 V2"
    " S13 V3 S14 V4 S15 S16 S17 S18 S19"
)


def layer(
    lengths, frames, cotangent, vectors, w_qkv, w_out, w_gate_up, w_down, tables,
):
    bf, f32 = jnp.bfloat16, jnp.float32
    hbm = pl.BlockSpec(memory_space=pl.ANY)
    vmem = pl.BlockSpec(memory_space=pltpu.VMEM)
    smem = pl.BlockSpec(memory_space=pltpu.SMEM)
    shape = jax.ShapeDtypeStruct
    size = (PARTS[1], PARTS[2] - PARTS[1], PARTS[3] - PARTS[2])
    dma = pltpu.SemaphoreType.DMA
    ext = TOK + 2 * HALF
    scratch = [
        pltpu.VMEM((RING, 2, 2, 4, size[0], 256), bf),
        pltpu.VMEM((RING, 2, 2, 4, size[1], 256), bf),
        pltpu.VMEM((RING, 4, 2, 2, size[2], 256), bf),
        pltpu.VMEM((RING, 2, 4, size[0], 256), bf),
        pltpu.VMEM((RING, 4, size[0], 256), bf),
        pltpu.VMEM((RING, 2, 3, size[0], 256), bf),
        pltpu.VMEM((RING, 2, 4, size[1], 256), bf),
        pltpu.VMEM((RING, 4, size[1], 256), bf),
        pltpu.VMEM((RING, 2, 3, size[1], 256), bf),
        pltpu.VMEM((RING, 2, 3, 2, 2, size[2], 256), bf),
        pltpu.VMEM((RING, 2, size[2], 256), bf),
        pltpu.VMEM((RING, size[2], 256), bf),
        pltpu.VMEM((8, D, 256), bf),
        pltpu.VMEM((2, 512, D), bf),
        pltpu.VMEM((2, ext, D), f32),
        pltpu.VMEM((2, 2, TOK, D), bf),
        pltpu.VMEM((2, 2, TOK, 256), bf),
        pltpu.VMEM((4, 2, TOK, 256), bf),
        pltpu.VMEM((2, TOK, 256), bf),
        pltpu.VMEM((2, TOK, 256), bf),
        pltpu.VMEM((2, 2, TOK, 256), bf),
        pltpu.VMEM((2, TOK, 512), bf),
        pltpu.VMEM((TOK, D), bf),
        pltpu.VMEM((TOK, D), bf),
        pltpu.VMEM((TOK, D), bf),
        pltpu.VMEM((TOK, D), bf),
        pltpu.VMEM((TOK, D), bf),
        pltpu.VMEM((TOK, D), f32),
        pltpu.VMEM((TOK, D), bf),
        pltpu.VMEM((2, ext, D), bf),
        pltpu.VMEM((TOK, 3 * D), bf),
        pltpu.VMEM((TOK // 128, 256, 256), f32),
        pltpu.VMEM((TOK, 128), f32),
        pltpu.VMEM((TOK, 128), f32),
        pltpu.VMEM((2, 2, HALF, D), bf),
        pltpu.VMEM((2, 2, HALF, D), bf),
        pltpu.VMEM((4, 8, D), f32),
        pltpu.VMEM((3, 8, D), f32),
        pltpu.VMEM((4, 8, D), f32),
        dma((RING, 3, 4)),
        dma((RING, 3, 4)),
        dma((7,)),
        dma((7,)),
        dma((7,)),
        dma((2, 6)),
        dma((2, 2)),
        dma((2, 2)),
        dma((8, 2)),
        dma((2,)),
        dma((4,)),
        dma((3, 2)),
        dma((3, 2)),
        dma((2, 2, 8)),
        dma((2,)),
        dma((2,)),
        dma((6,)),
        dma((6,)),
        dma((4,)),
        dma((2,)),
        dma((2,)),
    ]
    results = pl.pallas_call(
        layer_kernel,
        out_shape=[
            shape((TOK, D), bf),
            shape((TOK, D), f32),
            shape((128, 768), f32),
            shape((128, 256), f32),
            shape((128, 2048), f32),
            shape((512, 256), f32),
            shape((8, D), f32),
        ]
        + [shape((TOK, D), bf)] * 4
        + [
            shape((TOK, FF), bf),
            shape((TOK, FF), bf),
        ],
        in_specs=[smem] + [hbm] * 2 + [vmem] * 6 + [hbm] * 6,
        out_specs=[hbm] * 2 + [vmem] * 5 + [hbm] * 6,
        scratch_shapes=scratch,
        compiler_params=pltpu.CompilerParams(
            collective_id=4, has_side_effects=True, vmem_limit_bytes=64 * 2**20 - 2**16
        ),
        name="layer",
    )(
        lengths, frames, cotangent, *[v[None] for v in vectors], w_qkv, w_out, w_gate_up, w_down, *tables,
    )[:7]
    finished = pl.pallas_call(
        finish_kernel,
        out_shape=[shape(v.shape, v.dtype) for v in results[:6]] + [shape((1, D), f32)] * 6,
        in_specs=[hbm] * 6 + [vmem],
        out_specs=[hbm] * 6 + [vmem] * 6,
        scratch_shapes=[pltpu.VMEM(v.shape, v.dtype) for v in results[:6]] + [dma((2, 6))],
        compiler_params=pltpu.CompilerParams(vmem_limit_bytes=64 * 2**20 - 2**16),
        name="finish",
    )(*results)
    return finished[:6], [v[0] for v in finished[6:]]


def finish_kernel(*refs):
    sources, targets, held, sems = refs[:6], refs[7:13], refs[19:25], refs[25]
    arrivals = [
        pltpu.make_async_copy(source, target, sems.at[0, k])
        for k, (source, target) in enumerate(zip(sources, held))
    ]
    departures = [
        pltpu.make_async_copy(source, target, sems.at[1, k])
        for k, (source, target) in enumerate(zip(held, targets))
    ]
    for copy in arrivals:
        copy.start()
    for k in range(6):
        refs[13 + k][...] = refs[6][k : k + 1]
    for arrival, departure in zip(arrivals, departures):
        arrival.wait()
        departure.start()
    for copy in departures:
        copy.wait()


def local(
    frames,
    cotangent,
    clip_len,
    ln1_gain,
    ln1_bias,
    w_qkv,
    w_out,
    scale_attn,
    ln2_gain,
    ln2_bias,
    w_gate_up,
    w_down,
    scale_mlp,
):
    row_count = frames.shape[0]
    seq_count = lax.axis_size("seq")
    tables = rotary_tables(row_count * seq_count)
    data_count = lax.axis_size("dp")
    if (data_count, seq_count, row_count) == (8, 4, TOK):
        sums, vector_total = layer(
            clip_len, frames, cotangent,
            (ln1_gain, ln1_bias, ln2_gain, ln2_bias, scale_attn, scale_mlp),
            w_qkv, w_out, w_gate_up, w_down, tables,
        )
        out_frames, input_grad, sum_qkv, sum_out, sum_gate_up, sum_down = sums
    else:
        normed_b, queries, kv, attended_t, branch = forward_attention(
            frames, clip_len, ln1_gain, ln1_bias, scale_attn, w_qkv, w_out, tables, seq_count
        )
        out_frames, normed_two_b, hidden_b, gate_up_b, mlp_grad, branch_grad, middle_grad, vec_two = (
            feed_forward(
                frames, cotangent, branch, ln2_gain, ln2_bias, scale_attn, scale_mlp, w_gate_up, w_down
            )
        )
        projected_grad, input_grad, vec_one = backward_attention(
            frames, clip_len, ln1_gain, queries, kv, branch_grad, middle_grad, w_qkv, w_out, tables,
            seq_count,
        )
        vector_grads = jnp.stack(
            [vec_one[0], vec_one[1], vec_two[3], vec_two[1], vec_two[2], vec_two[0]], 0
        )
        lefts = (normed_b, attended_t, normed_two_b, hidden_b)
        rights = (projected_grad, branch_grad, gate_up_b, mlp_grad)
        vector_total = lax.psum(vector_grads, ("dp", "seq"))
        sum_qkv, sum_out, sum_gate_up, sum_down = [
            lax.psum_scatter(
                to_blocks(contract_rows(left, right), data_count, seq_count),
                ("dp", "seq"),
                scatter_dimension=0,
                tiled=True,
            )[0]
            for left, right in zip(lefts, rights)
        ]
    return (
        out_frames,
        input_grad,
        vector_total[0],
        vector_total[1],
        sum_qkv,
        sum_out,
        vector_total[2],
        vector_total[3],
        vector_total[4],
        sum_gate_up,
        sum_down,
        vector_total[5],
    )


def solution(mesh):
    return jax.shard_map(
        local,
        mesh=mesh,
        in_specs=(
            P(("dp", "seq"), None),
            P(("dp", "seq"), None),
            P("dp", None),
            P(),
            P(),
            P(),
            P(),
            P(),
            P(),
            P(),
            P(),
            P(),
            P(),
        ),
        out_specs=(
            P(("dp", "seq"), None),
            P(("dp", "seq"), None),
            P(),
            P(),
            P("dp", "seq"),
            P("dp", "seq"),
            P(),
            P(),
            P(),
            P("dp", "seq"),
            P("dp", "seq"),
            P(),
        ),
        check_vma=False,
    )
```

```python
import functools

import jax
import jax.numpy as jnp
import numpy as np
from jax import lax
from jax.experimental import pallas as pl
from jax.experimental.pallas import tpu as pltpu
from jax.sharding import PartitionSpec as P

D = 1024
HEADS = 16
HEAD_DIM = 64
FF = 4096
HALF = 64
QBLK = 512


EPS = 1e-05
NEG = -1e30


def contract_rows(left, right):
    return lax.dot_general(
        left, right, (((0,), (0,)), ((), ())), preferred_element_type=jnp.float32
    )


def contract_back(grads, weight):
    return lax.dot_general(
        grads, weight, (((1,), (1,)), ((), ())), preferred_element_type=jnp.float32
    )


def to_blocks(matrix, data_count, seq_count):
    row_total, col_total = matrix.shape
    shaped = matrix.reshape(data_count, row_total // data_count, seq_count, col_total // seq_count)
    return shaped.transpose(0, 2, 1, 3).reshape(
        data_count * seq_count, row_total // data_count, col_total // seq_count
    )


MESH = pl.DeviceIdType.MESH
TOK = 512
PARTS = (0, 48, 96, 128)
LAST_PARTS = (0, 64, 128, 128)
LAST_UNITS = 1

UNITS = (
    [(2, 0, 128, 2, 2048, 256 * v, 2, 0) for v in range(8)]
    + [(3, 128 * v, 512, 3, 256, 0, 3, 128 * v) for v in range(4)]
    + [(1, 0, 128, 1, 256, 0, 1, 0)]
    + [(0, 0, 128, 0, 768, 256 * v, 0, 0) for v in range(3)]
)


def tn_dot(left, right):
    return lax.dot_general(
        left, right, (((0,), (0,)), ((), ())), preferred_element_type=jnp.float32
    )


def rotated(values, cosines, sines):
    lane = lax.broadcasted_iota(jnp.int32, values.shape, 1)
    partner = jnp.where(
        lane % HEAD_DIM < HEAD_DIM // 2,
        pltpu.roll(values, 128 - HEAD_DIM // 2, 1),
        pltpu.roll(values, HEAD_DIM // 2, 1),
    )
    return values * cosines + partner * sines


def head_masks():
    lane = lax.broadcasted_iota(jnp.int32, (128, 128), 1)
    return lane < HEAD_DIM


def stacked(pair):
    first = head_masks()
    zero = jnp.zeros_like(pair)
    return jnp.concatenate([jnp.where(first, pair, zero), jnp.where(first, zero, pair)], 0)


def merged(rows):
    return jnp.where(head_masks(), rows[:128], rows[128:])


def clip_number(positions, ends, group_len):
    total = jnp.zeros_like(positions)
    for end in ends:
        total = total + (positions >= end).astype(jnp.int32)
    return jnp.where((positions >= 0) & (positions < group_len), total, -1)


def normalize(values):
    average = jnp.mean(values, -1, keepdims=True)
    centered = values - average
    inverse = lax.rsqrt(jnp.mean(centered * centered, -1, keepdims=True) + EPS)
    return centered * inverse, inverse


def dot(left, right):
    return jnp.dot(left, right, preferred_element_type=jnp.float32)


def norm_backward(grads, hat, inverse, gain):
    scaled = grads * gain
    return inverse * (
        scaled
        - jnp.mean(scaled, -1, keepdims=True)
        - hat * jnp.mean(scaled * hat, -1, keepdims=True)
    )


def window_bias(bias_ref, clip_ref, group_len, keys_first):
    seq = lax.axis_index("seq")
    first_end = clip_ref[0, 0]
    second_end = first_end + clip_ref[0, 1]
    ends = (first_end, second_end, second_end + clip_ref[0, 2])
    for block in range(TOK // 128):
        start = seq * TOK + block * 128
        shape = (2 * 128, 2 * 128)
        k_axis = 0 if keys_first else 1
        k_at = lax.broadcasted_iota(jnp.int32, shape, k_axis)
        q_at = lax.rem(lax.broadcasted_iota(jnp.int32, shape, 1 - k_axis), 128)
        q_shape = (1, 256) if keys_first else (256, 1)
        k_shape = (256, 1) if keys_first else (1, 256)
        q_ids = clip_number(
            start + lax.rem(lax.broadcasted_iota(jnp.int32, q_shape, 1 - k_axis), 128),
            ends, group_len,
        )
        k_ids = clip_number(
            start - HALF + lax.broadcasted_iota(jnp.int32, k_shape, k_axis), ends, group_len
        )
        seen = (q_ids == k_ids) & (k_at >= q_at) & (k_at < q_at + 2 * HALF)
        bias_ref[block] = jnp.where(seen, 0.0, NEG)


def greet_sides(seq_count):
    dp, seq = lax.axis_index("dp"), lax.axis_index("seq")
    barrier = pltpu.get_barrier_semaphore()
    has_left, has_right = seq > 0, seq < seq_count - 1

    @pl.when(has_left)
    def _():
        pl.semaphore_signal(barrier, inc=1, device_id=(dp, seq - 1), device_id_type=MESH)

    @pl.when(has_right)
    def _():
        pl.semaphore_signal(barrier, inc=1, device_id=(dp, seq + 1), device_id_type=MESH)

    pl.semaphore_wait(barrier, has_left.astype(jnp.int32) + has_right.astype(jnp.int32))

    return (dp, seq - 1), (dp, seq + 1), has_left, has_right


def forward_kernel(
    seq_count, clip_ref, x_ref, gain_ref, gain_bias_ref, scale_ref, w_qkv, w_out, cos_all, sin_all,
    normed_ref, q_ref, kv_ref, att_ref, branch_ref,
    wq_v, wo_v, cos_v, sin_v, bias_v, load_sem, send_sem, recv_sem,
):
    dp, seq = lax.axis_index("dp"), lax.axis_index("seq")
    rows = pl.ds(pl.multiple_of(seq * TOK, TOK), TOK)
    copies = []
    order = [2, 3, 4, 5, 0, 1]
    tables = [
        pltpu.make_async_copy(cos_all.at[rows], cos_v, load_sem.at[0]),
        pltpu.make_async_copy(sin_all.at[rows], sin_v, load_sem.at[1]),
    ]
    chunks = {
        k: pltpu.make_async_copy(
            w_qkv.at[:, pl.ds(k * 512, 512)], wq_v.at[k], load_sem.at[2 + k]
        )
        for k in order
    }
    out_copy = pltpu.make_async_copy(w_out, wo_v, load_sem.at[8])
    for copy in tables + [chunks[k] for k in order] + [out_copy]:
        copy.start()
    left, right, has_left, has_right = greet_sides(seq_count)

    hat, _ = normalize(x_ref[...].astype(jnp.float32))
    normed_ref[...] = (hat * gain_ref[...] + gain_bias_ref[...]).astype(jnp.bfloat16)
    for copy in tables:
        copy.wait()

    def project(k):
        chunks[k].wait()
        for part in range(2):
            cols = slice(part * 256, part * 256 + 256)
            full = dot(normed_ref[...], wq_v[k, :, cols])
            for half in range(2):
                block = full[:, half * 128 : half * 128 + 128]
                at = (k % 2) * 512 + part * 256 + half * 128
                if k < 4:
                    block = rotated(block, cos_v[...], sin_v[...])
                block = block.astype(jnp.bfloat16)
                if k < 2:
                    q_ref[:, at : at + 128] = block
                else:
                    kv_ref[k // 2 - 1, HALF : HALF + TOK, at : at + 128] = block

    for k in order[:4]:
        project(k)

    to_left = pltpu.make_async_remote_copy(
        src_ref=kv_ref.at[:, pl.ds(HALF, HALF)], dst_ref=kv_ref.at[:, pl.ds(HALF + TOK, HALF)],
        send_sem=send_sem.at[0], recv_sem=recv_sem.at[0], device_id=left, device_id_type=MESH,
    )
    to_right = pltpu.make_async_remote_copy(
        src_ref=kv_ref.at[:, pl.ds(TOK, HALF)], dst_ref=kv_ref.at[:, pl.ds(0, HALF)],
        send_sem=send_sem.at[1], recv_sem=recv_sem.at[1], device_id=right, device_id_type=MESH,
    )

    @pl.when(has_left)
    def _():
        to_left.start()

    @pl.when(has_right)
    def _():
        to_right.start()

    @pl.when(jnp.logical_not(has_left))
    def _():
        kv_ref[:, 0:HALF] = jnp.zeros((2, HALF, D), jnp.bfloat16)

    @pl.when(jnp.logical_not(has_right))
    def _():
        kv_ref[:, HALF + TOK :] = jnp.zeros((2, HALF, D), jnp.bfloat16)

    for k in order[4:]:
        project(k)
    window_bias(bias_v, clip_ref, seq_count * TOK, False)

    heads = 4
    lanes_of = heads * HEAD_DIM

    def attend(blocks):
        def step(group, carry):
            lanes = pl.ds(pl.multiple_of(group * lanes_of, lanes_of), lanes_of)
            scores = []
            for block in blocks:
                queries = q_ref[block * 128 : block * 128 + 128, lanes] * 0.125
                keys = kv_ref[0, block * 128 : block * 128 + 256, lanes]
                bias = jnp.concatenate([bias_v[block]] * (heads // 2), 0)
                scores.append(contract_back(stacked_heads(queries, heads), keys) + bias)
            probs = []
            for score in scores:
                exponent = jnp.exp(score - jnp.max(score, -1, keepdims=True))
                total = jnp.sum(exponent, -1, keepdims=True)
                probs.append((exponent * (1.0 / total)).astype(jnp.bfloat16))
            for block, prob in zip(blocks, probs):
                values = kv_ref[1, block * 128 : block * 128 + 256, lanes]
                att_ref[block * 128 : block * 128 + 128, lanes] = merged_heads(
                    dot(prob, values), heads
                ).astype(jnp.bfloat16)
            return carry

        lax.fori_loop(0, D // lanes_of, step, 0)

    last = TOK // 128 - 1
    attend(list(range(1, last)))

    @pl.when(has_left)
    def _():
        to_right.wait_recv()

    @pl.when(has_right)
    def _():
        to_left.wait_recv()

    attend([0, last])
    out_copy.wait()
    for part in range(4):
        cols = slice(part * 256, part * 256 + 256)
        branch_ref[:, cols] = dot(att_ref[...], wo_v[:, cols])

    @pl.when(has_left)
    def _():
        to_left.wait_send()

    @pl.when(has_right)
    def _():
        to_right.wait_send()


def rotary_tables(group_len):
    half = HEAD_DIM // 2
    inv_freq = (10000.0 ** (-np.arange(half) / half)).astype(np.float32)[None, :]
    angles = np.arange(group_len, dtype=np.float32)[:, None] * inv_freq
    cosine, sine = np.cos(angles), np.sin(angles)
    return (
        np.concatenate([cosine] * 4, 1).astype(np.float32),
        np.concatenate([-sine, sine] * 2, 1).astype(np.float32),
    )


def forward_attention(frames, lengths, gain, bias, scale, w_qkv, w_out, tables, seq_count):
    bf, f32 = jnp.bfloat16, jnp.float32
    hbm = pl.BlockSpec(memory_space=pl.ANY)
    vmem = pl.BlockSpec(memory_space=pltpu.VMEM)
    smem = pl.BlockSpec(memory_space=pltpu.SMEM)
    shape = jax.ShapeDtypeStruct
    return pl.pallas_call(
        functools.partial(forward_kernel, seq_count),
        out_shape=[
            shape((TOK, D), bf),
            shape((TOK, D), bf),
            shape((2, TOK + 2 * HALF, D), bf),
            shape((TOK, D), bf),
            shape((TOK, D), f32),
        ],
        in_specs=[smem] + [vmem] * 4 + [hbm] * 4,
        out_specs=[vmem] * 5,
        scratch_shapes=[
            pltpu.VMEM((6, D, 512), bf),
            pltpu.VMEM((D, D), bf),
            pltpu.VMEM((TOK, 128), f32),
            pltpu.VMEM((TOK, 128), f32),
            pltpu.VMEM((TOK // 128, 256, 256), f32),
            pltpu.SemaphoreType.DMA((9,)),
            pltpu.SemaphoreType.DMA((2,)),
            pltpu.SemaphoreType.DMA((2,)),
        ],
        compiler_params=pltpu.CompilerParams(
            collective_id=2, has_side_effects=True, vmem_limit_bytes=56 * 2**20
        ),
        name="attention_forward",
    )(lengths, frames, gain[None], bias[None], scale[None], w_qkv, w_out, *tables)


FBLK = 512


def mlp_kernel(
    x_ref, c_ref, branch_ref, gain_ref, bias_ref, scale_attn_ref, scale_mlp_ref, w_gate_up, w_down,
    out_ref, n2_ref, hidden_ref, dgu_ref, dm_ref, db_ref, dmid_ref, vec_ref,
    wg_v, wu_v, wd_v, mlp_v, dn_v, load_sem,
):
    count = FF // FBLK

    def copies(step, slot):
        at = pl.multiple_of(step * FBLK, FBLK)
        return [
            pltpu.make_async_copy(
                w_gate_up.at[:, pl.ds(at, FBLK)], wg_v.at[slot], load_sem.at[slot, 0]
            ),
            pltpu.make_async_copy(
                w_gate_up.at[:, pl.ds(FF + at, FBLK)], wu_v.at[slot], load_sem.at[slot, 1]
            ),
            pltpu.make_async_copy(
                w_down.at[pl.ds(at, FBLK)], wd_v.at[slot], load_sem.at[slot, 2]
            ),
        ]

    for copy in copies(0, 0):
        copy.start()
    middle = x_ref[...].astype(jnp.float32) + scale_attn_ref[...] * branch_ref[...]
    hat, inverse = normalize(middle)
    n2_ref[...] = (hat * gain_ref[...] + bias_ref[...]).astype(jnp.bfloat16)
    dm_ref[...] = (c_ref[...].astype(jnp.float32) * scale_mlp_ref[...]).astype(jnp.bfloat16)
    mlp_v[...] = jnp.zeros_like(mlp_v)
    dn_v[...] = jnp.zeros_like(dn_v)

    def step(number, carry):
        slot = lax.rem(number, 2)

        @pl.when(number + 1 < count)
        def _():
            for copy in copies(number + 1, 1 - slot):
                copy.start()

        for copy in copies(number, slot):
            copy.wait()
        for part in range(FBLK // 256):
            cols = slice(part * 256, part * 256 + 256)
            at = pl.multiple_of(number * FBLK + part * 256, 256)
            gate = dot(n2_ref[...], wg_v[slot, :, cols])
            up = dot(n2_ref[...], wu_v[slot, :, cols])
            dh = contract_back(dm_ref[...], wd_v[slot, cols, :])
            sigmoid = 1.0 / (1.0 + jnp.exp(-gate))
            silu = gate * sigmoid
            hidden_ref[:, pl.ds(at, 256)] = (silu * up).astype(jnp.bfloat16)
            dgate = dh * up * (sigmoid * (1.0 + gate * (1.0 - sigmoid)))
            dgu_ref[:, pl.ds(at, 256)] = dgate.astype(jnp.bfloat16)
            dgu_ref[:, pl.ds(FF + at, 256)] = (dh * silu).astype(jnp.bfloat16)
        at = pl.multiple_of(number * FBLK, FBLK)
        mlp_v[...] += dot(hidden_ref[:, pl.ds(at, FBLK)], wd_v[slot])
        dn_v[...] += contract_back(dgu_ref[:, pl.ds(at, FBLK)], wg_v[slot]) + contract_back(
            dgu_ref[:, pl.ds(FF + at, FBLK)], wu_v[slot]
        )
        return carry

    lax.fori_loop(0, count, step, 0)
    cot = c_ref[...].astype(jnp.float32)
    branch = branch_ref[...]
    middle = x_ref[...].astype(jnp.float32) + scale_attn_ref[...] * branch
    mlp_out = mlp_v[...]
    out_ref[...] = (middle + scale_mlp_ref[...] * mlp_out).astype(jnp.bfloat16)
    vec_ref[0:1] = jnp.sum(cot * mlp_out, 0, keepdims=True)
    hat, inverse = normalize(middle)
    dn = dn_v[...]
    vec_ref[1:2] = jnp.sum(dn * hat, 0, keepdims=True)
    vec_ref[2:3] = jnp.sum(dn, 0, keepdims=True)
    dmid = cot + norm_backward(dn, hat, inverse, gain_ref[...])
    dmid_ref[...] = dmid
    vec_ref[3:4] = jnp.sum(dmid * branch, 0, keepdims=True)
    vec_ref[4:8] = jnp.zeros((4, D), jnp.float32)
    db_ref[...] = (dmid * scale_attn_ref[...]).astype(jnp.bfloat16)


def feed_forward(frames, cotangent, branch, gain, bias, scale_attn, scale_mlp, w_gate_up, w_down):
    bf, f32 = jnp.bfloat16, jnp.float32
    hbm = pl.BlockSpec(memory_space=pl.ANY)
    vmem = pl.BlockSpec(memory_space=pltpu.VMEM)
    shape = jax.ShapeDtypeStruct
    return pl.pallas_call(
        mlp_kernel,
        out_shape=[
            shape((TOK, D), bf),
            shape((TOK, D), bf),
            shape((TOK, FF), bf),
            shape((TOK, 2 * FF), bf),
            shape((TOK, D), bf),
            shape((TOK, D), bf),
            shape((TOK, D), f32),
            shape((8, D), f32),
        ],
        in_specs=[vmem] * 7 + [hbm] * 2,
        out_specs=[vmem] * 8,
        scratch_shapes=[
            pltpu.VMEM((2, D, FBLK), bf),
            pltpu.VMEM((2, D, FBLK), bf),
            pltpu.VMEM((2, FBLK, D), bf),
            pltpu.VMEM((TOK, D), f32),
            pltpu.VMEM((TOK, D), f32),
            pltpu.SemaphoreType.DMA((2, 3)),
        ],
        compiler_params=pltpu.CompilerParams(vmem_limit_bytes=56 * 2**20),
        name="feed_forward",
    )(
        frames, cotangent, branch, gain[None], bias[None], scale_attn[None], scale_mlp[None],
        w_gate_up, w_down,
    )


def backward_kernel(
    seq_count, clip_ref, x_ref, gain_ref, q_ref, kv_ref, db_ref, dmid_ref, w_qkv, w_out,
    cos_all, sin_all,
    dproj_ref, grad_ref, vec_ref,
    wq_v, wo_v, cos_v, sin_v, bias_v, datt_v, dkv_v, edge_v, far_v, load_sem, send_sem, recv_sem,
):
    seq = lax.axis_index("seq")
    rows = pl.ds(pl.multiple_of(seq * TOK, TOK), TOK)
    out_copy = pltpu.make_async_copy(w_out, wo_v, load_sem.at[8])
    tables = [
        pltpu.make_async_copy(cos_all.at[rows], cos_v, load_sem.at[0]),
        pltpu.make_async_copy(sin_all.at[rows], sin_v, load_sem.at[1]),
    ]
    chunks = [
        pltpu.make_async_copy(
            w_qkv.at[:, pl.ds(k * 512, 512)], wq_v.at[k], load_sem.at[2 + k]
        )
        for k in range(6)
    ]
    for copy in [out_copy] + tables + chunks:
        copy.start()
    left, right, has_left, has_right = greet_sides(seq_count)
    window_bias(bias_v, clip_ref, seq_count * TOK, True)
    out_copy.wait()
    for part in range(4):
        cols = slice(part * 256, part * 256 + 256)
        datt_v[:, cols] = contract_back(db_ref[...], wo_v[cols, :]).astype(jnp.bfloat16)
    for copy in tables:
        copy.wait()
    last = TOK // 128 - 1

    def attend(blocks):
        def step(pair, carry):
            lanes = pl.ds(pl.multiple_of(pair * 128, 128), 128)
            for block in blocks:
                own = slice(block * 128, block * 128 + 128)
                window = slice(block * 128, block * 128 + 256)
                queries = stacked(q_ref[own, lanes] * 0.125)
                grads = stacked(datt_v[own, lanes])
                keys = kv_ref[0, window, lanes]
                scores = contract_back(keys, queries) + bias_v[block]
                exponent = jnp.exp(scores - jnp.max(scores, 0, keepdims=True))
                total = jnp.sum(exponent, 0, keepdims=True)
                probs = exponent * (1.0 / total)
                d_probs = contract_back(kv_ref[1, window, lanes], grads)
                inner = jnp.sum(probs * d_probs, 0, keepdims=True)
                d_scores = (probs * (d_probs - inner)).astype(jnp.bfloat16)
                d_keys = dot(d_scores, queries)
                d_values = dot(probs.astype(jnp.bfloat16), grads)
                for which, update in ((0, d_keys), (1, d_values)):
                    if block in (0, last):
                        dkv_v[which, window, lanes] = update
                    elif block == 1:
                        dkv_v[which, 128:256, lanes] += update[:128]
                        dkv_v[which, 256:384, lanes] = update[128:]
                    else:
                        dkv_v[which, window, lanes] += update
                d_queries = merged(tn_dot(d_scores, keys)) * 0.125
                dproj_ref[own, lanes] = rotated(
                    d_queries, cos_v[own, :], -sin_v[own, :]
                ).astype(jnp.bfloat16)
            return carry

        lax.fori_loop(0, D // 128, step, 0)

    attend([0, last])
    edge_v[0] = dkv_v[:, 0:HALF].astype(jnp.bfloat16)
    edge_v[1] = dkv_v[:, HALF + TOK :].astype(jnp.bfloat16)
    to_left = pltpu.make_async_remote_copy(
        src_ref=edge_v.at[0], dst_ref=far_v.at[1],
        send_sem=send_sem.at[0], recv_sem=recv_sem.at[0], device_id=left, device_id_type=MESH,
    )
    to_right = pltpu.make_async_remote_copy(
        src_ref=edge_v.at[1], dst_ref=far_v.at[0],
        send_sem=send_sem.at[1], recv_sem=recv_sem.at[1], device_id=right, device_id_type=MESH,
    )

    @pl.when(has_left)
    def _():
        to_left.start()

    @pl.when(has_right)
    def _():
        to_right.start()

    attend(list(range(1, last)))

    @pl.when(has_left)
    def _():
        to_right.wait_recv()
        dkv_v[:, HALF : 2 * HALF] += far_v[0].astype(jnp.float32)

    @pl.when(has_right)
    def _():
        to_left.wait_recv()
        dkv_v[:, TOK : TOK + HALF] += far_v[1].astype(jnp.float32)

    for k in range(D // 128):
        lanes = slice(k * 128, k * 128 + 128)
        dproj_ref[:, D + k * 128 : D + k * 128 + 128] = rotated(
            dkv_v[0, HALF : HALF + TOK, lanes], cos_v[...], -sin_v[...]
        ).astype(jnp.bfloat16)
        dproj_ref[:, 2 * D + k * 128 : 2 * D + k * 128 + 128] = dkv_v[
            1, HALF : HALF + TOK, lanes
        ].astype(jnp.bfloat16)
    for copy in chunks:
        copy.wait()
    dn = contract_back(dproj_ref[:, 0:512], wq_v[0])
    for k in range(1, 6):
        dn += contract_back(dproj_ref[:, k * 512 : k * 512 + 512], wq_v[k])
    hat, inverse = normalize(x_ref[...].astype(jnp.float32))
    vec_ref[0:1] = jnp.sum(dn * hat, 0, keepdims=True)
    vec_ref[1:2] = jnp.sum(dn, 0, keepdims=True)
    vec_ref[2:8] = jnp.zeros((6, D), jnp.float32)
    grad_ref[...] = dmid_ref[...] + norm_backward(dn, hat, inverse, gain_ref[...])

    @pl.when(has_left)
    def _():
        to_left.wait_send()

    @pl.when(has_right)
    def _():
        to_right.wait_send()


def backward_attention(
    frames, lengths, gain, queries, kv, db, dmid, w_qkv, w_out, tables, seq_count
):
    bf, f32 = jnp.bfloat16, jnp.float32
    hbm = pl.BlockSpec(memory_space=pl.ANY)
    vmem = pl.BlockSpec(memory_space=pltpu.VMEM)
    smem = pl.BlockSpec(memory_space=pltpu.SMEM)
    shape = jax.ShapeDtypeStruct
    ext = TOK + 2 * HALF
    return pl.pallas_call(
        functools.partial(backward_kernel, seq_count),
        out_shape=[shape((TOK, 3 * D), bf), shape((TOK, D), f32), shape((8, D), f32)],
        in_specs=[smem] + [vmem] * 6 + [hbm] * 4,
        out_specs=[vmem] * 3,
        scratch_shapes=[
            pltpu.VMEM((6, D, 512), bf),
            pltpu.VMEM((D, D), bf),
            pltpu.VMEM((TOK, 128), f32),
            pltpu.VMEM((TOK, 128), f32),
            pltpu.VMEM((TOK // 128, 256, 256), f32),
            pltpu.VMEM((TOK, D), bf),
            pltpu.VMEM((2, ext, D), f32),
            pltpu.VMEM((2, 2, HALF, D), bf),
            pltpu.VMEM((2, 2, HALF, D), bf),
            pltpu.SemaphoreType.DMA((9,)),
            pltpu.SemaphoreType.DMA((2,)),
            pltpu.SemaphoreType.DMA((2,)),
        ],
        compiler_params=pltpu.CompilerParams(
            collective_id=3, has_side_effects=True, vmem_limit_bytes=56 * 2**20
        ),
        name="attention_backward",
    )(lengths, frames, gain[None], queries, kv, db, dmid, w_qkv, w_out, *tables)


RING = 8
COUNT = len(UNITS)


def parts_of(unit):
    late = isinstance(unit, int) and unit >= COUNT - LAST_UNITS
    return LAST_PARTS if late else PARTS


def stacked_heads(block, heads):
    lane = lax.broadcasted_iota(jnp.int32, block.shape, 1) // HEAD_DIM
    zero = jnp.zeros_like(block)
    return jnp.concatenate([jnp.where(lane == h, block, zero) for h in range(heads)], 0)


def merged_heads(rows, heads):
    lane = lax.broadcasted_iota(jnp.int32, (128, rows.shape[1]), 1) // HEAD_DIM
    total = rows[:128]
    for h in range(1, heads):
        total = jnp.where(lane == h, rows[128 * h : 128 * h + 128], total)
    return total


def layer_kernel(
    clip_ref, x_hbm, c_hbm, gain1_ref, bias1_ref, gain2_ref, bias2_ref, scale_attn_ref, scale_mlp_ref,
    w_qkv, w_out, w_gate_up, w_down, cos_all, sin_all,
    out_hbm, grad_hbm, out0, out1, out2, out3, vec_out, att_hbm, normed_hbm, far_att, far_normed, hid_hbm, far_hid,
    part_a, part_b, part_c,
    recv_a1, recv_a2, recv_az, recv_b1, recv_b2, recv_bz, recv_cz, recv_c1, recv_c2,
    wide_v, deep_v, dkv_v, xbuf, ybuf, yfar, ydown, yout, other_v, hid_v,
    dm_v, x_v, c_v, grad_v, q_v, kv_v, dproj_v, bias_v, cos_v, sin_v, far_v,
    vec_sum, vec_recv, vec_z,
    send_sem, recv_sem, load_sem, far_send, far_recv, w_sem, hid_sem, hid_send, hid_recv,
    oth_send, oth_recv, q_send, q_recv, x_sem, edge_send, edge_recv, vec_send, vec_rsem, out_sem, halo_send, halo_recv,
):
    outs = (out0, out1, out2, out3)
    dp = lax.axis_index("dp")
    seq = lax.axis_index("seq")
    z, y = dp // 2, dp % 2
    x, c = seq // 2, seq % 2
    dev_c = (dp, x * 2 + 1 - c)
    dev_x = (dp, (1 - x) * 2 + c)
    dev_y = (z * 2 + 1 - y, seq)
    dev_d = (dp, (1 - x) * 2 + 1 - c)
    dev_z = [(lax.rem(z + k, 4) * 2 + y, seq) for k in (1, 2, 3)]
    bf, f32 = jnp.bfloat16, jnp.float32

    def local_copy(src, dst, sem):
        return pltpu.make_async_copy(src, dst, sem)

    def remote(src, dst, ssem, rsem, device):
        return pltpu.make_async_remote_copy(
            src_ref=src, dst_ref=dst, send_sem=ssem, recv_sem=rsem,
            device_id=device, device_id_type=MESH,
        )

    def weights(step, slot):
        result = []
        for i in range(2):
            at = pl.multiple_of((c if i == 0 else 1 - c) * (FF // 2) + step * 256, 256)
            result += [
                local_copy(
                    w_gate_up.at[:, pl.ds(at, 256)], wide_v.at[4 * slot + i], w_sem.at[slot, i]
                ),
                local_copy(
                    w_gate_up.at[:, pl.ds(FF + at, 256)], wide_v.at[4 * slot + 2 + i],
                    w_sem.at[slot, 2 + i],
                ),
                local_copy(
                    w_down.at[pl.ds(at, 256)], deep_v.at[slot, pl.ds(256 * i, 256)],
                    w_sem.at[slot, 4 + i],
                ),
            ]
        return result

    rows = pl.ds(pl.multiple_of(seq * TOK, TOK), TOK)
    x_copy = local_copy(x_hbm, x_v, load_sem.at[0])
    c_copy = local_copy(c_hbm, c_v, load_sem.at[1])
    tables = [
        local_copy(cos_all.at[rows], cos_v, load_sem.at[2]),
        local_copy(sin_all.at[rows], sin_v, load_sem.at[3]),
    ]
    wo_first = [
        local_copy(
            w_out.at[pl.ds(512 * k, 512)], dproj_v.at[:, pl.ds(D * k, D)], load_sem.at[4 + k]
        )
        for k in range(2)
    ]
    wq_copies = [
        local_copy(w_qkv.at[:, pl.ds(256 * k, 256)], wide_v.at[k % 8], w_sem.at[k % 8 // 4, k % 4])
        for k in range(12)
    ]
    wq_first = {
        k: local_copy(
            w_qkv.at[:, pl.ds(256 * k, 256)], wide_v.at[k - 4 if k >= 4 else k],
            w_sem.at[k // 8, k % 4],
        )
        for k in [4, 5, 6, 7, 8, 9, 10, 11, 0, 1, 2, 3]
    }
    x_copy.start()
    for k in range(4, 8):
        wq_first[k].start()
    for copy in tables:
        copy.start()
    for k in range(8, 12):
        wq_first[k].start()
    for copy in wo_first + [c_copy]:
        copy.start()

    barrier = pltpu.get_barrier_semaphore()
    for device in [dev_c, dev_x, dev_y, dev_d] + dev_z:
        pl.semaphore_signal(barrier, inc=1, device_id=device, device_id_type=MESH)

    is_end = (z == 0) | (z == 3)
    is_mid = (z == 1) | (z == 2)
    end_low = jnp.where(z == 0, 1, 0)
    end_dir = jnp.where(z == 0, 0, 1)
    end_next = (jnp.where(z == 0, 1, 2) * 2 + y, seq)
    mid_dir = jnp.where(z == 1, 0, 1)
    mid_low = jnp.where(z == 1, 1, 0)
    mid_keep = jnp.where(z == 1, 2, 0)
    mid_next = ((3 - z) * 2 + y, seq)
    back_dir = 1 - mid_dir
    back_low = jnp.where(z == 2, 2, 0)
    back_keep = jnp.where(z == 2, 3, 0)
    back_next = (jnp.where(z == 2, 3, 0) * 2 + y, seq)

    def z_send(slot, which, pieces, recv, number):
        ssem, rsem = send_sem.at[slot, which], recv_sem.at[slot, which]
        if number == 0:
            low, size, way, device = end_low, 3, end_dir, end_next
        elif number == 1:
            low, size, way, device = mid_keep, 2, mid_dir, mid_next
        else:
            low, size, way, device = back_keep, 1, back_dir, back_next
        return remote(
            pieces.at[pl.ds(low, size)], recv.at[way, pl.ds(low - 1 + way, size)],
            ssem.at[2 + number // 2], rsem.at[2 + way], device,
        )

    def z_wait(slot, which, recv, way, low, size):
        view = recv.at[way, pl.ds(low - 1 + way, size)]
        local_copy(view, view, recv_sem.at[slot, which, 2 + way]).wait()

    def z_round0(slot, which, pieces, recv):
        @pl.when(is_end)
        def _():
            z_send(slot, which, pieces, recv, 0).start()

    def z_round1(slot, which, pieces, recv):
        @pl.when(is_mid)
        def _():
            z_wait(slot, which, recv, mid_dir, mid_low, 3)
            keep = pl.ds(mid_keep, 2)
            pieces[keep] = pieces[keep] + recv[mid_dir, pl.ds(mid_keep - 1 + mid_dir, 2)]
            z_send(slot, which, pieces, recv, 1).start()

    def z_round2(slot, which, pieces, recv):
        @pl.when(is_mid)
        def _():
            z_wait(slot, which, recv, back_dir, back_low, 2)
            keep = pl.ds(back_keep, 1)
            pieces[keep] = pieces[keep] + recv[back_dir, pl.ds(back_keep - 1 + back_dir, 1)]
            z_send(slot, which, pieces, recv, 2).start()

    def z_final(slot, which, pieces, recv, finish):
        @pl.when(is_end)
        def _():
            way = 1 - end_dir
            z_wait(slot, which, recv, way, z, 1)
            finish(pieces[z].astype(f32) + recv[way, z - 1 + way].astype(f32))

        @pl.when(is_mid)
        def _():
            finish(
                pieces[z].astype(f32) + recv[0, z - 1].astype(f32) + recv[1, z].astype(f32)
            )

    def views(unit):
        slot = unit % RING if isinstance(unit, int) else lax.rem(unit, RING)
        parts = parts_of(unit)
        a, b = pl.ds(0, parts[1]), pl.ds(0, parts[2] - parts[1])
        return (
            slot,
            part_a.at[slot, :, :, :, a], recv_a1.at[slot, :, :, a], recv_a2.at[slot, :, a],
            recv_az.at[slot, :, :, a],
            part_b.at[slot, :, :, :, b], recv_b1.at[slot, :, :, b], recv_b2.at[slot, :, b],
            recv_bz.at[slot, :, :, b],
            part_c.at[slot], recv_c1.at[slot], recv_c2.at[slot], recv_cz.at[slot],
            parts[3] > parts[2],
        )

    def hop(unit, which, index):
        slot, a, a1, a2, _, b, b1, b2, _, cc, c1, c2, _, _ = views(unit)
        source, target, device = {
            (0, 0): lambda: (a.at[1 - x], a1, dev_x),
            (0, 1): lambda: (a.at[x, 1 - y], a2, dev_y),
            (1, 0): lambda: (b.at[1 - y], b1, dev_y),
            (1, 1): lambda: (b.at[y, 1 - x], b2, dev_x),
            (2, 0): lambda: (cc.at[z, 1 - x], c1, dev_x),
            (2, 1): lambda: (cc.at[z, x, 1 - y], c2, dev_y),
        }[which, index]()
        return remote(
            source, target, send_sem.at[slot, which, index], recv_sem.at[slot, which, index], device
        )

    def put(unit, which, block):
        low, high = parts_of(unit)[which : which + 2]
        if not isinstance(unit, int):
            columns = pl.ds(pl.multiple_of(unit * 256, 256), 256)
            out2[low:high, columns] = block
            return
        _, _, _, _, _, offset, out, row = UNITS[unit]
        outs[out][row + low : row + high, offset : offset + 256] = block

    def stage(unit, number):
        slot, a, a1, a2, rz_a, b, b1, b2, rz_b, cc, c1, c2, rz_c, thirds = views(unit)
        a_z, b_z = a.at[x, y], b.at[y, x]
        if number == 0:
            hop(unit, 0, 0).start()
            hop(unit, 1, 0).start()
            if thirds:
                z_round0(slot, 2, cc, rz_c)
        if number == 1:
            hop(unit, 0, 0).wait_recv()
            a[x] = a[x] + a1[...]
            hop(unit, 0, 1).start()
            hop(unit, 1, 0).wait_recv()
            b[y] = b[y] + b1[...]
            hop(unit, 1, 1).start()
            if thirds:
                z_round1(slot, 2, cc, rz_c)
        if number == 2:
            hop(unit, 0, 1).wait_recv()
            a[x, y] = a[x, y] + a2[...]
            z_round0(slot, 0, a_z, rz_a)
            hop(unit, 1, 1).wait_recv()
            b[y, x] = b[y, x] + b2[...]
            z_round0(slot, 1, b_z, rz_b)
            if thirds:
                z_round2(slot, 2, cc, rz_c)
        if number == 3:
            z_round1(slot, 0, a_z, rz_a)
            z_round1(slot, 1, b_z, rz_b)

            def keep(value):
                cc[z] = value.astype(bf)

            if thirds:
                z_final(slot, 2, cc, rz_c, keep)
                hop(unit, 2, 0).start()
        if number == 4:
            z_round2(slot, 0, a_z, rz_a)
            z_round2(slot, 1, b_z, rz_b)
            if thirds:
                hop(unit, 2, 0).wait_recv()
                cc[z, x] = cc[z, x] + c1[...]
                hop(unit, 2, 1).start()
        if number == 5:
            z_final(slot, 0, a_z, rz_a, functools.partial(put, unit, 0))
            z_final(slot, 1, b_z, rz_b, functools.partial(put, unit, 1))
            if thirds:
                hop(unit, 2, 1).wait_recv()
                put(unit, 2, cc[z, x, y].astype(f32) + c2[...].astype(f32))

    def sums(step):
        for number in range(1, 6):
            unit = step - number + 1
            if isinstance(step, int):
                if 0 <= unit < COUNT:
                    stage(unit, number)
            else:

                @pl.when(unit >= 0)
                def _():
                    stage(unit, number)

    def sent(unit):
        slot, a, _, _, rz_a, b, _, _, rz_b, cc, _, _, rz_c, thirds = views(unit)
        whole = [(a.at[x, y], rz_a), (b.at[y, x], rz_b)] + ([(cc, rz_c)] if thirds else [])
        for which, (pieces, recv) in enumerate(whole):
            for index in range(2):
                hop(unit, which, index).wait_send()

            @pl.when(is_end)
            def _():
                z_send(slot, which, pieces, recv, 0).wait_send()

            @pl.when(is_mid)
            def _():
                z_send(slot, which, pieces, recv, 1).wait_send()
                z_send(slot, which, pieces, recv, 2).wait_send()

    def multiply(unit, xslot, own, far):
        slot, parts = views(unit)[0], parts_of(unit)

        def step(i, carry):
            columns = pl.ds(pl.multiple_of(i * 512, 512), 512)
            for xi in range(2):
                total = (
                    tn_dot(xbuf[xslot, 0, :, columns], own(xi))
                    + tn_dot(xbuf[xslot, 1, :, columns], far(xi))
                ).astype(bf)
                for k in range(4):
                    zi, yi = 2 * i + k // 2, k % 2
                    block = total[k * 128 : k * 128 + 128]
                    part_a[slot, xi, yi, zi, : parts[1]] = block[: parts[1]]
                    part_b[slot, yi, xi, zi, : parts[2] - parts[1]] = block[parts[1] : parts[2]]
                    if parts[3] > parts[2]:
                        part_c[slot, zi, xi, yi] = block[parts[2] :]
            return carry

        lax.fori_loop(0, 2, step, 0)

    def far_copy(src, dst, index):
        return remote(src, dst, far_send.at[index], far_recv.at[index], dev_c)

    def pair_columns(array, width, offset, core, xi):
        return array.at[:, pl.ds(pl.multiple_of((2 * xi + core) * width + offset, 256), 256)]

    far_n2 = far_copy(xbuf.at[0, 0], xbuf.at[0, 1], 0)
    far_a = far_copy(xbuf.at[1, 1], far_att, 1)
    far_n = far_copy(xbuf.at[1, 0], far_normed, 2)
    far_dm = [
        far_copy(pair_columns(dm_v, 256, 0, 1 - c, xi), ydown.at[xi], 3 + xi) for xi in range(2)
    ]
    far_db = [
        far_copy(other_v.at[xi, 1 - c], yout.at[xi], 5 + xi) for xi in range(2)
    ]
    far_dq = [
        remote(
            pair_columns(dproj_v, 768, 256 * v, 1 - c, xi), yfar.at[v, xi],
            q_send.at[v, xi], q_recv.at[v, xi], dev_c,
        )
        for v in range(3)
        for xi in range(2)
    ]

    def far_other(step):
        return remote(
            other_v.at[lax.rem(step, 2)], yfar.at[lax.rem(step, 4)],
            oth_send.at[lax.rem(step, 2)], oth_recv.at[lax.rem(step, 4)], dev_c,
        )

    def hidden_copies(step):
        slot = lax.rem(step, 2)
        result = []
        for i in range(2):
            at = pl.multiple_of((c if i == 0 else 1 - c) * (FF // 2) + step * 256, 256)
            block = hid_v.at[slot, :, pl.ds(256 * i, 256)]
            result.append(local_copy(block, hid_hbm.at[:, pl.ds(at, 256)], hid_sem.at[slot, i]))
            result.append(
                remote(
                    block, far_hid.at[:, pl.ds(at, 256)],
                    hid_send.at[slot, i], hid_recv.at[step, i], dev_c,
                )
            )
        return result

    window_bias(bias_v, clip_ref, 4 * TOK, True)
    vec_sum[0] = jnp.zeros((8, D), f32)
    x_copy.wait()

    def first_norm(i, carry):
        at = pl.ds(pl.multiple_of(i * 128, 128), 128)
        hat, _ = normalize(x_v[at, :].astype(f32))
        xbuf[1, 0, at, :] = (hat * gain1_ref[...] + bias1_ref[...]).astype(bf)
        return carry

    lax.fori_loop(0, TOK // 128, first_norm, 0)
    normed_copy = local_copy(xbuf.at[1, 0], normed_hbm, out_sem.at[2])
    att_copy = local_copy(xbuf.at[1, 1], att_hbm, out_sem.at[3])
    normed_copy.start()
    for copy in tables:
        copy.wait()

    def project(k):
        full = dot(xbuf[1, 0], wide_v[k - 4 if k >= 4 else k])
        for half in range(2):
            block = full[:, half * 128 : half * 128 + 128]
            at = (k % 4) * 256 + half * 128
            if k < 8:
                block = rotated(block, cos_v[...], sin_v[...])
            block = block.astype(bf)
            if k < 4:
                q_v[:, at : at + 128] = block
            else:
                kv_v[k // 4 - 1, HALF : HALF + TOK, at : at + 128] = block

    def project_all(chunks):
        for k in chunks:
            wq_first[k].wait()
        for k in chunks:
            project(k)

    project_all(range(4, 8))
    for k in range(4):
        wq_first[k].start()
    project_all(range(8, 12))
    pl.semaphore_wait(barrier, 7)
    has_left, has_right = seq > 0, seq < 3
    halo_left = remote(
        kv_v.at[:, pl.ds(HALF, HALF)], kv_v.at[:, pl.ds(HALF + TOK, HALF)],
        halo_send.at[0], halo_recv.at[0], (dp, seq - 1),
    )
    halo_right = remote(
        kv_v.at[:, pl.ds(TOK, HALF)], kv_v.at[:, pl.ds(0, HALF)],
        halo_send.at[1], halo_recv.at[1], (dp, seq + 1),
    )

    @pl.when(has_left)
    def _():
        halo_left.start()

    @pl.when(has_right)
    def _():
        halo_right.start()

    @pl.when(jnp.logical_not(has_left))
    def _():
        kv_v[:, 0:HALF] = jnp.zeros((2, HALF, D), bf)

    @pl.when(jnp.logical_not(has_right))
    def _():
        kv_v[:, HALF + TOK :] = jnp.zeros((2, HALF, D), bf)

    far_n.start()
    project_all(range(4))
    for copy in weights(0, 0) + weights(1, 1):
        copy.start()
    last = TOK // 128 - 1
    heads = 4
    lanes_of = heads * HEAD_DIM

    def attend_forward(blocks):
        def step(group, carry):
            lanes = pl.ds(pl.multiple_of(group * lanes_of, lanes_of), lanes_of)
            scores = []
            for block in blocks:
                queries = q_v[block * 128 : block * 128 + 128, lanes] * 0.125
                keys = kv_v[0, block * 128 : block * 128 + 256, lanes]
                bias = jnp.concatenate([bias_v[block]] * (heads // 2), 1)
                scores.append(contract_back(keys, stacked_heads(queries, heads)) + bias)
            probs = []
            for score in scores:
                exponent = jnp.exp(score - jnp.max(score, 0, keepdims=True))
                total = jnp.sum(exponent, 0, keepdims=True)
                probs.append((exponent * (1.0 / total)).astype(bf))
            for block, prob in zip(blocks, probs):
                values = kv_v[1, block * 128 : block * 128 + 256, lanes]
                xbuf[1, 1, block * 128 : block * 128 + 128, lanes] = merged_heads(
                    tn_dot(prob, values), heads
                ).astype(bf)
            return carry

        lax.fori_loop(0, D // lanes_of, step, 0)

    attend_forward(list(range(1, last)))
    c_copy.wait()

    def scaled(i, carry):
        at = pl.ds(pl.multiple_of(i * 128, 128), 128)
        dm_v[at, :] = (c_v[at, :].astype(f32) * scale_mlp_ref[...]).astype(bf)
        return carry

    lax.fori_loop(0, TOK // 128, scaled, 0)
    for copy in far_dm:
        copy.start()
    dkv_v[...] = jnp.zeros_like(dkv_v)

    @pl.when(has_left)
    def _():
        halo_right.wait_recv()

    @pl.when(has_right)
    def _():
        halo_left.wait_recv()

    attend_forward([0, last])
    att_copy.start()
    far_a.start()
    for copy in wo_first:
        copy.wait()
    for part in range(4):
        cols = slice(part * 256, part * 256 + 256)
        grad_v[:, cols] = dot(xbuf[1, 1, :, 0:512], dproj_v[:, cols]) + dot(
            xbuf[1, 1, :, 512:1024], dproj_v[:, D + part * 256 : D + part * 256 + 256]
        )


    def before(i, carry):
        at = pl.ds(pl.multiple_of(i * 128, 128), 128)
        middle = x_v[at, :].astype(f32) + scale_attn_ref[...] * grad_v[at, :]
        hat, _ = normalize(middle)
        xbuf[0, 0, at, :] = (hat * gain2_ref[...] + bias2_ref[...]).astype(bf)
        return carry

    lax.fori_loop(0, TOK // 128, before, 0)
    far_n2.start()

    def mlp(step):
        slot = lax.rem(step, 2)

        @pl.when(step >= 2)
        def _():
            far_other(step - 2).wait_send()
            for copy in hidden_copies(step - 2)[0::2]:
                copy.wait()
            for copy in hidden_copies(step - 2)[1::2]:
                copy.wait_send()

        for copy in weights(step, slot):
            copy.wait()
        normed = xbuf.at[0, 0]
        for i in range(2):
            gate = dot(normed[...], wide_v[4 * slot + i])
            up = dot(normed[...], wide_v[4 * slot + 2 + i])
            dh = contract_back(dm_v[...], deep_v[slot, 256 * i : 256 * i + 256])
            sigmoid = 1.0 / (1.0 + jnp.exp(-gate))
            silu = gate * sigmoid
            hid_v[slot, :, 256 * i : 256 * i + 256] = (silu * up).astype(bf)
            target = ybuf if i == 0 else other_v
            dgate = dh * up * (sigmoid * (1.0 + gate * (1.0 - sigmoid)))
            target[slot, 0] = dgate.astype(bf)
            target[slot, 1] = (dh * silu).astype(bf)
        far_other(step).start()
        for copy in hidden_copies(step):
            copy.start()
        dkv_v[0, 0:TOK] += dot(hid_v[slot], deep_v[slot])
        dkv_v[1, 0:TOK] += (
            contract_back(ybuf[slot, 0], wide_v[4 * slot])
            + contract_back(other_v[slot, 0], wide_v[4 * slot + 1])
            + contract_back(ybuf[slot, 1], wide_v[4 * slot + 2])
            + contract_back(other_v[slot, 1], wide_v[4 * slot + 3])
        )

        @pl.when(step + 2 < 8)
        def _():
            for copy in weights(step + 2, slot):
                copy.start()

    def gate_unit(step):
        far_other(step).wait_recv()
        multiply(
            step, 0, lambda xi: ybuf[lax.rem(step, 2), xi], lambda xi: yfar[lax.rem(step, 4), xi]
        )
        stage(step, 0)

    def mlp_step(step, carry):
        mlp(step)

        @pl.when(step == 0)
        def _():
            far_n2.wait_recv()

        @pl.when(step >= BEHIND)
        def _():
            sums(step - BEHIND)

        gate_unit(step)

        return carry

    lax.fori_loop(0, 8, mlp_step, 0)

    wo_copies = [
        local_copy(w_out.at[pl.ds(512 * k, 512)], deep_v.at[k], w_sem.at[k, 4]) for k in range(2)
    ]
    for copy in wo_copies + wq_copies[:8]:
        copy.start()
    for step in (6, 7):
        far_other(step).wait_send()
        for copy in hidden_copies(step)[0::2]:
            copy.wait()
        for copy in hidden_copies(step)[1::2]:
            copy.wait_send()
    for step in range(8):
        for copy in hidden_copies(step)[1::2]:
            copy.wait_recv()

    def load_left(unit):
        left, offset, width, _, _, _, _, _ = UNITS[unit]
        slot = {8: 1, 9: 0, 10: 1, 11: 0, 12: 1, 13: 0}[unit]
        arrays = {3: (hid_hbm, far_hid), 1: (att_hbm, far_att), 0: (normed_hbm, far_normed)}[left]
        result = []
        for side in range(2):
            if width == 128:
                result.append(
                    local_copy(arrays[side], xbuf.at[slot, side], x_sem.at[slot, side, 0])
                )
                continue
            for block in range(8):
                result.append(
                    local_copy(
                        arrays[side].at[:, pl.ds(block * width + offset, 128)],
                        xbuf.at[slot, side, :, pl.ds(block * 128, 128)],
                        x_sem.at[slot, side, block],
                    )
                )
        return result

    def unit_sum(unit):
        if unit <= 13:
            for copy in load_left(unit):
                copy.wait()
        _, _, _, right, width, offset, _, _ = UNITS[unit]
        if unit >= RING:
            sent(unit - RING)
        xslot = {8: 1, 9: 0, 10: 1, 11: 0, 12: 1}.get(unit, 0)
        if right == 1:
            own = lambda xi: other_v[xi, c]
        else:
            own = lambda xi: pair_columns({3: dm_v, 0: dproj_v}[right], width, offset, c, xi)[...]
        far = {3: ydown, 1: yout}.get(right, yfar.at[max(unit - 13, 0)])
        multiply(
            unit, xslot,
            own,
            lambda xi: far[xi],
        )
        stage(unit, 0)
        if unit + 2 <= 13:
            if unit + 2 == 12:
                far_a.wait_recv()
            if unit + 2 == 13:
                far_n.wait_recv()
            for copy in load_left(unit + 2):
                copy.start()

    for copy in [far_n2, far_a, far_n] + far_dm:
        copy.wait_send()
    normed_copy.wait()
    att_copy.wait()
    for copy in load_left(8):
        copy.start()
    for copy in load_left(9):
        copy.start()
    for copy in far_dm:
        copy.wait_recv()

    def after(i, carry):
        at = pl.ds(pl.multiple_of(i * 128, 128), 128)
        cot = c_v[at, :].astype(f32)
        branch = grad_v[at, :]
        middle = x_v[at, :].astype(f32) + scale_attn_ref[...] * branch
        mlp_out = dkv_v[0, at, :]
        dn = dkv_v[1, at, :]
        vec_sum[0, 5:6] += jnp.sum(cot * mlp_out, 0, keepdims=True)
        c_v[at, :] = (middle + scale_mlp_ref[...] * mlp_out).astype(bf)
        hat, inverse = normalize(middle)
        vec_sum[0, 3:4] += jnp.sum(dn * hat, 0, keepdims=True)
        vec_sum[0, 4:5] += jnp.sum(dn, 0, keepdims=True)
        dmid = cot + norm_backward(dn, hat, inverse, gain2_ref[...])
        vec_sum[0, 2:3] += jnp.sum(dmid * branch, 0, keepdims=True)
        grad_v[at, :] = dmid
        branch_grad = (dmid * scale_attn_ref[...]).astype(bf)
        for k in range(4):
            other_v[k // 2, k % 2, at, :] = branch_grad[:, 256 * k : 256 * k + 256]
        return carry

    out_copy = local_copy(c_v, out_hbm, out_sem.at[0])
    grad_copy = local_copy(grad_v, grad_hbm, out_sem.at[1])

    def norm_two_back():
        lax.fori_loop(0, TOK // 128, after, 0)
        out_copy.start()
        for copy in far_db:
            copy.start()

    def attended_grads():
        for k in range(2):
            wo_copies[k].wait()
        out_copy.wait()
        for k in range(2):
            total = None
            for j in range(4):
                term = contract_back(other_v[j // 2, j % 2], deep_v[k, :, 256 * j : 256 * j + 256])
                total = term if total is None else total + term
            c_v[:, 512 * k : 512 * k + 512] = total.astype(bf)
        for copy in far_db:
            copy.wait_recv()

    def attend(blocks):
        def step(group, carry):
            lanes = pl.ds(pl.multiple_of(group * lanes_of, lanes_of), lanes_of)
            held = []
            for block in blocks:
                own = slice(block * 128, block * 128 + 128)
                window = slice(block * 128, block * 128 + 256)
                queries = stacked_heads(q_v[own, lanes] * 0.125, heads)
                grads = stacked_heads(c_v[own, lanes], heads)
                keys = kv_v[0, window, lanes]
                bias = jnp.concatenate([bias_v[block]] * (heads // 2), 1)
                scores = contract_back(keys, queries) + bias
                d_probs = contract_back(kv_v[1, window, lanes], grads)
                held.append((queries, grads, keys, scores, d_probs))
            ready = []
            for queries, grads, keys, scores, d_probs in held:
                exponent = jnp.exp(scores - jnp.max(scores, 0, keepdims=True))
                probs = exponent * (1.0 / jnp.sum(exponent, 0, keepdims=True))
                inner = jnp.sum(probs * d_probs, 0, keepdims=True)
                d_scores = (probs * (d_probs - inner)).astype(bf)
                ready.append((queries, grads, keys, d_scores, probs.astype(bf)))
            for block, (queries, grads, keys, d_scores, probs) in zip(blocks, ready):
                own = slice(block * 128, block * 128 + 128)
                window = slice(block * 128, block * 128 + 256)
                for which, update in ((0, dot(d_scores, queries)), (1, dot(probs, grads))):
                    if block in (0, last):
                        dkv_v[which, window, lanes] = update
                    elif block == 1:
                        dkv_v[which, 128:256, lanes] += update[:128]
                        dkv_v[which, 256:384, lanes] = update[128:]
                    else:
                        dkv_v[which, window, lanes] += update
                d_queries = merged_heads(tn_dot(d_scores, keys), heads) * 0.125
                for k in range(lanes_of // 128):
                    at = pl.ds(pl.multiple_of(group * lanes_of + 128 * k, 128), 128)
                    dproj_v[own, at] = rotated(
                        d_queries[:, 128 * k : 128 * k + 128], cos_v[own, :], -sin_v[own, :]
                    ).astype(bf)
            return carry

        lax.fori_loop(0, D // lanes_of, step, 0)

    to_left = remote(
        hid_v.at[0, pl.ds(0, 256)], far_v.at[1], edge_send.at[0], edge_recv.at[0], (dp, seq - 1)
    )
    to_right = remote(
        hid_v.at[1, pl.ds(0, 256)], far_v.at[0], edge_send.at[1], edge_recv.at[1], (dp, seq + 1)
    )

    def edges_out():
        for side, first in ((0, 0), (1, HALF + TOK)):
            for k in range(4):
                hid_v[side, 64 * k : 64 * k + 64] = dkv_v[
                    k // 2, first : first + HALF, 512 * (k % 2) : 512 * (k % 2) + 512
                ].astype(bf)

        @pl.when(has_left)
        def _():
            to_left.start()

        @pl.when(has_right)
        def _():
            to_right.start()

    def edges_in():
        @pl.when(has_left)
        def _():
            to_right.wait_recv()
            for k in range(4):
                dkv_v[k // 2, HALF : 2 * HALF, 512 * (k % 2) : 512 * (k % 2) + 512] += far_v[
                    0, 64 * k : 64 * k + 64
                ].astype(f32)

        @pl.when(has_right)
        def _():
            to_left.wait_recv()
            for k in range(4):
                dkv_v[k // 2, TOK : TOK + HALF, 512 * (k % 2) : 512 * (k % 2) + 512] += far_v[
                    1, 64 * k : 64 * k + 64
                ].astype(f32)

        for k in range(D // 128):
            lanes = slice(k * 128, k * 128 + 128)
            dproj_v[:, D + k * 128 : D + k * 128 + 128] = rotated(
                dkv_v[0, HALF : HALF + TOK, lanes], cos_v[...], -sin_v[...]
            ).astype(bf)
            dproj_v[:, 2 * D + k * 128 : 2 * D + k * 128 + 128] = dkv_v[
                1, HALF : HALF + TOK, lanes
            ].astype(bf)
        for copy in far_dq:
            copy.start()

    def project_back(chunks, fresh):
        for k in chunks:
            wq_copies[k].wait()
        total = None
        for k in chunks:
            term = contract_back(dproj_v[:, 256 * k : 256 * k + 256], wide_v[k % 8])
            total = term if total is None else total + term
        if fresh:
            dkv_v[0, 0:TOK] = total
        else:
            dkv_v[0, 0:TOK] += total

    def last_norm(i, carry):
        at = pl.ds(pl.multiple_of(i * 128, 128), 128)
        hat, inverse = normalize(x_v[at, :].astype(f32))
        dn = dkv_v[0, at, :]
        vec_sum[0, 0:1] += jnp.sum(dn * hat, 0, keepdims=True)
        vec_sum[0, 1:2] += jnp.sum(dn, 0, keepdims=True)
        grad_v[at, :] += norm_backward(dn, hat, inverse, gain1_ref[...])
        return carry

    def norm_one_back():
        lax.fori_loop(0, TOK // 128, last_norm, 0)
        grad_copy.start()

    def vec_copy(number):
        return remote(
            vec_sum.at[number], vec_recv.at[number], vec_send.at[number], vec_rsem.at[number],
            (dev_c, dev_x, dev_y)[number],
        )

    vec_planes = [
        remote(vec_sum.at[3], vec_z.at[z], vec_send.at[3 + k], vec_rsem.at[3 + k], dev_z[k])
        for k in range(3)
    ]

    def vectors(number):
        if 0 < number <= 3:
            vec_copy(number - 1).wait_recv()
            vec_sum[number] = vec_sum[number - 1] + vec_recv[number - 1]
        if number < 3:
            vec_copy(number).start()
        elif number == 3:
            vec_z[z] = vec_sum[3]
            for copy in vec_planes:
                copy.start()
        else:
            for k in range(3):
                view = vec_z.at[lax.rem(z + 3 - k, 4)]
                local_copy(view, view, vec_rsem.at[3 + k]).wait()
            vec_out[...] = vec_z[0] + vec_z[1] + vec_z[2] + vec_z[3]

    def start_wq():
        for copy in wq_copies[8:]:
            copy.start()

    def far_dq_wait():
        for copy in far_dq:
            copy.wait_recv()

    actions = {
        "E": norm_two_back,
        "D": attended_grads,
        "A0": lambda: attend([0, last]),
        "O": edges_out,
        "A1": lambda: attend(list(range(1, last))),
        "I": edges_in,
        "W0": lambda: (project_back(range(8), True), start_wq()),
        "W1": lambda: project_back(range(8, 12), False),
        "N": norm_one_back,
        "Q": far_dq_wait,
    }
    for word in ORDER.split():
        if word in actions:
            actions[word]()
        elif word[0] == "P":
            unit_sum(int(word[1:]))
        elif word[0] == "S":
            sums(int(word[1:]))
        elif word[0] == "V":
            vectors(int(word[1:]))

    for unit in range(COUNT - RING, COUNT):
        sent(unit)
    for copy in far_db + far_dq + [vec_copy(k) for k in range(3)] + vec_planes:
        copy.wait_send()

    @pl.when(has_left)
    def _():
        halo_left.wait_send()
        to_left.wait_send()

    @pl.when(has_right)
    def _():
        halo_right.wait_send()
        to_right.wait_send()

    grad_copy.wait()


BEHIND = 2
ORDER = (
    "P8 P9 E S6 P10 D A0 O S7 P11 A1 S8 P12 I Q S9 P13 W0 S10 P14 W1 N S11 P15 V0 S12 V1 S13 V2 S14 V3 S15 V4 S16 S17 S18 S19"
)


def layer(
    lengths, frames, cotangent, vectors, w_qkv, w_out, w_gate_up, w_down, tables,
):
    bf, f32 = jnp.bfloat16, jnp.float32
    hbm = pl.BlockSpec(memory_space=pl.ANY)
    vmem = pl.BlockSpec(memory_space=pltpu.VMEM)
    smem = pl.BlockSpec(memory_space=pltpu.SMEM)
    shape = jax.ShapeDtypeStruct
    size = (LAST_PARTS[1], LAST_PARTS[2] - LAST_PARTS[1], PARTS[3] - PARTS[2])
    dma = pltpu.SemaphoreType.DMA
    ext = TOK + 2 * HALF
    scratch = [
        pltpu.VMEM((RING, 2, 2, 4, size[0], 256), bf),
        pltpu.VMEM((RING, 2, 2, 4, size[1], 256), bf),
        pltpu.VMEM((RING, 4, 2, 2, size[2], 256), bf),
        pltpu.VMEM((RING, 2, 4, size[0], 256), bf),
        pltpu.VMEM((RING, 4, size[0], 256), bf),
        pltpu.VMEM((RING, 2, 3, size[0], 256), bf),
        pltpu.VMEM((RING, 2, 4, size[1], 256), bf),
        pltpu.VMEM((RING, 4, size[1], 256), bf),
        pltpu.VMEM((RING, 2, 3, size[1], 256), bf),
        pltpu.VMEM((RING, 2, 3, 2, 2, size[2], 256), bf),
        pltpu.VMEM((RING, 2, size[2], 256), bf),
        pltpu.VMEM((RING, size[2], 256), bf),
        pltpu.VMEM((8, D, 256), bf),
        pltpu.VMEM((2, 512, D), bf),
        pltpu.VMEM((2, ext, D), f32),
        pltpu.VMEM((2, 2, TOK, D), bf),
        pltpu.VMEM((2, 2, TOK, 256), bf),
        pltpu.VMEM((4, 2, TOK, 256), bf),
        pltpu.VMEM((2, TOK, 256), bf),
        pltpu.VMEM((2, TOK, 256), bf),
        pltpu.VMEM((2, 2, TOK, 256), bf),
        pltpu.VMEM((2, TOK, 512), bf),
        pltpu.VMEM((TOK, D), bf),
        pltpu.VMEM((TOK, D), bf),
        pltpu.VMEM((TOK, D), bf),
        pltpu.VMEM((TOK, D), f32),
        pltpu.VMEM((TOK, D), bf),
        pltpu.VMEM((2, ext, D), bf),
        pltpu.VMEM((TOK, 3 * D), bf),
        pltpu.VMEM((TOK // 128, 256, 256), f32),
        pltpu.VMEM((TOK, 128), f32),
        pltpu.VMEM((TOK, 128), f32),
        pltpu.VMEM((2, 256, 512), bf),
        pltpu.VMEM((4, 8, D), f32),
        pltpu.VMEM((3, 8, D), f32),
        pltpu.VMEM((4, 8, D), f32),
        dma((RING, 3, 4)),
        dma((RING, 3, 4)),
        dma((7,)),
        dma((7,)),
        dma((7,)),
        dma((2, 6)),
        dma((2, 2)),
        dma((2, 2)),
        dma((8, 2)),
        dma((2,)),
        dma((4,)),
        dma((3, 2)),
        dma((3, 2)),
        dma((2, 2, 8)),
        dma((2,)),
        dma((2,)),
        dma((6,)),
        dma((6,)),
        dma((4,)),
        dma((2,)),
        dma((2,)),
    ]
    results = pl.pallas_call(
        layer_kernel,
        out_shape=[
            shape((TOK, D), bf),
            shape((TOK, D), f32),
            shape((128, 768), f32),
            shape((128, 256), f32),
            shape((128, 2048), f32),
            shape((512, 256), f32),
            shape((8, D), f32),
        ]
        + [shape((TOK, D), bf)] * 4
        + [
            shape((TOK, FF), bf),
            shape((TOK, FF), bf),
        ],
        in_specs=[smem] + [hbm] * 2 + [vmem] * 6 + [hbm] * 6,
        out_specs=[hbm] * 2 + [vmem] * 5 + [hbm] * 6,
        scratch_shapes=scratch,
        compiler_params=pltpu.CompilerParams(
            collective_id=4, has_side_effects=True, vmem_limit_bytes=64 * 2**20 - 2**16
        ),
        name="layer",
    )(
        lengths, frames, cotangent, *[v[None] for v in vectors], w_qkv, w_out, w_gate_up, w_down, *tables,
    )[:7]
    finished = pl.pallas_call(
        finish_kernel,
        out_shape=[shape(v.shape, v.dtype) for v in results[:6]] + [shape((1, D), f32)] * 6,
        in_specs=[hbm] * 6 + [vmem],
        out_specs=[hbm] * 6 + [vmem] * 6,
        scratch_shapes=[pltpu.VMEM(v.shape, v.dtype) for v in results[:6]] + [dma((2, 6))],
        compiler_params=pltpu.CompilerParams(vmem_limit_bytes=64 * 2**20 - 2**16),
        name="finish",
    )(*results)
    return finished[:6], [v[0] for v in finished[6:]]


def finish_kernel(*refs):
    sources, targets, held, sems = refs[:6], refs[7:13], refs[19:25], refs[25]
    arrivals = [
        pltpu.make_async_copy(source, target, sems.at[0, k])
        for k, (source, target) in enumerate(zip(sources, held))
    ]
    departures = [
        pltpu.make_async_copy(source, target, sems.at[1, k])
        for k, (source, target) in enumerate(zip(held, targets))
    ]
    for copy in arrivals:
        copy.start()
    for k in range(6):
        refs[13 + k][...] = refs[6][k : k + 1]
    for arrival, departure in zip(arrivals, departures):
        arrival.wait()
        departure.start()
    for copy in departures:
        copy.wait()


def local(
    frames,
    cotangent,
    clip_len,
    ln1_gain,
    ln1_bias,
    w_qkv,
    w_out,
    scale_attn,
    ln2_gain,
    ln2_bias,
    w_gate_up,
    w_down,
    scale_mlp,
):
    row_count = frames.shape[0]
    seq_count = lax.axis_size("seq")
    tables = rotary_tables(row_count * seq_count)
    data_count = lax.axis_size("dp")
    if (data_count, seq_count, row_count) == (8, 4, TOK):
        sums, vector_total = layer(
            clip_len, frames, cotangent,
            (ln1_gain, ln1_bias, ln2_gain, ln2_bias, scale_attn, scale_mlp),
            w_qkv, w_out, w_gate_up, w_down, tables,
        )
        out_frames, input_grad, sum_qkv, sum_out, sum_gate_up, sum_down = sums
    else:
        normed_b, queries, kv, attended_t, branch = forward_attention(
            frames, clip_len, ln1_gain, ln1_bias, scale_attn, w_qkv, w_out, tables, seq_count
        )
        out_frames, normed_two_b, hidden_b, gate_up_b, mlp_grad, branch_grad, middle_grad, vec_two = (
            feed_forward(
                frames, cotangent, branch, ln2_gain, ln2_bias, scale_attn, scale_mlp, w_gate_up, w_down
            )
        )
        projected_grad, input_grad, vec_one = backward_attention(
            frames, clip_len, ln1_gain, queries, kv, branch_grad, middle_grad, w_qkv, w_out, tables,
            seq_count,
        )
        vector_grads = jnp.stack(
            [vec_one[0], vec_one[1], vec_two[3], vec_two[1], vec_two[2], vec_two[0]], 0
        )
        lefts = (normed_b, attended_t, normed_two_b, hidden_b)
        rights = (projected_grad, branch_grad, gate_up_b, mlp_grad)
        vector_total = lax.psum(vector_grads, ("dp", "seq"))
        sum_qkv, sum_out, sum_gate_up, sum_down = [
            lax.psum_scatter(
                to_blocks(contract_rows(left, right), data_count, seq_count),
                ("dp", "seq"),
                scatter_dimension=0,
                tiled=True,
            )[0]
            for left, right in zip(lefts, rights)
        ]
    return (
        out_frames,
        input_grad,
        vector_total[0],
        vector_total[1],
        sum_qkv,
        sum_out,
        vector_total[2],
        vector_total[3],
        vector_total[4],
        sum_gate_up,
        sum_down,
        vector_total[5],
    )


def solution(mesh):
    return jax.shard_map(
        local,
        mesh=mesh,
        in_specs=(
            P(("dp", "seq"), None),
            P(("dp", "seq"), None),
            P("dp", None),
            P(),
            P(),
            P(),
            P(),
            P(),
            P(),
            P(),
            P(),
            P(),
            P(),
        ),
        out_specs=(
            P(("dp", "seq"), None),
            P(("dp", "seq"), None),
            P(),
            P(),
            P("dp", "seq"),
            P("dp", "seq"),
            P(),
            P(),
            P(),
            P("dp", "seq"),
            P("dp", "seq"),
            P(),
        ),
        check_vma=False,
    )
```

```python
import functools

import jax
import jax.numpy as jnp
import numpy as np
from jax import lax
from jax.experimental import pallas as pl
from jax.experimental.pallas import tpu as pltpu
from jax.sharding import PartitionSpec as P

D = 1024
HEADS = 16
HEAD_DIM = 64
FF = 4096
HALF = 64
QBLK = 512


EPS = 1e-05
NEG = -1e30


def contract_rows(left, right):
    return lax.dot_general(
        left, right, (((0,), (0,)), ((), ())), preferred_element_type=jnp.float32
    )


def contract_back(grads, weight):
    return lax.dot_general(
        grads, weight, (((1,), (1,)), ((), ())), preferred_element_type=jnp.float32
    )


def to_blocks(matrix, data_count, seq_count):
    row_total, col_total = matrix.shape
    shaped = matrix.reshape(data_count, row_total // data_count, seq_count, col_total // seq_count)
    return shaped.transpose(0, 2, 1, 3).reshape(
        data_count * seq_count, row_total // data_count, col_total // seq_count
    )


MESH = pl.DeviceIdType.MESH
TOK = 512
PARTS = (0, 48, 96, 128)
LAST_PARTS = (0, 64, 128, 128)
LAST_UNITS = 1

UNITS = (
    [(2, 0, 128, 2, 2048, 256 * v, 2, 0) for v in range(8)]
    + [(3, 128 * v, 512, 3, 256, 0, 3, 128 * v) for v in range(4)]
    + [(1, 0, 128, 1, 256, 0, 1, 0)]
    + [(0, 0, 128, 0, 768, 256 * v, 0, 0) for v in range(3)]
)


def tn_dot(left, right):
    return lax.dot_general(
        left, right, (((0,), (0,)), ((), ())), preferred_element_type=jnp.float32
    )


def rotated(values, cosines, sines):
    lane = lax.broadcasted_iota(jnp.int32, values.shape, 1)
    partner = jnp.where(
        lane % HEAD_DIM < HEAD_DIM // 2,
        pltpu.roll(values, 128 - HEAD_DIM // 2, 1),
        pltpu.roll(values, HEAD_DIM // 2, 1),
    )
    return values * cosines + partner * sines


def head_masks():
    lane = lax.broadcasted_iota(jnp.int32, (128, 128), 1)
    return lane < HEAD_DIM


def stacked(pair):
    first = head_masks()
    zero = jnp.zeros_like(pair)
    return jnp.concatenate([jnp.where(first, pair, zero), jnp.where(first, zero, pair)], 0)


def merged(rows):
    return jnp.where(head_masks(), rows[:128], rows[128:])


def clip_number(positions, ends, group_len):
    total = jnp.zeros_like(positions)
    for end in ends:
        total = total + (positions >= end).astype(jnp.int32)
    return jnp.where((positions >= 0) & (positions < group_len), total, -1)


def normalize(values):
    average = jnp.mean(values, -1, keepdims=True)
    centered = values - average
    inverse = lax.rsqrt(jnp.mean(centered * centered, -1, keepdims=True) + EPS)
    return centered * inverse, inverse


def dot(left, right):
    return jnp.dot(left, right, preferred_element_type=jnp.float32)


def norm_backward(grads, hat, inverse, gain):
    scaled = grads * gain
    return inverse * (
        scaled
        - jnp.mean(scaled, -1, keepdims=True)
        - hat * jnp.mean(scaled * hat, -1, keepdims=True)
    )


def window_bias(bias_ref, clip_ref, group_len, keys_first):
    seq = lax.axis_index("seq")
    first_end = clip_ref[0, 0]
    second_end = first_end + clip_ref[0, 1]
    ends = (first_end, second_end, second_end + clip_ref[0, 2])
    for block in range(TOK // 128):
        start = seq * TOK + block * 128
        shape = (2 * 128, 2 * 128)
        k_axis = 0 if keys_first else 1
        k_at = lax.broadcasted_iota(jnp.int32, shape, k_axis)
        q_at = lax.rem(lax.broadcasted_iota(jnp.int32, shape, 1 - k_axis), 128)
        q_shape = (1, 256) if keys_first else (256, 1)
        k_shape = (256, 1) if keys_first else (1, 256)
        q_ids = clip_number(
            start + lax.rem(lax.broadcasted_iota(jnp.int32, q_shape, 1 - k_axis), 128),
            ends, group_len,
        )
        k_ids = clip_number(
            start - HALF + lax.broadcasted_iota(jnp.int32, k_shape, k_axis), ends, group_len
        )
        seen = (q_ids == k_ids) & (k_at >= q_at) & (k_at < q_at + 2 * HALF)
        bias_ref[block] = jnp.where(seen, 0.0, NEG)


def greet_sides(seq_count):
    dp, seq = lax.axis_index("dp"), lax.axis_index("seq")
    barrier = pltpu.get_barrier_semaphore()
    has_left, has_right = seq > 0, seq < seq_count - 1

    @pl.when(has_left)
    def _():
        pl.semaphore_signal(barrier, inc=1, device_id=(dp, seq - 1), device_id_type=MESH)

    @pl.when(has_right)
    def _():
        pl.semaphore_signal(barrier, inc=1, device_id=(dp, seq + 1), device_id_type=MESH)

    pl.semaphore_wait(barrier, has_left.astype(jnp.int32) + has_right.astype(jnp.int32))

    return (dp, seq - 1), (dp, seq + 1), has_left, has_right


def forward_kernel(
    seq_count, clip_ref, x_ref, gain_ref, gain_bias_ref, scale_ref, w_qkv, w_out, cos_all, sin_all,
    normed_ref, q_ref, kv_ref, att_ref, branch_ref,
    wq_v, wo_v, cos_v, sin_v, bias_v, load_sem, send_sem, recv_sem,
):
    dp, seq = lax.axis_index("dp"), lax.axis_index("seq")
    rows = pl.ds(pl.multiple_of(seq * TOK, TOK), TOK)
    copies = []
    order = [2, 3, 4, 5, 0, 1]
    tables = [
        pltpu.make_async_copy(cos_all.at[rows], cos_v, load_sem.at[0]),
        pltpu.make_async_copy(sin_all.at[rows], sin_v, load_sem.at[1]),
    ]
    chunks = {
        k: pltpu.make_async_copy(
            w_qkv.at[:, pl.ds(k * 512, 512)], wq_v.at[k], load_sem.at[2 + k]
        )
        for k in order
    }
    out_copy = pltpu.make_async_copy(w_out, wo_v, load_sem.at[8])
    for copy in tables + [chunks[k] for k in order] + [out_copy]:
        copy.start()
    left, right, has_left, has_right = greet_sides(seq_count)

    hat, _ = normalize(x_ref[...].astype(jnp.float32))
    normed_ref[...] = (hat * gain_ref[...] + gain_bias_ref[...]).astype(jnp.bfloat16)
    for copy in tables:
        copy.wait()

    def project(k):
        chunks[k].wait()
        for part in range(2):
            cols = slice(part * 256, part * 256 + 256)
            full = dot(normed_ref[...], wq_v[k, :, cols])
            for half in range(2):
                block = full[:, half * 128 : half * 128 + 128]
                at = (k % 2) * 512 + part * 256 + half * 128
                if k < 4:
                    block = rotated(block, cos_v[...], sin_v[...])
                block = block.astype(jnp.bfloat16)
                if k < 2:
                    q_ref[:, at : at + 128] = block
                else:
                    kv_ref[k // 2 - 1, HALF : HALF + TOK, at : at + 128] = block

    for k in order[:4]:
        project(k)

    to_left = pltpu.make_async_remote_copy(
        src_ref=kv_ref.at[:, pl.ds(HALF, HALF)], dst_ref=kv_ref.at[:, pl.ds(HALF + TOK, HALF)],
        send_sem=send_sem.at[0], recv_sem=recv_sem.at[0], device_id=left, device_id_type=MESH,
    )
    to_right = pltpu.make_async_remote_copy(
        src_ref=kv_ref.at[:, pl.ds(TOK, HALF)], dst_ref=kv_ref.at[:, pl.ds(0, HALF)],
        send_sem=send_sem.at[1], recv_sem=recv_sem.at[1], device_id=right, device_id_type=MESH,
    )

    @pl.when(has_left)
    def _():
        to_left.start()

    @pl.when(has_right)
    def _():
        to_right.start()

    @pl.when(jnp.logical_not(has_left))
    def _():
        kv_ref[:, 0:HALF] = jnp.zeros((2, HALF, D), jnp.bfloat16)

    @pl.when(jnp.logical_not(has_right))
    def _():
        kv_ref[:, HALF + TOK :] = jnp.zeros((2, HALF, D), jnp.bfloat16)

    for k in order[4:]:
        project(k)
    window_bias(bias_v, clip_ref, seq_count * TOK, False)

    heads = 4
    lanes_of = heads * HEAD_DIM

    def attend(blocks):
        def step(group, carry):
            lanes = pl.ds(pl.multiple_of(group * lanes_of, lanes_of), lanes_of)
            scores = []
            for block in blocks:
                queries = q_ref[block * 128 : block * 128 + 128, lanes] * 0.125
                keys = kv_ref[0, block * 128 : block * 128 + 256, lanes]
                bias = jnp.concatenate([bias_v[block]] * (heads // 2), 0)
                scores.append(contract_back(stacked_heads(queries, heads), keys) + bias)
            probs = []
            for score in scores:
                exponent = jnp.exp(score - jnp.max(score, -1, keepdims=True))
                total = jnp.sum(exponent, -1, keepdims=True)
                probs.append((exponent * (1.0 / total)).astype(jnp.bfloat16))
            for block, prob in zip(blocks, probs):
                values = kv_ref[1, block * 128 : block * 128 + 256, lanes]
                att_ref[block * 128 : block * 128 + 128, lanes] = merged_heads(
                    dot(prob, values), heads
                ).astype(jnp.bfloat16)
            return carry

        lax.fori_loop(0, D // lanes_of, step, 0)

    last = TOK // 128 - 1
    attend(list(range(1, last)))

    @pl.when(has_left)
    def _():
        to_right.wait_recv()

    @pl.when(has_right)
    def _():
        to_left.wait_recv()

    attend([0, last])
    out_copy.wait()
    for part in range(4):
        cols = slice(part * 256, part * 256 + 256)
        branch_ref[:, cols] = dot(att_ref[...], wo_v[:, cols])

    @pl.when(has_left)
    def _():
        to_left.wait_send()

    @pl.when(has_right)
    def _():
        to_right.wait_send()


def rotary_tables(group_len):
    half = HEAD_DIM // 2
    inv_freq = (10000.0 ** (-np.arange(half) / half)).astype(np.float32)[None, :]
    angles = np.arange(group_len, dtype=np.float32)[:, None] * inv_freq
    cosine, sine = np.cos(angles), np.sin(angles)
    return (
        np.concatenate([cosine] * 4, 1).astype(np.float32),
        np.concatenate([-sine, sine] * 2, 1).astype(np.float32),
    )


def forward_attention(frames, lengths, gain, bias, scale, w_qkv, w_out, tables, seq_count):
    bf, f32 = jnp.bfloat16, jnp.float32
    hbm = pl.BlockSpec(memory_space=pl.ANY)
    vmem = pl.BlockSpec(memory_space=pltpu.VMEM)
    smem = pl.BlockSpec(memory_space=pltpu.SMEM)
    shape = jax.ShapeDtypeStruct
    return pl.pallas_call(
        functools.partial(forward_kernel, seq_count),
        out_shape=[
            shape((TOK, D), bf),
            shape((TOK, D), bf),
            shape((2, TOK + 2 * HALF, D), bf),
            shape((TOK, D), bf),
            shape((TOK, D), f32),
        ],
        in_specs=[smem] + [vmem] * 4 + [hbm] * 4,
        out_specs=[vmem] * 5,
        scratch_shapes=[
            pltpu.VMEM((6, D, 512), bf),
            pltpu.VMEM((D, D), bf),
            pltpu.VMEM((TOK, 128), f32),
            pltpu.VMEM((TOK, 128), f32),
            pltpu.VMEM((TOK // 128, 256, 256), f32),
            pltpu.SemaphoreType.DMA((9,)),
            pltpu.SemaphoreType.DMA((2,)),
            pltpu.SemaphoreType.DMA((2,)),
        ],
        compiler_params=pltpu.CompilerParams(
            collective_id=2, has_side_effects=True, vmem_limit_bytes=56 * 2**20
        ),
        name="attention_forward",
    )(lengths, frames, gain[None], bias[None], scale[None], w_qkv, w_out, *tables)


FBLK = 512


def mlp_kernel(
    x_ref, c_ref, branch_ref, gain_ref, bias_ref, scale_attn_ref, scale_mlp_ref, w_gate_up, w_down,
    out_ref, n2_ref, hidden_ref, dgu_ref, dm_ref, db_ref, dmid_ref, vec_ref,
    wg_v, wu_v, wd_v, mlp_v, dn_v, load_sem,
):
    count = FF // FBLK

    def copies(step, slot):
        at = pl.multiple_of(step * FBLK, FBLK)
        return [
            pltpu.make_async_copy(
                w_gate_up.at[:, pl.ds(at, FBLK)], wg_v.at[slot], load_sem.at[slot, 0]
            ),
            pltpu.make_async_copy(
                w_gate_up.at[:, pl.ds(FF + at, FBLK)], wu_v.at[slot], load_sem.at[slot, 1]
            ),
            pltpu.make_async_copy(
                w_down.at[pl.ds(at, FBLK)], wd_v.at[slot], load_sem.at[slot, 2]
            ),
        ]

    for copy in copies(0, 0):
        copy.start()
    middle = x_ref[...].astype(jnp.float32) + scale_attn_ref[...] * branch_ref[...]
    hat, inverse = normalize(middle)
    n2_ref[...] = (hat * gain_ref[...] + bias_ref[...]).astype(jnp.bfloat16)
    dm_ref[...] = (c_ref[...].astype(jnp.float32) * scale_mlp_ref[...]).astype(jnp.bfloat16)
    mlp_v[...] = jnp.zeros_like(mlp_v)
    dn_v[...] = jnp.zeros_like(dn_v)

    def step(number, carry):
        slot = lax.rem(number, 2)

        @pl.when(number + 1 < count)
        def _():
            for copy in copies(number + 1, 1 - slot):
                copy.start()

        for copy in copies(number, slot):
            copy.wait()
        for part in range(FBLK // 256):
            cols = slice(part * 256, part * 256 + 256)
            at = pl.multiple_of(number * FBLK + part * 256, 256)
            gate = dot(n2_ref[...], wg_v[slot, :, cols])
            up = dot(n2_ref[...], wu_v[slot, :, cols])
            dh = contract_back(dm_ref[...], wd_v[slot, cols, :])
            sigmoid = 1.0 / (1.0 + jnp.exp(-gate))
            silu = gate * sigmoid
            hidden_ref[:, pl.ds(at, 256)] = (silu * up).astype(jnp.bfloat16)
            dgate = dh * up * (sigmoid * (1.0 + gate * (1.0 - sigmoid)))
            dgu_ref[:, pl.ds(at, 256)] = dgate.astype(jnp.bfloat16)
            dgu_ref[:, pl.ds(FF + at, 256)] = (dh * silu).astype(jnp.bfloat16)
        at = pl.multiple_of(number * FBLK, FBLK)
        mlp_v[...] += dot(hidden_ref[:, pl.ds(at, FBLK)], wd_v[slot])
        dn_v[...] += contract_back(dgu_ref[:, pl.ds(at, FBLK)], wg_v[slot]) + contract_back(
            dgu_ref[:, pl.ds(FF + at, FBLK)], wu_v[slot]
        )
        return carry

    lax.fori_loop(0, count, step, 0)
    cot = c_ref[...].astype(jnp.float32)
    branch = branch_ref[...]
    middle = x_ref[...].astype(jnp.float32) + scale_attn_ref[...] * branch
    mlp_out = mlp_v[...]
    out_ref[...] = (middle + scale_mlp_ref[...] * mlp_out).astype(jnp.bfloat16)
    vec_ref[0:1] = jnp.sum(cot * mlp_out, 0, keepdims=True)
    hat, inverse = normalize(middle)
    dn = dn_v[...]
    vec_ref[1:2] = jnp.sum(dn * hat, 0, keepdims=True)
    vec_ref[2:3] = jnp.sum(dn, 0, keepdims=True)
    dmid = cot + norm_backward(dn, hat, inverse, gain_ref[...])
    dmid_ref[...] = dmid
    vec_ref[3:4] = jnp.sum(dmid * branch, 0, keepdims=True)
    vec_ref[4:8] = jnp.zeros((4, D), jnp.float32)
    db_ref[...] = (dmid * scale_attn_ref[...]).astype(jnp.bfloat16)


def feed_forward(frames, cotangent, branch, gain, bias, scale_attn, scale_mlp, w_gate_up, w_down):
    bf, f32 = jnp.bfloat16, jnp.float32
    hbm = pl.BlockSpec(memory_space=pl.ANY)
    vmem = pl.BlockSpec(memory_space=pltpu.VMEM)
    shape = jax.ShapeDtypeStruct
    return pl.pallas_call(
        mlp_kernel,
        out_shape=[
            shape((TOK, D), bf),
            shape((TOK, D), bf),
            shape((TOK, FF), bf),
            shape((TOK, 2 * FF), bf),
            shape((TOK, D), bf),
            shape((TOK, D), bf),
            shape((TOK, D), f32),
            shape((8, D), f32),
        ],
        in_specs=[vmem] * 7 + [hbm] * 2,
        out_specs=[vmem] * 8,
        scratch_shapes=[
            pltpu.VMEM((2, D, FBLK), bf),
            pltpu.VMEM((2, D, FBLK), bf),
            pltpu.VMEM((2, FBLK, D), bf),
            pltpu.VMEM((TOK, D), f32),
            pltpu.VMEM((TOK, D), f32),
            pltpu.SemaphoreType.DMA((2, 3)),
        ],
        compiler_params=pltpu.CompilerParams(vmem_limit_bytes=56 * 2**20),
        name="feed_forward",
    )(
        frames, cotangent, branch, gain[None], bias[None], scale_attn[None], scale_mlp[None],
        w_gate_up, w_down,
    )


def backward_kernel(
    seq_count, clip_ref, x_ref, gain_ref, q_ref, kv_ref, db_ref, dmid_ref, w_qkv, w_out,
    cos_all, sin_all,
    dproj_ref, grad_ref, vec_ref,
    wq_v, wo_v, cos_v, sin_v, bias_v, datt_v, dkv_v, edge_v, far_v, load_sem, send_sem, recv_sem,
):
    seq = lax.axis_index("seq")
    rows = pl.ds(pl.multiple_of(seq * TOK, TOK), TOK)
    out_copy = pltpu.make_async_copy(w_out, wo_v, load_sem.at[8])
    tables = [
        pltpu.make_async_copy(cos_all.at[rows], cos_v, load_sem.at[0]),
        pltpu.make_async_copy(sin_all.at[rows], sin_v, load_sem.at[1]),
    ]
    chunks = [
        pltpu.make_async_copy(
            w_qkv.at[:, pl.ds(k * 512, 512)], wq_v.at[k], load_sem.at[2 + k]
        )
        for k in range(6)
    ]
    for copy in [out_copy] + tables + chunks:
        copy.start()
    left, right, has_left, has_right = greet_sides(seq_count)
    window_bias(bias_v, clip_ref, seq_count * TOK, True)
    out_copy.wait()
    for part in range(4):
        cols = slice(part * 256, part * 256 + 256)
        datt_v[:, cols] = contract_back(db_ref[...], wo_v[cols, :]).astype(jnp.bfloat16)
    for copy in tables:
        copy.wait()
    last = TOK // 128 - 1

    def attend(blocks):
        def step(pair, carry):
            lanes = pl.ds(pl.multiple_of(pair * 128, 128), 128)
            for block in blocks:
                own = slice(block * 128, block * 128 + 128)
                window = slice(block * 128, block * 128 + 256)
                queries = stacked(q_ref[own, lanes] * 0.125)
                grads = stacked(datt_v[own, lanes])
                keys = kv_ref[0, window, lanes]
                scores = contract_back(keys, queries) + bias_v[block]
                exponent = jnp.exp(scores - jnp.max(scores, 0, keepdims=True))
                total = jnp.sum(exponent, 0, keepdims=True)
                probs = exponent * (1.0 / total)
                d_probs = contract_back(kv_ref[1, window, lanes], grads)
                inner = jnp.sum(probs * d_probs, 0, keepdims=True)
                d_scores = (probs * (d_probs - inner)).astype(jnp.bfloat16)
                d_keys = dot(d_scores, queries)
                d_values = dot(probs.astype(jnp.bfloat16), grads)
                for which, update in ((0, d_keys), (1, d_values)):
                    if block in (0, last):
                        dkv_v[which, window, lanes] = update
                    elif block == 1:
                        dkv_v[which, 128:256, lanes] += update[:128]
                        dkv_v[which, 256:384, lanes] = update[128:]
                    else:
                        dkv_v[which, window, lanes] += update
                d_queries = merged(tn_dot(d_scores, keys)) * 0.125
                dproj_ref[own, lanes] = rotated(
                    d_queries, cos_v[own, :], -sin_v[own, :]
                ).astype(jnp.bfloat16)
            return carry

        lax.fori_loop(0, D // 128, step, 0)

    attend([0, last])
    edge_v[0] = dkv_v[:, 0:HALF].astype(jnp.bfloat16)
    edge_v[1] = dkv_v[:, HALF + TOK :].astype(jnp.bfloat16)
    to_left = pltpu.make_async_remote_copy(
        src_ref=edge_v.at[0], dst_ref=far_v.at[1],
        send_sem=send_sem.at[0], recv_sem=recv_sem.at[0], device_id=left, device_id_type=MESH,
    )
    to_right = pltpu.make_async_remote_copy(
        src_ref=edge_v.at[1], dst_ref=far_v.at[0],
        send_sem=send_sem.at[1], recv_sem=recv_sem.at[1], device_id=right, device_id_type=MESH,
    )

    @pl.when(has_left)
    def _():
        to_left.start()

    @pl.when(has_right)
    def _():
        to_right.start()

    attend(list(range(1, last)))

    @pl.when(has_left)
    def _():
        to_right.wait_recv()
        dkv_v[:, HALF : 2 * HALF] += far_v[0].astype(jnp.float32)

    @pl.when(has_right)
    def _():
        to_left.wait_recv()
        dkv_v[:, TOK : TOK + HALF] += far_v[1].astype(jnp.float32)

    for k in range(D // 128):
        lanes = slice(k * 128, k * 128 + 128)
        dproj_ref[:, D + k * 128 : D + k * 128 + 128] = rotated(
            dkv_v[0, HALF : HALF + TOK, lanes], cos_v[...], -sin_v[...]
        ).astype(jnp.bfloat16)
        dproj_ref[:, 2 * D + k * 128 : 2 * D + k * 128 + 128] = dkv_v[
            1, HALF : HALF + TOK, lanes
        ].astype(jnp.bfloat16)
    for copy in chunks:
        copy.wait()
    dn = contract_back(dproj_ref[:, 0:512], wq_v[0])
    for k in range(1, 6):
        dn += contract_back(dproj_ref[:, k * 512 : k * 512 + 512], wq_v[k])
    hat, inverse = normalize(x_ref[...].astype(jnp.float32))
    vec_ref[0:1] = jnp.sum(dn * hat, 0, keepdims=True)
    vec_ref[1:2] = jnp.sum(dn, 0, keepdims=True)
    vec_ref[2:8] = jnp.zeros((6, D), jnp.float32)
    grad_ref[...] = dmid_ref[...] + norm_backward(dn, hat, inverse, gain_ref[...])

    @pl.when(has_left)
    def _():
        to_left.wait_send()

    @pl.when(has_right)
    def _():
        to_right.wait_send()


def backward_attention(
    frames, lengths, gain, queries, kv, db, dmid, w_qkv, w_out, tables, seq_count
):
    bf, f32 = jnp.bfloat16, jnp.float32
    hbm = pl.BlockSpec(memory_space=pl.ANY)
    vmem = pl.BlockSpec(memory_space=pltpu.VMEM)
    smem = pl.BlockSpec(memory_space=pltpu.SMEM)
    shape = jax.ShapeDtypeStruct
    ext = TOK + 2 * HALF
    return pl.pallas_call(
        functools.partial(backward_kernel, seq_count),
        out_shape=[shape((TOK, 3 * D), bf), shape((TOK, D), f32), shape((8, D), f32)],
        in_specs=[smem] + [vmem] * 6 + [hbm] * 4,
        out_specs=[vmem] * 3,
        scratch_shapes=[
            pltpu.VMEM((6, D, 512), bf),
            pltpu.VMEM((D, D), bf),
            pltpu.VMEM((TOK, 128), f32),
            pltpu.VMEM((TOK, 128), f32),
            pltpu.VMEM((TOK // 128, 256, 256), f32),
            pltpu.VMEM((TOK, D), bf),
            pltpu.VMEM((2, ext, D), f32),
            pltpu.VMEM((2, 2, HALF, D), bf),
            pltpu.VMEM((2, 2, HALF, D), bf),
            pltpu.SemaphoreType.DMA((9,)),
            pltpu.SemaphoreType.DMA((2,)),
            pltpu.SemaphoreType.DMA((2,)),
        ],
        compiler_params=pltpu.CompilerParams(
            collective_id=3, has_side_effects=True, vmem_limit_bytes=56 * 2**20
        ),
        name="attention_backward",
    )(lengths, frames, gain[None], queries, kv, db, dmid, w_qkv, w_out, *tables)


RING = 8
COUNT = len(UNITS)


def parts_of(unit):
    late = isinstance(unit, int) and unit >= COUNT - LAST_UNITS
    return LAST_PARTS if late else PARTS


def stacked_heads(block, heads):
    lane = lax.broadcasted_iota(jnp.int32, block.shape, 1) // HEAD_DIM
    zero = jnp.zeros_like(block)
    return jnp.concatenate([jnp.where(lane == h, block, zero) for h in range(heads)], 0)


def merged_heads(rows, heads):
    lane = lax.broadcasted_iota(jnp.int32, (128, rows.shape[1]), 1) // HEAD_DIM
    total = rows[:128]
    for h in range(1, heads):
        total = jnp.where(lane == h, rows[128 * h : 128 * h + 128], total)
    return total


def layer_kernel(
    clip_ref, x_hbm, c_hbm, gain1_ref, bias1_ref, gain2_ref, bias2_ref, scale_attn_ref, scale_mlp_ref,
    w_qkv, w_out, w_gate_up, w_down, cos_all, sin_all,
    out_hbm, grad_hbm, out0, out1, out2, out3, vec_out, att_hbm, normed_hbm, far_att, far_normed, hid_hbm, far_hid,
    part_a, part_b, part_c,
    recv_a1, recv_a2, recv_az, recv_b1, recv_b2, recv_bz, recv_cz, recv_c1, recv_c2,
    wide_v, deep_v, dkv_v, xbuf, ybuf, yfar, ydown, yout, other_v, hid_v,
    dm_v, x_v, c_v, grad_v, q_v, kv_v, dproj_v, bias_v, cos_v, sin_v, far_v,
    vec_sum, vec_recv, vec_z,
    send_sem, recv_sem, load_sem, far_send, far_recv, w_sem, hid_sem, hid_send, hid_recv,
    oth_send, oth_recv, q_send, q_recv, x_sem, edge_send, edge_recv, vec_send, vec_rsem, out_sem, halo_send, halo_recv,
):
    outs = (out0, out1, out2, out3)
    dp = lax.axis_index("dp")
    seq = lax.axis_index("seq")
    z, y = dp // 2, dp % 2
    x, c = seq // 2, seq % 2
    dev_c = (dp, x * 2 + 1 - c)
    dev_x = (dp, (1 - x) * 2 + c)
    dev_y = (z * 2 + 1 - y, seq)
    dev_d = (dp, (1 - x) * 2 + 1 - c)
    dev_z = [(lax.rem(z + k, 4) * 2 + y, seq) for k in (1, 2, 3)]
    bf, f32 = jnp.bfloat16, jnp.float32

    def local_copy(src, dst, sem):
        return pltpu.make_async_copy(src, dst, sem)

    def remote(src, dst, ssem, rsem, device):
        return pltpu.make_async_remote_copy(
            src_ref=src, dst_ref=dst, send_sem=ssem, recv_sem=rsem,
            device_id=device, device_id_type=MESH,
        )

    def weights(step, slot):
        result = []
        for i in range(2):
            at = pl.multiple_of((c if i == 0 else 1 - c) * (FF // 2) + step * 256, 256)
            result += [
                local_copy(
                    w_gate_up.at[:, pl.ds(at, 256)], wide_v.at[4 * slot + i], w_sem.at[slot, i]
                ),
                local_copy(
                    w_gate_up.at[:, pl.ds(FF + at, 256)], wide_v.at[4 * slot + 2 + i],
                    w_sem.at[slot, 2 + i],
                ),
                local_copy(
                    w_down.at[pl.ds(at, 256)], deep_v.at[slot, pl.ds(256 * i, 256)],
                    w_sem.at[slot, 4 + i],
                ),
            ]
        return result

    rows = pl.ds(pl.multiple_of(seq * TOK, TOK), TOK)
    x_copy = local_copy(x_hbm, x_v, load_sem.at[0])
    c_copy = local_copy(c_hbm, c_v, load_sem.at[1])
    tables = [
        local_copy(cos_all.at[rows], cos_v, load_sem.at[2]),
        local_copy(sin_all.at[rows], sin_v, load_sem.at[3]),
    ]
    wo_first = [
        local_copy(
            w_out.at[pl.ds(512 * k, 512)], dproj_v.at[:, pl.ds(D * k, D)], load_sem.at[4 + k]
        )
        for k in range(2)
    ]
    wq_copies = [
        local_copy(w_qkv.at[:, pl.ds(256 * k, 256)], wide_v.at[k % 8], w_sem.at[k % 8 // 4, k % 4])
        for k in range(12)
    ]
    wq_first = {
        k: local_copy(
            w_qkv.at[:, pl.ds(256 * k, 256)], wide_v.at[k - 4 if k >= 4 else k],
            w_sem.at[k // 8, k % 4],
        )
        for k in [4, 5, 6, 7, 8, 9, 10, 11, 0, 1, 2, 3]
    }
    x_copy.start()
    for k in range(4, 8):
        wq_first[k].start()
    for copy in tables:
        copy.start()
    for k in range(8, 12):
        wq_first[k].start()
    for copy in wo_first + [c_copy]:
        copy.start()

    barrier = pltpu.get_barrier_semaphore()
    for device in [dev_c, dev_x, dev_y, dev_d] + dev_z:
        pl.semaphore_signal(barrier, inc=1, device_id=device, device_id_type=MESH)

    is_end = (z == 0) | (z == 3)
    is_mid = (z == 1) | (z == 2)
    end_low = jnp.where(z == 0, 1, 0)
    end_dir = jnp.where(z == 0, 0, 1)
    end_next = (jnp.where(z == 0, 1, 2) * 2 + y, seq)
    mid_dir = jnp.where(z == 1, 0, 1)
    mid_low = jnp.where(z == 1, 1, 0)
    mid_keep = jnp.where(z == 1, 2, 0)
    mid_next = ((3 - z) * 2 + y, seq)
    back_dir = 1 - mid_dir
    back_low = jnp.where(z == 2, 2, 0)
    back_keep = jnp.where(z == 2, 3, 0)
    back_next = (jnp.where(z == 2, 3, 0) * 2 + y, seq)

    def z_send(slot, which, pieces, recv, number):
        ssem, rsem = send_sem.at[slot, which], recv_sem.at[slot, which]
        if number == 0:
            low, size, way, device = end_low, 3, end_dir, end_next
        elif number == 1:
            low, size, way, device = mid_keep, 2, mid_dir, mid_next
        else:
            low, size, way, device = back_keep, 1, back_dir, back_next
        return remote(
            pieces.at[pl.ds(low, size)], recv.at[way, pl.ds(low - 1 + way, size)],
            ssem.at[2 + number // 2], rsem.at[2 + way], device,
        )

    def z_wait(slot, which, recv, way, low, size):
        view = recv.at[way, pl.ds(low - 1 + way, size)]
        local_copy(view, view, recv_sem.at[slot, which, 2 + way]).wait()

    def z_round0(slot, which, pieces, recv):
        @pl.when(is_end)
        def _():
            z_send(slot, which, pieces, recv, 0).start()

    def z_round1(slot, which, pieces, recv):
        @pl.when(is_mid)
        def _():
            z_wait(slot, which, recv, mid_dir, mid_low, 3)
            keep = pl.ds(mid_keep, 2)
            pieces[keep] = pieces[keep] + recv[mid_dir, pl.ds(mid_keep - 1 + mid_dir, 2)]
            z_send(slot, which, pieces, recv, 1).start()

    def z_round2(slot, which, pieces, recv):
        @pl.when(is_mid)
        def _():
            z_wait(slot, which, recv, back_dir, back_low, 2)
            keep = pl.ds(back_keep, 1)
            pieces[keep] = pieces[keep] + recv[back_dir, pl.ds(back_keep - 1 + back_dir, 1)]
            z_send(slot, which, pieces, recv, 2).start()

    def z_final(slot, which, pieces, recv, finish):
        @pl.when(is_end)
        def _():
            way = 1 - end_dir
            z_wait(slot, which, recv, way, z, 1)
            finish(pieces[z].astype(f32) + recv[way, z - 1 + way].astype(f32))

        @pl.when(is_mid)
        def _():
            finish(
                pieces[z].astype(f32) + recv[0, z - 1].astype(f32) + recv[1, z].astype(f32)
            )

    def views(unit):
        slot = unit % RING if isinstance(unit, int) else lax.rem(unit, RING)
        parts = parts_of(unit)
        a, b = pl.ds(0, parts[1]), pl.ds(0, parts[2] - parts[1])
        return (
            slot,
            part_a.at[slot, :, :, :, a], recv_a1.at[slot, :, :, a], recv_a2.at[slot, :, a],
            recv_az.at[slot, :, :, a],
            part_b.at[slot, :, :, :, b], recv_b1.at[slot, :, :, b], recv_b2.at[slot, :, b],
            recv_bz.at[slot, :, :, b],
            part_c.at[slot], recv_c1.at[slot], recv_c2.at[slot], recv_cz.at[slot],
            parts[3] > parts[2],
        )

    def hop(unit, which, index):
        slot, a, a1, a2, _, b, b1, b2, _, cc, c1, c2, _, _ = views(unit)
        source, target, device = {
            (0, 0): lambda: (a.at[1 - x], a1, dev_x),
            (0, 1): lambda: (a.at[x, 1 - y], a2, dev_y),
            (1, 0): lambda: (b.at[1 - y], b1, dev_y),
            (1, 1): lambda: (b.at[y, 1 - x], b2, dev_x),
            (2, 0): lambda: (cc.at[z, 1 - x], c1, dev_x),
            (2, 1): lambda: (cc.at[z, x, 1 - y], c2, dev_y),
        }[which, index]()
        return remote(
            source, target, send_sem.at[slot, which, index], recv_sem.at[slot, which, index], device
        )

    def put(unit, which, block):
        low, high = parts_of(unit)[which : which + 2]
        if not isinstance(unit, int):
            columns = pl.ds(pl.multiple_of(unit * 256, 256), 256)
            out2[low:high, columns] = block
            return
        _, _, _, _, _, offset, out, row = UNITS[unit]
        outs[out][row + low : row + high, offset : offset + 256] = block

    def stage(unit, number):
        slot, a, a1, a2, rz_a, b, b1, b2, rz_b, cc, c1, c2, rz_c, thirds = views(unit)
        a_z, b_z = a.at[x, y], b.at[y, x]
        if number == 0:
            hop(unit, 0, 0).start()
            hop(unit, 1, 0).start()
            if thirds:
                z_round0(slot, 2, cc, rz_c)
        if number == 1:
            hop(unit, 0, 0).wait_recv()
            a[x] = a[x] + a1[...]
            hop(unit, 0, 1).start()
            hop(unit, 1, 0).wait_recv()
            b[y] = b[y] + b1[...]
            hop(unit, 1, 1).start()
            if thirds:
                z_round1(slot, 2, cc, rz_c)
        if number == 2:
            hop(unit, 0, 1).wait_recv()
            a[x, y] = a[x, y] + a2[...]
            z_round0(slot, 0, a_z, rz_a)
            hop(unit, 1, 1).wait_recv()
            b[y, x] = b[y, x] + b2[...]
            z_round0(slot, 1, b_z, rz_b)
            if thirds:
                z_round2(slot, 2, cc, rz_c)
        if number == 3:
            z_round1(slot, 0, a_z, rz_a)
            z_round1(slot, 1, b_z, rz_b)

            def keep(value):
                cc[z] = value.astype(bf)

            if thirds:
                z_final(slot, 2, cc, rz_c, keep)
                hop(unit, 2, 0).start()
        if number == 4:
            z_round2(slot, 0, a_z, rz_a)
            z_round2(slot, 1, b_z, rz_b)
            if thirds:
                hop(unit, 2, 0).wait_recv()
                cc[z, x] = cc[z, x] + c1[...]
                hop(unit, 2, 1).start()
        if number == 5:
            z_final(slot, 0, a_z, rz_a, functools.partial(put, unit, 0))
            z_final(slot, 1, b_z, rz_b, functools.partial(put, unit, 1))
            if thirds:
                hop(unit, 2, 1).wait_recv()
                put(unit, 2, cc[z, x, y].astype(f32) + c2[...].astype(f32))

    def sums(step):
        for number in range(1, 6):
            unit = step - number + 1
            if isinstance(step, int):
                if 0 <= unit < COUNT:
                    stage(unit, number)
            else:

                @pl.when(unit >= 0)
                def _():
                    stage(unit, number)

    def sent(unit):
        slot, a, _, _, rz_a, b, _, _, rz_b, cc, _, _, rz_c, thirds = views(unit)
        whole = [(a.at[x, y], rz_a), (b.at[y, x], rz_b)] + ([(cc, rz_c)] if thirds else [])
        for which, (pieces, recv) in enumerate(whole):
            for index in range(2):
                hop(unit, which, index).wait_send()

            @pl.when(is_end)
            def _():
                z_send(slot, which, pieces, recv, 0).wait_send()

            @pl.when(is_mid)
            def _():
                z_send(slot, which, pieces, recv, 1).wait_send()
                z_send(slot, which, pieces, recv, 2).wait_send()

    def multiply(unit, xslot, own, far):
        slot, parts = views(unit)[0], parts_of(unit)

        def step(i, carry):
            columns = pl.ds(pl.multiple_of(i * 512, 512), 512)
            for xi in range(2):
                total = (
                    tn_dot(xbuf[xslot, 0, :, columns], own(xi))
                    + tn_dot(xbuf[xslot, 1, :, columns], far(xi))
                ).astype(bf)
                for k in range(4):
                    zi, yi = 2 * i + k // 2, k % 2
                    block = total[k * 128 : k * 128 + 128]
                    part_a[slot, xi, yi, zi, : parts[1]] = block[: parts[1]]
                    part_b[slot, yi, xi, zi, : parts[2] - parts[1]] = block[parts[1] : parts[2]]
                    if parts[3] > parts[2]:
                        part_c[slot, zi, xi, yi] = block[parts[2] :]
            return carry

        lax.fori_loop(0, 2, step, 0)

    def far_copy(src, dst, index):
        return remote(src, dst, far_send.at[index], far_recv.at[index], dev_c)

    def pair_columns(array, width, offset, core, xi):
        return array.at[:, pl.ds(pl.multiple_of((2 * xi + core) * width + offset, 256), 256)]

    far_n2 = far_copy(xbuf.at[0, 0], xbuf.at[0, 1], 0)
    far_a = far_copy(xbuf.at[1, 1], far_att, 1)
    far_n = far_copy(xbuf.at[1, 0], far_normed, 2)
    far_dm = [
        far_copy(pair_columns(dm_v, 256, 0, 1 - c, xi), ydown.at[xi], 3 + xi) for xi in range(2)
    ]
    far_db = [
        far_copy(other_v.at[xi, 1 - c], yout.at[xi], 5 + xi) for xi in range(2)
    ]
    far_dq = [
        remote(
            pair_columns(dproj_v, 768, 256 * v, 1 - c, xi), yfar.at[v, xi],
            q_send.at[v, xi], q_recv.at[v, xi], dev_c,
        )
        for v in range(3)
        for xi in range(2)
    ]

    def far_other(step):
        return remote(
            other_v.at[lax.rem(step, 2)], yfar.at[lax.rem(step, 4)],
            oth_send.at[lax.rem(step, 2)], oth_recv.at[lax.rem(step, 4)], dev_c,
        )

    def hidden_copies(step):
        slot = lax.rem(step, 2)
        result = []
        for i in range(2):
            at = pl.multiple_of((c if i == 0 else 1 - c) * (FF // 2) + step * 256, 256)
            block = hid_v.at[slot, :, pl.ds(256 * i, 256)]
            result.append(local_copy(block, hid_hbm.at[:, pl.ds(at, 256)], hid_sem.at[slot, i]))
            result.append(
                remote(
                    block, far_hid.at[:, pl.ds(at, 256)],
                    hid_send.at[slot, i], hid_recv.at[step, i], dev_c,
                )
            )
        return result

    window_bias(bias_v, clip_ref, 4 * TOK, True)
    vec_sum[0] = jnp.zeros((8, D), f32)
    x_copy.wait()

    def first_norm(i, carry):
        at = pl.ds(pl.multiple_of(i * 128, 128), 128)
        hat, _ = normalize(x_v[at, :].astype(f32))
        xbuf[1, 0, at, :] = (hat * gain1_ref[...] + bias1_ref[...]).astype(bf)
        return carry

    lax.fori_loop(0, TOK // 128, first_norm, 0)
    normed_copy = local_copy(xbuf.at[1, 0], normed_hbm, out_sem.at[2])
    att_copy = local_copy(xbuf.at[1, 1], att_hbm, out_sem.at[3])
    normed_copy.start()
    for copy in tables:
        copy.wait()

    def project(k):
        full = dot(xbuf[1, 0], wide_v[k - 4 if k >= 4 else k])
        for half in range(2):
            block = full[:, half * 128 : half * 128 + 128]
            at = (k % 4) * 256 + half * 128
            if k < 8:
                block = rotated(block, cos_v[...], sin_v[...])
            block = block.astype(bf)
            if k < 4:
                q_v[:, at : at + 128] = block
            else:
                kv_v[k // 4 - 1, HALF : HALF + TOK, at : at + 128] = block

    def project_all(chunks):
        for k in chunks:
            wq_first[k].wait()
        for k in chunks:
            project(k)

    project_all(range(4, 8))
    for k in range(4):
        wq_first[k].start()
    project_all(range(8, 12))
    pl.semaphore_wait(barrier, 7)
    has_left, has_right = seq > 0, seq < 3
    halo_left = remote(
        kv_v.at[:, pl.ds(HALF, HALF)], kv_v.at[:, pl.ds(HALF + TOK, HALF)],
        halo_send.at[0], halo_recv.at[0], (dp, seq - 1),
    )
    halo_right = remote(
        kv_v.at[:, pl.ds(TOK, HALF)], kv_v.at[:, pl.ds(0, HALF)],
        halo_send.at[1], halo_recv.at[1], (dp, seq + 1),
    )

    @pl.when(has_left)
    def _():
        halo_left.start()

    @pl.when(has_right)
    def _():
        halo_right.start()

    @pl.when(jnp.logical_not(has_left))
    def _():
        kv_v[:, 0:HALF] = jnp.zeros((2, HALF, D), bf)

    @pl.when(jnp.logical_not(has_right))
    def _():
        kv_v[:, HALF + TOK :] = jnp.zeros((2, HALF, D), bf)

    far_n.start()
    project_all(range(4))
    for copy in weights(0, 0) + weights(1, 1):
        copy.start()
    last = TOK // 128 - 1
    heads = 4
    lanes_of = heads * HEAD_DIM

    def attend_forward(blocks):
        def step(group, carry):
            lanes = pl.ds(pl.multiple_of(group * lanes_of, lanes_of), lanes_of)
            scores = []
            for block in blocks:
                queries = q_v[block * 128 : block * 128 + 128, lanes] * 0.125
                keys = kv_v[0, block * 128 : block * 128 + 256, lanes]
                bias = jnp.concatenate([bias_v[block]] * (heads // 2), 1)
                scores.append(contract_back(keys, stacked_heads(queries, heads)) + bias)
            probs = []
            for score in scores:
                exponent = jnp.exp(score - jnp.max(score, 0, keepdims=True))
                total = jnp.sum(exponent, 0, keepdims=True)
                probs.append((exponent * (1.0 / total)).astype(bf))
            for block, prob in zip(blocks, probs):
                values = kv_v[1, block * 128 : block * 128 + 256, lanes]
                xbuf[1, 1, block * 128 : block * 128 + 128, lanes] = merged_heads(
                    tn_dot(prob, values), heads
                ).astype(bf)
            return carry

        lax.fori_loop(0, D // lanes_of, step, 0)

    attend_forward(list(range(1, last)))
    c_copy.wait()

    def scaled(i, carry):
        at = pl.ds(pl.multiple_of(i * 128, 128), 128)
        dm_v[at, :] = (c_v[at, :].astype(f32) * scale_mlp_ref[...]).astype(bf)
        return carry

    lax.fori_loop(0, TOK // 128, scaled, 0)
    for copy in far_dm:
        copy.start()
    dkv_v[...] = jnp.zeros_like(dkv_v)

    @pl.when(has_left)
    def _():
        halo_right.wait_recv()

    @pl.when(has_right)
    def _():
        halo_left.wait_recv()

    attend_forward([0, last])
    att_copy.start()
    far_a.start()
    for copy in wo_first:
        copy.wait()
    for part in range(4):
        cols = slice(part * 256, part * 256 + 256)
        grad_v[:, cols] = dot(xbuf[1, 1, :, 0:512], dproj_v[:, cols]) + dot(
            xbuf[1, 1, :, 512:1024], dproj_v[:, D + part * 256 : D + part * 256 + 256]
        )


    def before(i, carry):
        at = pl.ds(pl.multiple_of(i * 128, 128), 128)
        middle = x_v[at, :].astype(f32) + scale_attn_ref[...] * grad_v[at, :]
        hat, _ = normalize(middle)
        xbuf[0, 0, at, :] = (hat * gain2_ref[...] + bias2_ref[...]).astype(bf)
        return carry

    lax.fori_loop(0, TOK // 128, before, 0)
    far_n2.start()

    def mlp(step):
        slot = lax.rem(step, 2)

        @pl.when(step >= 2)
        def _():
            far_other(step - 2).wait_send()
            for copy in hidden_copies(step - 2)[0::2]:
                copy.wait()
            for copy in hidden_copies(step - 2)[1::2]:
                copy.wait_send()

        for copy in weights(step, slot):
            copy.wait()
        normed = xbuf.at[0, 0]
        for i in range(2):
            gate = dot(normed[...], wide_v[4 * slot + i])
            up = dot(normed[...], wide_v[4 * slot + 2 + i])
            dh = contract_back(dm_v[...], deep_v[slot, 256 * i : 256 * i + 256])
            sigmoid = 1.0 / (1.0 + jnp.exp(-gate))
            silu = gate * sigmoid
            hid_v[slot, :, 256 * i : 256 * i + 256] = (silu * up).astype(bf)
            target = ybuf if i == 0 else other_v
            dgate = dh * up * (sigmoid * (1.0 + gate * (1.0 - sigmoid)))
            target[slot, 0] = dgate.astype(bf)
            target[slot, 1] = (dh * silu).astype(bf)
        far_other(step).start()
        for copy in hidden_copies(step):
            copy.start()
        dkv_v[0, 0:TOK] += dot(hid_v[slot], deep_v[slot])
        dkv_v[1, 0:TOK] += (
            contract_back(ybuf[slot, 0], wide_v[4 * slot])
            + contract_back(other_v[slot, 0], wide_v[4 * slot + 1])
            + contract_back(ybuf[slot, 1], wide_v[4 * slot + 2])
            + contract_back(other_v[slot, 1], wide_v[4 * slot + 3])
        )

        @pl.when(step + 2 < 8)
        def _():
            for copy in weights(step + 2, slot):
                copy.start()

    def gate_unit(step):
        far_other(step).wait_recv()
        multiply(
            step, 0, lambda xi: ybuf[lax.rem(step, 2), xi], lambda xi: yfar[lax.rem(step, 4), xi]
        )
        stage(step, 0)

    def mlp_step(step, carry):
        mlp(step)

        @pl.when(step == 0)
        def _():
            far_n2.wait_recv()

        @pl.when(step >= BEHIND)
        def _():
            sums(step - BEHIND)

        gate_unit(step)

        return carry

    lax.fori_loop(0, 8, mlp_step, 0)

    wo_copies = [
        local_copy(w_out.at[pl.ds(512 * k, 512)], deep_v.at[k], w_sem.at[k, 4]) for k in range(2)
    ]
    for copy in wo_copies + wq_copies[:8]:
        copy.start()
    for step in (6, 7):
        far_other(step).wait_send()
        for copy in hidden_copies(step)[0::2]:
            copy.wait()
        for copy in hidden_copies(step)[1::2]:
            copy.wait_send()
    for step in range(8):
        for copy in hidden_copies(step)[1::2]:
            copy.wait_recv()

    def load_left(unit):
        left, offset, width, _, _, _, _, _ = UNITS[unit]
        slot = {8: 1, 9: 0, 10: 1, 11: 0, 12: 1, 13: 0}[unit]
        arrays = {3: (hid_hbm, far_hid), 1: (att_hbm, far_att), 0: (normed_hbm, far_normed)}[left]
        result = []
        for side in range(2):
            if width == 128:
                result.append(
                    local_copy(arrays[side], xbuf.at[slot, side], x_sem.at[slot, side, 0])
                )
                continue
            for block in range(8):
                result.append(
                    local_copy(
                        arrays[side].at[:, pl.ds(block * width + offset, 128)],
                        xbuf.at[slot, side, :, pl.ds(block * 128, 128)],
                        x_sem.at[slot, side, block],
                    )
                )
        return result

    def unit_sum(unit):
        if unit <= 13:
            for copy in load_left(unit):
                copy.wait()
        _, _, _, right, width, offset, _, _ = UNITS[unit]
        if unit >= RING:
            sent(unit - RING)
        xslot = {8: 1, 9: 0, 10: 1, 11: 0, 12: 1}.get(unit, 0)
        if right == 1:
            own = lambda xi: other_v[xi, c]
        else:
            own = lambda xi: pair_columns({3: dm_v, 0: dproj_v}[right], width, offset, c, xi)[...]
        far = {3: ydown, 1: yout}.get(right, yfar.at[max(unit - 13, 0)])
        multiply(
            unit, xslot,
            own,
            lambda xi: far[xi],
        )
        stage(unit, 0)
        if unit + 2 <= 13:
            if unit + 2 == 12:
                far_a.wait_recv()
            if unit + 2 == 13:
                far_n.wait_recv()
            for copy in load_left(unit + 2):
                copy.start()

    for copy in [far_n2, far_a, far_n] + far_dm:
        copy.wait_send()
    normed_copy.wait()
    att_copy.wait()
    for copy in load_left(8):
        copy.start()
    for copy in load_left(9):
        copy.start()
    for copy in far_dm:
        copy.wait_recv()

    def after(i, carry):
        at = pl.ds(pl.multiple_of(i * 128, 128), 128)
        cot = c_v[at, :].astype(f32)
        branch = grad_v[at, :]
        middle = x_v[at, :].astype(f32) + scale_attn_ref[...] * branch
        mlp_out = dkv_v[0, at, :]
        dn = dkv_v[1, at, :]
        vec_sum[0, 5:6] += jnp.sum(cot * mlp_out, 0, keepdims=True)
        c_v[at, :] = (middle + scale_mlp_ref[...] * mlp_out).astype(bf)
        hat, inverse = normalize(middle)
        vec_sum[0, 3:4] += jnp.sum(dn * hat, 0, keepdims=True)
        vec_sum[0, 4:5] += jnp.sum(dn, 0, keepdims=True)
        dmid = cot + norm_backward(dn, hat, inverse, gain2_ref[...])
        vec_sum[0, 2:3] += jnp.sum(dmid * branch, 0, keepdims=True)
        grad_v[at, :] = dmid
        branch_grad = (dmid * scale_attn_ref[...]).astype(bf)
        for k in range(4):
            other_v[k // 2, k % 2, at, :] = branch_grad[:, 256 * k : 256 * k + 256]
        return carry

    out_copy = local_copy(c_v, out_hbm, out_sem.at[0])
    grad_copy = local_copy(grad_v, grad_hbm, out_sem.at[1])

    def norm_two_back():
        lax.fori_loop(0, TOK // 128, after, 0)
        out_copy.start()
        for copy in far_db:
            copy.start()

    def attended_grads():
        for k in range(2):
            wo_copies[k].wait()
        out_copy.wait()
        for k in range(2):
            total = None
            for j in range(4):
                term = contract_back(other_v[j // 2, j % 2], deep_v[k, :, 256 * j : 256 * j + 256])
                total = term if total is None else total + term
            c_v[:, 512 * k : 512 * k + 512] = total.astype(bf)
        for copy in far_db:
            copy.wait_recv()

    def attend(blocks):
        def step(group, carry):
            lanes = pl.ds(pl.multiple_of(group * lanes_of, lanes_of), lanes_of)
            held = []
            for block in blocks:
                own = slice(block * 128, block * 128 + 128)
                window = slice(block * 128, block * 128 + 256)
                queries = stacked_heads(q_v[own, lanes] * 0.125, heads)
                grads = stacked_heads(c_v[own, lanes], heads)
                keys = kv_v[0, window, lanes]
                bias = jnp.concatenate([bias_v[block]] * (heads // 2), 1)
                scores = contract_back(keys, queries) + bias
                d_probs = contract_back(kv_v[1, window, lanes], grads)
                held.append((queries, grads, keys, scores, d_probs))
            ready = []
            for queries, grads, keys, scores, d_probs in held:
                exponent = jnp.exp(scores - jnp.max(scores, 0, keepdims=True))
                probs = exponent * (1.0 / jnp.sum(exponent, 0, keepdims=True))
                inner = jnp.sum(probs * d_probs, 0, keepdims=True)
                d_scores = (probs * (d_probs - inner)).astype(bf)
                ready.append((queries, grads, keys, d_scores, probs.astype(bf)))
            for block, (queries, grads, keys, d_scores, probs) in zip(blocks, ready):
                own = slice(block * 128, block * 128 + 128)
                window = slice(block * 128, block * 128 + 256)
                for which, update in ((0, dot(d_scores, queries)), (1, dot(probs, grads))):
                    if block in (0, last):
                        dkv_v[which, window, lanes] = update
                    elif block == 1:
                        dkv_v[which, 128:256, lanes] += update[:128]
                        dkv_v[which, 256:384, lanes] = update[128:]
                    else:
                        dkv_v[which, window, lanes] += update
                d_queries = merged_heads(tn_dot(d_scores, keys), heads) * 0.125
                for k in range(lanes_of // 128):
                    at = pl.ds(pl.multiple_of(group * lanes_of + 128 * k, 128), 128)
                    dproj_v[own, at] = rotated(
                        d_queries[:, 128 * k : 128 * k + 128], cos_v[own, :], -sin_v[own, :]
                    ).astype(bf)
            return carry

        lax.fori_loop(0, D // lanes_of, step, 0)

    to_left = remote(
        hid_v.at[0, pl.ds(0, 256)], far_v.at[1], edge_send.at[0], edge_recv.at[0], (dp, seq - 1)
    )
    to_right = remote(
        hid_v.at[1, pl.ds(0, 256)], far_v.at[0], edge_send.at[1], edge_recv.at[1], (dp, seq + 1)
    )

    def edges_out():
        for side, first in ((0, 0), (1, HALF + TOK)):
            for k in range(4):
                hid_v[side, 64 * k : 64 * k + 64] = dkv_v[
                    k // 2, first : first + HALF, 512 * (k % 2) : 512 * (k % 2) + 512
                ].astype(bf)

        @pl.when(has_left)
        def _():
            to_left.start()

        @pl.when(has_right)
        def _():
            to_right.start()

    def edges_in():
        @pl.when(has_left)
        def _():
            to_right.wait_recv()
            for k in range(4):
                dkv_v[k // 2, HALF : 2 * HALF, 512 * (k % 2) : 512 * (k % 2) + 512] += far_v[
                    0, 64 * k : 64 * k + 64
                ].astype(f32)

        @pl.when(has_right)
        def _():
            to_left.wait_recv()
            for k in range(4):
                dkv_v[k // 2, TOK : TOK + HALF, 512 * (k % 2) : 512 * (k % 2) + 512] += far_v[
                    1, 64 * k : 64 * k + 64
                ].astype(f32)

        for k in range(D // 128):
            lanes = slice(k * 128, k * 128 + 128)
            dproj_v[:, D + k * 128 : D + k * 128 + 128] = rotated(
                dkv_v[0, HALF : HALF + TOK, lanes], cos_v[...], -sin_v[...]
            ).astype(bf)
            dproj_v[:, 2 * D + k * 128 : 2 * D + k * 128 + 128] = dkv_v[
                1, HALF : HALF + TOK, lanes
            ].astype(bf)
        for copy in far_dq:
            copy.start()

    def project_back(chunks, fresh):
        for k in chunks:
            wq_copies[k].wait()
        total = None
        for k in chunks:
            term = contract_back(dproj_v[:, 256 * k : 256 * k + 256], wide_v[k % 8])
            total = term if total is None else total + term
        if fresh:
            dkv_v[0, 0:TOK] = total
        else:
            dkv_v[0, 0:TOK] += total

    def last_norm(i, carry):
        at = pl.ds(pl.multiple_of(i * 128, 128), 128)
        hat, inverse = normalize(x_v[at, :].astype(f32))
        dn = dkv_v[0, at, :]
        vec_sum[0, 0:1] += jnp.sum(dn * hat, 0, keepdims=True)
        vec_sum[0, 1:2] += jnp.sum(dn, 0, keepdims=True)
        grad_v[at, :] += norm_backward(dn, hat, inverse, gain1_ref[...])
        return carry

    def norm_one_back():
        lax.fori_loop(0, TOK // 128, last_norm, 0)
        grad_copy.start()

    def vec_copy(number):
        return remote(
            vec_sum.at[number], vec_recv.at[number], vec_send.at[number], vec_rsem.at[number],
            (dev_c, dev_x, dev_y)[number],
        )

    vec_planes = [
        remote(vec_sum.at[3], vec_z.at[z], vec_send.at[3 + k], vec_rsem.at[3 + k], dev_z[k])
        for k in range(3)
    ]

    def vectors(number):
        if 0 < number <= 3:
            vec_copy(number - 1).wait_recv()
            vec_sum[number] = vec_sum[number - 1] + vec_recv[number - 1]
        if number < 3:
            vec_copy(number).start()
        elif number == 3:
            vec_z[z] = vec_sum[3]
            for copy in vec_planes:
                copy.start()
        else:
            for k in range(3):
                view = vec_z.at[lax.rem(z + 3 - k, 4)]
                local_copy(view, view, vec_rsem.at[3 + k]).wait()
            vec_out[...] = vec_z[0] + vec_z[1] + vec_z[2] + vec_z[3]

    def start_wq():
        for copy in wq_copies[8:]:
            copy.start()

    def far_dq_wait():
        for copy in far_dq:
            copy.wait_recv()

    actions = {
        "E": norm_two_back,
        "D": attended_grads,
        "A0": lambda: attend([0, last]),
        "O": edges_out,
        "A1": lambda: attend(list(range(1, last))),
        "I": edges_in,
        "W0": lambda: (project_back(range(8), True), start_wq()),
        "W1": lambda: project_back(range(8, 12), False),
        "N": norm_one_back,
        "Q": far_dq_wait,
    }
    for word in " ".join(ORDER).split():
        if word in actions:
            actions[word]()
        elif word[0] == "P":
            unit_sum(int(word[1:]))
        elif word[0] == "S":
            sums(int(word[1:]))
        elif word[0] == "V":
            vectors(int(word[1:]))

    for unit in range(COUNT - RING, COUNT):
        sent(unit)
    for copy in far_db + far_dq + [vec_copy(k) for k in range(3)] + vec_planes:
        copy.wait_send()

    @pl.when(has_left)
    def _():
        halo_left.wait_send()
        to_left.wait_send()

    @pl.when(has_right)
    def _():
        halo_right.wait_send()
        to_right.wait_send()

    grad_copy.wait()


BEHIND = 2
ORDER = (
    "P8 P9 E S6",
    "P10 D A0 O",
    "S7 P11 A1 S8",
    "P12 I Q S9",
    "P13 W0 S10 P14",
    "W1 N S11 P15",
    "V0 S12 V1 S13",
    "V2 S14 V3 S15",
    "V4 S16 S17 S18",
    "S19",
)


def layer(
    lengths, frames, cotangent, vectors, w_qkv, w_out, w_gate_up, w_down, tables,
):
    bf, f32 = jnp.bfloat16, jnp.float32
    hbm = pl.BlockSpec(memory_space=pl.ANY)
    vmem = pl.BlockSpec(memory_space=pltpu.VMEM)
    smem = pl.BlockSpec(memory_space=pltpu.SMEM)
    shape = jax.ShapeDtypeStruct
    size = (LAST_PARTS[1], LAST_PARTS[2] - LAST_PARTS[1], PARTS[3] - PARTS[2])
    dma = pltpu.SemaphoreType.DMA
    ext = TOK + 2 * HALF
    scratch = [
        pltpu.VMEM((RING, 2, 2, 4, size[0], 256), bf),
        pltpu.VMEM((RING, 2, 2, 4, size[1], 256), bf),
        pltpu.VMEM((RING, 4, 2, 2, size[2], 256), bf),
        pltpu.VMEM((RING, 2, 4, size[0], 256), bf),
        pltpu.VMEM((RING, 4, size[0], 256), bf),
        pltpu.VMEM((RING, 2, 3, size[0], 256), bf),
        pltpu.VMEM((RING, 2, 4, size[1], 256), bf),
        pltpu.VMEM((RING, 4, size[1], 256), bf),
        pltpu.VMEM((RING, 2, 3, size[1], 256), bf),
        pltpu.VMEM((RING, 2, 3, 2, 2, size[2], 256), bf),
        pltpu.VMEM((RING, 2, size[2], 256), bf),
        pltpu.VMEM((RING, size[2], 256), bf),
        pltpu.VMEM((8, D, 256), bf),
        pltpu.VMEM((2, 512, D), bf),
        pltpu.VMEM((2, ext, D), f32),
        pltpu.VMEM((2, 2, TOK, D), bf),
        pltpu.VMEM((2, 2, TOK, 256), bf),
        pltpu.VMEM((4, 2, TOK, 256), bf),
        pltpu.VMEM((2, TOK, 256), bf),
        pltpu.VMEM((2, TOK, 256), bf),
        pltpu.VMEM((2, 2, TOK, 256), bf),
        pltpu.VMEM((2, TOK, 512), bf),
        pltpu.VMEM((TOK, D), bf),
        pltpu.VMEM((TOK, D), bf),
        pltpu.VMEM((TOK, D), bf),
        pltpu.VMEM((TOK, D), f32),
        pltpu.VMEM((TOK, D), bf),
        pltpu.VMEM((2, ext, D), bf),
        pltpu.VMEM((TOK, 3 * D), bf),
        pltpu.VMEM((TOK // 128, 256, 256), f32),
        pltpu.VMEM((TOK, 128), f32),
        pltpu.VMEM((TOK, 128), f32),
        pltpu.VMEM((2, 256, 512), bf),
        pltpu.VMEM((4, 8, D), f32),
        pltpu.VMEM((3, 8, D), f32),
        pltpu.VMEM((4, 8, D), f32),
        dma((RING, 3, 4)),
        dma((RING, 3, 4)),
        dma((7,)),
        dma((7,)),
        dma((7,)),
        dma((2, 6)),
        dma((2, 2)),
        dma((2, 2)),
        dma((8, 2)),
        dma((2,)),
        dma((4,)),
        dma((3, 2)),
        dma((3, 2)),
        dma((2, 2, 8)),
        dma((2,)),
        dma((2,)),
        dma((6,)),
        dma((6,)),
        dma((4,)),
        dma((2,)),
        dma((2,)),
    ]
    results = pl.pallas_call(
        layer_kernel,
        out_shape=[
            shape((TOK, D), bf),
            shape((TOK, D), f32),
            shape((128, 768), f32),
            shape((128, 256), f32),
            shape((128, 2048), f32),
            shape((512, 256), f32),
            shape((8, D), f32),
        ]
        + [shape((TOK, D), bf)] * 4
        + [
            shape((TOK, FF), bf),
            shape((TOK, FF), bf),
        ],
        in_specs=[smem] + [hbm] * 2 + [vmem] * 6 + [hbm] * 6,
        out_specs=[hbm] * 2 + [vmem] * 5 + [hbm] * 6,
        scratch_shapes=scratch,
        compiler_params=pltpu.CompilerParams(
            collective_id=4, has_side_effects=True, vmem_limit_bytes=64 * 2**20 - 2**16
        ),
        name="layer",
    )(
        lengths, frames, cotangent, *[v[None] for v in vectors], w_qkv, w_out, w_gate_up, w_down, *tables,
    )[:7]
    finished = pl.pallas_call(
        finish_kernel,
        out_shape=[shape(v.shape, v.dtype) for v in results[:6]] + [shape((1, D), f32)] * 6,
        in_specs=[hbm] * 6 + [vmem],
        out_specs=[hbm] * 6 + [vmem] * 6,
        scratch_shapes=[pltpu.VMEM(v.shape, v.dtype) for v in results[:6]] + [dma((2, 6))],
        compiler_params=pltpu.CompilerParams(vmem_limit_bytes=64 * 2**20 - 2**16),
        name="finish",
    )(*results)
    return finished[:6], [v[0] for v in finished[6:]]


def finish_kernel(*refs):
    sources, targets, held, sems = refs[:6], refs[7:13], refs[19:25], refs[25]
    arrivals = [
        pltpu.make_async_copy(source, target, sems.at[0, k])
        for k, (source, target) in enumerate(zip(sources, held))
    ]
    departures = [
        pltpu.make_async_copy(source, target, sems.at[1, k])
        for k, (source, target) in enumerate(zip(held, targets))
    ]
    for copy in arrivals:
        copy.start()
    for k in range(6):
        refs[13 + k][...] = refs[6][k : k + 1]
    for arrival, departure in zip(arrivals, departures):
        arrival.wait()
        departure.start()
    for copy in departures:
        copy.wait()


def local(
    frames,
    cotangent,
    clip_len,
    ln1_gain,
    ln1_bias,
    w_qkv,
    w_out,
    scale_attn,
    ln2_gain,
    ln2_bias,
    w_gate_up,
    w_down,
    scale_mlp,
):
    row_count = frames.shape[0]
    seq_count = lax.axis_size("seq")
    tables = rotary_tables(row_count * seq_count)
    data_count = lax.axis_size("dp")
    if (data_count, seq_count, row_count) == (8, 4, TOK):
        sums, vector_total = layer(
            clip_len, frames, cotangent,
            (ln1_gain, ln1_bias, ln2_gain, ln2_bias, scale_attn, scale_mlp),
            w_qkv, w_out, w_gate_up, w_down, tables,
        )
        out_frames, input_grad, sum_qkv, sum_out, sum_gate_up, sum_down = sums
    else:
        normed_b, queries, kv, attended_t, branch = forward_attention(
            frames, clip_len, ln1_gain, ln1_bias, scale_attn, w_qkv, w_out, tables, seq_count
        )
        out_frames, normed_two_b, hidden_b, gate_up_b, mlp_grad, branch_grad, middle_grad, vec_two = (
            feed_forward(
                frames, cotangent, branch, ln2_gain, ln2_bias, scale_attn, scale_mlp, w_gate_up, w_down
            )
        )
        projected_grad, input_grad, vec_one = backward_attention(
            frames, clip_len, ln1_gain, queries, kv, branch_grad, middle_grad, w_qkv, w_out, tables,
            seq_count,
        )
        vector_grads = jnp.stack(
            [vec_one[0], vec_one[1], vec_two[3], vec_two[1], vec_two[2], vec_two[0]], 0
        )
        lefts = (normed_b, attended_t, normed_two_b, hidden_b)
        rights = (projected_grad, branch_grad, gate_up_b, mlp_grad)
        vector_total = lax.psum(vector_grads, ("dp", "seq"))
        sum_qkv, sum_out, sum_gate_up, sum_down = [
            lax.psum_scatter(
                to_blocks(contract_rows(left, right), data_count, seq_count),
                ("dp", "seq"),
                scatter_dimension=0,
                tiled=True,
            )[0]
            for left, right in zip(lefts, rights)
        ]
    return (
        out_frames,
        input_grad,
        vector_total[0],
        vector_total[1],
        sum_qkv,
        sum_out,
        vector_total[2],
        vector_total[3],
        vector_total[4],
        sum_gate_up,
        sum_down,
        vector_total[5],
    )


def solution(mesh):
    return jax.shard_map(
        local,
        mesh=mesh,
        in_specs=(
            P(("dp", "seq"), None),
            P(("dp", "seq"), None),
            P("dp", None),
            P(),
            P(),
            P(),
            P(),
            P(),
            P(),
            P(),
            P(),
            P(),
            P(),
        ),
        out_specs=(
            P(("dp", "seq"), None),
            P(("dp", "seq"), None),
            P(),
            P(),
            P("dp", "seq"),
            P("dp", "seq"),
            P(),
            P(),
            P(),
            P("dp", "seq"),
            P("dp", "seq"),
            P(),
        ),
        check_vma=False,
    )
```

```python
import functools

import jax
import jax.numpy as jnp
import numpy as np
from jax import lax
from jax.experimental import pallas as pl
from jax.experimental.pallas import tpu as pltpu
from jax.sharding import PartitionSpec as P

D = 1024
HEADS = 16
HEAD_DIM = 64
FF = 4096
HALF = 64
QBLK = 512


EPS = 1e-05
NEG = -1e30


def contract_rows(left, right):
    return lax.dot_general(
        left, right, (((0,), (0,)), ((), ())), preferred_element_type=jnp.float32
    )


def contract_back(grads, weight):
    return lax.dot_general(
        grads, weight, (((1,), (1,)), ((), ())), preferred_element_type=jnp.float32
    )


def to_blocks(matrix, data_count, seq_count):
    row_total, col_total = matrix.shape
    shaped = matrix.reshape(data_count, row_total // data_count, seq_count, col_total // seq_count)
    return shaped.transpose(0, 2, 1, 3).reshape(
        data_count * seq_count, row_total // data_count, col_total // seq_count
    )


MESH = pl.DeviceIdType.MESH
TOK = 512
PARTS = (0, 48, 96, 128)
LAST_PARTS = (0, 64, 128, 128)
LAST_UNITS = 1

UNITS = (
    [(2, 0, 128, 2, 2048, 256 * v, 2, 0) for v in range(8)]
    + [(3, 128 * v, 512, 3, 256, 0, 3, 128 * v) for v in range(4)]
    + [(1, 0, 128, 1, 256, 0, 1, 0)]
    + [(0, 0, 128, 0, 768, 256 * v, 0, 0) for v in range(3)]
)


def tn_dot(left, right):
    return lax.dot_general(
        left, right, (((0,), (0,)), ((), ())), preferred_element_type=jnp.float32
    )


def rotated(values, cosines, sines):
    lane = lax.broadcasted_iota(jnp.int32, values.shape, 1)
    partner = jnp.where(
        lane % HEAD_DIM < HEAD_DIM // 2,
        pltpu.roll(values, 128 - HEAD_DIM // 2, 1),
        pltpu.roll(values, HEAD_DIM // 2, 1),
    )
    return values * cosines + partner * sines


def head_masks():
    lane = lax.broadcasted_iota(jnp.int32, (128, 128), 1)
    return lane < HEAD_DIM


def stacked(pair):
    first = head_masks()
    zero = jnp.zeros_like(pair)
    return jnp.concatenate([jnp.where(first, pair, zero), jnp.where(first, zero, pair)], 0)


def merged(rows):
    return jnp.where(head_masks(), rows[:128], rows[128:])


def clip_number(positions, ends, group_len):
    total = jnp.zeros_like(positions)
    for end in ends:
        total = total + (positions >= end).astype(jnp.int32)
    return jnp.where((positions >= 0) & (positions < group_len), total, -1)


def normalize(values):
    average = jnp.mean(values, -1, keepdims=True)
    centered = values - average
    inverse = lax.rsqrt(jnp.mean(centered * centered, -1, keepdims=True) + EPS)
    return centered * inverse, inverse


def dot(left, right):
    return jnp.dot(left, right, preferred_element_type=jnp.float32)


def norm_backward(grads, hat, inverse, gain):
    scaled = grads * gain
    return inverse * (
        scaled
        - jnp.mean(scaled, -1, keepdims=True)
        - hat * jnp.mean(scaled * hat, -1, keepdims=True)
    )


def window_bias(bias_ref, clip_ref, group_len, keys_first):
    seq = lax.axis_index("seq")
    first_end = clip_ref[0, 0]
    second_end = first_end + clip_ref[0, 1]
    ends = (first_end, second_end, second_end + clip_ref[0, 2])
    for block in range(TOK // 128):
        start = seq * TOK + block * 128
        shape = (2 * 128, 2 * 128)
        k_axis = 0 if keys_first else 1
        k_at = lax.broadcasted_iota(jnp.int32, shape, k_axis)
        q_at = lax.rem(lax.broadcasted_iota(jnp.int32, shape, 1 - k_axis), 128)
        q_shape = (1, 256) if keys_first else (256, 1)
        k_shape = (256, 1) if keys_first else (1, 256)
        q_ids = clip_number(
            start + lax.rem(lax.broadcasted_iota(jnp.int32, q_shape, 1 - k_axis), 128),
            ends, group_len,
        )
        k_ids = clip_number(
            start - HALF + lax.broadcasted_iota(jnp.int32, k_shape, k_axis), ends, group_len
        )
        seen = (q_ids == k_ids) & (k_at >= q_at) & (k_at < q_at + 2 * HALF)
        bias_ref[block] = jnp.where(seen, 0.0, NEG)


def greet_sides(seq_count):
    dp, seq = lax.axis_index("dp"), lax.axis_index("seq")
    barrier = pltpu.get_barrier_semaphore()
    has_left, has_right = seq > 0, seq < seq_count - 1

    @pl.when(has_left)
    def _():
        pl.semaphore_signal(barrier, inc=1, device_id=(dp, seq - 1), device_id_type=MESH)

    @pl.when(has_right)
    def _():
        pl.semaphore_signal(barrier, inc=1, device_id=(dp, seq + 1), device_id_type=MESH)

    pl.semaphore_wait(barrier, has_left.astype(jnp.int32) + has_right.astype(jnp.int32))

    return (dp, seq - 1), (dp, seq + 1), has_left, has_right


def forward_kernel(
    seq_count, clip_ref, x_ref, gain_ref, gain_bias_ref, scale_ref, w_qkv, w_out, cos_all, sin_all,
    normed_ref, q_ref, kv_ref, att_ref, branch_ref,
    wq_v, wo_v, cos_v, sin_v, bias_v, load_sem, send_sem, recv_sem,
):
    dp, seq = lax.axis_index("dp"), lax.axis_index("seq")
    rows = pl.ds(pl.multiple_of(seq * TOK, TOK), TOK)
    copies = []
    order = [2, 3, 4, 5, 0, 1]
    tables = [
        pltpu.make_async_copy(cos_all.at[rows], cos_v, load_sem.at[0]),
        pltpu.make_async_copy(sin_all.at[rows], sin_v, load_sem.at[1]),
    ]
    chunks = {
        k: pltpu.make_async_copy(
            w_qkv.at[:, pl.ds(k * 512, 512)], wq_v.at[k], load_sem.at[2 + k]
        )
        for k in order
    }
    out_copy = pltpu.make_async_copy(w_out, wo_v, load_sem.at[8])
    for copy in tables + [chunks[k] for k in order] + [out_copy]:
        copy.start()
    left, right, has_left, has_right = greet_sides(seq_count)

    hat, _ = normalize(x_ref[...].astype(jnp.float32))
    normed_ref[...] = (hat * gain_ref[...] + gain_bias_ref[...]).astype(jnp.bfloat16)
    for copy in tables:
        copy.wait()

    def project(k):
        chunks[k].wait()
        for part in range(2):
            cols = slice(part * 256, part * 256 + 256)
            full = dot(normed_ref[...], wq_v[k, :, cols])
            for half in range(2):
                block = full[:, half * 128 : half * 128 + 128]
                at = (k % 2) * 512 + part * 256 + half * 128
                if k < 4:
                    block = rotated(block, cos_v[...], sin_v[...])
                block = block.astype(jnp.bfloat16)
                if k < 2:
                    q_ref[:, at : at + 128] = block
                else:
                    kv_ref[k // 2 - 1, HALF : HALF + TOK, at : at + 128] = block

    for k in order[:4]:
        project(k)

    to_left = pltpu.make_async_remote_copy(
        src_ref=kv_ref.at[:, pl.ds(HALF, HALF)], dst_ref=kv_ref.at[:, pl.ds(HALF + TOK, HALF)],
        send_sem=send_sem.at[0], recv_sem=recv_sem.at[0], device_id=left, device_id_type=MESH,
    )
    to_right = pltpu.make_async_remote_copy(
        src_ref=kv_ref.at[:, pl.ds(TOK, HALF)], dst_ref=kv_ref.at[:, pl.ds(0, HALF)],
        send_sem=send_sem.at[1], recv_sem=recv_sem.at[1], device_id=right, device_id_type=MESH,
    )

    @pl.when(has_left)
    def _():
        to_left.start()

    @pl.when(has_right)
    def _():
        to_right.start()

    @pl.when(jnp.logical_not(has_left))
    def _():
        kv_ref[:, 0:HALF] = jnp.zeros((2, HALF, D), jnp.bfloat16)

    @pl.when(jnp.logical_not(has_right))
    def _():
        kv_ref[:, HALF + TOK :] = jnp.zeros((2, HALF, D), jnp.bfloat16)

    for k in order[4:]:
        project(k)
    window_bias(bias_v, clip_ref, seq_count * TOK, False)

    heads = 4
    lanes_of = heads * HEAD_DIM

    def attend(blocks):
        def step(group, carry):
            lanes = pl.ds(pl.multiple_of(group * lanes_of, lanes_of), lanes_of)
            scores = []
            for block in blocks:
                queries = q_ref[block * 128 : block * 128 + 128, lanes] * 0.125
                keys = kv_ref[0, block * 128 : block * 128 + 256, lanes]
                bias = jnp.concatenate([bias_v[block]] * (heads // 2), 0)
                scores.append(contract_back(stacked_heads(queries, heads), keys) + bias)
            probs = []
            for score in scores:
                exponent = jnp.exp(score - jnp.max(score, -1, keepdims=True))
                total = jnp.sum(exponent, -1, keepdims=True)
                probs.append((exponent * (1.0 / total)).astype(jnp.bfloat16))
            for block, prob in zip(blocks, probs):
                values = kv_ref[1, block * 128 : block * 128 + 256, lanes]
                att_ref[block * 128 : block * 128 + 128, lanes] = merged_heads(
                    dot(prob, values), heads
                ).astype(jnp.bfloat16)
            return carry

        lax.fori_loop(0, D // lanes_of, step, 0)

    last = TOK // 128 - 1
    attend(list(range(1, last)))

    @pl.when(has_left)
    def _():
        to_right.wait_recv()

    @pl.when(has_right)
    def _():
        to_left.wait_recv()

    attend([0, last])
    out_copy.wait()
    for part in range(4):
        cols = slice(part * 256, part * 256 + 256)
        branch_ref[:, cols] = dot(att_ref[...], wo_v[:, cols])

    @pl.when(has_left)
    def _():
        to_left.wait_send()

    @pl.when(has_right)
    def _():
        to_right.wait_send()


def rotary_tables(group_len):
    half = HEAD_DIM // 2
    inv_freq = (10000.0 ** (-np.arange(half) / half)).astype(np.float32)[None, :]
    angles = np.arange(group_len, dtype=np.float32)[:, None] * inv_freq
    cosine, sine = np.cos(angles), np.sin(angles)
    return (
        np.concatenate([cosine] * 4, 1).astype(np.float32),
        np.concatenate([-sine, sine] * 2, 1).astype(np.float32),
    )


def forward_attention(frames, lengths, gain, bias, scale, w_qkv, w_out, tables, seq_count):
    bf, f32 = jnp.bfloat16, jnp.float32
    hbm = pl.BlockSpec(memory_space=pl.ANY)
    vmem = pl.BlockSpec(memory_space=pltpu.VMEM)
    smem = pl.BlockSpec(memory_space=pltpu.SMEM)
    shape = jax.ShapeDtypeStruct
    return pl.pallas_call(
        functools.partial(forward_kernel, seq_count),
        out_shape=[
            shape((TOK, D), bf),
            shape((TOK, D), bf),
            shape((2, TOK + 2 * HALF, D), bf),
            shape((TOK, D), bf),
            shape((TOK, D), f32),
        ],
        in_specs=[smem] + [vmem] * 4 + [hbm] * 4,
        out_specs=[vmem] * 5,
        scratch_shapes=[
            pltpu.VMEM((6, D, 512), bf),
            pltpu.VMEM((D, D), bf),
            pltpu.VMEM((TOK, 128), f32),
            pltpu.VMEM((TOK, 128), f32),
            pltpu.VMEM((TOK // 128, 256, 256), f32),
            pltpu.SemaphoreType.DMA((9,)),
            pltpu.SemaphoreType.DMA((2,)),
            pltpu.SemaphoreType.DMA((2,)),
        ],
        compiler_params=pltpu.CompilerParams(
            collective_id=2, has_side_effects=True, vmem_limit_bytes=56 * 2**20
        ),
        name="attention_forward",
    )(lengths, frames, gain[None], bias[None], scale[None], w_qkv, w_out, *tables)


FBLK = 512


def mlp_kernel(
    x_ref, c_ref, branch_ref, gain_ref, bias_ref, scale_attn_ref, scale_mlp_ref, w_gate_up, w_down,
    out_ref, n2_ref, hidden_ref, dgu_ref, dm_ref, db_ref, dmid_ref, vec_ref,
    wg_v, wu_v, wd_v, mlp_v, dn_v, load_sem,
):
    count = FF // FBLK

    def copies(step, slot):
        at = pl.multiple_of(step * FBLK, FBLK)
        return [
            pltpu.make_async_copy(
                w_gate_up.at[:, pl.ds(at, FBLK)], wg_v.at[slot], load_sem.at[slot, 0]
            ),
            pltpu.make_async_copy(
                w_gate_up.at[:, pl.ds(FF + at, FBLK)], wu_v.at[slot], load_sem.at[slot, 1]
            ),
            pltpu.make_async_copy(
                w_down.at[pl.ds(at, FBLK)], wd_v.at[slot], load_sem.at[slot, 2]
            ),
        ]

    for copy in copies(0, 0):
        copy.start()
    middle = x_ref[...].astype(jnp.float32) + scale_attn_ref[...] * branch_ref[...]
    hat, inverse = normalize(middle)
    n2_ref[...] = (hat * gain_ref[...] + bias_ref[...]).astype(jnp.bfloat16)
    dm_ref[...] = (c_ref[...].astype(jnp.float32) * scale_mlp_ref[...]).astype(jnp.bfloat16)
    mlp_v[...] = jnp.zeros_like(mlp_v)
    dn_v[...] = jnp.zeros_like(dn_v)

    def step(number, carry):
        slot = lax.rem(number, 2)

        @pl.when(number + 1 < count)
        def _():
            for copy in copies(number + 1, 1 - slot):
                copy.start()

        for copy in copies(number, slot):
            copy.wait()
        for part in range(FBLK // 256):
            cols = slice(part * 256, part * 256 + 256)
            at = pl.multiple_of(number * FBLK + part * 256, 256)
            gate = dot(n2_ref[...], wg_v[slot, :, cols])
            up = dot(n2_ref[...], wu_v[slot, :, cols])
            dh = contract_back(dm_ref[...], wd_v[slot, cols, :])
            sigmoid = 1.0 / (1.0 + jnp.exp(-gate))
            silu = gate * sigmoid
            hidden_ref[:, pl.ds(at, 256)] = (silu * up).astype(jnp.bfloat16)
            dgate = dh * up * (sigmoid * (1.0 + gate * (1.0 - sigmoid)))
            dgu_ref[:, pl.ds(at, 256)] = dgate.astype(jnp.bfloat16)
            dgu_ref[:, pl.ds(FF + at, 256)] = (dh * silu).astype(jnp.bfloat16)
        at = pl.multiple_of(number * FBLK, FBLK)
        mlp_v[...] += dot(hidden_ref[:, pl.ds(at, FBLK)], wd_v[slot])
        dn_v[...] += contract_back(dgu_ref[:, pl.ds(at, FBLK)], wg_v[slot]) + contract_back(
            dgu_ref[:, pl.ds(FF + at, FBLK)], wu_v[slot]
        )
        return carry

    lax.fori_loop(0, count, step, 0)
    cot = c_ref[...].astype(jnp.float32)
    branch = branch_ref[...]
    middle = x_ref[...].astype(jnp.float32) + scale_attn_ref[...] * branch
    mlp_out = mlp_v[...]
    out_ref[...] = (middle + scale_mlp_ref[...] * mlp_out).astype(jnp.bfloat16)
    vec_ref[0:1] = jnp.sum(cot * mlp_out, 0, keepdims=True)
    hat, inverse = normalize(middle)
    dn = dn_v[...]
    vec_ref[1:2] = jnp.sum(dn * hat, 0, keepdims=True)
    vec_ref[2:3] = jnp.sum(dn, 0, keepdims=True)
    dmid = cot + norm_backward(dn, hat, inverse, gain_ref[...])
    dmid_ref[...] = dmid
    vec_ref[3:4] = jnp.sum(dmid * branch, 0, keepdims=True)
    vec_ref[4:8] = jnp.zeros((4, D), jnp.float32)
    db_ref[...] = (dmid * scale_attn_ref[...]).astype(jnp.bfloat16)


def feed_forward(frames, cotangent, branch, gain, bias, scale_attn, scale_mlp, w_gate_up, w_down):
    bf, f32 = jnp.bfloat16, jnp.float32
    hbm = pl.BlockSpec(memory_space=pl.ANY)
    vmem = pl.BlockSpec(memory_space=pltpu.VMEM)
    shape = jax.ShapeDtypeStruct
    return pl.pallas_call(
        mlp_kernel,
        out_shape=[
            shape((TOK, D), bf),
            shape((TOK, D), bf),
            shape((TOK, FF), bf),
            shape((TOK, 2 * FF), bf),
            shape((TOK, D), bf),
            shape((TOK, D), bf),
            shape((TOK, D), f32),
            shape((8, D), f32),
        ],
        in_specs=[vmem] * 7 + [hbm] * 2,
        out_specs=[vmem] * 8,
        scratch_shapes=[
            pltpu.VMEM((2, D, FBLK), bf),
            pltpu.VMEM((2, D, FBLK), bf),
            pltpu.VMEM((2, FBLK, D), bf),
            pltpu.VMEM((TOK, D), f32),
            pltpu.VMEM((TOK, D), f32),
            pltpu.SemaphoreType.DMA((2, 3)),
        ],
        compiler_params=pltpu.CompilerParams(vmem_limit_bytes=56 * 2**20),
        name="feed_forward",
    )(
        frames, cotangent, branch, gain[None], bias[None], scale_attn[None], scale_mlp[None],
        w_gate_up, w_down,
    )


def backward_kernel(
    seq_count, clip_ref, x_ref, gain_ref, q_ref, kv_ref, db_ref, dmid_ref, w_qkv, w_out,
    cos_all, sin_all,
    dproj_ref, grad_ref, vec_ref,
    wq_v, wo_v, cos_v, sin_v, bias_v, datt_v, dkv_v, edge_v, far_v, load_sem, send_sem, recv_sem,
):
    seq = lax.axis_index("seq")
    rows = pl.ds(pl.multiple_of(seq * TOK, TOK), TOK)
    out_copy = pltpu.make_async_copy(w_out, wo_v, load_sem.at[8])
    tables = [
        pltpu.make_async_copy(cos_all.at[rows], cos_v, load_sem.at[0]),
        pltpu.make_async_copy(sin_all.at[rows], sin_v, load_sem.at[1]),
    ]
    chunks = [
        pltpu.make_async_copy(
            w_qkv.at[:, pl.ds(k * 512, 512)], wq_v.at[k], load_sem.at[2 + k]
        )
        for k in range(6)
    ]
    for copy in [out_copy] + tables + chunks:
        copy.start()
    left, right, has_left, has_right = greet_sides(seq_count)
    window_bias(bias_v, clip_ref, seq_count * TOK, True)
    out_copy.wait()
    for part in range(4):
        cols = slice(part * 256, part * 256 + 256)
        datt_v[:, cols] = contract_back(db_ref[...], wo_v[cols, :]).astype(jnp.bfloat16)
    for copy in tables:
        copy.wait()
    last = TOK // 128 - 1

    def attend(blocks):
        def step(pair, carry):
            lanes = pl.ds(pl.multiple_of(pair * 128, 128), 128)
            for block in blocks:
                own = slice(block * 128, block * 128 + 128)
                window = slice(block * 128, block * 128 + 256)
                queries = stacked(q_ref[own, lanes] * 0.125)
                grads = stacked(datt_v[own, lanes])
                keys = kv_ref[0, window, lanes]
                scores = contract_back(keys, queries) + bias_v[block]
                exponent = jnp.exp(scores - jnp.max(scores, 0, keepdims=True))
                total = jnp.sum(exponent, 0, keepdims=True)
                probs = exponent * (1.0 / total)
                d_probs = contract_back(kv_ref[1, window, lanes], grads)
                inner = jnp.sum(probs * d_probs, 0, keepdims=True)
                d_scores = (probs * (d_probs - inner)).astype(jnp.bfloat16)
                d_keys = dot(d_scores, queries)
                d_values = dot(probs.astype(jnp.bfloat16), grads)
                for which, update in ((0, d_keys), (1, d_values)):
                    if block in (0, last):
                        dkv_v[which, window, lanes] = update
                    elif block == 1:
                        dkv_v[which, 128:256, lanes] += update[:128]
                        dkv_v[which, 256:384, lanes] = update[128:]
                    else:
                        dkv_v[which, window, lanes] += update
                d_queries = merged(tn_dot(d_scores, keys)) * 0.125
                dproj_ref[own, lanes] = rotated(
                    d_queries, cos_v[own, :], -sin_v[own, :]
                ).astype(jnp.bfloat16)
            return carry

        lax.fori_loop(0, D // 128, step, 0)

    attend([0, last])
    edge_v[0] = dkv_v[:, 0:HALF].astype(jnp.bfloat16)
    edge_v[1] = dkv_v[:, HALF + TOK :].astype(jnp.bfloat16)
    to_left = pltpu.make_async_remote_copy(
        src_ref=edge_v.at[0], dst_ref=far_v.at[1],
        send_sem=send_sem.at[0], recv_sem=recv_sem.at[0], device_id=left, device_id_type=MESH,
    )
    to_right = pltpu.make_async_remote_copy(
        src_ref=edge_v.at[1], dst_ref=far_v.at[0],
        send_sem=send_sem.at[1], recv_sem=recv_sem.at[1], device_id=right, device_id_type=MESH,
    )

    @pl.when(has_left)
    def _():
        to_left.start()

    @pl.when(has_right)
    def _():
        to_right.start()

    attend(list(range(1, last)))

    @pl.when(has_left)
    def _():
        to_right.wait_recv()
        dkv_v[:, HALF : 2 * HALF] += far_v[0].astype(jnp.float32)

    @pl.when(has_right)
    def _():
        to_left.wait_recv()
        dkv_v[:, TOK : TOK + HALF] += far_v[1].astype(jnp.float32)

    for k in range(D // 128):
        lanes = slice(k * 128, k * 128 + 128)
        dproj_ref[:, D + k * 128 : D + k * 128 + 128] = rotated(
            dkv_v[0, HALF : HALF + TOK, lanes], cos_v[...], -sin_v[...]
        ).astype(jnp.bfloat16)
        dproj_ref[:, 2 * D + k * 128 : 2 * D + k * 128 + 128] = dkv_v[
            1, HALF : HALF + TOK, lanes
        ].astype(jnp.bfloat16)
    for copy in chunks:
        copy.wait()
    dn = contract_back(dproj_ref[:, 0:512], wq_v[0])
    for k in range(1, 6):
        dn += contract_back(dproj_ref[:, k * 512 : k * 512 + 512], wq_v[k])
    hat, inverse = normalize(x_ref[...].astype(jnp.float32))
    vec_ref[0:1] = jnp.sum(dn * hat, 0, keepdims=True)
    vec_ref[1:2] = jnp.sum(dn, 0, keepdims=True)
    vec_ref[2:8] = jnp.zeros((6, D), jnp.float32)
    grad_ref[...] = dmid_ref[...] + norm_backward(dn, hat, inverse, gain_ref[...])

    @pl.when(has_left)
    def _():
        to_left.wait_send()

    @pl.when(has_right)
    def _():
        to_right.wait_send()


def backward_attention(
    frames, lengths, gain, queries, kv, db, dmid, w_qkv, w_out, tables, seq_count
):
    bf, f32 = jnp.bfloat16, jnp.float32
    hbm = pl.BlockSpec(memory_space=pl.ANY)
    vmem = pl.BlockSpec(memory_space=pltpu.VMEM)
    smem = pl.BlockSpec(memory_space=pltpu.SMEM)
    shape = jax.ShapeDtypeStruct
    ext = TOK + 2 * HALF
    return pl.pallas_call(
        functools.partial(backward_kernel, seq_count),
        out_shape=[shape((TOK, 3 * D), bf), shape((TOK, D), f32), shape((8, D), f32)],
        in_specs=[smem] + [vmem] * 6 + [hbm] * 4,
        out_specs=[vmem] * 3,
        scratch_shapes=[
            pltpu.VMEM((6, D, 512), bf),
            pltpu.VMEM((D, D), bf),
            pltpu.VMEM((TOK, 128), f32),
            pltpu.VMEM((TOK, 128), f32),
            pltpu.VMEM((TOK // 128, 256, 256), f32),
            pltpu.VMEM((TOK, D), bf),
            pltpu.VMEM((2, ext, D), f32),
            pltpu.VMEM((2, 2, HALF, D), bf),
            pltpu.VMEM((2, 2, HALF, D), bf),
            pltpu.SemaphoreType.DMA((9,)),
            pltpu.SemaphoreType.DMA((2,)),
            pltpu.SemaphoreType.DMA((2,)),
        ],
        compiler_params=pltpu.CompilerParams(
            collective_id=3, has_side_effects=True, vmem_limit_bytes=56 * 2**20
        ),
        name="attention_backward",
    )(lengths, frames, gain[None], queries, kv, db, dmid, w_qkv, w_out, *tables)


RING = 8
COUNT = len(UNITS)


def parts_of(unit):
    late = isinstance(unit, int) and unit >= COUNT - LAST_UNITS
    return LAST_PARTS if late else PARTS


def stacked_heads(block, heads):
    lane = lax.broadcasted_iota(jnp.int32, block.shape, 1) // HEAD_DIM
    zero = jnp.zeros_like(block)
    return jnp.concatenate([jnp.where(lane == h, block, zero) for h in range(heads)], 0)


def merged_heads(rows, heads):
    lane = lax.broadcasted_iota(jnp.int32, (128, rows.shape[1]), 1) // HEAD_DIM
    total = rows[:128]
    for h in range(1, heads):
        total = jnp.where(lane == h, rows[128 * h : 128 * h + 128], total)
    return total


def layer_kernel(
    clip_ref, x_hbm, c_hbm, gain1_ref, bias1_ref, gain2_ref, bias2_ref, scale_attn_ref, scale_mlp_ref,
    w_qkv, w_out, w_gate_up, w_down, cos_all, sin_all,
    out_hbm, grad_hbm, out0, out1, out2, out3, vec_out, att_hbm, normed_hbm, far_att, far_normed, hid_hbm, far_hid,
    part_a, part_b, part_c,
    recv_a1, recv_a2, recv_az, recv_b1, recv_b2, recv_bz, recv_cz, recv_c1, recv_c2,
    wide_v, deep_v, dkv_v, xbuf, ybuf, yfar, ydown, yout, other_v, hid_v,
    dm_v, x_v, c_v, grad_v, q_v, kv_v, dproj_v, bias_v, cos_v, sin_v, far_v,
    vec_sum, vec_recv, vec_z,
    send_sem, recv_sem, load_sem, far_send, far_recv, w_sem, hid_sem, hid_send, hid_recv,
    oth_send, oth_recv, q_send, q_recv, x_sem, edge_send, edge_recv, vec_send, vec_rsem, out_sem, halo_send, halo_recv,
):
    outs = (out0, out1, out2, out3)
    dp = lax.axis_index("dp")
    seq = lax.axis_index("seq")
    z, y = dp // 2, dp % 2
    x, c = seq // 2, seq % 2
    dev_c = (dp, x * 2 + 1 - c)
    dev_x = (dp, (1 - x) * 2 + c)
    dev_y = (z * 2 + 1 - y, seq)
    dev_d = (dp, (1 - x) * 2 + 1 - c)
    dev_z = [(lax.rem(z + k, 4) * 2 + y, seq) for k in (1, 2, 3)]
    bf, f32 = jnp.bfloat16, jnp.float32

    def local_copy(src, dst, sem):
        return pltpu.make_async_copy(src, dst, sem)

    def remote(src, dst, ssem, rsem, device):
        return pltpu.make_async_remote_copy(
            src_ref=src, dst_ref=dst, send_sem=ssem, recv_sem=rsem,
            device_id=device, device_id_type=MESH,
        )

    def weights(step, slot):
        result = []
        for i in range(2):
            at = pl.multiple_of((c if i == 0 else 1 - c) * (FF // 2) + step * 256, 256)
            result += [
                local_copy(
                    w_gate_up.at[:, pl.ds(at, 256)], wide_v.at[4 * slot + i], w_sem.at[slot, i]
                ),
                local_copy(
                    w_gate_up.at[:, pl.ds(FF + at, 256)], wide_v.at[4 * slot + 2 + i],
                    w_sem.at[slot, 2 + i],
                ),
                local_copy(
                    w_down.at[pl.ds(at, 256)], deep_v.at[slot, pl.ds(256 * i, 256)],
                    w_sem.at[slot, 4 + i],
                ),
            ]
        return result

    rows = pl.ds(pl.multiple_of(seq * TOK, TOK), TOK)
    x_copy = local_copy(x_hbm, x_v, load_sem.at[0])
    c_copy = local_copy(c_hbm, c_v, load_sem.at[1])
    tables = [
        local_copy(cos_all.at[rows], cos_v, load_sem.at[2]),
        local_copy(sin_all.at[rows], sin_v, load_sem.at[3]),
    ]
    wo_first = [
        local_copy(
            w_out.at[pl.ds(512 * k, 512)], dproj_v.at[:, pl.ds(D * k, D)], load_sem.at[4 + k]
        )
        for k in range(2)
    ]
    wq_copies = [
        local_copy(w_qkv.at[:, pl.ds(256 * k, 256)], wide_v.at[k % 8], w_sem.at[k % 8 // 4, k % 4])
        for k in range(12)
    ]
    wq_first = {
        k: local_copy(
            w_qkv.at[:, pl.ds(256 * k, 256)], wide_v.at[k - 4 if k >= 4 else k],
            w_sem.at[k // 8, k % 4],
        )
        for k in [4, 5, 6, 7, 8, 9, 10, 11, 0, 1, 2, 3]
    }
    x_copy.start()
    for k in range(4, 8):
        wq_first[k].start()
    for copy in tables:
        copy.start()
    for k in range(8, 12):
        wq_first[k].start()
    for copy in wo_first + [c_copy]:
        copy.start()

    barrier = pltpu.get_barrier_semaphore()
    for device in [dev_c, dev_x, dev_y, dev_d] + dev_z:
        pl.semaphore_signal(barrier, inc=1, device_id=device, device_id_type=MESH)

    is_end = (z == 0) | (z == 3)
    is_mid = (z == 1) | (z == 2)
    end_low = jnp.where(z == 0, 1, 0)
    end_dir = jnp.where(z == 0, 0, 1)
    end_next = (jnp.where(z == 0, 1, 2) * 2 + y, seq)
    mid_dir = jnp.where(z == 1, 0, 1)
    mid_low = jnp.where(z == 1, 1, 0)
    mid_keep = jnp.where(z == 1, 2, 0)
    mid_next = ((3 - z) * 2 + y, seq)
    back_dir = 1 - mid_dir
    back_low = jnp.where(z == 2, 2, 0)
    back_keep = jnp.where(z == 2, 3, 0)
    back_next = (jnp.where(z == 2, 3, 0) * 2 + y, seq)

    def z_send(slot, which, pieces, recv, number):
        ssem, rsem = send_sem.at[slot, which], recv_sem.at[slot, which]
        if number == 0:
            low, size, way, device = end_low, 3, end_dir, end_next
        elif number == 1:
            low, size, way, device = mid_keep, 2, mid_dir, mid_next
        else:
            low, size, way, device = back_keep, 1, back_dir, back_next
        return remote(
            pieces.at[pl.ds(low, size)], recv.at[way, pl.ds(low - 1 + way, size)],
            ssem.at[2 + number // 2], rsem.at[2 + way], device,
        )

    def z_wait(slot, which, recv, way, low, size):
        view = recv.at[way, pl.ds(low - 1 + way, size)]
        local_copy(view, view, recv_sem.at[slot, which, 2 + way]).wait()

    def z_round0(slot, which, pieces, recv):
        @pl.when(is_end)
        def _():
            z_send(slot, which, pieces, recv, 0).start()

    def z_round1(slot, which, pieces, recv):
        @pl.when(is_mid)
        def _():
            z_wait(slot, which, recv, mid_dir, mid_low, 3)
            keep = pl.ds(mid_keep, 2)
            pieces[keep] = pieces[keep] + recv[mid_dir, pl.ds(mid_keep - 1 + mid_dir, 2)]
            z_send(slot, which, pieces, recv, 1).start()

    def z_round2(slot, which, pieces, recv):
        @pl.when(is_mid)
        def _():
            z_wait(slot, which, recv, back_dir, back_low, 2)
            keep = pl.ds(back_keep, 1)
            pieces[keep] = pieces[keep] + recv[back_dir, pl.ds(back_keep - 1 + back_dir, 1)]
            z_send(slot, which, pieces, recv, 2).start()

    def z_final(slot, which, pieces, recv, finish):
        @pl.when(is_end)
        def _():
            way = 1 - end_dir
            z_wait(slot, which, recv, way, z, 1)
            finish(pieces[z].astype(f32) + recv[way, z - 1 + way].astype(f32))

        @pl.when(is_mid)
        def _():
            finish(
                pieces[z].astype(f32) + recv[0, z - 1].astype(f32) + recv[1, z].astype(f32)
            )

    def views(unit):
        slot = unit % RING if isinstance(unit, int) else lax.rem(unit, RING)
        parts = parts_of(unit)
        a, b = pl.ds(0, parts[1]), pl.ds(0, parts[2] - parts[1])
        return (
            slot,
            part_a.at[slot, :, :, :, a], recv_a1.at[slot, :, :, a], recv_a2.at[slot, :, a],
            recv_az.at[slot, :, :, a],
            part_b.at[slot, :, :, :, b], recv_b1.at[slot, :, :, b], recv_b2.at[slot, :, b],
            recv_bz.at[slot, :, :, b],
            part_c.at[slot], recv_c1.at[slot], recv_c2.at[slot], recv_cz.at[slot],
            parts[3] > parts[2],
        )

    def hop(unit, which, index):
        slot, a, a1, a2, _, b, b1, b2, _, cc, c1, c2, _, _ = views(unit)
        source, target, device = {
            (0, 0): lambda: (a.at[1 - x], a1, dev_x),
            (0, 1): lambda: (a.at[x, 1 - y], a2, dev_y),
            (1, 0): lambda: (b.at[1 - y], b1, dev_y),
            (1, 1): lambda: (b.at[y, 1 - x], b2, dev_x),
            (2, 0): lambda: (cc.at[z, 1 - x], c1, dev_x),
            (2, 1): lambda: (cc.at[z, x, 1 - y], c2, dev_y),
        }[which, index]()
        return remote(
            source, target, send_sem.at[slot, which, index], recv_sem.at[slot, which, index], device
        )

    def put(unit, which, block):
        low, high = parts_of(unit)[which : which + 2]
        if not isinstance(unit, int):
            columns = pl.ds(pl.multiple_of(unit * 256, 256), 256)
            out2[low:high, columns] = block
            return
        _, _, _, _, _, offset, out, row = UNITS[unit]
        outs[out][row + low : row + high, offset : offset + 256] = block

    def stage(unit, number):
        slot, a, a1, a2, rz_a, b, b1, b2, rz_b, cc, c1, c2, rz_c, thirds = views(unit)
        a_z, b_z = a.at[x, y], b.at[y, x]
        if number == 0:
            hop(unit, 0, 0).start()
            hop(unit, 1, 0).start()
            if thirds:
                z_round0(slot, 2, cc, rz_c)
        if number == 1:
            hop(unit, 0, 0).wait_recv()
            a[x] = a[x] + a1[...]
            hop(unit, 0, 1).start()
            hop(unit, 1, 0).wait_recv()
            b[y] = b[y] + b1[...]
            hop(unit, 1, 1).start()
            if thirds:
                z_round1(slot, 2, cc, rz_c)
        if number == 2:
            hop(unit, 0, 1).wait_recv()
            a[x, y] = a[x, y] + a2[...]
            z_round0(slot, 0, a_z, rz_a)
            hop(unit, 1, 1).wait_recv()
            b[y, x] = b[y, x] + b2[...]
            z_round0(slot, 1, b_z, rz_b)
            if thirds:
                z_round2(slot, 2, cc, rz_c)
        if number == 3:
            z_round1(slot, 0, a_z, rz_a)
            z_round1(slot, 1, b_z, rz_b)

            def keep(value):
                cc[z] = value.astype(bf)

            if thirds:
                z_final(slot, 2, cc, rz_c, keep)
                hop(unit, 2, 0).start()
        if number == 4:
            z_round2(slot, 0, a_z, rz_a)
            z_round2(slot, 1, b_z, rz_b)
            if thirds:
                hop(unit, 2, 0).wait_recv()
                cc[z, x] = cc[z, x] + c1[...]
                hop(unit, 2, 1).start()
        if number == 5:
            z_final(slot, 0, a_z, rz_a, functools.partial(put, unit, 0))
            z_final(slot, 1, b_z, rz_b, functools.partial(put, unit, 1))
            if thirds:
                hop(unit, 2, 1).wait_recv()
                put(unit, 2, cc[z, x, y].astype(f32) + c2[...].astype(f32))

    def sums(step):
        for number in range(1, 6):
            unit = step - number + 1
            if isinstance(step, int):
                if 0 <= unit < COUNT:
                    stage(unit, number)
            else:

                @pl.when(unit >= 0)
                def _():
                    stage(unit, number)

    def sent(unit):
        slot, a, _, _, rz_a, b, _, _, rz_b, cc, _, _, rz_c, thirds = views(unit)
        whole = [(a.at[x, y], rz_a), (b.at[y, x], rz_b)] + ([(cc, rz_c)] if thirds else [])
        for which, (pieces, recv) in enumerate(whole):
            for index in range(2):
                hop(unit, which, index).wait_send()

            @pl.when(is_end)
            def _():
                z_send(slot, which, pieces, recv, 0).wait_send()

            @pl.when(is_mid)
            def _():
                z_send(slot, which, pieces, recv, 1).wait_send()
                z_send(slot, which, pieces, recv, 2).wait_send()

    def multiply(unit, xslot, own, far):
        slot, parts = views(unit)[0], parts_of(unit)

        def step(i, carry):
            columns = pl.ds(pl.multiple_of(i * 512, 512), 512)
            for xi in range(2):
                total = (
                    tn_dot(xbuf[xslot, 0, :, columns], own(xi))
                    + tn_dot(xbuf[xslot, 1, :, columns], far(xi))
                ).astype(bf)
                for k in range(4):
                    zi, yi = 2 * i + k // 2, k % 2
                    block = total[k * 128 : k * 128 + 128]
                    part_a[slot, xi, yi, zi, : parts[1]] = block[: parts[1]]
                    part_b[slot, yi, xi, zi, : parts[2] - parts[1]] = block[parts[1] : parts[2]]
                    if parts[3] > parts[2]:
                        part_c[slot, zi, xi, yi] = block[parts[2] :]
            return carry

        lax.fori_loop(0, 2, step, 0)

    def far_copy(src, dst, index):
        return remote(src, dst, far_send.at[index], far_recv.at[index], dev_c)

    def pair_columns(array, width, offset, core, xi):
        return array.at[:, pl.ds(pl.multiple_of((2 * xi + core) * width + offset, 256), 256)]

    far_n2 = far_copy(xbuf.at[0, 0], xbuf.at[0, 1], 0)
    far_a = far_copy(xbuf.at[1, 1], far_att, 1)
    far_n = far_copy(xbuf.at[1, 0], far_normed, 2)
    far_dm = [
        far_copy(pair_columns(dm_v, 256, 0, 1 - c, xi), ydown.at[xi], 3 + xi) for xi in range(2)
    ]
    far_db = [
        far_copy(other_v.at[xi, 1 - c], yout.at[xi], 5 + xi) for xi in range(2)
    ]
    far_dq = [
        remote(
            pair_columns(dproj_v, 768, 256 * v, 1 - c, xi), yfar.at[v, xi],
            q_send.at[v, xi], q_recv.at[v, xi], dev_c,
        )
        for v in range(3)
        for xi in range(2)
    ]

    def far_other(step):
        return remote(
            other_v.at[lax.rem(step, 2)], yfar.at[lax.rem(step, 4)],
            oth_send.at[lax.rem(step, 2)], oth_recv.at[lax.rem(step, 4)], dev_c,
        )

    def hidden_copies(step):
        slot = lax.rem(step, 2)
        result = []
        for i in range(2):
            at = pl.multiple_of((c if i == 0 else 1 - c) * (FF // 2) + step * 256, 256)
            block = hid_v.at[slot, :, pl.ds(256 * i, 256)]
            result.append(local_copy(block, hid_hbm.at[:, pl.ds(at, 256)], hid_sem.at[slot, i]))
            result.append(
                remote(
                    block, far_hid.at[:, pl.ds(at, 256)],
                    hid_send.at[slot, i], hid_recv.at[step, i], dev_c,
                )
            )
        return result

    window_bias(bias_v, clip_ref, 4 * TOK, True)
    vec_sum[0] = jnp.zeros((8, D), f32)
    x_copy.wait()

    def first_norm(i, carry):
        at = pl.ds(pl.multiple_of(i * 128, 128), 128)
        hat, _ = normalize(x_v[at, :].astype(f32))
        xbuf[1, 0, at, :] = (hat * gain1_ref[...] + bias1_ref[...]).astype(bf)
        return carry

    lax.fori_loop(0, TOK // 128, first_norm, 0)
    normed_copy = local_copy(xbuf.at[1, 0], normed_hbm, out_sem.at[2])
    att_copy = local_copy(xbuf.at[1, 1], att_hbm, out_sem.at[3])
    normed_copy.start()
    for copy in tables:
        copy.wait()

    def project(k):
        full = dot(xbuf[1, 0], wide_v[k - 4 if k >= 4 else k])
        for half in range(2):
            block = full[:, half * 128 : half * 128 + 128]
            at = (k % 4) * 256 + half * 128
            if k < 8:
                block = rotated(block, cos_v[...], sin_v[...])
            block = block.astype(bf)
            if k < 4:
                q_v[:, at : at + 128] = block
            else:
                kv_v[k // 4 - 1, HALF : HALF + TOK, at : at + 128] = block

    def project_all(chunks):
        for k in chunks:
            wq_first[k].wait()
        for k in chunks:
            project(k)

    project_all(range(4, 8))
    for k in range(4):
        wq_first[k].start()
    project_all(range(8, 12))
    pl.semaphore_wait(barrier, 7)
    has_left, has_right = seq > 0, seq < 3
    halo_left = remote(
        kv_v.at[:, pl.ds(HALF, HALF)], kv_v.at[:, pl.ds(HALF + TOK, HALF)],
        halo_send.at[0], halo_recv.at[0], (dp, seq - 1),
    )
    halo_right = remote(
        kv_v.at[:, pl.ds(TOK, HALF)], kv_v.at[:, pl.ds(0, HALF)],
        halo_send.at[1], halo_recv.at[1], (dp, seq + 1),
    )

    @pl.when(has_left)
    def _():
        halo_left.start()

    @pl.when(has_right)
    def _():
        halo_right.start()

    @pl.when(jnp.logical_not(has_left))
    def _():
        kv_v[:, 0:HALF] = jnp.zeros((2, HALF, D), bf)

    @pl.when(jnp.logical_not(has_right))
    def _():
        kv_v[:, HALF + TOK :] = jnp.zeros((2, HALF, D), bf)

    far_n.start()
    project_all(range(4))
    for copy in weights(0, 0) + weights(1, 1):
        copy.start()
    last = TOK // 128 - 1
    heads = 4
    lanes_of = heads * HEAD_DIM

    def attend_forward(blocks):
        def step(group, carry):
            lanes = pl.ds(pl.multiple_of(group * lanes_of, lanes_of), lanes_of)
            scores = []
            for block in blocks:
                queries = q_v[block * 128 : block * 128 + 128, lanes] * 0.125
                keys = kv_v[0, block * 128 : block * 128 + 256, lanes]
                bias = jnp.concatenate([bias_v[block]] * (heads // 2), 1)
                scores.append(contract_back(keys, stacked_heads(queries, heads)) + bias)
            probs = []
            for score in scores:
                exponent = jnp.exp(score - jnp.max(score, 0, keepdims=True))
                total = jnp.sum(exponent, 0, keepdims=True)
                probs.append((exponent * (1.0 / total)).astype(bf))
            for block, prob in zip(blocks, probs):
                values = kv_v[1, block * 128 : block * 128 + 256, lanes]
                xbuf[1, 1, block * 128 : block * 128 + 128, lanes] = merged_heads(
                    tn_dot(prob, values), heads
                ).astype(bf)
            return carry

        lax.fori_loop(0, D // lanes_of, step, 0)

    attend_forward(list(range(1, last)))
    c_copy.wait()

    def scaled(i, carry):
        at = pl.ds(pl.multiple_of(i * 128, 128), 128)
        dm_v[at, :] = (c_v[at, :].astype(f32) * scale_mlp_ref[...]).astype(bf)
        return carry

    lax.fori_loop(0, TOK // 128, scaled, 0)
    for copy in far_dm:
        copy.start()
    dkv_v[...] = jnp.zeros_like(dkv_v)

    @pl.when(has_left)
    def _():
        halo_right.wait_recv()

    @pl.when(has_right)
    def _():
        halo_left.wait_recv()

    attend_forward([0, last])
    att_copy.start()
    far_a.start()
    for copy in wo_first:
        copy.wait()
    for part in range(4):
        cols = slice(part * 256, part * 256 + 256)
        grad_v[:, cols] = dot(xbuf[1, 1, :, 0:512], dproj_v[:, cols]) + dot(
            xbuf[1, 1, :, 512:1024], dproj_v[:, D + part * 256 : D + part * 256 + 256]
        )


    def before(i, carry):
        at = pl.ds(pl.multiple_of(i * 128, 128), 128)
        middle = x_v[at, :].astype(f32) + scale_attn_ref[...] * grad_v[at, :]
        hat, _ = normalize(middle)
        xbuf[0, 0, at, :] = (hat * gain2_ref[...] + bias2_ref[...]).astype(bf)
        return carry

    lax.fori_loop(0, TOK // 128, before, 0)
    far_n2.start()

    def mlp(step):
        slot = lax.rem(step, 2)

        @pl.when(step >= 2)
        def _():
            far_other(step - 2).wait_send()
            for copy in hidden_copies(step - 2)[0::2]:
                copy.wait()
            for copy in hidden_copies(step - 2)[1::2]:
                copy.wait_send()

        for copy in weights(step, slot):
            copy.wait()
        normed = xbuf.at[0, 0]
        for i in range(2):
            gate = dot(normed[...], wide_v[4 * slot + i])
            up = dot(normed[...], wide_v[4 * slot + 2 + i])
            dh = contract_back(dm_v[...], deep_v[slot, 256 * i : 256 * i + 256])
            sigmoid = 1.0 / (1.0 + jnp.exp(-gate))
            silu = gate * sigmoid
            hid_v[slot, :, 256 * i : 256 * i + 256] = (silu * up).astype(bf)
            target = ybuf if i == 0 else other_v
            dgate = dh * up * (sigmoid * (1.0 + gate * (1.0 - sigmoid)))
            target[slot, 0] = dgate.astype(bf)
            target[slot, 1] = (dh * silu).astype(bf)
        far_other(step).start()
        for copy in hidden_copies(step):
            copy.start()
        dkv_v[0, 0:TOK] += dot(hid_v[slot], deep_v[slot])
        dkv_v[1, 0:TOK] += (
            contract_back(ybuf[slot, 0], wide_v[4 * slot])
            + contract_back(other_v[slot, 0], wide_v[4 * slot + 1])
            + contract_back(ybuf[slot, 1], wide_v[4 * slot + 2])
            + contract_back(other_v[slot, 1], wide_v[4 * slot + 3])
        )

        @pl.when(step + 2 < 8)
        def _():
            for copy in weights(step + 2, slot):
                copy.start()

    def gate_unit(step):
        far_other(step).wait_recv()
        multiply(
            step, 0, lambda xi: ybuf[lax.rem(step, 2), xi], lambda xi: yfar[lax.rem(step, 4), xi]
        )
        stage(step, 0)

    def mlp_step(step, carry):
        mlp(step)

        @pl.when(step == 0)
        def _():
            far_n2.wait_recv()

        @pl.when(step >= BEHIND)
        def _():
            sums(step - BEHIND)

        gate_unit(step)

        return carry

    lax.fori_loop(0, 8, mlp_step, 0)

    wo_copies = [
        local_copy(w_out.at[pl.ds(512 * k, 512)], deep_v.at[k], w_sem.at[k, 4]) for k in range(2)
    ]
    for copy in wo_copies + wq_copies[:8]:
        copy.start()
    for step in (6, 7):
        far_other(step).wait_send()
        for copy in hidden_copies(step)[0::2]:
            copy.wait()
        for copy in hidden_copies(step)[1::2]:
            copy.wait_send()
    for step in range(8):
        for copy in hidden_copies(step)[1::2]:
            copy.wait_recv()

    def load_left(unit):
        left, offset, width, _, _, _, _, _ = UNITS[unit]
        slot = {8: 1, 9: 0, 10: 1, 11: 0, 12: 1, 13: 0}[unit]
        arrays = {3: (hid_hbm, far_hid), 1: (att_hbm, far_att), 0: (normed_hbm, far_normed)}[left]
        result = []
        for side in range(2):
            if width == 128:
                result.append(
                    local_copy(arrays[side], xbuf.at[slot, side], x_sem.at[slot, side, 0])
                )
                continue
            for block in range(8):
                result.append(
                    local_copy(
                        arrays[side].at[:, pl.ds(block * width + offset, 128)],
                        xbuf.at[slot, side, :, pl.ds(block * 128, 128)],
                        x_sem.at[slot, side, block],
                    )
                )
        return result

    def unit_sum(unit):
        if unit <= 13:
            for copy in load_left(unit):
                copy.wait()
        _, _, _, right, width, offset, _, _ = UNITS[unit]
        if unit >= RING:
            sent(unit - RING)
        xslot = {8: 1, 9: 0, 10: 1, 11: 0, 12: 1}.get(unit, 0)
        if right == 1:
            own = lambda xi: other_v[xi, c]
        else:
            own = lambda xi: pair_columns({3: dm_v, 0: dproj_v}[right], width, offset, c, xi)[...]
        far = {3: ydown, 1: yout}.get(right, yfar.at[max(unit - 13, 0)])
        multiply(
            unit, xslot,
            own,
            lambda xi: far[xi],
        )
        stage(unit, 0)
        if unit + 2 <= 13:
            if unit + 2 == 12:
                far_a.wait_recv()
            if unit + 2 == 13:
                far_n.wait_recv()
            for copy in load_left(unit + 2):
                copy.start()

    for copy in [far_n2, far_a, far_n] + far_dm:
        copy.wait_send()
    normed_copy.wait()
    att_copy.wait()
    for copy in load_left(8):
        copy.start()
    for copy in load_left(9):
        copy.start()
    for copy in far_dm:
        copy.wait_recv()

    def after(i, carry):
        at = pl.ds(pl.multiple_of(i * 128, 128), 128)
        cot = c_v[at, :].astype(f32)
        branch = grad_v[at, :]
        middle = x_v[at, :].astype(f32) + scale_attn_ref[...] * branch
        mlp_out = dkv_v[0, at, :]
        dn = dkv_v[1, at, :]
        vec_sum[0, 5:6] += jnp.sum(cot * mlp_out, 0, keepdims=True)
        c_v[at, :] = (middle + scale_mlp_ref[...] * mlp_out).astype(bf)
        hat, inverse = normalize(middle)
        vec_sum[0, 3:4] += jnp.sum(dn * hat, 0, keepdims=True)
        vec_sum[0, 4:5] += jnp.sum(dn, 0, keepdims=True)
        dmid = cot + norm_backward(dn, hat, inverse, gain2_ref[...])
        vec_sum[0, 2:3] += jnp.sum(dmid * branch, 0, keepdims=True)
        grad_v[at, :] = dmid
        branch_grad = (dmid * scale_attn_ref[...]).astype(bf)
        for k in range(4):
            other_v[k // 2, k % 2, at, :] = branch_grad[:, 256 * k : 256 * k + 256]
        return carry

    out_copy = local_copy(c_v, out_hbm, out_sem.at[0])
    grad_copy = local_copy(grad_v, grad_hbm, out_sem.at[1])

    def norm_two_back():
        lax.fori_loop(0, TOK // 128, after, 0)
        out_copy.start()
        for copy in far_db:
            copy.start()

    def attended_grads():
        for k in range(2):
            wo_copies[k].wait()
        out_copy.wait()
        for k in range(2):
            total = None
            for j in range(4):
                term = contract_back(other_v[j // 2, j % 2], deep_v[k, :, 256 * j : 256 * j + 256])
                total = term if total is None else total + term
            c_v[:, 512 * k : 512 * k + 512] = total.astype(bf)
        for copy in far_db:
            copy.wait_recv()

    def attend(blocks):
        def step(group, carry):
            lanes = pl.ds(pl.multiple_of(group * lanes_of, lanes_of), lanes_of)
            held = []
            for block in blocks:
                own = slice(block * 128, block * 128 + 128)
                window = slice(block * 128, block * 128 + 256)
                queries = stacked_heads(q_v[own, lanes] * 0.125, heads)
                grads = stacked_heads(c_v[own, lanes], heads)
                keys = kv_v[0, window, lanes]
                bias = jnp.concatenate([bias_v[block]] * (heads // 2), 1)
                scores = contract_back(keys, queries) + bias
                d_probs = contract_back(kv_v[1, window, lanes], grads)
                held.append((queries, grads, keys, scores, d_probs))
            ready = []
            for queries, grads, keys, scores, d_probs in held:
                exponent = jnp.exp(scores - jnp.max(scores, 0, keepdims=True))
                probs = exponent * (1.0 / jnp.sum(exponent, 0, keepdims=True))
                inner = jnp.sum(probs * d_probs, 0, keepdims=True)
                d_scores = (probs * (d_probs - inner)).astype(bf)
                ready.append((queries, grads, keys, d_scores, probs.astype(bf)))
            for block, (queries, grads, keys, d_scores, probs) in zip(blocks, ready):
                own = slice(block * 128, block * 128 + 128)
                window = slice(block * 128, block * 128 + 256)
                for which, update in ((0, dot(d_scores, queries)), (1, dot(probs, grads))):
                    if block in (0, last):
                        dkv_v[which, window, lanes] = update
                    elif block == 1:
                        dkv_v[which, 128:256, lanes] += update[:128]
                        dkv_v[which, 256:384, lanes] = update[128:]
                    else:
                        dkv_v[which, window, lanes] += update
                d_queries = merged_heads(tn_dot(d_scores, keys), heads) * 0.125
                for k in range(lanes_of // 128):
                    at = pl.ds(pl.multiple_of(group * lanes_of + 128 * k, 128), 128)
                    dproj_v[own, at] = rotated(
                        d_queries[:, 128 * k : 128 * k + 128], cos_v[own, :], -sin_v[own, :]
                    ).astype(bf)
            return carry

        lax.fori_loop(0, D // lanes_of, step, 0)

    to_left = remote(
        hid_v.at[0, pl.ds(0, 256)], far_v.at[1], edge_send.at[0], edge_recv.at[0], (dp, seq - 1)
    )
    to_right = remote(
        hid_v.at[1, pl.ds(0, 256)], far_v.at[0], edge_send.at[1], edge_recv.at[1], (dp, seq + 1)
    )

    def edges_out():
        for side, first in ((0, 0), (1, HALF + TOK)):
            for k in range(4):
                hid_v[side, 64 * k : 64 * k + 64] = dkv_v[
                    k // 2, first : first + HALF, 512 * (k % 2) : 512 * (k % 2) + 512
                ].astype(bf)

        @pl.when(has_left)
        def _():
            to_left.start()

        @pl.when(has_right)
        def _():
            to_right.start()

    def edges_in():
        @pl.when(has_left)
        def _():
            to_right.wait_recv()
            for k in range(4):
                dkv_v[k // 2, HALF : 2 * HALF, 512 * (k % 2) : 512 * (k % 2) + 512] += far_v[
                    0, 64 * k : 64 * k + 64
                ].astype(f32)

        @pl.when(has_right)
        def _():
            to_left.wait_recv()
            for k in range(4):
                dkv_v[k // 2, TOK : TOK + HALF, 512 * (k % 2) : 512 * (k % 2) + 512] += far_v[
                    1, 64 * k : 64 * k + 64
                ].astype(f32)

        for k in range(D // 128):
            lanes = slice(k * 128, k * 128 + 128)
            dproj_v[:, D + k * 128 : D + k * 128 + 128] = rotated(
                dkv_v[0, HALF : HALF + TOK, lanes], cos_v[...], -sin_v[...]
            ).astype(bf)
            dproj_v[:, 2 * D + k * 128 : 2 * D + k * 128 + 128] = dkv_v[
                1, HALF : HALF + TOK, lanes
            ].astype(bf)
        for copy in far_dq:
            copy.start()

    def project_back(chunks, fresh):
        for k in chunks:
            wq_copies[k].wait()
        total = None
        for k in chunks:
            term = contract_back(dproj_v[:, 256 * k : 256 * k + 256], wide_v[k % 8])
            total = term if total is None else total + term
        if fresh:
            dkv_v[0, 0:TOK] = total
        else:
            dkv_v[0, 0:TOK] += total

    def last_norm(i, carry):
        at = pl.ds(pl.multiple_of(i * 128, 128), 128)
        hat, inverse = normalize(x_v[at, :].astype(f32))
        dn = dkv_v[0, at, :]
        vec_sum[0, 0:1] += jnp.sum(dn * hat, 0, keepdims=True)
        vec_sum[0, 1:2] += jnp.sum(dn, 0, keepdims=True)
        grad_v[at, :] += norm_backward(dn, hat, inverse, gain1_ref[...])
        return carry

    def norm_one_back():
        lax.fori_loop(0, TOK // 128, last_norm, 0)
        grad_copy.start()

    def vec_copy(number):
        return remote(
            vec_sum.at[number], vec_recv.at[number], vec_send.at[number], vec_rsem.at[number],
            (dev_c, dev_x, dev_y)[number],
        )

    vec_planes = [
        remote(vec_sum.at[3], vec_z.at[z], vec_send.at[3 + k], vec_rsem.at[3 + k], dev_z[k])
        for k in range(3)
    ]

    def vectors(number):
        if 0 < number <= 3:
            vec_copy(number - 1).wait_recv()
            vec_sum[number] = vec_sum[number - 1] + vec_recv[number - 1]
        if number < 3:
            vec_copy(number).start()
        elif number == 3:
            vec_z[z] = vec_sum[3]
            for copy in vec_planes:
                copy.start()
        else:
            for k in range(3):
                view = vec_z.at[lax.rem(z + 3 - k, 4)]
                local_copy(view, view, vec_rsem.at[3 + k]).wait()
            vec_out[...] = vec_z[0] + vec_z[1] + vec_z[2] + vec_z[3]

    def start_wq():
        for copy in wq_copies[8:]:
            copy.start()

    def far_dq_wait():
        for copy in far_dq:
            copy.wait_recv()

    actions = {
        "E": norm_two_back,
        "D": attended_grads,
        "A0": lambda: attend([0, last]),
        "O": edges_out,
        "A1": lambda: attend(list(range(1, last))),
        "I": edges_in,
        "W0": lambda: (project_back(range(8), True), start_wq()),
        "W1": lambda: project_back(range(8, 12), False),
        "N": norm_one_back,
        "Q": far_dq_wait,
    }
    for word in " ".join(ORDER).split():
        if word in actions:
            actions[word]()
        elif word[0] == "P":
            unit_sum(int(word[1:]))
        elif word[0] == "S":
            sums(int(word[1:]))
        elif word[0] == "V":
            vectors(int(word[1:]))

    for unit in range(COUNT - RING, COUNT):
        sent(unit)
    for copy in far_db + far_dq + [vec_copy(k) for k in range(3)] + vec_planes:
        copy.wait_send()

    @pl.when(has_left)
    def _():
        halo_left.wait_send()
        to_left.wait_send()

    @pl.when(has_right)
    def _():
        halo_right.wait_send()
        to_right.wait_send()

    grad_copy.wait()


BEHIND = 2
ORDER = (
    "P8 P9 E S6",
    "P10 D A0 O",
    "S7 P11 A1 S8",
    "P12 I Q S9",
    "P13 W0 S10 P14",
    "W1 N S11 P15",
    "V0 S12 V1 S13",
    "V2 S14 V3 S15",
    "V4 S16 S17 S18",
    "S19",
)


def layer(
    lengths, frames, cotangent, vectors, w_qkv, w_out, w_gate_up, w_down, tables,
):
    bf, f32 = jnp.bfloat16, jnp.float32
    hbm = pl.BlockSpec(memory_space=pl.ANY)
    vmem = pl.BlockSpec(memory_space=pltpu.VMEM)
    smem = pl.BlockSpec(memory_space=pltpu.SMEM)
    shape = jax.ShapeDtypeStruct
    size = (LAST_PARTS[1], LAST_PARTS[2] - LAST_PARTS[1], PARTS[3] - PARTS[2])
    dma = pltpu.SemaphoreType.DMA
    ext = TOK + 2 * HALF
    scratch = [
        pltpu.VMEM((RING, 2, 2, 4, size[0], 256), bf),
        pltpu.VMEM((RING, 2, 2, 4, size[1], 256), bf),
        pltpu.VMEM((RING, 4, 2, 2, size[2], 256), bf),
        pltpu.VMEM((RING, 2, 4, size[0], 256), bf),
        pltpu.VMEM((RING, 4, size[0], 256), bf),
        pltpu.VMEM((RING, 2, 3, size[0], 256), bf),
        pltpu.VMEM((RING, 2, 4, size[1], 256), bf),
        pltpu.VMEM((RING, 4, size[1], 256), bf),
        pltpu.VMEM((RING, 2, 3, size[1], 256), bf),
        pltpu.VMEM((RING, 2, 3, 2, 2, size[2], 256), bf),
        pltpu.VMEM((RING, 2, size[2], 256), bf),
        pltpu.VMEM((RING, size[2], 256), bf),
        pltpu.VMEM((8, D, 256), bf),
        pltpu.VMEM((2, 512, D), bf),
        pltpu.VMEM((2, ext, D), f32),
        pltpu.VMEM((2, 2, TOK, D), bf),
        pltpu.VMEM((2, 2, TOK, 256), bf),
        pltpu.VMEM((4, 2, TOK, 256), bf),
        pltpu.VMEM((2, TOK, 256), bf),
        pltpu.VMEM((2, TOK, 256), bf),
        pltpu.VMEM((2, 2, TOK, 256), bf),
        pltpu.VMEM((2, TOK, 512), bf),
        pltpu.VMEM((TOK, D), bf),
        pltpu.VMEM((TOK, D), bf),
        pltpu.VMEM((TOK, D), bf),
        pltpu.VMEM((TOK, D), f32),
        pltpu.VMEM((TOK, D), bf),
        pltpu.VMEM((2, ext, D), bf),
        pltpu.VMEM((TOK, 3 * D), bf),
        pltpu.VMEM((TOK // 128, 256, 256), f32),
        pltpu.VMEM((TOK, 128), f32),
        pltpu.VMEM((TOK, 128), f32),
        pltpu.VMEM((2, 256, 512), bf),
        pltpu.VMEM((4, 8, D), f32),
        pltpu.VMEM((3, 8, D), f32),
        pltpu.VMEM((4, 8, D), f32),
        dma((RING, 3, 4)),
        dma((RING, 3, 4)),
        dma((7,)),
        dma((7,)),
        dma((7,)),
        dma((2, 6)),
        dma((2, 2)),
        dma((2, 2)),
        dma((8, 2)),
        dma((2,)),
        dma((4,)),
        dma((3, 2)),
        dma((3, 2)),
        dma((2, 2, 8)),
        dma((2,)),
        dma((2,)),
        dma((6,)),
        dma((6,)),
        dma((4,)),
        dma((2,)),
        dma((2,)),
    ]
    results = pl.pallas_call(
        layer_kernel,
        out_shape=[
            shape((TOK, D), bf),
            shape((TOK, D), f32),
            shape((128, 768), f32),
            shape((128, 256), f32),
            shape((128, 2048), f32),
            shape((512, 256), f32),
            shape((8, D), f32),
        ]
        + [shape((TOK, D), bf)] * 4
        + [
            shape((TOK, FF), bf),
            shape((TOK, FF), bf),
        ],
        in_specs=[smem] + [hbm] * 2 + [vmem] * 6 + [hbm] * 6,
        out_specs=[hbm] * 2 + [vmem] * 5 + [hbm] * 6,
        scratch_shapes=scratch,
        compiler_params=pltpu.CompilerParams(
            collective_id=4, has_side_effects=True, vmem_limit_bytes=64 * 2**20 - 2**16
        ),
        name="layer",
    )(
        lengths, frames, cotangent, *[v[None] for v in vectors], w_qkv, w_out, w_gate_up, w_down, *tables,
    )[:7]
    finished = pl.pallas_call(
        finish_kernel,
        out_shape=[shape(v.shape, v.dtype) for v in results[:6]] + [shape((1, D), f32)] * 6,
        in_specs=[hbm] * 6 + [vmem],
        out_specs=[hbm] * 6 + [vmem] * 6,
        scratch_shapes=[pltpu.VMEM(v.shape, v.dtype) for v in results[:6]] + [dma((2, 24))],
        compiler_params=pltpu.CompilerParams(vmem_limit_bytes=64 * 2**20 - 2**16),
        name="finish",
    )(*results)
    return finished[:6], [v[0] for v in finished[6:]]


def finish_kernel(*refs):
    sources, targets, held, sems = refs[:6], refs[7:13], refs[19:25], refs[25]
    arrivals, departures = [], []
    for k, (source, middle, target) in enumerate(zip(sources, held, targets)):
        size = source.shape[0] // 4
        for n in range(4):
            rows = pl.ds(n * size, size)
            arrivals.append(
                pltpu.make_async_copy(source.at[rows], middle.at[rows], sems.at[0, 4 * k + n])
            )
            departures.append(
                pltpu.make_async_copy(middle.at[rows], target.at[rows], sems.at[1, 4 * k + n])
            )
    for copy in arrivals:
        copy.start()
    for k in range(6):
        refs[13 + k][...] = refs[6][k : k + 1]
    for arrival, departure in zip(arrivals, departures):
        arrival.wait()
        departure.start()
    for copy in departures:
        copy.wait()


def local(
    frames,
    cotangent,
    clip_len,
    ln1_gain,
    ln1_bias,
    w_qkv,
    w_out,
    scale_attn,
    ln2_gain,
    ln2_bias,
    w_gate_up,
    w_down,
    scale_mlp,
):
    row_count = frames.shape[0]
    seq_count = lax.axis_size("seq")
    tables = rotary_tables(row_count * seq_count)
    data_count = lax.axis_size("dp")
    if (data_count, seq_count, row_count) == (8, 4, TOK):
        sums, vector_total = layer(
            clip_len, frames, cotangent,
            (ln1_gain, ln1_bias, ln2_gain, ln2_bias, scale_attn, scale_mlp),
            w_qkv, w_out, w_gate_up, w_down, tables,
        )
        out_frames, input_grad, sum_qkv, sum_out, sum_gate_up, sum_down = sums
    else:
        normed_b, queries, kv, attended_t, branch = forward_attention(
            frames, clip_len, ln1_gain, ln1_bias, scale_attn, w_qkv, w_out, tables, seq_count
        )
        out_frames, normed_two_b, hidden_b, gate_up_b, mlp_grad, branch_grad, middle_grad, vec_two = (
            feed_forward(
                frames, cotangent, branch, ln2_gain, ln2_bias, scale_attn, scale_mlp, w_gate_up, w_down
            )
        )
        projected_grad, input_grad, vec_one = backward_attention(
            frames, clip_len, ln1_gain, queries, kv, branch_grad, middle_grad, w_qkv, w_out, tables,
            seq_count,
        )
        vector_grads = jnp.stack(
            [vec_one[0], vec_one[1], vec_two[3], vec_two[1], vec_two[2], vec_two[0]], 0
        )
        lefts = (normed_b, attended_t, normed_two_b, hidden_b)
        rights = (projected_grad, branch_grad, gate_up_b, mlp_grad)
        vector_total = lax.psum(vector_grads, ("dp", "seq"))
        sum_qkv, sum_out, sum_gate_up, sum_down = [
            lax.psum_scatter(
                to_blocks(contract_rows(left, right), data_count, seq_count),
                ("dp", "seq"),
                scatter_dimension=0,
                tiled=True,
            )[0]
            for left, right in zip(lefts, rights)
        ]
    return (
        out_frames,
        input_grad,
        vector_total[0],
        vector_total[1],
        sum_qkv,
        sum_out,
        vector_total[2],
        vector_total[3],
        vector_total[4],
        sum_gate_up,
        sum_down,
        vector_total[5],
    )


def solution(mesh):
    return jax.shard_map(
        local,
        mesh=mesh,
        in_specs=(
            P(("dp", "seq"), None),
            P(("dp", "seq"), None),
            P("dp", None),
            P(),
            P(),
            P(),
            P(),
            P(),
            P(),
            P(),
            P(),
            P(),
            P(),
        ),
        out_specs=(
            P(("dp", "seq"), None),
            P(("dp", "seq"), None),
            P(),
            P(),
            P("dp", "seq"),
            P("dp", "seq"),
            P(),
            P(),
            P(),
            P("dp", "seq"),
            P("dp", "seq"),
            P(),
        ),
        check_vma=False,
    )
```
